32 devices in a mesh: gx: 8 (over z, core), gy: 4 (over y, x).
Axes of the slice: x: 2, y: 2, z: 4, core: 2. Of those that a mesh axis runs over, the one named last changes fastest.
Arguments:
- velocity: float32 [4, 2, 512, 512], P(None, None, 'gx', 'gy'), may hold values from -6 to 6
- marker_cell: int32 [3, 8, 4, 2048], P(None, 'gx', 'gy'), may hold values from 0 to 511, as said below
- marker_frac: float32 [2, 8, 4, 2048], P(None, 'gx', 'gy'), may hold values from 0 to 1
- marker_force: float32 [2, 8, 4, 2048], P(None, 'gx', 'gy'), may hold values from -6 to 6
- fish_owner: int32 [48], replicated, may hold values from 0 to 31, as said below
Outputs:
- velocity_next: float32 [4, 2, 512, 512], P(None, None, 'gx', 'gy')
- marker_velocity: float32 [2, 8, 4, 2048], P(None, 'gx', 'gy')
The draws below stay inside these ranges and needn't reach their ends.
Inputs may be any that keep to these rules, and one draw needn't show every extreme that they name: `fish_owner`: device number i * 4 + j is the one at index i of gx and j of gy. No device holds more than 2 fish, and some device holds exactly 2. `marker_cell`: components are x cell, y cell and level. For the device at index i of gx and j of gy, every slot's x cell lies cyclically modulo 512 from i * 64 - 15 to (i + 1) * 64 + 13 and its y cell from j * 128 - 15 to (j + 1) * 128 + 13; on every device both ends are reached. A device holding k fish has their markers in slots 0 to k * 1024 - 1; its other slots are unused.
All inputs are finite; a program needn't handle non-finite values.
Results may differ from the reference program's by a relative error of at most 0.0025.
Values may be sent and summed in bfloat16 or wider, within the bound.
No kernel may reach another device: no remote copies, remote signals or barrier semaphores. Data moves between devices by JAX's collectives and lax.ppermute only.
A program may use at most 64 MiB of HBM per device.

```python
import jax
import jax.numpy as jnp
from jax import lax

CX = 64
CY = 128
LEV = 4
MARGIN = 16
FISH_MARK = 1024
FISH = 48
MARK_DEV = 2048
NX = 512
NY = 512
N_GX = 8
N_GY = 4


def draw_marker_cell(key, part):
    key_x, key_y, key_level = jax.random.split(key, 3)
    shape = (N_GX, N_GY, MARK_DEV)
    grid_row = lax.broadcasted_iota(jnp.int32, shape, 0)
    grid_col = lax.broadcasted_iota(jnp.int32, shape, 1)
    slot_index = lax.broadcasted_iota(jnp.int32, shape, 2)
    offset_x = jax.random.randint(key_x, shape, 1 - MARGIN, CX + MARGIN - 2)
    offset_x = jnp.where(slot_index == 0, 1 - MARGIN, jnp.where(slot_index == 1, CX + MARGIN - 3, offset_x))
    offset_y = jax.random.randint(key_y, shape, 1 - MARGIN, CY + MARGIN - 2)
    offset_y = jnp.where(slot_index == 1, 1 - MARGIN, jnp.where(slot_index == 0, CY + MARGIN - 3, offset_y))
    cell_x = jnp.mod(grid_row * CX + offset_x, NX)
    cell_y = jnp.mod(grid_col * CY + offset_y, NY)
    level = jax.random.randint(key_level, shape, 0, LEV)
    return jnp.stack([cell_x, cell_y, level], axis=0).astype(jnp.int32)


def draw_fish_owner(key, part):
    devices = N_GX * N_GY
    order = jax.random.permutation(key, devices)
    paired = max(FISH // 4, FISH - devices)
    fish_index = jnp.arange(FISH, dtype=jnp.int32)
    position = jnp.where(fish_index < 2 * paired, fish_index // 2, fish_index - paired)
    return order[position].astype(jnp.int32)


def level_of(rng, extent, shards, low, largest):
    gain, own = 1.0, jax.random.fold_in(rng, 6)
    for axis_at, parts in shards:
        steps = jnp.exp(jax.random.uniform(jax.random.fold_in(own, axis_at), (parts,), jnp.float32, low / len(shards), largest / len(shards)))
        gain = gain * jnp.repeat(steps, extent[axis_at] // parts).reshape([-1 if axis == axis_at else 1 for axis in range(len(extent))])
    return gain


def noise(key, dims, deviation, reach, cuts=(), held_as=jnp.bfloat16):
    factor_of = level_of(key, dims, cuts, -0.22, 0.18) if cuts else 1.0
    drawn = jax.random.normal(key, dims, jnp.float32) * deviation * factor_of
    return jnp.minimum(jnp.maximum(drawn, -reach), reach).astype(held_as)


def setup_inputs(seed: int = 0) -> dict:
    streams_of = jax.random.split(jax.random.key(seed), 6)
    return {
        "velocity": noise(streams_of[0], (LEV, 2, NX, NY), 1.0, 6.0, ((2, 8), (3, 4)), jnp.float32),
        "marker_cell": draw_marker_cell(jax.random.fold_in(streams_of[5], 71), 0),
        "marker_frac": jnp.clip(1.0 * jax.random.uniform(streams_of[2], (2, N_GX, N_GY, MARK_DEV), jnp.float32) ** level_of(streams_of[2], (2, N_GX, N_GY, MARK_DEV), ((1, 8), (2, 4)), -0.2, 0.2), 0.0, 1.0),
        "marker_force": noise(streams_of[3], (2, N_GX, N_GY, MARK_DEV), 1.0, 6.0, ((1, 8), (2, 4)), jnp.float32),
        "fish_owner": draw_fish_owner(jax.random.fold_in(streams_of[5], 71), 0),
    }


COURANT = 0.25
VISCOUS = 1.5


def kernel_weight(offset):
    return jnp.where(jnp.abs(offset) < 2.0, 0.25 * (1.0 + jnp.cos(0.5 * jnp.pi * offset)), 0.0)


def advect(padded):
    center = padded[:, :, 1:-1, 1:-1]
    speed_x = COURANT * center[:, 0:1]
    speed_y = COURANT * center[:, 1:2]
    back_x = center - padded[:, :, :-2, 1:-1]
    fore_x = padded[:, :, 2:, 1:-1] - center
    back_y = center - padded[:, :, 1:-1, :-2]
    fore_y = padded[:, :, 1:-1, 2:] - center
    change = jnp.maximum(speed_x, 0.0) * back_x + jnp.minimum(speed_x, 0.0) * fore_x
    change = change + jnp.maximum(speed_y, 0.0) * back_y + jnp.minimum(speed_y, 0.0) * fore_y
    return center - change


def smooth(source, padded):
    center = padded[:, :, 1:-1, 1:-1]
    above = jnp.concatenate([center[1:], center[-1:]], axis=0)
    below = jnp.concatenate([center[:1], center[:-1]], axis=0)
    summed = padded[:, :, 2:, 1:-1] + padded[:, :, :-2, 1:-1]
    summed = summed + padded[:, :, 1:-1, 2:] + padded[:, :, 1:-1, :-2]
    summed = summed + above + below
    return (source + VISCOUS * summed) / (1.0 + 6.0 * VISCOUS)


def wrap_pad(field):
    return jnp.pad(field, ((0, 0), (0, 0), (1, 1), (1, 1)), mode="wrap")


def reference(velocity, marker_cell, marker_frac, marker_force, fish_owner):
    levels, comps, extent_x, extent_y = velocity.shape
    devices = N_GX * N_GY
    slots = marker_cell.shape[3]
    owned = jnp.sum((fish_owner[:, None] == jnp.arange(devices, dtype=jnp.int32)[None, :]).astype(jnp.int32), axis=0)
    alive_count = (FISH_MARK * owned).reshape(N_GX, N_GY)
    alive_mask = (jnp.arange(slots, dtype=jnp.int32)[None, None, :] < alive_count[:, :, None]).astype(jnp.float32).reshape(-1)
    cell_x = marker_cell[0].reshape(-1)
    cell_y = marker_cell[1].reshape(-1)
    level = marker_cell[2].reshape(-1)
    frac_x = marker_frac[0].reshape(-1)
    frac_y = marker_frac[1].reshape(-1)
    force = marker_force.reshape(2, -1) * alive_mask[None, :]
    shifts = jnp.arange(-1, 3, dtype=jnp.int32)
    shift_float = shifts.astype(jnp.float32)
    weight_x = kernel_weight(shift_float[None, :] - frac_x[:, None])
    weight_y = kernel_weight(shift_float[None, :] - frac_y[:, None])
    weight_y = lax.optimization_barrier(weight_y.astype(jnp.bfloat16)).astype(jnp.float32)
    left = lax.optimization_barrier((force[:, :, None] * weight_x[None]).astype(jnp.bfloat16)).astype(jnp.float32)
    terms = left[:, :, :, None] * weight_y[None, :, None, :]
    index_x = jnp.mod(cell_x[:, None] + shifts[None, :], extent_x).astype(jnp.int32)
    index_y = jnp.mod(cell_y[:, None] + shifts[None, :], extent_y).astype(jnp.int32)
    component = jnp.arange(2, dtype=jnp.int32)
    forcing = jnp.zeros((levels, comps, extent_x, extent_y), jnp.float32)
    forcing = forcing.at[level[None, :, None, None], component[:, None, None, None], index_x[None, :, :, None], index_y[None, :, None, :]].add(terms)
    moved = velocity + forcing
    carried = advect(wrap_pad(moved))
    smoothed = carried
    for sweep_index in range(2):
        smoothed = smooth(carried, wrap_pad(smoothed))
    rounded = lax.optimization_barrier(smoothed.astype(jnp.bfloat16)).astype(jnp.float32)
    by_component = jnp.transpose(rounded, (1, 0, 2, 3))
    picked = by_component[:, level[:, None, None], index_x[:, :, None], index_y[:, None, :]]
    inner = jnp.sum(picked * weight_y[None, :, None, :], axis=3)
    sampled = jnp.sum(inner * weight_x[None], axis=2) * alive_mask[None, :]
    return smoothed, sampled.reshape(comps, N_GX, N_GY, slots)
```

```python
import functools

import jax
import jax.numpy as jnp
import numpy as np
from jax import lax
from jax.experimental import pallas as pl
from jax.experimental.pallas import tpu as pltpu
from jax.sharding import PartitionSpec as P

MARGIN = 16
FISH_MARK = 1024
HALO = 3
LANES = 128
COURANT = 0.25
VISCOUS = 1.5
ROWS = 8

REACH = MARGIN + HALO
PAD = -(-REACH // ROWS) * ROWS
STRIP = PAD + MARGIN
WIDE = REACH + MARGIN
EDGE_PER = LANES // (2 * MARGIN)
WIDE_PER = LANES // WIDE
WIDE_STEP = LANES // WIDE_PER


def half_turn(terms):
    nodes = 0.5 - 0.5 * np.cos(np.pi * (np.arange(64) + 0.5) / 64)
    square = nodes * nodes
    cosine = np.polynomial.polynomial.polyfit(square, np.cos(0.5 * np.pi * nodes), terms)
    sine = np.polynomial.polynomial.polyfit(square, np.sin(0.5 * np.pi * nodes) / nodes, terms)
    return [float(v) for v in cosine], [float(v) for v in sine]


COS_FIT, SIN_FIT = half_turn(6)


def horner(coefficients, value):
    total = jnp.full_like(value, coefficients[-1])
    for coefficient in coefficients[-2::-1]:
        total = total * value + coefficient
    return total


def four_weights(frac):
    square = frac * frac
    cosine = horner(COS_FIT, square)
    sine = frac * horner(SIN_FIT, square)
    return (0.25 - 0.25 * sine, 0.25 + 0.25 * cosine, 0.25 + 0.25 * sine, 0.25 - 0.25 * cosine)


def local_cell(cell, low, extent):
    offset = cell - low
    offset = jnp.where(offset < -MARGIN, offset + extent, offset)
    return jnp.where(offset >= extent - MARGIN, offset - extent, offset)


def placed_weights(first, rows, offset, weights):
    width = offset.shape[1]
    shift = lax.broadcasted_iota(jnp.int32, (rows, width), 0) + first - offset
    dense = jnp.where(shift == 2, weights[3], 0.0)
    dense = jnp.where(shift == 1, weights[2], dense)
    dense = jnp.where(shift == 0, weights[1], dense)
    return jnp.where(shift == -1, weights[0], dense)


def marker_weights(cell_ref, frac_ref, lanes, shape):
    cells_x, cells_y, extent_x, extent_y = shape
    low_x = lax.axis_index("gx") * cells_x
    low_y = lax.axis_index("gy") * cells_y
    offset_x = local_cell(cell_ref[0, 0, :, lanes], low_x, extent_x)
    offset_y = local_cell(cell_ref[1, 0, :, lanes], low_y, extent_y)
    weights_x = four_weights(frac_ref[0, 0, :, lanes])
    weights_y = four_weights(frac_ref[1, 0, :, lanes])
    dense_x = placed_weights(-MARGIN, cells_x + 2 * MARGIN, offset_x, weights_x)
    inner_y = placed_weights(0, cells_y + MARGIN, offset_y, weights_y)
    outer_y = placed_weights(-MARGIN, MARGIN, offset_y, weights_y)
    gap = jnp.zeros((LANES - 2 * MARGIN, offset_y.shape[1]), jnp.float32)
    dense_y = jnp.concatenate([inner_y, gap, outer_y], axis=0).astype(jnp.bfloat16)
    return dense_x, dense_y


def alive_count(fish_ref):
    me = lax.axis_index("gx") * lax.axis_size("gy") + lax.axis_index("gy")
    mine = jnp.where(fish_ref[...] == me, 1.0, 0.0)
    return FISH_MARK * jnp.sum(mine)


def alive_lanes(count, first, width):
    slot = lax.broadcasted_iota(jnp.int32, (1, width), 1) + first
    return jnp.where(slot.astype(jnp.float32) < count, 1.0, 0.0)


def spread_kernel(
    shape, chunk, fish_ref, velocity_ref, cell_ref, frac_ref, force_ref,
    grid_ref, up_ref, down_ref, left_ref, weight_ref,
):
    cells_x, cells_y, _, _ = shape
    levels, comps = velocity_ref.shape[:2]
    slots = cell_ref.shape[3]
    wide_x = cells_x + 2 * MARGIN
    count = alive_count(fish_ref)
    for first in range(0, slots, chunk):
        lanes = slice(first, first + chunk)
        dense_x, dense_y = marker_weights(cell_ref, frac_ref, lanes, shape)
        weight_ref[:, lanes] = dense_y
        alive = alive_lanes(count, first, chunk)
        level = cell_ref[2, 0, :, lanes]
        lefts = [
            ((force_ref[c, 0, :, lanes] * alive) * dense_x).astype(jnp.bfloat16)
            for c in range(comps)
        ]
        for l in range(levels):
            hot = jnp.broadcast_to(jnp.where(level == l, 1.0, 0.0), (16, chunk))
            hot = hot.astype(jnp.bfloat16)
            for c in range(comps):
                k = l * comps + c
                product = lefts[c].reshape(wide_x // 16, 16, chunk) * hot[None]
                left_ref[k * wide_x : (k + 1) * wide_x, lanes] = product.reshape(wide_x, chunk)
    total = lax.dot_general(
        left_ref[...], weight_ref[...], (((1,), (1,)), ((), ())),
        preferred_element_type=jnp.float32,
    )
    items = levels * comps
    grid_ref[...] = total.reshape(items, wide_x, cells_y + LANES)
    for k in range(items):
        grid_ref[k, MARGIN : MARGIN + cells_x, :cells_y] += velocity_ref[k // comps, k % comps]
    for out_ref, row in ((down_ref, 0), (up_ref, wide_x - STRIP)):
        parts = [grid_ref[k, row : row + STRIP, :cells_y] for k in range(items)]
        for group in range(0, items, EDGE_PER):
            edge = None
            for k in range(group, min(group + EDGE_PER, items)):
                piece = grid_ref[k, row : row + STRIP, cells_y:]
                if k > group:
                    piece = pltpu.roll(piece, 2 * MARGIN * (k - group), 1)
                    piece = piece + edge
                edge = piece
            parts.append(edge)
        out_ref[...] = jnp.concatenate(parts, axis=0).astype(jnp.bfloat16)


def lane_index(rows):
    return lax.broadcasted_iota(jnp.int32, (rows, LANES), 1)


def strip_parts(ref, k, items):
    lane = lane_index(STRIP)
    inner = ref[k * STRIP : (k + 1) * STRIP].astype(jnp.float32)
    row = (items + k // EDGE_PER) * STRIP
    edge = ref[row : row + STRIP].astype(jnp.float32)
    if k % EDGE_PER:
        edge = pltpu.roll(edge, LANES - 2 * MARGIN * (k % EDGE_PER), 1)
    edge = jnp.where((lane < MARGIN) | (lane >= LANES - MARGIN), edge, 0.0)
    return inner, edge


def joined(center, before, after):
    wide = center.shape[0]
    near = PAD - MARGIN
    overlap = STRIP - near
    return jnp.concatenate(
        [
            before[:near],
            center[:overlap] + before[near:],
            center[overlap : wide - overlap],
            center[wide - overlap :] + after[:overlap],
            after[overlap:],
        ],
        axis=0,
    )


def extended_rows(grid_ref, from_left, from_right, k, items, cells_y):
    before = strip_parts(from_left, k, items)
    after = strip_parts(from_right, k, items)
    inner = joined(grid_ref[k, :, :cells_y], before[0], after[0])
    edge = joined(grid_ref[k, :, cells_y:], before[1], after[1])
    return inner, edge


def pack_kernel(shape, grid_ref, from_left, from_right, up_ref, down_ref):
    cells_x, cells_y, _, _ = shape
    items = grid_ref.shape[0]
    rows = cells_x + 2 * PAD
    lane = lane_index(rows)
    for group in range(0, items, WIDE_PER):
        ups, downs = [], []
        for k in range(group, min(group + WIDE_PER, items)):
            inner, edge = extended_rows(grid_ref, from_left, from_right, k, items, cells_y)
            up = jnp.where(lane >= LANES - REACH, inner, jnp.where(lane < MARGIN, edge, 0.0))
            down = jnp.where(lane < REACH, inner, jnp.where(lane >= LANES - MARGIN, edge, 0.0))
            shift = WIDE_STEP * (k - group)
            ups.append(pltpu.roll(up, shift, 1) if shift else up)
            downs.append(pltpu.roll(down, shift, 1) if shift else down)
        row = group // WIDE_PER * rows
        up_ref[row : row + rows] = functools.reduce(jnp.add, ups).astype(jnp.bfloat16)
        down_ref[row : row + rows] = functools.reduce(jnp.add, downs).astype(jnp.bfloat16)


def shifted(inner, edge, lane):
    below_inner, below_edge = pltpu.roll(inner, 1, 1), pltpu.roll(edge, 1, 1)
    above_inner, above_edge = pltpu.roll(inner, LANES - 1, 1), pltpu.roll(edge, LANES - 1, 1)
    first, last = lane == 0, lane == LANES - 1
    below = (jnp.where(first, below_edge, below_inner), jnp.where(first, below_inner, below_edge))
    above = (jnp.where(last, above_edge, above_inner), jnp.where(last, above_inner, above_edge))
    return below, above


def finish_kernel(
    shape, chunk, fish_ref, cell_ref, frac_ref, grid_ref, left_x, right_x, left_y, right_y,
    next_ref, sampled_ref, moved_ref, carried_ref, sweep_ref, round_ref,
):
    cells_x, cells_y, _, _ = shape
    items = grid_ref.shape[0]
    levels, comps = next_ref.shape[:2]
    slots = cell_ref.shape[3]
    wide_x = cells_x + 2 * MARGIN
    rows = cells_x + 2 * PAD
    lane = lane_index(rows)
    for k in range(items):
        inner, edge = extended_rows(grid_ref, left_x, right_x, k, items, cells_y)
        row = k // WIDE_PER * rows
        before = left_y[row : row + rows].astype(jnp.float32)
        after = right_y[row : row + rows].astype(jnp.float32)
        shift = WIDE_STEP * (k % WIDE_PER)
        if shift:
            before = pltpu.roll(before, LANES - shift, 1)
            after = pltpu.roll(after, LANES - shift, 1)
        inner = inner + jnp.where(lane < MARGIN, before, 0.0)
        inner = inner + jnp.where(lane >= LANES - MARGIN, after, 0.0)
        edge = edge + jnp.where(lane >= LANES - REACH, before, 0.0)
        edge = edge + jnp.where(lane < REACH, after, 0.0)
        moved_ref[0, k, ROWS : ROWS + rows] = inner
        moved_ref[1, k, ROWS : ROWS + rows] = edge

    def around(ref, k, start, size, lane):
        center = tuple(ref[t, k, start : start + size] for t in range(2))
        back = tuple(ref[t, k, start - 1 : start - 1 + size] for t in range(2))
        fore = tuple(ref[t, k, start + 1 : start + 1 + size] for t in range(2))
        below, above = shifted(*center, lane)
        return center, back, fore, below, above

    size = ROWS
    small = lane_index(size)
    for start in range(ROWS, ROWS + rows, size):
        for l in range(levels):
            pieces = [around(moved_ref, l * comps + c, start, size, small) for c in range(comps)]
            for t in range(2):
                speed_x = COURANT * pieces[0][0][t]
                speed_y = COURANT * pieces[1][0][t]
                ahead_x, astern_x = jnp.maximum(speed_x, 0.0), jnp.minimum(speed_x, 0.0)
                ahead_y, astern_y = jnp.maximum(speed_y, 0.0), jnp.minimum(speed_y, 0.0)
                for c in range(comps):
                    center, back, fore, below, above = (part[t] for part in pieces[c])
                    change = ahead_x * (center - back) + astern_x * (fore - center)
                    change = change + ahead_y * (center - below) + astern_y * (above - center)
                    carried_ref[t, l * comps + c, start : start + size] = center - change

    scale = 1.0 / (1.0 + 6.0 * VISCOUS)

    def sweep(ref, start, size, lane):
        results = {}
        centers = {}
        for k in range(items):
            center, back, fore, below, above = around(ref, k, start, size, lane)
            centers[k] = center
            results[k] = [back[t] + fore[t] + below[t] + above[t] for t in range(2)]
        for k in range(items):
            higher = min(k // comps + 1, levels - 1) * comps + k % comps
            lower = max(k // comps - 1, 0) * comps + k % comps
            for t in range(2):
                summed = results[k][t] + centers[higher][t] + centers[lower][t]
                source = carried_ref[t, k, start : start + size]
                results[k][t] = scale * source + (VISCOUS * scale) * summed
        return results

    for start in range(ROWS, ROWS + rows, size):
        results = sweep(carried_ref, start, size, small)
        for k in range(items):
            for t in range(2):
                sweep_ref[t, k, start : start + size] = results[k][t]
    size = 2 * ROWS
    small = lane_index(size)
    near = PAD - MARGIN
    for row in range(0, wide_x, size):
        results = sweep(sweep_ref, ROWS + near + row, size, small)
        for k in range(items):
            place = slice(k * wide_x + row, k * wide_x + row + size)
            for t in range(2):
                lanes = slice(t * cells_y, t * cells_y + LANES)
                round_ref[place, lanes] = results[k][t].astype(jnp.bfloat16)
            if MARGIN <= row < MARGIN + cells_x:
                next_ref[k // comps, k % comps, row - MARGIN : row - MARGIN + size] = results[k][0]

    count = alive_count(fish_ref)
    for first in range(0, slots, chunk):
        lanes = slice(first, first + chunk)
        dense_x, dense_y = marker_weights(cell_ref, frac_ref, lanes, shape)
        alive = alive_lanes(count, first, chunk)
        level = cell_ref[2, 0, :, lanes]
        partial = jnp.dot(round_ref[...], dense_y, preferred_element_type=jnp.float32)
        partial = partial.reshape(levels, comps, wide_x, chunk)
        for c in range(comps):
            picked = partial[levels - 1, c]
            for l in range(levels - 2, -1, -1):
                picked = jnp.where(level == l, partial[l, c], picked)
            sampled = jnp.sum(picked * dense_x, axis=0, keepdims=True)
            sampled_ref[c, 0, :, lanes] = sampled * alive


def whole(count):
    return [pl.BlockSpec(memory_space=pltpu.VMEM)] * count


def exchange(up, down, axis):
    size = lax.axis_size(axis)
    forward = [(i, (i + 1) % size) for i in range(size)]
    backward = [(j, i) for i, j in forward]
    return lax.ppermute(up, axis, forward), lax.ppermute(down, axis, backward)


def body(velocity, marker_cell, marker_frac, marker_force, fish_owner):
    levels, comps, cells_x, cells_y = velocity.shape
    slots = marker_cell.shape[3]
    items = levels * comps
    shape = (cells_x, cells_y, cells_x * lax.axis_size("gx"), cells_y * lax.axis_size("gy"))
    wide_x = cells_x + 2 * MARGIN
    rows = cells_x + 2 * PAD
    chunk = min(512, slots)
    width = cells_y + LANES
    groups = -(-items // EDGE_PER)
    params = pltpu.CompilerParams(vmem_limit_bytes=40 * 1024 * 1024)
    edge_x = jax.ShapeDtypeStruct(((items + groups) * STRIP, LANES), jnp.bfloat16)
    grid, up, down = pl.pallas_call(
        functools.partial(spread_kernel, shape, chunk),
        out_shape=(
            jax.ShapeDtypeStruct((items, wide_x, width), jnp.float32),
            edge_x,
            edge_x,
        ),
        in_specs=whole(5),
        out_specs=tuple(whole(3)),
        scratch_shapes=[
            pltpu.VMEM((items * wide_x, slots), jnp.bfloat16),
            pltpu.VMEM((width, slots), jnp.bfloat16),
        ],
        compiler_params=params,
        name="spread",
    )(fish_owner, velocity, marker_cell, marker_frac, marker_force)
    left_x, right_x = exchange(up, down, "gx")
    edge_y = jax.ShapeDtypeStruct((-(-items // WIDE_PER) * rows, LANES), jnp.bfloat16)
    up, down = pl.pallas_call(
        functools.partial(pack_kernel, shape),
        out_shape=(edge_y, edge_y),
        in_specs=whole(3),
        out_specs=tuple(whole(2)),
        compiler_params=params,
        name="pack",
    )(grid, left_x, right_x)
    left_y, right_y = exchange(up, down, "gy")
    field = pltpu.VMEM((2, items, rows + 2 * ROWS, LANES), jnp.float32)
    return pl.pallas_call(
        functools.partial(finish_kernel, shape, chunk),
        out_shape=(
            jax.ShapeDtypeStruct(velocity.shape, jnp.float32),
            jax.ShapeDtypeStruct((comps, 1, 1, slots), jnp.float32),
        ),
        in_specs=whole(8),
        out_specs=tuple(whole(2)),
        scratch_shapes=[field, field, field, pltpu.VMEM((items * wide_x, width), jnp.bfloat16)],
        compiler_params=params,
        name="finish",
    )(fish_owner, marker_cell, marker_frac, grid, left_x, right_x, left_y, right_y)


def solution(mesh):
    placed = (
        P(None, None, "gx", "gy"),
        P(None, "gx", "gy", None),
        P(None, "gx", "gy", None),
        P(None, "gx", "gy", None),
        P(),
    )
    return jax.shard_map(
        body,
        mesh=mesh,
        in_specs=placed,
        out_specs=(P(None, None, "gx", "gy"), P(None, "gx", "gy", None)),
        check_vma=False,
    )
```

```python
import functools

import jax
import jax.numpy as jnp
import numpy as np
from jax import lax
from jax.experimental import pallas as pl
from jax.experimental.pallas import tpu as pltpu
from jax.sharding import PartitionSpec as P

MARGIN = 16
FISH_MARK = 1024
HALO = 3
LANES = 128
COURANT = 0.25
VISCOUS = 1.5
ROWS = 8

REACH = MARGIN + HALO
PAD = -(-REACH // ROWS) * ROWS
STRIP = PAD + MARGIN
SPAN = 2 * MARGIN
EDGE_PER = LANES // SPAN


def half_turn(terms):
    nodes = 0.5 - 0.5 * np.cos(np.pi * (np.arange(64) + 0.5) / 64)
    square = nodes * nodes
    cosine = np.polynomial.polynomial.polyfit(square, np.cos(0.5 * np.pi * nodes), terms)
    sine = np.polynomial.polynomial.polyfit(square, np.sin(0.5 * np.pi * nodes) / nodes, terms)
    return [float(v) for v in cosine], [float(v) for v in sine]


COS_FIT, SIN_FIT = half_turn(6)


def horner(coefficients, value):
    total = jnp.full_like(value, coefficients[-1])
    for coefficient in coefficients[-2::-1]:
        total = total * value + coefficient
    return total


def four_weights(frac):
    square = frac * frac
    cosine = horner(COS_FIT, square)
    sine = frac * horner(SIN_FIT, square)
    return (0.25 - 0.25 * sine, 0.25 + 0.25 * cosine, 0.25 + 0.25 * sine, 0.25 - 0.25 * cosine)


def local_cell(cell, low, extent):
    offset = cell - low
    offset = jnp.where(offset < -MARGIN, offset + extent, offset)
    return jnp.where(offset >= extent - MARGIN, offset - extent, offset)


def placed_weights(first, rows, offset, weights):
    width = offset.shape[1]
    shift = lax.broadcasted_iota(jnp.int32, (rows, width), 0) + first - offset
    dense = jnp.where(shift == 2, weights[3], 0.0)
    dense = jnp.where(shift == 1, weights[2], dense)
    dense = jnp.where(shift == 0, weights[1], dense)
    return jnp.where(shift == -1, weights[0], dense)


def marker_weights(cell_ref, frac_ref, lanes, shape):
    cells_x, cells_y, extent_x, extent_y = shape
    low_x = lax.axis_index("gx") * cells_x
    low_y = lax.axis_index("gy") * cells_y
    offset_x = local_cell(cell_ref[0, 0, :, lanes], low_x, extent_x)
    offset_y = local_cell(cell_ref[1, 0, :, lanes], low_y, extent_y)
    weights_x = four_weights(frac_ref[0, 0, :, lanes])
    weights_y = four_weights(frac_ref[1, 0, :, lanes])
    dense_x = placed_weights(-MARGIN, cells_x + 2 * MARGIN, offset_x, weights_x)
    inner_y = placed_weights(0, cells_y + MARGIN, offset_y, weights_y)
    outer_y = placed_weights(-MARGIN, MARGIN, offset_y, weights_y)
    gap = jnp.zeros((LANES - 2 * MARGIN, offset_y.shape[1]), jnp.float32)
    dense_y = jnp.concatenate([inner_y, gap, outer_y], axis=0).astype(jnp.bfloat16)
    return dense_x, dense_y


def alive_count(fish_ref):
    me = lax.axis_index("gx") * lax.axis_size("gy") + lax.axis_index("gy")
    mine = jnp.where(fish_ref[...] == me, 1.0, 0.0)
    return FISH_MARK * jnp.sum(mine)


def alive_lanes(count, first, width):
    slot = lax.broadcasted_iota(jnp.int32, (1, width), 1) + first
    return jnp.where(slot.astype(jnp.float32) < count, 1.0, 0.0)


def is_even(axis):
    return lax.axis_index(axis) % 2 == 0


def spread_kernel(
    shape, chunk, fish_hbm, velocity_hbm, cell_hbm, frac_hbm, force_hbm,
    grid_ref, near_ref, far_ref, dense_x_ref, dense_y_ref, level_ref,
    left_ref, fish_ref, velocity_ref, cell_ref, frac_ref, force_ref, sems,
):
    pairs = (
        (cell_hbm, cell_ref), (frac_hbm, frac_ref), (fish_hbm, fish_ref),
        (force_hbm, force_ref), (velocity_hbm, velocity_ref),
    )
    copies = [pltpu.make_async_copy(a, b, sems.at[i]) for i, (a, b) in enumerate(pairs)]
    for copy in copies:
        copy.start()
    for copy in copies[:-1]:
        copy.wait()
    cells_x, cells_y, _, _ = shape
    levels, comps = velocity_ref.shape[:2]
    slots = cell_ref.shape[3]
    wide_x = cells_x + SPAN
    count = alive_count(fish_ref)
    level_ref[...] = cell_ref[2, 0]
    for first in range(0, slots, chunk):
        lanes = slice(first, first + chunk)
        dense_x, dense_y = marker_weights(cell_ref, frac_ref, lanes, shape)
        dense_x = dense_x * alive_lanes(count, first, chunk)
        dense_x_ref[:, lanes] = dense_x
        dense_y_ref[:, lanes] = dense_y
        level = cell_ref[2, 0, :, lanes]
        lefts = [
            (force_ref[c, 0, :, lanes] * dense_x).astype(jnp.bfloat16) for c in range(comps)
        ]
        for l in range(levels):
            hot = jnp.broadcast_to(jnp.where(level == l, 1.0, 0.0), (16, chunk))
            hot = hot.astype(jnp.bfloat16)
            for c in range(comps):
                k = l * comps + c
                product = lefts[c].reshape(wide_x // 16, 16, chunk) * hot[None]
                left_ref[k * wide_x : (k + 1) * wide_x, lanes] = product.reshape(wide_x, chunk)
    total = lax.dot_general(
        left_ref[...], dense_y_ref[...], (((1,), (1,)), ((), ())),
        preferred_element_type=jnp.float32,
    )
    items = levels * comps
    grid_ref[...] = total.reshape(items, wide_x, cells_y + LANES)
    copies[-1].wait()
    for k in range(items):
        grid_ref[k, MARGIN : MARGIN + cells_x, :cells_y] += velocity_ref[k // comps, k % comps]
    even = is_even("gx")
    high = wide_x - STRIP
    for out_ref, row in ((far_ref, jnp.where(even, 0, high)), (near_ref, jnp.where(even, high, 0))):
        place = pl.ds(pl.multiple_of(row, ROWS), STRIP)
        parts = [grid_ref[k, place, :cells_y] for k in range(items)]
        for group in range(0, items, EDGE_PER):
            edges = []
            for k in range(group, min(group + EDGE_PER, items)):
                edges.append(rolled(grid_ref[k, place, cells_y:], SPAN * (k - group)))
            parts.append(functools.reduce(jnp.add, edges))
        out_ref[...] = jnp.concatenate(parts, axis=0).astype(jnp.bfloat16)


def rolled(value, shift):
    shift = shift % LANES
    return pltpu.roll(value, shift, 1) if shift else value


def lane_index(rows):
    return lax.broadcasted_iota(jnp.int32, (rows, LANES), 1)


def strip_parts(near, far, k, items):
    lane = lane_index(STRIP)
    even = is_even("gx")
    row = (items + k // EDGE_PER) * STRIP
    inners, edges = [], []
    for ref in (near, far):
        inners.append(ref[k * STRIP : (k + 1) * STRIP].astype(jnp.float32))
        edge = rolled(ref[row : row + STRIP].astype(jnp.float32), -SPAN * (k % EDGE_PER))
        edges.append(jnp.where((lane < MARGIN) | (lane >= LANES - MARGIN), edge, 0.0))
    before = (jnp.where(even, inners[1], inners[0]), jnp.where(even, edges[1], edges[0]))
    after = (jnp.where(even, inners[0], inners[1]), jnp.where(even, edges[0], edges[1]))
    return before, after


def joined(center, before, after):
    wide = center.shape[0]
    near = PAD - MARGIN
    overlap = STRIP - near
    return jnp.concatenate(
        [
            before[:near],
            center[:overlap] + before[near:],
            center[overlap : wide - overlap],
            center[wide - overlap :] + after[:overlap],
            after[overlap:],
        ],
        axis=0,
    )


def extended_rows(grid_ref, near, far, k, items, cells_y):
    before, after = strip_parts(near, far, k, items)
    inner = joined(grid_ref[k, :, :cells_y], before[0], after[0])
    edge = joined(grid_ref[k, :, cells_y:], before[1], after[1])
    return inner, edge


def folds(rows):
    return [(row, min(SPAN, rows - row)) for row in range(0, rows, SPAN)]


def pack_kernel(shape, grid_ref, near_x, far_x, near_ref, far_ref):
    cells_x, cells_y, _, _ = shape
    items = grid_ref.shape[0]
    groups = -(-items // EDGE_PER)
    rows = cells_x + 2 * PAD
    lane = lane_index(rows)
    even = is_even("gy")
    mains = [[[], []] for _ in range(groups)]
    halos = [[], []]
    for k in range(items):
        inner, edge = extended_rows(grid_ref, near_x, far_x, k, items, cells_y)
        up = jnp.where(lane >= LANES - MARGIN, inner, jnp.where(lane < MARGIN, edge, 0.0))
        down = jnp.where(lane < MARGIN, inner, jnp.where(lane >= LANES - MARGIN, edge, 0.0))
        up_halo = (lane >= LANES - REACH) & (lane < LANES - MARGIN)
        down_halo = (lane >= MARGIN) & (lane < REACH)
        send = (jnp.where(even, up, down), jnp.where(even, down, up))
        halo = (
            rolled(jnp.where(up_halo, inner, 0.0), REACH + HALO * k),
            rolled(jnp.where(down_halo, inner, 0.0), HALO * k - MARGIN),
        )
        halo = (jnp.where(even, halo[0], halo[1]), jnp.where(even, halo[1], halo[0]))
        for side in range(2):
            mains[k // EDGE_PER][side].append(rolled(send[side], SPAN * (k % EDGE_PER)))
            halos[side].append(halo[side])
    for side, out_ref in enumerate((near_ref, far_ref)):
        for group in range(groups):
            total = functools.reduce(jnp.add, mains[group][side])
            out_ref[group * rows : (group + 1) * rows] = total.astype(jnp.bfloat16)
        total = functools.reduce(jnp.add, halos[side])
        folded = rolled(total[:SPAN], 0)
        for index, (row, size) in enumerate(folds(rows)[1:]):
            piece = rolled(total[row : row + size], SPAN * (index + 1))
            if size < SPAN:
                gap = jnp.zeros((SPAN - size, LANES), jnp.float32)
                piece = jnp.concatenate([piece, gap], axis=0)
            folded = folded + piece
        out_ref[groups * rows : groups * rows + SPAN] = folded.astype(jnp.bfloat16)


def unfolded(ref, rows, groups):
    folded = ref[groups * rows : groups * rows + SPAN].astype(jnp.float32)
    return jnp.concatenate(
        [rolled(folded, -SPAN * index)[:size] for index, (_, size) in enumerate(folds(rows))],
        axis=0,
    )


def shifted(inner, edge, lane):
    below_inner, below_edge = pltpu.roll(inner, 1, 1), pltpu.roll(edge, 1, 1)
    above_inner, above_edge = pltpu.roll(inner, LANES - 1, 1), pltpu.roll(edge, LANES - 1, 1)
    first, last = lane == 0, lane == LANES - 1
    below = (jnp.where(first, below_edge, below_inner), jnp.where(first, below_inner, below_edge))
    above = (jnp.where(last, above_edge, above_inner), jnp.where(last, above_inner, above_edge))
    return below, above


def finish_kernel(
    shape, chunk, dense_x_ref, dense_y_ref, level_ref, grid_ref, near_x, far_x, near_y, far_y,
    next_ref, sampled_ref, moved_ref, carried_ref, sweep_ref, round_ref,
):
    cells_x, cells_y, _, _ = shape
    items = grid_ref.shape[0]
    groups = -(-items // EDGE_PER)
    levels, comps = next_ref.shape[:2]
    slots = level_ref.shape[1]
    wide_x = cells_x + SPAN
    rows = cells_x + 2 * PAD
    lane = lane_index(rows)
    even = is_even("gy")
    near_halo, far_halo = unfolded(near_y, rows, groups), unfolded(far_y, rows, groups)
    before_halo = jnp.where(even, far_halo, near_halo)
    after_halo = jnp.where(even, near_halo, far_halo)
    for k in range(items):
        inner, edge = extended_rows(grid_ref, near_x, far_x, k, items, cells_y)
        row = k // EDGE_PER * rows
        near = near_y[row : row + rows].astype(jnp.float32)
        far = far_y[row : row + rows].astype(jnp.float32)
        shift = -SPAN * (k % EDGE_PER)
        before = rolled(jnp.where(even, far, near), shift)
        after = rolled(jnp.where(even, near, far), shift)
        low = rolled(before_halo, -REACH - HALO * k)
        high = rolled(after_halo, MARGIN - HALO * k)
        inner = inner + jnp.where(lane < MARGIN, before, 0.0)
        inner = inner + jnp.where(lane >= LANES - MARGIN, after, 0.0)
        edge = edge + jnp.where(lane >= LANES - MARGIN, before, 0.0)
        edge = edge + jnp.where(lane < MARGIN, after, 0.0)
        edge = jnp.where((lane >= LANES - REACH) & (lane < LANES - MARGIN), low, edge)
        edge = jnp.where((lane >= MARGIN) & (lane < REACH), high, edge)
        moved_ref[0, k, ROWS : ROWS + rows] = inner
        moved_ref[1, k, ROWS : ROWS + rows] = edge

    def around(ref, k, start, size, lane):
        center = tuple(ref[t, k, start : start + size] for t in range(2))
        back = tuple(ref[t, k, start - 1 : start - 1 + size] for t in range(2))
        fore = tuple(ref[t, k, start + 1 : start + 1 + size] for t in range(2))
        below, above = shifted(*center, lane)
        return center, back, fore, below, above

    size = ROWS
    small = lane_index(size)
    for start in range(ROWS, ROWS + rows, size):
        for l in range(levels):
            pieces = [around(moved_ref, l * comps + c, start, size, small) for c in range(comps)]
            for t in range(2):
                speed_x = COURANT * pieces[0][0][t]
                speed_y = COURANT * pieces[1][0][t]
                ahead_x, astern_x = jnp.maximum(speed_x, 0.0), jnp.minimum(speed_x, 0.0)
                ahead_y, astern_y = jnp.maximum(speed_y, 0.0), jnp.minimum(speed_y, 0.0)
                for c in range(comps):
                    center, back, fore, below, above = (part[t] for part in pieces[c])
                    change = ahead_x * (center - back) + astern_x * (fore - center)
                    change = change + ahead_y * (center - below) + astern_y * (above - center)
                    carried_ref[t, l * comps + c, start : start + size] = center - change

    scale = 1.0 / (1.0 + 6.0 * VISCOUS)

    def sweep(ref, start, size, lane):
        results = {}
        centers = {}
        for k in range(items):
            center, back, fore, below, above = around(ref, k, start, size, lane)
            centers[k] = center
            results[k] = [back[t] + fore[t] + below[t] + above[t] for t in range(2)]
        for k in range(items):
            higher = min(k // comps + 1, levels - 1) * comps + k % comps
            lower = max(k // comps - 1, 0) * comps + k % comps
            for t in range(2):
                summed = results[k][t] + centers[higher][t] + centers[lower][t]
                source = carried_ref[t, k, start : start + size]
                results[k][t] = scale * source + (VISCOUS * scale) * summed
        return results

    for start in range(ROWS, ROWS + rows, size):
        results = sweep(carried_ref, start, size, small)
        for k in range(items):
            for t in range(2):
                sweep_ref[t, k, start : start + size] = results[k][t]
    size = 2 * ROWS
    small = lane_index(size)
    near = PAD - MARGIN
    for row in range(0, wide_x, size):
        results = sweep(sweep_ref, ROWS + near + row, size, small)
        for k in range(items):
            place = slice(k * wide_x + row, k * wide_x + row + size)
            for t in range(2):
                lanes = slice(t * cells_y, t * cells_y + LANES)
                round_ref[place, lanes] = results[k][t].astype(jnp.bfloat16)
            if MARGIN <= row < MARGIN + cells_x:
                next_ref[k // comps, k % comps, row - MARGIN : row - MARGIN + size] = results[k][0]

    for first in range(0, slots, chunk):
        lanes = slice(first, first + chunk)
        level = level_ref[:, lanes]
        partial = jnp.dot(
            round_ref[...], dense_y_ref[:, lanes], preferred_element_type=jnp.float32
        )
        partial = partial.reshape(levels, comps, wide_x, chunk)
        for c in range(comps):
            picked = partial[levels - 1, c]
            for l in range(levels - 2, -1, -1):
                picked = jnp.where(level == l, partial[l, c], picked)
            sampled_ref[c, 0, :, lanes] = jnp.sum(
                picked * dense_x_ref[:, lanes], axis=0, keepdims=True
            )


def whole(count):
    return [pl.BlockSpec(memory_space=pltpu.VMEM)] * count


def exchange(near, far, axis):
    size = lax.axis_size(axis)
    if size % 2:
        raise ValueError("odd axis")
    near_pairs = [(i, i ^ 1) for i in range(size)]
    far_pairs = [(i, (i - 1 if i % 2 == 0 else i + 1) % size) for i in range(size)]
    return lax.ppermute(near, axis, near_pairs), lax.ppermute(far, axis, far_pairs)


def body(velocity, marker_cell, marker_frac, marker_force, fish_owner):
    levels, comps, cells_x, cells_y = velocity.shape
    slots = marker_cell.shape[3]
    items = levels * comps
    shape = (cells_x, cells_y, cells_x * lax.axis_size("gx"), cells_y * lax.axis_size("gy"))
    wide_x = cells_x + SPAN
    rows = cells_x + 2 * PAD
    chunk = min(512, slots)
    width = cells_y + LANES
    groups = -(-items // EDGE_PER)
    params = pltpu.CompilerParams(vmem_limit_bytes=40 * 1024 * 1024)
    edge_x = jax.ShapeDtypeStruct(((items + groups) * STRIP, LANES), jnp.bfloat16)
    arrays = (fish_owner, velocity, marker_cell, marker_frac, marker_force)
    grid, near, far, dense_x, dense_y, level = pl.pallas_call(
        functools.partial(spread_kernel, shape, chunk),
        out_shape=(
            jax.ShapeDtypeStruct((items, wide_x, width), jnp.float32),
            edge_x,
            edge_x,
            jax.ShapeDtypeStruct((wide_x, slots), jnp.float32),
            jax.ShapeDtypeStruct((width, slots), jnp.bfloat16),
            jax.ShapeDtypeStruct((1, slots), jnp.int32),
        ),
        in_specs=[pl.BlockSpec(memory_space=pltpu.HBM)] * 5,
        out_specs=tuple(whole(6)),
        scratch_shapes=[pltpu.VMEM((items * wide_x, slots), jnp.bfloat16)]
        + [pltpu.VMEM(a.shape, a.dtype) for a in arrays]
        + [pltpu.SemaphoreType.DMA((5,))],
        compiler_params=params,
        name="spread",
    )(*(pltpu.with_memory_space_constraint(a, pltpu.HBM) for a in arrays))
    near_x, far_x = exchange(near, far, "gx")
    edge_y = jax.ShapeDtypeStruct((groups * rows + SPAN, LANES), jnp.bfloat16)
    near, far = pl.pallas_call(
        functools.partial(pack_kernel, shape),
        out_shape=(edge_y, edge_y),
        in_specs=whole(3),
        out_specs=tuple(whole(2)),
        compiler_params=params,
        name="pack",
    )(grid, near_x, far_x)
    near_y, far_y = exchange(near, far, "gy")
    field = pltpu.VMEM((2, items, rows + 2 * ROWS, LANES), jnp.float32)
    return pl.pallas_call(
        functools.partial(finish_kernel, shape, chunk),
        out_shape=(
            jax.ShapeDtypeStruct(velocity.shape, jnp.float32),
            jax.ShapeDtypeStruct((comps, 1, 1, slots), jnp.float32),
        ),
        in_specs=whole(8),
        out_specs=tuple(whole(2)),
        scratch_shapes=[field, field, field, pltpu.VMEM((items * wide_x, width), jnp.bfloat16)],
        compiler_params=params,
        name="finish",
    )(dense_x, dense_y, level, grid, near_x, far_x, near_y, far_y)


def solution(mesh):
    placed = (
        P(None, None, "gx", "gy"),
        P(None, "gx", "gy", None),
        P(None, "gx", "gy", None),
        P(None, "gx", "gy", None),
        P(),
    )
    return jax.shard_map(
        body,
        mesh=mesh,
        in_specs=placed,
        out_specs=(P(None, None, "gx", "gy"), P(None, "gx", "gy", None)),
        check_vma=False,
    )
```

```python
import functools

import jax
import jax.numpy as jnp
import numpy as np
from jax import lax
from jax.experimental import pallas as pl
from jax.experimental.pallas import tpu as pltpu
from jax.sharding import PartitionSpec as P

MARGIN = 16
FISH_MARK = 1024
HALO = 3
LANES = 128
COURANT = 0.25
VISCOUS = 1.5
ROWS = 8

REACH = MARGIN + HALO
PAD = -(-REACH // ROWS) * ROWS
STRIP = PAD + MARGIN
SPAN = 2 * MARGIN
EDGE_PER = LANES // SPAN


def half_turn(terms):
    nodes = 0.5 - 0.5 * np.cos(np.pi * (np.arange(64) + 0.5) / 64)
    square = nodes * nodes
    cosine = np.polynomial.polynomial.polyfit(square, np.cos(0.5 * np.pi * nodes), terms)
    sine = np.polynomial.polynomial.polyfit(square, np.sin(0.5 * np.pi * nodes) / nodes, terms)
    return [float(v) for v in cosine], [float(v) for v in sine]


COS_FIT, SIN_FIT = half_turn(6)


def horner(coefficients, value):
    total = jnp.full_like(value, coefficients[-1])
    for coefficient in coefficients[-2::-1]:
        total = total * value + coefficient
    return total


def four_weights(frac):
    square = frac * frac
    cosine = horner(COS_FIT, square)
    sine = frac * horner(SIN_FIT, square)
    return (0.25 - 0.25 * sine, 0.25 + 0.25 * cosine, 0.25 + 0.25 * sine, 0.25 - 0.25 * cosine)


def local_cell(cell, low, extent):
    offset = cell - low
    offset = jnp.where(offset < -MARGIN, offset + extent, offset)
    return jnp.where(offset >= extent - MARGIN, offset - extent, offset)


def placed_weights(first, rows, offset, weights):
    width = offset.shape[1]
    shift = lax.broadcasted_iota(jnp.int32, (rows, width), 0) + first - offset
    dense = jnp.where(shift == 2, weights[3], 0.0)
    dense = jnp.where(shift == 1, weights[2], dense)
    dense = jnp.where(shift == 0, weights[1], dense)
    return jnp.where(shift == -1, weights[0], dense)


def marker_weights(cell_ref, frac_ref, lanes, shape):
    cells_x, cells_y, extent_x, extent_y = shape
    low_x = lax.axis_index("gx") * cells_x
    low_y = lax.axis_index("gy") * cells_y
    offset_x = local_cell(cell_ref[0, 0, :, lanes], low_x, extent_x)
    offset_y = local_cell(cell_ref[1, 0, :, lanes], low_y, extent_y)
    weights_x = four_weights(frac_ref[0, 0, :, lanes])
    weights_y = four_weights(frac_ref[1, 0, :, lanes])
    dense_x = placed_weights(-MARGIN, cells_x + 2 * MARGIN, offset_x, weights_x)
    inner_y = placed_weights(0, cells_y + MARGIN, offset_y, weights_y)
    outer_y = placed_weights(-MARGIN, MARGIN, offset_y, weights_y)
    gap = jnp.zeros((LANES - 2 * MARGIN, offset_y.shape[1]), jnp.float32)
    dense_y = jnp.concatenate([inner_y, gap, outer_y], axis=0).astype(jnp.bfloat16)
    return dense_x, dense_y


def alive_count(fish_ref):
    me = lax.axis_index("gx") * lax.axis_size("gy") + lax.axis_index("gy")
    mine = jnp.where(fish_ref[...] == me, 1.0, 0.0)
    return FISH_MARK * jnp.sum(mine)


def alive_lanes(count, first, width):
    slot = lax.broadcasted_iota(jnp.int32, (1, width), 1) + first
    return jnp.where(slot.astype(jnp.float32) < count, 1.0, 0.0)


def is_even(axis):
    return lax.axis_index(axis) % 2 == 0


def spread_kernel(
    shape, chunk, fish_hbm, velocity_hbm, cell_hbm, frac_hbm, force_hbm,
    grid_ref, near_ref, far_ref, dense_x_ref, dense_y_ref, level_ref,
    left_ref, fish_ref, velocity_ref, cell_ref, frac_ref, force_ref, sems,
):
    pairs = (
        (cell_hbm, cell_ref), (frac_hbm, frac_ref), (fish_hbm, fish_ref),
        (force_hbm, force_ref), (velocity_hbm, velocity_ref),
    )
    copies = [pltpu.make_async_copy(a, b, sems.at[i]) for i, (a, b) in enumerate(pairs)]
    for copy in copies:
        copy.start()
    for copy in copies[:-1]:
        copy.wait()
    cells_x, cells_y, _, _ = shape
    levels, comps = velocity_ref.shape[:2]
    slots = cell_ref.shape[3]
    wide_x = cells_x + SPAN
    count = alive_count(fish_ref)
    level_ref[...] = cell_ref[2, 0]
    for first in range(0, slots, chunk):
        lanes = slice(first, first + chunk)
        dense_x, dense_y = marker_weights(cell_ref, frac_ref, lanes, shape)
        dense_x = dense_x * alive_lanes(count, first, chunk)
        dense_x_ref[:, lanes] = dense_x
        dense_y_ref[:, lanes] = dense_y
        level = cell_ref[2, 0, :, lanes]
        lefts = [
            (force_ref[c, 0, :, lanes] * dense_x).astype(jnp.bfloat16) for c in range(comps)
        ]
        for l in range(levels):
            hot = jnp.broadcast_to(jnp.where(level == l, 1.0, 0.0), (16, chunk))
            hot = hot.astype(jnp.bfloat16)
            for c in range(comps):
                k = l * comps + c
                product = lefts[c].reshape(wide_x // 16, 16, chunk) * hot[None]
                left_ref[k * wide_x : (k + 1) * wide_x, lanes] = product.reshape(wide_x, chunk)
    total = lax.dot_general(
        left_ref[...], dense_y_ref[...], (((1,), (1,)), ((), ())),
        preferred_element_type=jnp.float32,
    )
    items = levels * comps
    grid_ref[...] = total.reshape(items, wide_x, cells_y + LANES)
    copies[-1].wait()
    for k in range(items):
        grid_ref[k, MARGIN : MARGIN + cells_x, :cells_y] += velocity_ref[k // comps, k % comps]
    even = is_even("gx")
    high = wide_x - STRIP
    for out_ref, row in ((far_ref, jnp.where(even, 0, high)), (near_ref, jnp.where(even, high, 0))):
        place = pl.ds(pl.multiple_of(row, ROWS), STRIP)
        parts = [grid_ref[k, place, :cells_y] for k in range(items)]
        for group in range(0, items, EDGE_PER):
            edges = []
            for k in range(group, min(group + EDGE_PER, items)):
                edges.append(rolled(grid_ref[k, place, cells_y:], SPAN * (k - group)))
            parts.append(functools.reduce(jnp.add, edges))
        out_ref[...] = jnp.concatenate(parts, axis=0).astype(jnp.bfloat16)


def rolled(value, shift):
    shift = shift % LANES
    return pltpu.roll(value, shift, 1) if shift else value


def lane_index(rows):
    return lax.broadcasted_iota(jnp.int32, (rows, LANES), 1)


def strip_parts(near, far, k, items):
    lane = lane_index(STRIP)
    even = is_even("gx")
    row = (items + k // EDGE_PER) * STRIP
    inners, edges = [], []
    for ref in (near, far):
        inners.append(ref[k * STRIP : (k + 1) * STRIP].astype(jnp.float32))
        edge = rolled(ref[row : row + STRIP].astype(jnp.float32), -SPAN * (k % EDGE_PER))
        edges.append(jnp.where((lane < MARGIN) | (lane >= LANES - MARGIN), edge, 0.0))
    before = (jnp.where(even, inners[1], inners[0]), jnp.where(even, edges[1], edges[0]))
    after = (jnp.where(even, inners[0], inners[1]), jnp.where(even, edges[0], edges[1]))
    return before, after


def joined(center, before, after):
    wide = center.shape[0]
    near = PAD - MARGIN
    overlap = STRIP - near
    return jnp.concatenate(
        [
            before[:near],
            center[:overlap] + before[near:],
            center[overlap : wide - overlap],
            center[wide - overlap :] + after[:overlap],
            after[overlap:],
        ],
        axis=0,
    )


def extended_rows(grid_ref, near, far, k, items, cells_y):
    before, after = strip_parts(near, far, k, items)
    inner = joined(grid_ref[k, :, :cells_y], before[0], after[0])
    edge = joined(grid_ref[k, :, cells_y:], before[1], after[1])
    return inner, edge


def folds(rows):
    return [(row, min(SPAN, rows - row)) for row in range(0, rows, SPAN)]


def pack_kernel(shape, grid_ref, near_x, far_x, near_ref, far_ref):
    cells_x, cells_y, _, _ = shape
    items = grid_ref.shape[0]
    groups = -(-items // EDGE_PER)
    rows = cells_x + 2 * PAD
    lane = lane_index(rows)
    even = is_even("gy")
    mains = [[[], []] for _ in range(groups)]
    halos = [[], []]
    for k in range(items):
        inner, edge = extended_rows(grid_ref, near_x, far_x, k, items, cells_y)
        up = jnp.where(lane >= LANES - MARGIN, inner, jnp.where(lane < MARGIN, edge, 0.0))
        down = jnp.where(lane < MARGIN, inner, jnp.where(lane >= LANES - MARGIN, edge, 0.0))
        up_halo = (lane >= LANES - REACH) & (lane < LANES - MARGIN)
        down_halo = (lane >= MARGIN) & (lane < REACH)
        send = (jnp.where(even, up, down), jnp.where(even, down, up))
        halo = (
            rolled(jnp.where(up_halo, inner, 0.0), REACH + HALO * k),
            rolled(jnp.where(down_halo, inner, 0.0), HALO * k - MARGIN),
        )
        halo = (jnp.where(even, halo[0], halo[1]), jnp.where(even, halo[1], halo[0]))
        for side in range(2):
            mains[k // EDGE_PER][side].append(rolled(send[side], SPAN * (k % EDGE_PER)))
            halos[side].append(halo[side])
    for side, out_ref in enumerate((near_ref, far_ref)):
        for group in range(groups):
            total = functools.reduce(jnp.add, mains[group][side])
            out_ref[group * rows : (group + 1) * rows] = total.astype(jnp.bfloat16)
        total = functools.reduce(jnp.add, halos[side])
        folded = rolled(total[:SPAN], 0)
        for index, (row, size) in enumerate(folds(rows)[1:]):
            piece = rolled(total[row : row + size], SPAN * (index + 1))
            if size < SPAN:
                gap = jnp.zeros((SPAN - size, LANES), jnp.float32)
                piece = jnp.concatenate([piece, gap], axis=0)
            folded = folded + piece
        out_ref[groups * rows : groups * rows + SPAN] = folded.astype(jnp.bfloat16)


def unfolded(ref, rows, groups):
    folded = ref[groups * rows : groups * rows + SPAN].astype(jnp.float32)
    return jnp.concatenate(
        [rolled(folded, -SPAN * index)[:size] for index, (_, size) in enumerate(folds(rows))],
        axis=0,
    )


def around(ref, k, start, size):
    center = ref[k, start : start + size]
    back = ref[k, start - 1 : start - 1 + size]
    fore = ref[k, start + 1 : start + 1 + size]
    return center, back, fore, rolled(center, 1), rolled(center, -1)


def advect(moved_ref, carried_ref, levels, comps, rows):
    for start in range(ROWS, ROWS + rows, ROWS):
        for l in range(levels):
            pieces = [around(moved_ref, l * comps + c, start, ROWS) for c in range(comps)]
            speed_x, speed_y = COURANT * pieces[0][0], COURANT * pieces[1][0]
            ahead_x, astern_x = jnp.maximum(speed_x, 0.0), jnp.minimum(speed_x, 0.0)
            ahead_y, astern_y = jnp.maximum(speed_y, 0.0), jnp.minimum(speed_y, 0.0)
            for c in range(comps):
                center, back, fore, below, above = pieces[c]
                change = ahead_x * (center - back) + astern_x * (fore - center)
                change = change + ahead_y * (center - below) + astern_y * (above - center)
                carried_ref[l * comps + c, start : start + ROWS] = center - change


def sweep(ref, carried_ref, levels, comps, start, size):
    scale = 1.0 / (1.0 + 6.0 * VISCOUS)
    centers, results = [], []
    for k in range(levels * comps):
        center, back, fore, below, above = around(ref, k, start, size)
        centers.append(center)
        results.append(back + fore + below + above)
    for k in range(levels * comps):
        higher = min(k // comps + 1, levels - 1) * comps + k % comps
        lower = max(k // comps - 1, 0) * comps + k % comps
        summed = results[k] + centers[higher] + centers[lower]
        source = carried_ref[k, start : start + size]
        results[k] = scale * source + (VISCOUS * scale) * summed
    return results


def first_steps(moved_ref, carried_ref, sweep_ref, levels, comps, rows):
    advect(moved_ref, carried_ref, levels, comps, rows)
    for start in range(ROWS, ROWS + rows, ROWS):
        results = sweep(carried_ref, carried_ref, levels, comps, start, ROWS)
        for k in range(levels * comps):
            sweep_ref[k, start : start + ROWS] = results[k]


RIM = REACH + HALO
HALF = LANES // 2


def inner_kernel(
    shape, levels, grid_ref, near_x, far_x, inner_ref, rim_ref, moved_ref, carried_ref, sweep_ref,
):
    cells_x, cells_y, _, _ = shape
    items = grid_ref.shape[0]
    comps = items // levels
    wide_x = cells_x + SPAN
    rows = cells_x + 2 * PAD
    lane = lane_index(rows)
    for k in range(items):
        inner, edge = extended_rows(grid_ref, near_x, far_x, k, items, cells_y)
        moved_ref[k, ROWS : ROWS + rows] = inner
        low = jnp.where(lane < RIM, inner, jnp.where(lane >= LANES - MARGIN, edge, 0.0))
        high = jnp.where(lane >= LANES - RIM, inner, jnp.where(lane < MARGIN, edge, 0.0))
        rim_ref[k] = low + rolled(high, HALF)
    first_steps(moved_ref, carried_ref, sweep_ref, levels, comps, rows)
    for row in range(0, wide_x, ROWS):
        start = ROWS + PAD - MARGIN + row
        results = sweep(sweep_ref, carried_ref, levels, comps, start, ROWS)
        for k in range(items):
            inner_ref[k, row : row + ROWS] = results[k]


def finish_kernel(
    shape, chunk, dense_x_ref, dense_y_ref, level_ref, inner_ref, rim_ref, near_y, far_y,
    next_ref, sampled_ref, moved_ref, carried_ref, sweep_ref, round_ref,
):
    cells_x, cells_y, _, _ = shape
    items = rim_ref.shape[0]
    groups = -(-items // EDGE_PER)
    levels, comps = next_ref.shape[:2]
    slots = level_ref.shape[1]
    wide_x = cells_x + SPAN
    rows = cells_x + 2 * PAD
    lane = lane_index(rows)
    even = is_even("gy")
    near_halo, far_halo = unfolded(near_y, rows, groups), unfolded(far_y, rows, groups)
    before = jnp.where(even, far_halo, near_halo)
    after = rolled(jnp.where(even, near_halo, far_halo), HALF + MARGIN + REACH)
    turned = (HALF + MARGIN + REACH) % LANES
    halo = jnp.where((lane >= turned) & (lane < turned + HALO * items), after, before)
    for group in range(groups):
        row = group * rows
        near = near_y[row : row + rows].astype(jnp.float32)
        far = far_y[row : row + rows].astype(jnp.float32)
        before = jnp.where(even, far, near)
        after = rolled(jnp.where(even, near, far), HALF)
        for k in range(group * EDGE_PER, min((group + 1) * EDGE_PER, items)):
            slot = k % EDGE_PER
            place = (lane + (LANES + MARGIN - SPAN * slot)) % LANES
            main = rolled(jnp.where(place < SPAN, before, after), -SPAN * slot)
            place = (lane + MARGIN) % HALF
            value = rim_ref[k] + jnp.where(place < SPAN, main, 0.0)
            outer = rolled(halo, -REACH - HALO * k)
            low = (lane >= LANES - REACH) & (lane < LANES - MARGIN)
            high = (lane >= HALF + MARGIN) & (lane < HALF + REACH)
            moved_ref[k, ROWS : ROWS + rows] = jnp.where(low | high, outer, value)

    first_steps(moved_ref, carried_ref, sweep_ref, levels, comps, rows)
    size = 2 * ROWS
    lane = lane_index(size)
    for row in range(0, wide_x, size):
        start = ROWS + PAD - MARGIN + row
        results = sweep(sweep_ref, carried_ref, levels, comps, start, size)
        for k in range(items):
            low, high = results[k], rolled(results[k], HALF)
            inner = inner_ref[k, row : row + size]
            inner = jnp.where(lane < REACH, low, jnp.where(lane >= LANES - REACH, high, inner))
            edge = jnp.where(lane < MARGIN, high, low)
            place = slice(k * wide_x + row, k * wide_x + row + size)
            round_ref[place, :cells_y] = inner.astype(jnp.bfloat16)
            round_ref[place, cells_y:] = edge.astype(jnp.bfloat16)
            if MARGIN <= row < MARGIN + cells_x:
                next_ref[k // comps, k % comps, row - MARGIN : row - MARGIN + size] = inner

    for first in range(0, slots, chunk):
        lanes = slice(first, first + chunk)
        level = level_ref[:, lanes]
        partial = jnp.dot(
            round_ref[...], dense_y_ref[:, lanes], preferred_element_type=jnp.float32
        )
        partial = partial.reshape(levels, comps, wide_x, chunk)
        for c in range(comps):
            picked = partial[levels - 1, c]
            for l in range(levels - 2, -1, -1):
                picked = jnp.where(level == l, partial[l, c], picked)
            sampled_ref[c, 0, :, lanes] = jnp.sum(
                picked * dense_x_ref[:, lanes], axis=0, keepdims=True
            )


def whole(count):
    return [pl.BlockSpec(memory_space=pltpu.VMEM)] * count


def exchange(near, far, axis):
    size = lax.axis_size(axis)
    if size % 2:
        raise ValueError("odd axis")
    near_pairs = [(i, i ^ 1) for i in range(size)]
    far_pairs = [(i, (i - 1 if i % 2 == 0 else i + 1) % size) for i in range(size)]
    far = lax.ppermute(far, axis, far_pairs)
    return lax.ppermute(near, axis, near_pairs), far


def body(velocity, marker_cell, marker_frac, marker_force, fish_owner):
    levels, comps, cells_x, cells_y = velocity.shape
    slots = marker_cell.shape[3]
    items = levels * comps
    shape = (cells_x, cells_y, cells_x * lax.axis_size("gx"), cells_y * lax.axis_size("gy"))
    wide_x = cells_x + SPAN
    rows = cells_x + 2 * PAD
    chunk = min(512, slots)
    width = cells_y + LANES
    groups = -(-items // EDGE_PER)
    params = pltpu.CompilerParams(vmem_limit_bytes=40 * 1024 * 1024)
    edge_x = jax.ShapeDtypeStruct(((items + groups) * STRIP, LANES), jnp.bfloat16)
    arrays = (fish_owner, velocity, marker_cell, marker_frac, marker_force)
    grid, near, far, dense_x, dense_y, level = pl.pallas_call(
        functools.partial(spread_kernel, shape, chunk),
        out_shape=(
            jax.ShapeDtypeStruct((items, wide_x, width), jnp.float32),
            edge_x,
            edge_x,
            jax.ShapeDtypeStruct((wide_x, slots), jnp.float32),
            jax.ShapeDtypeStruct((width, slots), jnp.bfloat16),
            jax.ShapeDtypeStruct((1, slots), jnp.int32),
        ),
        in_specs=[pl.BlockSpec(memory_space=pltpu.HBM)] * 5,
        out_specs=tuple(whole(6)),
        scratch_shapes=[pltpu.VMEM((items * wide_x, slots), jnp.bfloat16)]
        + [pltpu.VMEM(a.shape, a.dtype) for a in arrays]
        + [pltpu.SemaphoreType.DMA((5,))],
        compiler_params=params,
        name="spread",
    )(*(pltpu.with_memory_space_constraint(a, pltpu.HBM) for a in arrays))
    near_x, far_x = exchange(near, far, "gx")
    edge_y = jax.ShapeDtypeStruct((groups * rows + SPAN, LANES), jnp.bfloat16)
    near, far = pl.pallas_call(
        functools.partial(pack_kernel, shape),
        out_shape=(edge_y, edge_y),
        in_specs=whole(3),
        out_specs=tuple(whole(2)),
        compiler_params=params,
        name="pack",
    )(grid, near_x, far_x)
    near_y, far_y = exchange(near, far, "gy")
    field = pltpu.VMEM((items, rows + 2 * ROWS, LANES), jnp.float32)
    inner, rim = pl.pallas_call(
        functools.partial(inner_kernel, shape, levels),
        out_shape=(
            jax.ShapeDtypeStruct((items, wide_x, LANES), jnp.float32),
            jax.ShapeDtypeStruct((items, rows, LANES), jnp.float32),
        ),
        in_specs=whole(3),
        out_specs=tuple(whole(2)),
        scratch_shapes=[field, field, field],
        compiler_params=params,
        cost_estimate=pl.CostEstimate(
            flops=40 * items * rows * LANES, bytes_accessed=16 * items * rows * LANES,
            transcendentals=0,
        ),
        name="inner",
    )(grid, near_x, far_x)
    return pl.pallas_call(
        functools.partial(finish_kernel, shape, chunk),
        out_shape=(
            jax.ShapeDtypeStruct(velocity.shape, jnp.float32),
            jax.ShapeDtypeStruct((comps, 1, 1, slots), jnp.float32),
        ),
        in_specs=whole(7),
        out_specs=tuple(whole(2)),
        scratch_shapes=[field, field, field, pltpu.VMEM((items * wide_x, width), jnp.bfloat16)],
        compiler_params=params,
        name="finish",
    )(dense_x, dense_y, level, inner, rim, near_y, far_y)


def solution(mesh):
    placed = (
        P(None, None, "gx", "gy"),
        P(None, "gx", "gy", None),
        P(None, "gx", "gy", None),
        P(None, "gx", "gy", None),
        P(),
    )
    return jax.shard_map(
        body,
        mesh=mesh,
        in_specs=placed,
        out_specs=(P(None, None, "gx", "gy"), P(None, "gx", "gy", None)),
        check_vma=False,
    )
```

```python
import functools

import jax
import jax.numpy as jnp
import numpy as np
from jax import lax
from jax.experimental import pallas as pl
from jax.experimental.pallas import tpu as pltpu
from jax.sharding import PartitionSpec as P

MARGIN = 16
FISH_MARK = 1024
HALO = 3
LANES = 128
COURANT = 0.25
VISCOUS = 1.5
ROWS = 8

REACH = MARGIN + HALO
PAD = -(-REACH // ROWS) * ROWS
STRIP = PAD + MARGIN
SPAN = 2 * MARGIN
EDGE_PER = LANES // SPAN


def half_turn(terms):
    nodes = 0.5 - 0.5 * np.cos(np.pi * (np.arange(64) + 0.5) / 64)
    square = nodes * nodes
    cosine = np.polynomial.polynomial.polyfit(square, np.cos(0.5 * np.pi * nodes), terms)
    sine = np.polynomial.polynomial.polyfit(square, np.sin(0.5 * np.pi * nodes) / nodes, terms)
    return [float(v) for v in cosine], [float(v) for v in sine]


COS_FIT, SIN_FIT = half_turn(6)


def horner(coefficients, value):
    total = jnp.full_like(value, coefficients[-1])
    for coefficient in coefficients[-2::-1]:
        total = total * value + coefficient
    return total


def four_weights(frac):
    square = frac * frac
    cosine = horner(COS_FIT, square)
    sine = frac * horner(SIN_FIT, square)
    return (0.25 - 0.25 * sine, 0.25 + 0.25 * cosine, 0.25 + 0.25 * sine, 0.25 - 0.25 * cosine)


def local_cell(cell, low, extent):
    offset = cell - low
    offset = jnp.where(offset < -MARGIN, offset + extent, offset)
    return jnp.where(offset >= extent - MARGIN, offset - extent, offset)


def placed_weights(first, rows, offset, weights):
    width = offset.shape[1]
    shift = lax.broadcasted_iota(jnp.int32, (rows, width), 0) + first - offset
    dense = jnp.where(shift == 2, weights[3], 0.0)
    dense = jnp.where(shift == 1, weights[2], dense)
    dense = jnp.where(shift == 0, weights[1], dense)
    return jnp.where(shift == -1, weights[0], dense)


def marker_weights(cell_ref, frac_ref, lanes, shape):
    cells_x, cells_y, extent_x, extent_y = shape
    low_x = lax.axis_index("gx") * cells_x
    low_y = lax.axis_index("gy") * cells_y
    offset_x = local_cell(cell_ref[0, 0, :, lanes], low_x, extent_x)
    offset_y = local_cell(cell_ref[1, 0, :, lanes], low_y, extent_y)
    weights_x = four_weights(frac_ref[0, 0, :, lanes])
    weights_y = four_weights(frac_ref[1, 0, :, lanes])
    dense_x = placed_weights(-MARGIN, cells_x + 2 * MARGIN, offset_x, weights_x)
    inner_y = placed_weights(0, cells_y + MARGIN, offset_y, weights_y)
    outer_y = placed_weights(-MARGIN, MARGIN, offset_y, weights_y)
    gap = jnp.zeros((LANES - 2 * MARGIN, offset_y.shape[1]), jnp.float32)
    dense_y = jnp.concatenate([inner_y, gap, outer_y], axis=0).astype(jnp.bfloat16)
    return dense_x, dense_y


def alive_count(fish_ref):
    me = lax.axis_index("gx") * lax.axis_size("gy") + lax.axis_index("gy")
    mine = jnp.where(fish_ref[...] == me, 1.0, 0.0)
    return FISH_MARK * jnp.sum(mine)


def alive_lanes(count, first, width):
    slot = lax.broadcasted_iota(jnp.int32, (1, width), 1) + first
    return jnp.where(slot.astype(jnp.float32) < count, 1.0, 0.0)


def is_even(axis):
    return lax.axis_index(axis) % 2 == 0


def spread_kernel(
    shape, chunk, fish_hbm, velocity_hbm, cell_hbm, frac_hbm, force_hbm,
    grid_ref, far_ref, near_ref, dense_x_ref, dense_y_ref, level_ref,
    fish_ref, velocity_ref, cell_ref, frac_ref, force_ref, sems,
):
    pairs = (
        (cell_hbm, cell_ref), (frac_hbm, frac_ref), (fish_hbm, fish_ref),
        (force_hbm, force_ref), (velocity_hbm, velocity_ref),
    )
    copies = [pltpu.make_async_copy(a, b, sems.at[i]) for i, (a, b) in enumerate(pairs)]
    for copy in copies:
        copy.start()
    for copy in copies[:-1]:
        copy.wait()
    cells_x, cells_y, _, _ = shape
    levels, comps = velocity_ref.shape[:2]
    slots = cell_ref.shape[3]
    wide_x = cells_x + SPAN
    items = levels * comps
    count = alive_count(fish_ref)
    level_ref[...] = cell_ref[2, 0]
    for first in range(0, slots, chunk):
        lanes = slice(first, first + chunk)
        dense_x, dense_y = marker_weights(cell_ref, frac_ref, lanes, shape)
        dense_x = dense_x * alive_lanes(count, first, chunk)
        dense_x_ref[:, lanes] = dense_x
        dense_y_ref[:, lanes] = dense_y
        level = cell_ref[2, 0, :, lanes]
        lefts = [
            (force_ref[c, 0, :, lanes] * dense_x).astype(jnp.bfloat16) for c in range(comps)
        ]
        pieces = []
        for l in range(levels):
            hot = jnp.broadcast_to(jnp.where(level == l, 1.0, 0.0), (16, chunk))
            hot = hot.astype(jnp.bfloat16)
            for c in range(comps):
                product = lefts[c].reshape(wide_x // 16, 16, chunk) * hot[None]
                pieces.append(product.reshape(wide_x, chunk))
        total = lax.dot_general(
            jnp.concatenate(pieces, axis=0), dense_y, (((1,), (1,)), ((), ())),
            preferred_element_type=jnp.float32,
        )
        total = total.reshape(items, wide_x, cells_y + LANES)
        if first:
            grid_ref[...] += total
        else:
            grid_ref[...] = total
    copies[-1].wait()
    for k in range(items):
        grid_ref[k, MARGIN : MARGIN + cells_x, :cells_y] += velocity_ref[k // comps, k % comps]
    even = is_even("gx")
    high = wide_x - STRIP
    for out_ref, row in ((far_ref, jnp.where(even, 0, high)), (near_ref, jnp.where(even, high, 0))):
        place = pl.ds(pl.multiple_of(row, ROWS), STRIP)
        parts = [grid_ref[k, place, :cells_y] for k in range(items)]
        for group in range(0, items, EDGE_PER):
            edges = []
            for k in range(group, min(group + EDGE_PER, items)):
                edges.append(rolled(grid_ref[k, place, cells_y:], SPAN * (k - group)))
            parts.append(functools.reduce(jnp.add, edges))
        out_ref[...] = jnp.concatenate(parts, axis=0).astype(jnp.bfloat16)


def rolled(value, shift):
    shift = shift % LANES
    return pltpu.roll(value, shift, 1) if shift else value


def lane_index(rows):
    return lax.broadcasted_iota(jnp.int32, (rows, LANES), 1)


def strip_parts(near, far, k, items):
    lane = lane_index(STRIP)
    even = is_even("gx")
    row = (items + k // EDGE_PER) * STRIP
    parts = []
    for first, second in ((far, near), (near, far)):
        inner = jnp.where(
            even,
            first[k * STRIP : (k + 1) * STRIP].astype(jnp.float32),
            second[k * STRIP : (k + 1) * STRIP].astype(jnp.float32),
        )
        edge = jnp.where(
            even,
            first[row : row + STRIP].astype(jnp.float32),
            second[row : row + STRIP].astype(jnp.float32),
        )
        edge = rolled(edge, -SPAN * (k % EDGE_PER))
        edge = jnp.where((lane < MARGIN) | (lane >= LANES - MARGIN), edge, 0.0)
        parts.append((inner, edge))
    return parts


def joined(center, before, after):
    wide = center.shape[0]
    near = PAD - MARGIN
    overlap = STRIP - near
    return jnp.concatenate(
        [
            before[:near],
            center[:overlap] + before[near:],
            center[overlap : wide - overlap],
            center[wide - overlap :] + after[:overlap],
            after[overlap:],
        ],
        axis=0,
    )


def extended_rows(grid_ref, near, far, k, items, cells_y):
    before, after = strip_parts(near, far, k, items)
    inner = joined(grid_ref[k, :, :cells_y], before[0], after[0])
    edge = joined(grid_ref[k, :, cells_y:], before[1], after[1])
    return inner, edge


def folds(rows):
    return [(row, min(SPAN, rows - row)) for row in range(0, rows, SPAN)]


def pack_kernel(shape, grid_ref, far_x, near_x, far_ref, near_ref):
    cells_x, cells_y, _, _ = shape
    items = grid_ref.shape[0]
    groups = -(-items // EDGE_PER)
    rows = cells_x + 2 * PAD
    lane = lane_index(rows)
    even = is_even("gy")
    up_halo = (lane >= LANES - REACH) & (lane < LANES - MARGIN)
    down_halo = (lane >= MARGIN) & (lane < REACH)
    halos = None
    for group in range(groups):
        ups, downs = None, None
        for k in range(group * EDGE_PER, min((group + 1) * EDGE_PER, items)):
            inner, edge = extended_rows(grid_ref, near_x, far_x, k, items, cells_y)
            shift = SPAN * (k % EDGE_PER)
            up = rolled(jnp.where(lane >= LANES - MARGIN, inner, edge), shift)
            down = rolled(jnp.where(lane < MARGIN, inner, edge), shift)
            halo = rolled(jnp.where(up_halo | down_halo, inner, 0.0), REACH + HALO * k)
            ups = up if ups is None else ups + up
            downs = down if downs is None else downs + down
            halos = halo if halos is None else halos + halo
        place = slice(group * rows, (group + 1) * rows)
        near_ref[place] = jnp.where(even, ups, downs).astype(jnp.bfloat16)
        far_ref[place] = jnp.where(even, downs, ups).astype(jnp.bfloat16)
    ups = jnp.where(lane < HALO * items, halos, 0.0)
    downs = jnp.where(lane < HALO * items, rolled(halos, -MARGIN - REACH), 0.0)
    for out_ref, total in (
        (near_ref, jnp.where(even, ups, downs)), (far_ref, jnp.where(even, downs, ups)),
    ):
        folded = total[:SPAN]
        for index, (row, size) in enumerate(folds(rows)[1:]):
            piece = rolled(total[row : row + size], SPAN * (index + 1))
            if size < SPAN:
                gap = jnp.zeros((SPAN - size, LANES), jnp.float32)
                piece = jnp.concatenate([piece, gap], axis=0)
            folded = folded + piece
        out_ref[groups * rows : groups * rows + SPAN] = folded.astype(jnp.bfloat16)


def unfolded(ref, rows, groups):
    folded = ref[groups * rows : groups * rows + SPAN].astype(jnp.float32)
    return jnp.concatenate(
        [rolled(folded, -SPAN * index)[:size] for index, (_, size) in enumerate(folds(rows))],
        axis=0,
    )


def around(ref, k, start, size):
    center = ref[k, start : start + size]
    back = ref[k, start - 1 : start - 1 + size]
    fore = ref[k, start + 1 : start + 1 + size]
    return center, back, fore, rolled(center, 1), rolled(center, -1)


def advect(moved_ref, carried_ref, levels, comps, rows):
    for start in range(ROWS, ROWS + rows, ROWS):
        for l in range(levels):
            pieces = [around(moved_ref, l * comps + c, start, ROWS) for c in range(comps)]
            speed_x, speed_y = COURANT * pieces[0][0], COURANT * pieces[1][0]
            ahead_x, astern_x = jnp.maximum(speed_x, 0.0), jnp.minimum(speed_x, 0.0)
            ahead_y, astern_y = jnp.maximum(speed_y, 0.0), jnp.minimum(speed_y, 0.0)
            for c in range(comps):
                center, back, fore, below, above = pieces[c]
                change = ahead_x * (center - back) + astern_x * (fore - center)
                change = change + ahead_y * (center - below) + astern_y * (above - center)
                carried_ref[l * comps + c, start : start + ROWS] = center - change


def sweep(ref, carried_ref, levels, comps, start, size):
    scale = 1.0 / (1.0 + 6.0 * VISCOUS)
    centers, results = [], []
    for k in range(levels * comps):
        center, back, fore, below, above = around(ref, k, start, size)
        centers.append(center)
        results.append(back + fore + below + above)
    for k in range(levels * comps):
        higher = min(k // comps + 1, levels - 1) * comps + k % comps
        lower = max(k // comps - 1, 0) * comps + k % comps
        summed = results[k] + centers[higher] + centers[lower]
        source = carried_ref[k, start : start + size]
        results[k] = scale * source + (VISCOUS * scale) * summed
    return results


def first_steps(moved_ref, carried_ref, sweep_ref, levels, comps, rows):
    advect(moved_ref, carried_ref, levels, comps, rows)
    for start in range(ROWS, ROWS + rows, ROWS):
        results = sweep(carried_ref, carried_ref, levels, comps, start, ROWS)
        for k in range(levels * comps):
            sweep_ref[k, start : start + ROWS] = results[k]


RIM = REACH + HALO
HALF = LANES // 2


def inner_kernel(
    shape, levels, grid_ref, far_x, near_x, inner_ref, rim_ref, moved_ref, carried_ref, sweep_ref,
):
    cells_x, cells_y, _, _ = shape
    items = grid_ref.shape[0]
    comps = items // levels
    wide_x = cells_x + SPAN
    rows = cells_x + 2 * PAD
    lane = lane_index(rows)
    for k in range(items):
        inner, edge = extended_rows(grid_ref, near_x, far_x, k, items, cells_y)
        moved_ref[k, ROWS : ROWS + rows] = inner
        low = jnp.where(lane < RIM, inner, jnp.where(lane >= LANES - MARGIN, edge, 0.0))
        high = jnp.where(lane >= LANES - RIM, inner, jnp.where(lane < MARGIN, edge, 0.0))
        rim_ref[k] = low + rolled(high, HALF)
    first_steps(moved_ref, carried_ref, sweep_ref, levels, comps, rows)
    for row in range(0, wide_x, ROWS):
        start = ROWS + PAD - MARGIN + row
        results = sweep(sweep_ref, carried_ref, levels, comps, start, ROWS)
        for k in range(items):
            inner_ref[k, row : row + ROWS] = results[k]


def finish_kernel(
    shape, chunk, dense_x_ref, dense_y_ref, level_ref, inner_ref, rim_ref, far_y, near_y,
    next_ref, sampled_ref, moved_ref, carried_ref, sweep_ref, round_ref,
):
    cells_x, cells_y, _, _ = shape
    items = rim_ref.shape[0]
    groups = -(-items // EDGE_PER)
    levels, comps = next_ref.shape[:2]
    slots = level_ref.shape[1]
    wide_x = cells_x + SPAN
    rows = cells_x + 2 * PAD
    lane = lane_index(rows)
    even = is_even("gy")
    near_halo, far_halo = unfolded(near_y, rows, groups), unfolded(far_y, rows, groups)
    before = jnp.where(even, far_halo, near_halo)
    after = rolled(jnp.where(even, near_halo, far_halo), HALF + MARGIN + REACH)
    turned = (HALF + MARGIN + REACH) % LANES
    halo = jnp.where((lane >= turned) & (lane < turned + HALO * items), after, before)
    for group in range(groups):
        row = group * rows
        near = near_y[row : row + rows].astype(jnp.float32)
        far = far_y[row : row + rows].astype(jnp.float32)
        before = jnp.where(even, far, near)
        after = rolled(jnp.where(even, near, far), HALF)
        for k in range(group * EDGE_PER, min((group + 1) * EDGE_PER, items)):
            slot = k % EDGE_PER
            place = (lane + (LANES + MARGIN - SPAN * slot)) % LANES
            main = rolled(jnp.where(place < SPAN, before, after), -SPAN * slot)
            place = (lane + MARGIN) % HALF
            value = rim_ref[k] + jnp.where(place < SPAN, main, 0.0)
            outer = rolled(halo, -REACH - HALO * k)
            low = (lane >= LANES - REACH) & (lane < LANES - MARGIN)
            high = (lane >= HALF + MARGIN) & (lane < HALF + REACH)
            moved_ref[k, ROWS : ROWS + rows] = jnp.where(low | high, outer, value)

    first_steps(moved_ref, carried_ref, sweep_ref, levels, comps, rows)
    size = 2 * ROWS
    lane = lane_index(size)
    for row in range(0, wide_x, size):
        start = ROWS + PAD - MARGIN + row
        results = sweep(sweep_ref, carried_ref, levels, comps, start, size)
        for k in range(items):
            low, high = results[k], rolled(results[k], HALF)
            inner = inner_ref[k, row : row + size]
            inner = jnp.where(lane < REACH, low, jnp.where(lane >= LANES - REACH, high, inner))
            edge = jnp.where(lane < MARGIN, high, low)
            place = slice(k * wide_x + row, k * wide_x + row + size)
            round_ref[place, :cells_y] = inner.astype(jnp.bfloat16)
            round_ref[place, cells_y:] = edge.astype(jnp.bfloat16)
            if MARGIN <= row < MARGIN + cells_x:
                next_ref[k // comps, k % comps, row - MARGIN : row - MARGIN + size] = inner

    for first in range(0, slots, chunk):
        lanes = slice(first, first + chunk)
        level = level_ref[:, lanes]
        partial = jnp.dot(
            round_ref[...], dense_y_ref[:, lanes], preferred_element_type=jnp.float32
        )
        partial = partial.reshape(levels, comps, wide_x, chunk)
        for c in range(comps):
            picked = partial[levels - 1, c]
            for l in range(levels - 2, -1, -1):
                picked = jnp.where(level == l, partial[l, c], picked)
            sampled_ref[c, 0, :, lanes] = jnp.sum(
                picked * dense_x_ref[:, lanes], axis=0, keepdims=True
            )


def whole(count):
    return [pl.BlockSpec(memory_space=pltpu.VMEM)] * count


def exchange(near, far, axis):
    size = lax.axis_size(axis)
    if size % 2:
        raise ValueError("odd axis")
    near_pairs = [(i, i ^ 1) for i in range(size)]
    far_pairs = [(i, (i - 1 if i % 2 == 0 else i + 1) % size) for i in range(size)]
    far = lax.ppermute(far, axis, far_pairs)
    return far, lax.ppermute(near, axis, near_pairs)


def body(velocity, marker_cell, marker_frac, marker_force, fish_owner):
    levels, comps, cells_x, cells_y = velocity.shape
    slots = marker_cell.shape[3]
    items = levels * comps
    shape = (cells_x, cells_y, cells_x * lax.axis_size("gx"), cells_y * lax.axis_size("gy"))
    wide_x = cells_x + SPAN
    rows = cells_x + 2 * PAD
    chunk = min(512, slots)
    width = cells_y + LANES
    groups = -(-items // EDGE_PER)
    params = pltpu.CompilerParams(vmem_limit_bytes=40 * 1024 * 1024)
    edge_x = jax.ShapeDtypeStruct(((items + groups) * STRIP, LANES), jnp.bfloat16)
    arrays = (fish_owner, velocity, marker_cell, marker_frac, marker_force)
    grid, far, near, dense_x, dense_y, level = pl.pallas_call(
        functools.partial(spread_kernel, shape, chunk),
        out_shape=(
            jax.ShapeDtypeStruct((items, wide_x, width), jnp.float32),
            edge_x,
            edge_x,
            jax.ShapeDtypeStruct((wide_x, slots), jnp.float32),
            jax.ShapeDtypeStruct((width, slots), jnp.bfloat16),
            jax.ShapeDtypeStruct((1, slots), jnp.int32),
        ),
        in_specs=[pl.BlockSpec(memory_space=pltpu.HBM)] * 5,
        out_specs=tuple(whole(6)),
        scratch_shapes=[pltpu.VMEM(a.shape, a.dtype) for a in arrays]
        + [pltpu.SemaphoreType.DMA((5,))],
        compiler_params=params,
        name="spread",
    )(*(pltpu.with_memory_space_constraint(a, pltpu.HBM) for a in arrays))
    far_x, near_x = exchange(near, far, "gx")
    edge_y = jax.ShapeDtypeStruct((groups * rows + SPAN, LANES), jnp.bfloat16)
    far, near = pl.pallas_call(
        functools.partial(pack_kernel, shape),
        out_shape=(edge_y, edge_y),
        in_specs=whole(3),
        out_specs=tuple(whole(2)),
        compiler_params=params,
        name="pack",
    )(grid, far_x, near_x)
    far_y, near_y = exchange(near, far, "gy")
    field = pltpu.VMEM((items, rows + 2 * ROWS, LANES), jnp.float32)
    inner, rim = pl.pallas_call(
        functools.partial(inner_kernel, shape, levels),
        out_shape=(
            jax.ShapeDtypeStruct((items, wide_x, LANES), jnp.float32),
            jax.ShapeDtypeStruct((items, rows, LANES), jnp.float32),
        ),
        in_specs=whole(3),
        out_specs=tuple(whole(2)),
        scratch_shapes=[field, field, field],
        compiler_params=params,
        cost_estimate=pl.CostEstimate(
            flops=40 * items * rows * LANES, bytes_accessed=16 * items * rows * LANES,
            transcendentals=0,
        ),
        name="inner",
    )(grid, far_x, near_x)
    return pl.pallas_call(
        functools.partial(finish_kernel, shape, chunk),
        out_shape=(
            jax.ShapeDtypeStruct(velocity.shape, jnp.float32),
            jax.ShapeDtypeStruct((comps, 1, 1, slots), jnp.float32),
        ),
        in_specs=whole(7),
        out_specs=tuple(whole(2)),
        scratch_shapes=[field, field, field, pltpu.VMEM((items * wide_x, width), jnp.bfloat16)],
        compiler_params=params,
        name="finish",
    )(dense_x, dense_y, level, inner, rim, far_y, near_y)


def solution(mesh):
    placed = (
        P(None, None, "gx", "gy"),
        P(None, "gx", "gy", None),
        P(None, "gx", "gy", None),
        P(None, "gx", "gy", None),
        P(),
    )
    return jax.shard_map(
        body,
        mesh=mesh,
        in_specs=placed,
        out_specs=(P(None, None, "gx", "gy"), P(None, "gx", "gy", None)),
        check_vma=False,
    )
```

```python
import functools

import jax
import jax.numpy as jnp
import numpy as np
from jax import lax
from jax.experimental import pallas as pl
from jax.experimental.pallas import tpu as pltpu
from jax.sharding import PartitionSpec as P

MARGIN = 16
FISH_MARK = 1024
HALO = 3
LANES = 128
COURANT = 0.25
VISCOUS = 1.5
ROWS = 8

REACH = MARGIN + HALO
PAD = -(-REACH // ROWS) * ROWS
STRIP = PAD + MARGIN
SPAN = 2 * MARGIN
EDGE_PER = LANES // SPAN


def half_turn(terms):
    nodes = 0.5 - 0.5 * np.cos(np.pi * (np.arange(64) + 0.5) / 64)
    square = nodes * nodes
    cosine = np.polynomial.polynomial.polyfit(square, np.cos(0.5 * np.pi * nodes), terms)
    sine = np.polynomial.polynomial.polyfit(square, np.sin(0.5 * np.pi * nodes) / nodes, terms)
    return [float(v) for v in cosine], [float(v) for v in sine]


COS_FIT, SIN_FIT = half_turn(6)


def horner(coefficients, value):
    total = jnp.full_like(value, coefficients[-1])
    for coefficient in coefficients[-2::-1]:
        total = total * value + coefficient
    return total


def four_weights(frac):
    square = frac * frac
    cosine = horner(COS_FIT, square)
    sine = frac * horner(SIN_FIT, square)
    return (0.25 - 0.25 * sine, 0.25 + 0.25 * cosine, 0.25 + 0.25 * sine, 0.25 - 0.25 * cosine)


def local_cell(cell, low, extent):
    offset = cell - low
    offset = jnp.where(offset < -MARGIN, offset + extent, offset)
    return jnp.where(offset >= extent - MARGIN, offset - extent, offset)


def position():
    row, col = lax.axis_index("gx"), lax.axis_index("gy")
    return row, col, row % 2 == 0, col % 2 == 0


def tile_weights(offset, weights):
    shift = lax.broadcasted_iota(jnp.int32, (ROWS, offset.shape[1]), 0) + 1 - offset
    quarter, phase = shift >> 2, shift & 3
    value = jnp.where(phase == 3, weights[3], weights[2])
    value = jnp.where(phase == 1, weights[1], value)
    return quarter, jnp.where(phase == 0, weights[0], value)


def doubled(quarter, value):
    quarter = jnp.concatenate([quarter, quarter + 2], axis=0).astype(jnp.float32)
    return quarter.astype(jnp.bfloat16), twice(value)


def twice(value):
    return jnp.concatenate([value, value], axis=0).astype(jnp.bfloat16)


def picked_tile(quarter, value, first):
    zero = jnp.zeros_like(value)
    return jnp.where(quarter == jnp.array(-first // 4, quarter.dtype), value, zero)


def half_spread(quarter_ref, force_ref, dense_y_ref, half_ref, base, lanes):
    items, rows = half_ref.shape[:2]
    quarter = quarter_ref[:, lanes] + base
    quarter = jnp.concatenate([quarter, quarter + 2], axis=0).astype(jnp.float32)
    quarter = quarter.astype(jnp.bfloat16)
    left = jnp.concatenate(
        [
            picked_tile(quarter, force_ref[k, :, lanes], row)
            for k in range(items)
            for row in range(0, rows, 2 * ROWS)
        ],
        axis=0,
    )
    total = lax.dot_general(
        left, dense_y_ref[:, lanes], (((1,), (1,)), ((), ())),
        preferred_element_type=jnp.float32,
    )
    total = total.reshape(half_ref.shape)
    if lanes.start:
        half_ref[...] += total
    else:
        half_ref[...] = total


def finish_half(half_ref, velocity_ref, out_ref, low, cells_y):
    items, rows = half_ref.shape[:2]
    comps = items // velocity_ref.shape[0]
    count = rows - MARGIN
    source = pl.ds(pl.multiple_of(jnp.where(low, 0, count), ROWS), count)
    target = pl.ds(pl.multiple_of(jnp.where(low, MARGIN, 0), ROWS), count)
    for k in range(items):
        half_ref[k, target, :cells_y] += velocity_ref[k // comps, k % comps, source]
    place = pl.ds(pl.multiple_of(jnp.where(low, 0, rows - STRIP), ROWS), STRIP)
    parts = [half_ref[k, place, :cells_y] for k in range(items)]
    for group in range(0, items, EDGE_PER):
        edges = []
        for k in range(group, min(group + EDGE_PER, items)):
            edges.append(rolled(half_ref[k, place, cells_y:], SPAN * (k - group)))
        parts.append(functools.reduce(jnp.add, edges))
    out_ref[...] = jnp.concatenate(parts, axis=0).astype(jnp.bfloat16)


def far_kernel(
    shape, chunk, fish_hbm, velocity_hbm, cell_hbm, frac_hbm, force_hbm,
    half_ref, far_ref, force_out, dense_y_ref, quarter_ref, value_ref, level_ref,
    fish_ref, velocity_ref, cell_ref, frac_ref, force_ref, sems,
):
    pairs = (
        (cell_hbm, cell_ref), (frac_hbm, frac_ref), (fish_hbm, fish_ref),
        (force_hbm, force_ref), (velocity_hbm, velocity_ref),
    )
    copies = [pltpu.make_async_copy(a, b, sems.at[i]) for i, (a, b) in enumerate(pairs)]
    for copy in copies:
        copy.start()
    cells_x, cells_y, extent_x, extent_y = shape
    levels, comps = velocity_ref.shape[:2]
    slots = cell_ref.shape[3]
    row, col, even, _ = position()
    base = jnp.where(even, -MARGIN // 4, cells_x // 8)
    for copy in copies[:-1]:
        copy.wait()
    mine = jnp.where(fish_ref[...] == row * lax.axis_size("gy") + col, 1.0, 0.0)
    count = FISH_MARK * jnp.sum(mine)
    level_ref[...] = cell_ref[2, 0]
    for first in range(0, slots, chunk):
        lanes = slice(first, first + chunk)
        offset_x = local_cell(cell_ref[0, 0, :, lanes], row * cells_x, extent_x)
        offset_y = local_cell(cell_ref[1, 0, :, lanes], col * cells_y, extent_y)
        slot = lax.broadcasted_iota(jnp.int32, (1, chunk), 1) + first
        alive = jnp.where(slot.astype(jnp.float32) < count, 1.0, 0.0)
        quarter, value = tile_weights(offset_x, four_weights(frac_ref[0, 0, :, lanes]))
        value = value * alive
        quarter_ref[:, lanes] = quarter
        value_ref[:, lanes] = value
        level = cell_ref[2, 0, :, lanes]
        pushes = [force_ref[c, 0, :, lanes] * value for c in range(comps)]
        for l in range(levels):
            for c in range(comps):
                force_out[l * comps + c, :, lanes] = twice(jnp.where(level == l, pushes[c], 0.0))
        quarter, value = doubled(
            *tile_weights(offset_y, four_weights(frac_ref[1, 0, :, lanes]))
        )
        dense_y_ref[:, lanes] = jnp.concatenate(
            [picked_tile(quarter, value, n) for n in range(0, cells_y + MARGIN, 2 * ROWS)]
            + [jnp.zeros((LANES - SPAN, chunk), jnp.bfloat16)]
            + [picked_tile(quarter, value, n) for n in range(-MARGIN, 0, 2 * ROWS)],
            axis=0,
        )
        half_spread(quarter_ref, force_out, dense_y_ref, half_ref, base, lanes)
    copies[-1].wait()
    finish_half(half_ref, velocity_ref, far_ref, even, cells_y)


def near_kernel(
    shape, chunk, velocity_ref, far_half_ref, force_ref, dense_y_ref, quarter_ref,
    grid_ref, near_ref, half_ref,
):
    cells_x, cells_y, _, _ = shape
    slots = quarter_ref.shape[1]
    rows = half_ref.shape[1]
    _, _, even, _ = position()
    base = jnp.where(even, cells_x // 8, -MARGIN // 4)
    for first in range(0, slots, chunk):
        lanes = slice(first, first + chunk)
        half_spread(quarter_ref, force_ref, dense_y_ref, half_ref, base, lanes)
    finish_half(half_ref, velocity_ref, near_ref, jnp.logical_not(even), cells_y)
    for ref, row in ((far_half_ref, jnp.where(even, 0, rows)), (half_ref, jnp.where(even, rows, 0))):
        place = pl.ds(pl.multiple_of(row, ROWS), rows)
        for k in range(ref.shape[0]):
            grid_ref[k, place] = ref[k]


def rolled(value, shift):
    shift = shift % LANES
    return pltpu.roll(value, shift, 1) if shift else value


def lane_index(rows):
    return lax.broadcasted_iota(jnp.int32, (rows, LANES), 1)


def strip_parts(near, far, k, items, even):
    lane = lane_index(STRIP)
    row = (items + k // EDGE_PER) * STRIP
    parts = []
    for first, second in ((far, near), (near, far)):
        inner = jnp.where(
            even,
            first[k * STRIP : (k + 1) * STRIP].astype(jnp.float32),
            second[k * STRIP : (k + 1) * STRIP].astype(jnp.float32),
        )
        edge = jnp.where(
            even,
            first[row : row + STRIP].astype(jnp.float32),
            second[row : row + STRIP].astype(jnp.float32),
        )
        edge = rolled(edge, -SPAN * (k % EDGE_PER))
        edge = jnp.where((lane < MARGIN) | (lane >= LANES - MARGIN), edge, 0.0)
        parts.append((inner, edge))
    return parts


def joined(center, before, after):
    wide = center.shape[0]
    near = PAD - MARGIN
    overlap = STRIP - near
    return jnp.concatenate(
        [
            before[:near],
            center[:overlap] + before[near:],
            center[overlap : wide - overlap],
            center[wide - overlap :] + after[:overlap],
            after[overlap:],
        ],
        axis=0,
    )


def extended_rows(grid_ref, near, far, k, items, cells_y, even):
    before, after = strip_parts(near, far, k, items, even)
    inner = joined(grid_ref[k, :, :cells_y], before[0], after[0])
    edge = joined(grid_ref[k, :, cells_y:], before[1], after[1])
    return inner, edge


def folds(rows):
    return [(row, min(SPAN, rows - row)) for row in range(0, rows, SPAN)]


def pack_kernel(shape, grid_ref, far_x, near_x, far_ref, near_ref):
    cells_x, cells_y, _, _ = shape
    items = grid_ref.shape[0]
    groups = -(-items // EDGE_PER)
    rows = cells_x + 2 * PAD
    lane = lane_index(rows)
    _, _, even_x, even = position()
    up_halo = (lane >= LANES - REACH) & (lane < LANES - MARGIN)
    down_halo = (lane >= MARGIN) & (lane < REACH)
    halos = None
    for group in range(groups):
        ups, downs = None, None
        for k in range(group * EDGE_PER, min((group + 1) * EDGE_PER, items)):
            inner, edge = extended_rows(grid_ref, near_x, far_x, k, items, cells_y, even_x)
            shift = SPAN * (k % EDGE_PER)
            up = rolled(jnp.where(lane >= LANES - MARGIN, inner, edge), shift)
            down = rolled(jnp.where(lane < MARGIN, inner, edge), shift)
            halo = rolled(jnp.where(up_halo | down_halo, inner, 0.0), REACH + HALO * k)
            ups = up if ups is None else ups + up
            downs = down if downs is None else downs + down
            halos = halo if halos is None else halos + halo
        place = slice(group * rows, (group + 1) * rows)
        near_ref[place] = jnp.where(even, ups, downs).astype(jnp.bfloat16)
        far_ref[place] = jnp.where(even, downs, ups).astype(jnp.bfloat16)
    ups = jnp.where(lane < HALO * items, halos, 0.0)
    downs = jnp.where(lane < HALO * items, rolled(halos, -MARGIN - REACH), 0.0)
    for out_ref, total in (
        (near_ref, jnp.where(even, ups, downs)), (far_ref, jnp.where(even, downs, ups)),
    ):
        folded = total[:SPAN]
        for index, (row, size) in enumerate(folds(rows)[1:]):
            piece = rolled(total[row : row + size], SPAN * (index + 1))
            if size < SPAN:
                gap = jnp.zeros((SPAN - size, LANES), jnp.float32)
                piece = jnp.concatenate([piece, gap], axis=0)
            folded = folded + piece
        out_ref[groups * rows : groups * rows + SPAN] = folded.astype(jnp.bfloat16)


def unfolded(ref, rows, groups):
    folded = ref[groups * rows : groups * rows + SPAN].astype(jnp.float32)
    return jnp.concatenate(
        [rolled(folded, -SPAN * index)[:size] for index, (_, size) in enumerate(folds(rows))],
        axis=0,
    )


def around(ref, k, start, size):
    center = ref[k, start : start + size]
    back = ref[k, start - 1 : start - 1 + size]
    fore = ref[k, start + 1 : start + 1 + size]
    return center, back, fore, rolled(center, 1), rolled(center, -1)


def advect(moved_ref, carried_ref, levels, comps, rows):
    for start in range(ROWS, ROWS + rows, ROWS):
        for l in range(levels):
            pieces = [around(moved_ref, l * comps + c, start, ROWS) for c in range(comps)]
            speed_x, speed_y = COURANT * pieces[0][0], COURANT * pieces[1][0]
            ahead_x, astern_x = jnp.maximum(speed_x, 0.0), jnp.minimum(speed_x, 0.0)
            ahead_y, astern_y = jnp.maximum(speed_y, 0.0), jnp.minimum(speed_y, 0.0)
            for c in range(comps):
                center, back, fore, below, above = pieces[c]
                change = ahead_x * (center - back) + astern_x * (fore - center)
                change = change + ahead_y * (center - below) + astern_y * (above - center)
                carried_ref[l * comps + c, start : start + ROWS] = center - change


def sweep(ref, carried_ref, levels, comps, start, size):
    scale = 1.0 / (1.0 + 6.0 * VISCOUS)
    centers, results = [], []
    for k in range(levels * comps):
        center, back, fore, below, above = around(ref, k, start, size)
        centers.append(center)
        results.append(back + fore + below + above)
    for k in range(levels * comps):
        higher = min(k // comps + 1, levels - 1) * comps + k % comps
        lower = max(k // comps - 1, 0) * comps + k % comps
        summed = results[k] + centers[higher] + centers[lower]
        source = carried_ref[k, start : start + size]
        results[k] = scale * source + (VISCOUS * scale) * summed
    return results


def first_steps(moved_ref, carried_ref, sweep_ref, levels, comps, rows):
    advect(moved_ref, carried_ref, levels, comps, rows)
    for start in range(ROWS, ROWS + rows, ROWS):
        results = sweep(carried_ref, carried_ref, levels, comps, start, ROWS)
        for k in range(levels * comps):
            sweep_ref[k, start : start + ROWS] = results[k]


RIM = REACH + HALO
HALF = LANES // 2


def inner_kernel(
    shape, levels, grid_ref, far_x, near_x, inner_ref, rim_ref, moved_ref, carried_ref, sweep_ref,
):
    cells_x, cells_y, _, _ = shape
    items = grid_ref.shape[0]
    comps = items // levels
    wide_x = cells_x + SPAN
    rows = cells_x + 2 * PAD
    lane = lane_index(rows)
    _, _, even_x, _ = position()
    for k in range(items):
        inner, edge = extended_rows(grid_ref, near_x, far_x, k, items, cells_y, even_x)
        moved_ref[k, ROWS : ROWS + rows] = inner
        low = jnp.where(lane < RIM, inner, jnp.where(lane >= LANES - MARGIN, edge, 0.0))
        high = jnp.where(lane >= LANES - RIM, inner, jnp.where(lane < MARGIN, edge, 0.0))
        rim_ref[k] = low + rolled(high, HALF)
    first_steps(moved_ref, carried_ref, sweep_ref, levels, comps, rows)
    for row in range(0, wide_x, ROWS):
        start = ROWS + PAD - MARGIN + row
        results = sweep(sweep_ref, carried_ref, levels, comps, start, ROWS)
        for k in range(items):
            inner_ref[k, row : row + ROWS] = results[k]


def finish_kernel(
    shape, chunk, quarter_ref, value_ref, dense_y_ref, level_ref, inner_ref, rim_ref, far_y, near_y,
    next_ref, sampled_ref, moved_ref, carried_ref, sweep_ref, round_ref,
):
    cells_x, cells_y, _, _ = shape
    items = rim_ref.shape[0]
    groups = -(-items // EDGE_PER)
    levels, comps = next_ref.shape[:2]
    slots = level_ref.shape[1]
    wide_x = cells_x + SPAN
    rows = cells_x + 2 * PAD
    lane = lane_index(rows)
    _, _, _, even = position()
    near_halo, far_halo = unfolded(near_y, rows, groups), unfolded(far_y, rows, groups)
    before = jnp.where(even, far_halo, near_halo)
    after = rolled(jnp.where(even, near_halo, far_halo), HALF + MARGIN + REACH)
    turned = (HALF + MARGIN + REACH) % LANES
    halo = jnp.where((lane >= turned) & (lane < turned + HALO * items), after, before)
    for group in range(groups):
        row = group * rows
        near = near_y[row : row + rows].astype(jnp.float32)
        far = far_y[row : row + rows].astype(jnp.float32)
        before = jnp.where(even, far, near)
        after = rolled(jnp.where(even, near, far), HALF)
        for k in range(group * EDGE_PER, min((group + 1) * EDGE_PER, items)):
            slot = k % EDGE_PER
            place = (lane + (LANES + MARGIN - SPAN * slot)) % LANES
            main = rolled(jnp.where(place < SPAN, before, after), -SPAN * slot)
            place = (lane + MARGIN) % HALF
            value = rim_ref[k] + jnp.where(place < SPAN, main, 0.0)
            outer = rolled(halo, -REACH - HALO * k)
            low = (lane >= LANES - REACH) & (lane < LANES - MARGIN)
            high = (lane >= HALF + MARGIN) & (lane < HALF + REACH)
            moved_ref[k, ROWS : ROWS + rows] = jnp.where(low | high, outer, value)

    first_steps(moved_ref, carried_ref, sweep_ref, levels, comps, rows)
    size = 2 * ROWS
    lane = lane_index(size)
    for row in range(0, wide_x, size):
        start = ROWS + PAD - MARGIN + row
        results = sweep(sweep_ref, carried_ref, levels, comps, start, size)
        for k in range(items):
            low, high = results[k], rolled(results[k], HALF)
            inner = inner_ref[k, row : row + size]
            inner = jnp.where(lane < REACH, low, jnp.where(lane >= LANES - REACH, high, inner))
            edge = jnp.where(lane < MARGIN, high, low)
            place = slice(k * wide_x + row, k * wide_x + row + size)
            round_ref[place, :cells_y] = inner.astype(jnp.bfloat16)
            round_ref[place, cells_y:] = edge.astype(jnp.bfloat16)
            if MARGIN <= row < MARGIN + cells_x:
                next_ref[k // comps, k % comps, row - MARGIN : row - MARGIN + size] = inner

    for first in range(0, slots, chunk):
        lanes = slice(first, first + chunk)
        level = level_ref[:, lanes]
        partial = jnp.dot(
            round_ref[...], dense_y_ref[:, lanes], preferred_element_type=jnp.float32
        )
        partial = partial.reshape(levels, comps, wide_x, chunk)
        quarter, value = quarter_ref[:, lanes], value_ref[:, lanes]
        heres = [quarter == (MARGIN - row) // 4 for row in range(0, wide_x, ROWS)]
        aboves = [level == l for l in range(levels - 1)]
        for c in range(comps):
            total = jnp.zeros((ROWS, chunk), jnp.float32)
            for row in range(0, wide_x, ROWS):
                picked = partial[levels - 1, c, row : row + ROWS]
                for l in range(levels - 2, -1, -1):
                    picked = jnp.where(aboves[l], partial[l, c, row : row + ROWS], picked)
                total = jnp.where(heres[row // ROWS], picked, total)
            sampled_ref[c, 0, :, lanes] = jnp.sum(total * value, axis=0, keepdims=True)


def whole(count):
    return [pl.BlockSpec(memory_space=pltpu.VMEM)] * count


def swap_pairs(axis):
    size = lax.axis_size(axis)
    if size % 2:
        raise ValueError("odd axis")
    far_pairs = [(i, (i - 1 if i % 2 == 0 else i + 1) % size) for i in range(size)]
    return far_pairs, [(i, i ^ 1) for i in range(size)]


def body(velocity, marker_cell, marker_frac, marker_force, fish_owner):
    levels, comps, cells_x, cells_y = velocity.shape
    slots = marker_cell.shape[3]
    items = levels * comps
    shape = (cells_x, cells_y, cells_x * lax.axis_size("gx"), cells_y * lax.axis_size("gy"))
    wide_x = cells_x + SPAN
    rows = cells_x + 2 * PAD
    chunk = min(512, slots)
    width = cells_y + LANES
    groups = -(-items // EDGE_PER)
    params = pltpu.CompilerParams(vmem_limit_bytes=40 * 1024 * 1024)
    edge_x = jax.ShapeDtypeStruct(((items + groups) * STRIP, LANES), jnp.bfloat16)
    half = (items, wide_x // 2, width)
    arrays = (fish_owner, velocity, marker_cell, marker_frac, marker_force)
    far_half, far, force, dense_y, quarter, value, level = pl.pallas_call(
        functools.partial(far_kernel, shape, chunk),
        out_shape=(
            jax.ShapeDtypeStruct(half, jnp.float32),
            edge_x,
            jax.ShapeDtypeStruct((items, 2 * ROWS, slots), jnp.bfloat16),
            jax.ShapeDtypeStruct((width, slots), jnp.bfloat16),
            jax.ShapeDtypeStruct((ROWS, slots), jnp.int32),
            jax.ShapeDtypeStruct((ROWS, slots), jnp.float32),
            jax.ShapeDtypeStruct((1, slots), jnp.int32),
        ),
        in_specs=[pl.BlockSpec(memory_space=pltpu.HBM)] * 5,
        out_specs=tuple(whole(7)),
        scratch_shapes=[pltpu.VMEM(a.shape, a.dtype) for a in arrays]
        + [pltpu.SemaphoreType.DMA((5,))],
        compiler_params=params,
        name="spread_far",
    )(*(pltpu.with_memory_space_constraint(a, pltpu.HBM) for a in arrays))
    far_pairs, near_pairs = swap_pairs("gx")
    far_x = lax.ppermute(far, "gx", far_pairs)
    grid, near = pl.pallas_call(
        functools.partial(near_kernel, shape, chunk),
        out_shape=(jax.ShapeDtypeStruct((items, wide_x, width), jnp.float32), edge_x),
        in_specs=whole(5),
        out_specs=tuple(whole(2)),
        scratch_shapes=[pltpu.VMEM(half, jnp.float32)],
        compiler_params=params,
        cost_estimate=pl.CostEstimate(
            flops=items * wide_x * width * slots, bytes_accessed=4 * items * wide_x * width,
            transcendentals=0,
        ),
        name="spread_near",
    )(velocity, far_half, force, dense_y, quarter)
    near_x = lax.ppermute(near, "gx", near_pairs)
    edge_y = jax.ShapeDtypeStruct((groups * rows + SPAN, LANES), jnp.bfloat16)
    far, near = pl.pallas_call(
        functools.partial(pack_kernel, shape),
        out_shape=(edge_y, edge_y),
        in_specs=whole(3),
        out_specs=tuple(whole(2)),
        compiler_params=params,
        name="pack",
    )(grid, far_x, near_x)
    far_pairs, near_pairs = swap_pairs("gy")
    far_y = lax.ppermute(far, "gy", far_pairs)
    near_y = lax.ppermute(near, "gy", near_pairs)
    field = pltpu.VMEM((items, rows + 2 * ROWS, LANES), jnp.float32)
    inner, rim = pl.pallas_call(
        functools.partial(inner_kernel, shape, levels),
        out_shape=(
            jax.ShapeDtypeStruct((items, wide_x, LANES), jnp.float32),
            jax.ShapeDtypeStruct((items, rows, LANES), jnp.float32),
        ),
        in_specs=whole(3),
        out_specs=tuple(whole(2)),
        scratch_shapes=[field, field, field],
        compiler_params=params,
        cost_estimate=pl.CostEstimate(
            flops=40 * items * rows * LANES, bytes_accessed=16 * items * rows * LANES,
            transcendentals=0,
        ),
        name="inner",
    )(grid, far_x, near_x)
    return pl.pallas_call(
        functools.partial(finish_kernel, shape, chunk),
        out_shape=(
            jax.ShapeDtypeStruct(velocity.shape, jnp.float32),
            jax.ShapeDtypeStruct((comps, 1, 1, slots), jnp.float32),
        ),
        in_specs=whole(8),
        out_specs=tuple(whole(2)),
        scratch_shapes=[field, field, field, pltpu.VMEM((items * wide_x, width), jnp.bfloat16)],
        compiler_params=params,
        name="finish",
    )(quarter, value, dense_y, level, inner, rim, far_y, near_y)


def solution(mesh):
    placed = (
        P(None, None, "gx", "gy"),
        P(None, "gx", "gy", None),
        P(None, "gx", "gy", None),
        P(None, "gx", "gy", None),
        P(),
    )
    return jax.shard_map(
        body,
        mesh=mesh,
        in_specs=placed,
        out_specs=(P(None, None, "gx", "gy"), P(None, "gx", "gy", None)),
        check_vma=False,
    )
```

```python
import functools

import jax
import jax.numpy as jnp
import numpy as np
from jax import lax
from jax.experimental import pallas as pl
from jax.experimental.pallas import tpu as pltpu
from jax.sharding import PartitionSpec as P

MARGIN = 16
FISH_MARK = 1024
HALO = 3
LANES = 128
COURANT = 0.25
VISCOUS = 1.5
ROWS = 8

REACH = MARGIN + HALO
PAD = -(-REACH // ROWS) * ROWS
STRIP = PAD + MARGIN
SPAN = 2 * MARGIN
EDGE_PER = LANES // SPAN


def half_turn(terms):
    nodes = 0.5 - 0.5 * np.cos(np.pi * (np.arange(64) + 0.5) / 64)
    square = nodes * nodes
    cosine = np.polynomial.polynomial.polyfit(square, np.cos(0.5 * np.pi * nodes), terms)
    sine = np.polynomial.polynomial.polyfit(square, np.sin(0.5 * np.pi * nodes) / nodes, terms)
    return [float(v) for v in cosine], [float(v) for v in sine]


COS_FIT, SIN_FIT = half_turn(6)


def horner(coefficients, value):
    total = jnp.full_like(value, coefficients[-1])
    for coefficient in coefficients[-2::-1]:
        total = total * value + coefficient
    return total


def four_weights(frac):
    square = frac * frac
    cosine = horner(COS_FIT, square)
    sine = frac * horner(SIN_FIT, square)
    return (0.25 - 0.25 * sine, 0.25 + 0.25 * cosine, 0.25 + 0.25 * sine, 0.25 - 0.25 * cosine)


def local_cell(cell, low, extent):
    offset = cell - low
    offset = jnp.where(offset < -MARGIN, offset + extent, offset)
    return jnp.where(offset >= extent - MARGIN, offset - extent, offset)


def position():
    row, col = lax.axis_index("gx"), lax.axis_index("gy")
    return row, col, row % 2 == 0, col % 2 == 0


def tile_weights(offset, weights):
    shift = lax.broadcasted_iota(jnp.int32, (ROWS, offset.shape[1]), 0) + 1 - offset
    quarter, phase = shift >> 2, shift & 3
    value = jnp.where(phase == 3, weights[3], weights[2])
    value = jnp.where(phase == 1, weights[1], value)
    return quarter, jnp.where(phase == 0, weights[0], value)


def doubled(quarter, value):
    quarter = jnp.concatenate([quarter, quarter + 2], axis=0).astype(jnp.float32)
    return quarter.astype(jnp.bfloat16), twice(value)


def twice(value):
    return jnp.concatenate([value, value], axis=0).astype(jnp.bfloat16)


def picked_tile(quarter, value, first):
    zero = jnp.zeros_like(value)
    return jnp.where(quarter == jnp.array(-first // 4, quarter.dtype), value, zero)


def half_spread(quarter_ref, force_ref, dense_y_ref, half_ref, base, lanes):
    items, rows = half_ref.shape[:2]
    quarter = quarter_ref[:, lanes] + base
    quarter = jnp.concatenate([quarter, quarter + 2], axis=0).astype(jnp.float32)
    quarter = quarter.astype(jnp.bfloat16)
    left = jnp.concatenate(
        [
            picked_tile(quarter, force_ref[k, :, lanes], row)
            for k in range(items)
            for row in range(0, rows, 2 * ROWS)
        ],
        axis=0,
    )
    total = lax.dot_general(
        left, dense_y_ref[:, lanes], (((1,), (1,)), ((), ())),
        preferred_element_type=jnp.float32,
    )
    total = total.reshape(half_ref.shape)
    if lanes.start:
        half_ref[...] += total
    else:
        half_ref[...] = total


def finish_half(half_ref, velocity_ref, out_ref, low, cells_y):
    items, rows = half_ref.shape[:2]
    comps = items // velocity_ref.shape[0]
    count = rows - MARGIN
    source = pl.ds(pl.multiple_of(jnp.where(low, 0, count), ROWS), count)
    target = pl.ds(pl.multiple_of(jnp.where(low, MARGIN, 0), ROWS), count)
    for k in range(items):
        half_ref[k, target, :cells_y] += velocity_ref[k // comps, k % comps, source]
    place = pl.ds(pl.multiple_of(jnp.where(low, 0, rows - STRIP), ROWS), STRIP)
    parts = [half_ref[k, place, :cells_y] for k in range(items)]
    for group in range(0, items, EDGE_PER):
        edges = []
        for k in range(group, min(group + EDGE_PER, items)):
            edges.append(rolled(half_ref[k, place, cells_y:], SPAN * (k - group)))
        parts.append(functools.reduce(jnp.add, edges))
    out_ref[...] = jnp.concatenate(parts, axis=0).astype(jnp.bfloat16)


def far_kernel(
    shape, chunk, fish_hbm, velocity_hbm, cell_hbm, frac_hbm, force_hbm,
    half_ref, far_ref, force_out, dense_y_ref, quarter_ref, value_ref, level_ref,
    fish_ref, velocity_ref, cell_ref, frac_ref, force_ref, sems,
):
    pairs = (
        (cell_hbm, cell_ref), (frac_hbm, frac_ref), (fish_hbm, fish_ref),
        (force_hbm, force_ref), (velocity_hbm, velocity_ref),
    )
    copies = [pltpu.make_async_copy(a, b, sems.at[i]) for i, (a, b) in enumerate(pairs)]
    for copy in copies:
        copy.start()
    cells_x, cells_y, extent_x, extent_y = shape
    levels, comps = velocity_ref.shape[:2]
    slots = cell_ref.shape[3]
    row, col, even, _ = position()
    base = jnp.where(even, -MARGIN // 4, cells_x // 8)
    for copy in copies[:-1]:
        copy.wait()
    mine = jnp.where(fish_ref[...] == row * lax.axis_size("gy") + col, 1.0, 0.0)
    count = FISH_MARK * jnp.sum(mine)
    level_ref[...] = cell_ref[2, 0]
    for first in range(0, slots, chunk):
        lanes = slice(first, first + chunk)
        offset_x = local_cell(cell_ref[0, 0, :, lanes], row * cells_x, extent_x)
        offset_y = local_cell(cell_ref[1, 0, :, lanes], col * cells_y, extent_y)
        slot = lax.broadcasted_iota(jnp.int32, (1, chunk), 1) + first
        alive = jnp.where(slot.astype(jnp.float32) < count, 1.0, 0.0)
        quarter, value = tile_weights(offset_x, four_weights(frac_ref[0, 0, :, lanes]))
        value = value * alive
        quarter_ref[:, lanes] = quarter
        value_ref[:, lanes] = value
        level = cell_ref[2, 0, :, lanes]
        pushes = [force_ref[c, 0, :, lanes] * value for c in range(comps)]
        for l in range(levels):
            for c in range(comps):
                force_out[l * comps + c, :, lanes] = twice(jnp.where(level == l, pushes[c], 0.0))
        quarter, value = doubled(
            *tile_weights(offset_y, four_weights(frac_ref[1, 0, :, lanes]))
        )
        dense_y_ref[:, lanes] = jnp.concatenate(
            [picked_tile(quarter, value, n) for n in range(0, cells_y + MARGIN, 2 * ROWS)]
            + [jnp.zeros((LANES - SPAN, chunk), jnp.bfloat16)]
            + [picked_tile(quarter, value, n) for n in range(-MARGIN, 0, 2 * ROWS)],
            axis=0,
        )
        half_spread(quarter_ref, force_out, dense_y_ref, half_ref, base, lanes)
    copies[-1].wait()
    finish_half(half_ref, velocity_ref, far_ref, even, cells_y)


def near_kernel(
    shape, chunk, velocity_ref, far_half_ref, force_ref, dense_y_ref, quarter_ref,
    grid_ref, near_ref, half_ref,
):
    cells_x, cells_y, _, _ = shape
    slots = quarter_ref.shape[1]
    rows = half_ref.shape[1]
    _, _, even, _ = position()
    base = jnp.where(even, cells_x // 8, -MARGIN // 4)
    for first in range(0, slots, chunk):
        lanes = slice(first, first + chunk)
        half_spread(quarter_ref, force_ref, dense_y_ref, half_ref, base, lanes)
    finish_half(half_ref, velocity_ref, near_ref, jnp.logical_not(even), cells_y)
    for ref, row in ((far_half_ref, jnp.where(even, 0, rows)), (half_ref, jnp.where(even, rows, 0))):
        place = pl.ds(pl.multiple_of(row, ROWS), rows)
        for k in range(ref.shape[0]):
            grid_ref[k, place] = ref[k]


def rolled(value, shift):
    shift = shift % LANES
    return pltpu.roll(value, shift, 1) if shift else value


def lane_index(rows):
    return lax.broadcasted_iota(jnp.int32, (rows, LANES), 1)


def strip_parts(near, far, k, items, even):
    lane = lane_index(STRIP)
    row = (items + k // EDGE_PER) * STRIP
    parts = []
    for first, second in ((far, near), (near, far)):
        inner = jnp.where(
            even,
            first[k * STRIP : (k + 1) * STRIP].astype(jnp.float32),
            second[k * STRIP : (k + 1) * STRIP].astype(jnp.float32),
        )
        edge = jnp.where(
            even,
            first[row : row + STRIP].astype(jnp.float32),
            second[row : row + STRIP].astype(jnp.float32),
        )
        edge = rolled(edge, -SPAN * (k % EDGE_PER))
        edge = jnp.where((lane < MARGIN) | (lane >= LANES - MARGIN), edge, 0.0)
        parts.append((inner, edge))
    return parts


def joined(center, before, after):
    wide = center.shape[0]
    near = PAD - MARGIN
    overlap = STRIP - near
    return jnp.concatenate(
        [
            before[:near],
            center[:overlap] + before[near:],
            center[overlap : wide - overlap],
            center[wide - overlap :] + after[:overlap],
            after[overlap:],
        ],
        axis=0,
    )


def extended_rows(grid_ref, near, far, k, items, cells_y, even):
    before, after = strip_parts(near, far, k, items, even)
    inner = joined(grid_ref[k, :, :cells_y], before[0], after[0])
    edge = joined(grid_ref[k, :, cells_y:], before[1], after[1])
    return inner, edge


def folds(rows):
    return [(row, min(SPAN, rows - row)) for row in range(0, rows, SPAN)]


def partners():
    col, size = lax.axis_index("gy"), lax.axis_size("gy")
    even = col % 2 == 0
    return jnp.where(even, (col + size - 1) % size, (col + 1) % size), jnp.where(even, col + 1, col - 1)


def by_partner(refs):
    if len(refs) == 2:
        return refs
    count = refs[0].shape[0] // lax.axis_size("gy")
    return [refs[0].at[pl.ds(pl.multiple_of(p * count, 16), count)] for p in partners()]


def pack_kernel(shape, grid_ref, far_x, near_x, *out_refs):
    far_ref, near_ref = by_partner(out_refs)
    cells_x, cells_y, _, _ = shape
    items = grid_ref.shape[0]
    groups = -(-items // EDGE_PER)
    rows = cells_x + 2 * PAD
    lane = lane_index(rows)
    _, _, even_x, even = position()
    up_halo = (lane >= LANES - REACH) & (lane < LANES - MARGIN)
    down_halo = (lane >= MARGIN) & (lane < REACH)
    halos = None
    for group in range(groups):
        ups, downs = None, None
        for k in range(group * EDGE_PER, min((group + 1) * EDGE_PER, items)):
            inner, edge = extended_rows(grid_ref, near_x, far_x, k, items, cells_y, even_x)
            shift = SPAN * (k % EDGE_PER)
            up = rolled(jnp.where(lane >= LANES - MARGIN, inner, edge), shift)
            down = rolled(jnp.where(lane < MARGIN, inner, edge), shift)
            halo = rolled(jnp.where(up_halo | down_halo, inner, 0.0), REACH + HALO * k)
            ups = up if ups is None else ups + up
            downs = down if downs is None else downs + down
            halos = halo if halos is None else halos + halo
        place = slice(group * rows, (group + 1) * rows)
        near_ref[place] = jnp.where(even, ups, downs).astype(jnp.bfloat16)
        far_ref[place] = jnp.where(even, downs, ups).astype(jnp.bfloat16)
    ups = jnp.where(lane < HALO * items, halos, 0.0)
    downs = jnp.where(lane < HALO * items, rolled(halos, -MARGIN - REACH), 0.0)
    for out_ref, total in (
        (near_ref, jnp.where(even, ups, downs)), (far_ref, jnp.where(even, downs, ups)),
    ):
        folded = total[:SPAN]
        for index, (row, size) in enumerate(folds(rows)[1:]):
            piece = rolled(total[row : row + size], SPAN * (index + 1))
            if size < SPAN:
                gap = jnp.zeros((SPAN - size, LANES), jnp.float32)
                piece = jnp.concatenate([piece, gap], axis=0)
            folded = folded + piece
        out_ref[groups * rows : groups * rows + SPAN] = folded.astype(jnp.bfloat16)


def unfolded(ref, rows, groups):
    folded = ref[groups * rows : groups * rows + SPAN].astype(jnp.float32)
    return jnp.concatenate(
        [rolled(folded, -SPAN * index)[:size] for index, (_, size) in enumerate(folds(rows))],
        axis=0,
    )


def around(ref, k, start, size):
    center = ref[k, start : start + size]
    back = ref[k, start - 1 : start - 1 + size]
    fore = ref[k, start + 1 : start + 1 + size]
    return center, back, fore, rolled(center, 1), rolled(center, -1)


def advect(moved_ref, carried_ref, levels, comps, rows):
    for start in range(ROWS, ROWS + rows, ROWS):
        for l in range(levels):
            pieces = [around(moved_ref, l * comps + c, start, ROWS) for c in range(comps)]
            speed_x, speed_y = COURANT * pieces[0][0], COURANT * pieces[1][0]
            ahead_x, astern_x = jnp.maximum(speed_x, 0.0), jnp.minimum(speed_x, 0.0)
            ahead_y, astern_y = jnp.maximum(speed_y, 0.0), jnp.minimum(speed_y, 0.0)
            for c in range(comps):
                center, back, fore, below, above = pieces[c]
                change = ahead_x * (center - back) + astern_x * (fore - center)
                change = change + ahead_y * (center - below) + astern_y * (above - center)
                carried_ref[l * comps + c, start : start + ROWS] = center - change


def sweep(ref, carried_ref, levels, comps, start, size):
    scale = 1.0 / (1.0 + 6.0 * VISCOUS)
    centers, results = [], []
    for k in range(levels * comps):
        center, back, fore, below, above = around(ref, k, start, size)
        centers.append(center)
        results.append(back + fore + below + above)
    for k in range(levels * comps):
        higher = min(k // comps + 1, levels - 1) * comps + k % comps
        lower = max(k // comps - 1, 0) * comps + k % comps
        summed = results[k] + centers[higher] + centers[lower]
        source = carried_ref[k, start : start + size]
        results[k] = scale * source + (VISCOUS * scale) * summed
    return results


def first_steps(moved_ref, carried_ref, sweep_ref, levels, comps, rows):
    advect(moved_ref, carried_ref, levels, comps, rows)
    for start in range(ROWS, ROWS + rows, ROWS):
        results = sweep(carried_ref, carried_ref, levels, comps, start, ROWS)
        for k in range(levels * comps):
            sweep_ref[k, start : start + ROWS] = results[k]


RIM = REACH + HALO
HALF = LANES // 2


def inner_kernel(
    shape, levels, grid_ref, far_x, near_x, inner_ref, rim_ref, moved_ref, carried_ref, sweep_ref,
):
    cells_x, cells_y, _, _ = shape
    items = grid_ref.shape[0]
    comps = items // levels
    wide_x = cells_x + SPAN
    rows = cells_x + 2 * PAD
    lane = lane_index(rows)
    _, _, even_x, _ = position()
    for k in range(items):
        inner, edge = extended_rows(grid_ref, near_x, far_x, k, items, cells_y, even_x)
        moved_ref[k, ROWS : ROWS + rows] = inner
        low = jnp.where(lane < RIM, inner, jnp.where(lane >= LANES - MARGIN, edge, 0.0))
        high = jnp.where(lane >= LANES - RIM, inner, jnp.where(lane < MARGIN, edge, 0.0))
        rim_ref[k] = low + rolled(high, HALF)
    first_steps(moved_ref, carried_ref, sweep_ref, levels, comps, rows)
    for row in range(0, wide_x, ROWS):
        start = ROWS + PAD - MARGIN + row
        results = sweep(sweep_ref, carried_ref, levels, comps, start, ROWS)
        for k in range(items):
            inner_ref[k, row : row + ROWS] = results[k]


def finish_kernel(
    shape, chunk, quarter_ref, value_ref, dense_y_ref, level_ref, inner_ref, rim_ref, *refs,
):
    far_y, near_y = by_partner(refs[:-6])
    next_ref, sampled_ref, moved_ref, carried_ref, sweep_ref, round_ref = refs[-6:]
    cells_x, cells_y, _, _ = shape
    items = rim_ref.shape[0]
    groups = -(-items // EDGE_PER)
    levels, comps = next_ref.shape[:2]
    slots = level_ref.shape[1]
    wide_x = cells_x + SPAN
    rows = cells_x + 2 * PAD
    lane = lane_index(rows)
    _, _, _, even = position()
    near_halo, far_halo = unfolded(near_y, rows, groups), unfolded(far_y, rows, groups)
    before = jnp.where(even, far_halo, near_halo)
    after = rolled(jnp.where(even, near_halo, far_halo), HALF + MARGIN + REACH)
    turned = (HALF + MARGIN + REACH) % LANES
    halo = jnp.where((lane >= turned) & (lane < turned + HALO * items), after, before)
    for group in range(groups):
        row = group * rows
        near = near_y[row : row + rows].astype(jnp.float32)
        far = far_y[row : row + rows].astype(jnp.float32)
        before = jnp.where(even, far, near)
        after = rolled(jnp.where(even, near, far), HALF)
        for k in range(group * EDGE_PER, min((group + 1) * EDGE_PER, items)):
            slot = k % EDGE_PER
            place = (lane + (LANES + MARGIN - SPAN * slot)) % LANES
            main = rolled(jnp.where(place < SPAN, before, after), -SPAN * slot)
            place = (lane + MARGIN) % HALF
            value = rim_ref[k] + jnp.where(place < SPAN, main, 0.0)
            outer = rolled(halo, -REACH - HALO * k)
            low = (lane >= LANES - REACH) & (lane < LANES - MARGIN)
            high = (lane >= HALF + MARGIN) & (lane < HALF + REACH)
            moved_ref[k, ROWS : ROWS + rows] = jnp.where(low | high, outer, value)

    first_steps(moved_ref, carried_ref, sweep_ref, levels, comps, rows)
    size = 2 * ROWS
    lane = lane_index(size)
    for row in range(0, wide_x, size):
        start = ROWS + PAD - MARGIN + row
        results = sweep(sweep_ref, carried_ref, levels, comps, start, size)
        for k in range(items):
            low, high = results[k], rolled(results[k], HALF)
            inner = inner_ref[k, row : row + size]
            inner = jnp.where(lane < REACH, low, jnp.where(lane >= LANES - REACH, high, inner))
            edge = jnp.where(lane < MARGIN, high, low)
            place = slice(k * wide_x + row, k * wide_x + row + size)
            round_ref[place, :cells_y] = inner.astype(jnp.bfloat16)
            round_ref[place, cells_y:] = edge.astype(jnp.bfloat16)
            if MARGIN <= row < MARGIN + cells_x:
                next_ref[k // comps, k % comps, row - MARGIN : row - MARGIN + size] = inner

    for first in range(0, slots, chunk):
        lanes = slice(first, first + chunk)
        level = level_ref[:, lanes]
        partial = jnp.dot(
            round_ref[...], dense_y_ref[:, lanes], preferred_element_type=jnp.float32
        )
        partial = partial.reshape(levels, comps, wide_x, chunk)
        quarter, value = quarter_ref[:, lanes], value_ref[:, lanes]
        heres = [quarter == (MARGIN - row) // 4 for row in range(0, wide_x, ROWS)]
        aboves = [level == l for l in range(levels - 1)]
        for c in range(comps):
            total = jnp.zeros((ROWS, chunk), jnp.float32)
            for row in range(0, wide_x, ROWS):
                picked = partial[levels - 1, c, row : row + ROWS]
                for l in range(levels - 2, -1, -1):
                    picked = jnp.where(aboves[l], partial[l, c, row : row + ROWS], picked)
                total = jnp.where(heres[row // ROWS], picked, total)
            sampled_ref[c, 0, :, lanes] = jnp.sum(total * value, axis=0, keepdims=True)


def whole(count):
    return [pl.BlockSpec(memory_space=pltpu.VMEM)] * count


def swap_pairs(axis):
    size = lax.axis_size(axis)
    if size % 2:
        raise ValueError("odd axis")
    far_pairs = [(i, (i - 1 if i % 2 == 0 else i + 1) % size) for i in range(size)]
    return far_pairs, [(i, i ^ 1) for i in range(size)]


def body(velocity, marker_cell, marker_frac, marker_force, fish_owner):
    levels, comps, cells_x, cells_y = velocity.shape
    slots = marker_cell.shape[3]
    items = levels * comps
    shape = (cells_x, cells_y, cells_x * lax.axis_size("gx"), cells_y * lax.axis_size("gy"))
    wide_x = cells_x + SPAN
    rows = cells_x + 2 * PAD
    chunk = min(512, slots)
    width = cells_y + LANES
    groups = -(-items // EDGE_PER)
    params = pltpu.CompilerParams(vmem_limit_bytes=40 * 1024 * 1024)
    edge_x = jax.ShapeDtypeStruct(((items + groups) * STRIP, LANES), jnp.bfloat16)
    half = (items, wide_x // 2, width)
    arrays = (fish_owner, velocity, marker_cell, marker_frac, marker_force)
    far_half, far, force, dense_y, quarter, value, level = pl.pallas_call(
        functools.partial(far_kernel, shape, chunk),
        out_shape=(
            jax.ShapeDtypeStruct(half, jnp.float32),
            edge_x,
            jax.ShapeDtypeStruct((items, 2 * ROWS, slots), jnp.bfloat16),
            jax.ShapeDtypeStruct((width, slots), jnp.bfloat16),
            jax.ShapeDtypeStruct((ROWS, slots), jnp.int32),
            jax.ShapeDtypeStruct((ROWS, slots), jnp.float32),
            jax.ShapeDtypeStruct((1, slots), jnp.int32),
        ),
        in_specs=[pl.BlockSpec(memory_space=pltpu.HBM)] * 5,
        out_specs=tuple(whole(7)),
        scratch_shapes=[pltpu.VMEM(a.shape, a.dtype) for a in arrays]
        + [pltpu.SemaphoreType.DMA((5,))],
        compiler_params=params,
        name="spread_far",
    )(*(pltpu.with_memory_space_constraint(a, pltpu.HBM) for a in arrays))
    far_pairs, near_pairs = swap_pairs("gx")
    far_x = lax.ppermute(far, "gx", far_pairs)
    grid, near = pl.pallas_call(
        functools.partial(near_kernel, shape, chunk),
        out_shape=(jax.ShapeDtypeStruct((items, wide_x, width), jnp.float32), edge_x),
        in_specs=whole(5),
        out_specs=tuple(whole(2)),
        scratch_shapes=[pltpu.VMEM(half, jnp.float32)],
        compiler_params=params,
        cost_estimate=pl.CostEstimate(
            flops=items * wide_x * width * slots, bytes_accessed=4 * items * wide_x * width,
            transcendentals=0,
        ),
        name="spread_near",
    )(velocity, far_half, force, dense_y, quarter)
    near_x = lax.ppermute(near, "gx", near_pairs)
    size_y = lax.axis_size("gy")
    together = size_y <= 4
    edge_rows = groups * rows + SPAN
    if together:
        edges_y = (jax.ShapeDtypeStruct((size_y * edge_rows, LANES), jnp.bfloat16),)
    else:
        edges_y = (jax.ShapeDtypeStruct((edge_rows, LANES), jnp.bfloat16),) * 2
    sent = pl.pallas_call(
        functools.partial(pack_kernel, shape),
        out_shape=edges_y,
        in_specs=whole(3),
        out_specs=tuple(whole(len(edges_y))),
        compiler_params=params,
        name="pack",
    )(grid, far_x, near_x)
    if together:
        received = (lax.all_to_all(sent[0], "gy", 0, 0, tiled=True),)
    else:
        received = tuple(lax.ppermute(a, "gy", p) for a, p in zip(sent, swap_pairs("gy")))
    field = pltpu.VMEM((items, rows + 2 * ROWS, LANES), jnp.float32)
    inner, rim = pl.pallas_call(
        functools.partial(inner_kernel, shape, levels),
        out_shape=(
            jax.ShapeDtypeStruct((items, wide_x, LANES), jnp.float32),
            jax.ShapeDtypeStruct((items, rows, LANES), jnp.float32),
        ),
        in_specs=whole(3),
        out_specs=tuple(whole(2)),
        scratch_shapes=[field, field, field],
        compiler_params=params,
        cost_estimate=pl.CostEstimate(
            flops=40 * items * rows * LANES, bytes_accessed=16 * items * rows * LANES,
            transcendentals=0,
        ),
        name="inner",
    )(grid, far_x, near_x)
    return pl.pallas_call(
        functools.partial(finish_kernel, shape, chunk),
        out_shape=(
            jax.ShapeDtypeStruct(velocity.shape, jnp.float32),
            jax.ShapeDtypeStruct((comps, 1, 1, slots), jnp.float32),
        ),
        in_specs=whole(6 + len(received)),
        out_specs=tuple(whole(2)),
        scratch_shapes=[field, field, field, pltpu.VMEM((items * wide_x, width), jnp.bfloat16)],
        compiler_params=params,
        name="finish",
    )(quarter, value, dense_y, level, inner, rim, *received)


def solution(mesh):
    placed = (
        P(None, None, "gx", "gy"),
        P(None, "gx", "gy", None),
        P(None, "gx", "gy", None),
        P(None, "gx", "gy", None),
        P(),
    )
    return jax.shard_map(
        body,
        mesh=mesh,
        in_specs=placed,
        out_specs=(P(None, None, "gx", "gy"), P(None, "gx", "gy", None)),
        check_vma=False,
    )
```

```python
import functools

import jax
import jax.numpy as jnp
import numpy as np
from jax import lax
from jax.experimental import pallas as pl
from jax.experimental.pallas import tpu as pltpu
from jax.sharding import PartitionSpec as P

MARGIN = 16
FISH_MARK = 1024
HALO = 3
LANES = 128
COURANT = 0.25
VISCOUS = 1.5
ROWS = 8

REACH = MARGIN + HALO
PAD = -(-REACH // ROWS) * ROWS
STRIP = PAD + MARGIN
SPAN = 2 * MARGIN
EDGE_PER = LANES // SPAN


def half_turn(terms):
    nodes = 0.5 - 0.5 * np.cos(np.pi * (np.arange(64) + 0.5) / 64)
    square = nodes * nodes
    cosine = np.polynomial.polynomial.polyfit(square, np.cos(0.5 * np.pi * nodes), terms)
    sine = np.polynomial.polynomial.polyfit(square, np.sin(0.5 * np.pi * nodes) / nodes, terms)
    return [float(v) for v in cosine], [float(v) for v in sine]


COS_FIT, SIN_FIT = half_turn(6)


def horner(coefficients, value):
    total = jnp.full_like(value, coefficients[-1])
    for coefficient in coefficients[-2::-1]:
        total = total * value + coefficient
    return total


def four_weights(frac):
    square = frac * frac
    cosine = horner(COS_FIT, square)
    sine = frac * horner(SIN_FIT, square)
    return (0.25 - 0.25 * sine, 0.25 + 0.25 * cosine, 0.25 + 0.25 * sine, 0.25 - 0.25 * cosine)


def local_cell(cell, low, extent):
    offset = cell - low
    offset = jnp.where(offset < -MARGIN, offset + extent, offset)
    return jnp.where(offset >= extent - MARGIN, offset - extent, offset)


def position():
    row, col = lax.axis_index("gx"), lax.axis_index("gy")
    return row, col, row % 2 == 0, col % 2 == 0


def tile_weights(offset, weights):
    shift = lax.broadcasted_iota(jnp.int32, (ROWS, offset.shape[1]), 0) + 1 - offset
    quarter, phase = shift >> 2, shift & 3
    value = jnp.where(phase == 3, weights[3], weights[2])
    value = jnp.where(phase == 1, weights[1], value)
    return quarter, jnp.where(phase == 0, weights[0], value)


def doubled(quarter, value):
    quarter = jnp.concatenate([quarter, quarter + 2], axis=0).astype(jnp.float32)
    return quarter.astype(jnp.bfloat16), twice(value)


def twice(value):
    return jnp.concatenate([value, value], axis=0).astype(jnp.bfloat16)


def picked_tile(quarter, value, first):
    zero = jnp.zeros_like(value)
    return jnp.where(quarter == jnp.array(-first // 4, quarter.dtype), value, zero)


def half_spread(quarter_ref, force_ref, dense_y_ref, half_ref, base, lanes):
    items, rows = half_ref.shape[:2]
    quarter = quarter_ref[:, lanes] + base
    quarter = jnp.concatenate([quarter, quarter + 2], axis=0).astype(jnp.float32)
    quarter = quarter.astype(jnp.bfloat16)
    left = jnp.concatenate(
        [
            picked_tile(quarter, force_ref[k, :, lanes], row)
            for k in range(items)
            for row in range(0, rows, 2 * ROWS)
        ],
        axis=0,
    )
    total = lax.dot_general(
        left, dense_y_ref[:, lanes], (((1,), (1,)), ((), ())),
        preferred_element_type=jnp.float32,
    )
    total = total.reshape(half_ref.shape)
    if lanes.start:
        half_ref[...] += total
    else:
        half_ref[...] = total


def finish_half(half_ref, velocity_ref, out_ref, low, cells_y):
    items, rows = half_ref.shape[:2]
    comps = items // velocity_ref.shape[0]
    count = rows - MARGIN
    source = pl.ds(pl.multiple_of(jnp.where(low, 0, count), ROWS), count)
    target = pl.ds(pl.multiple_of(jnp.where(low, MARGIN, 0), ROWS), count)
    for k in range(items):
        half_ref[k, target, :cells_y] += velocity_ref[k // comps, k % comps, source]
    place = pl.ds(pl.multiple_of(jnp.where(low, 0, rows - STRIP), ROWS), STRIP)
    parts = [half_ref[k, place, :cells_y] for k in range(items)]
    for group in range(0, items, EDGE_PER):
        edges = []
        for k in range(group, min(group + EDGE_PER, items)):
            edges.append(rolled(half_ref[k, place, cells_y:], SPAN * (k - group)))
        parts.append(functools.reduce(jnp.add, edges))
    out_ref[...] = jnp.concatenate(parts, axis=0).astype(jnp.bfloat16)


def far_kernel(
    shape, chunk, fish_hbm, velocity_hbm, cell_hbm, frac_hbm, force_hbm,
    half_ref, far_ref, force_out, dense_y_ref, quarter_ref, value_ref, level_ref, parity_ref,
    fish_ref, velocity_ref, cell_ref, frac_ref, force_ref, sems,
):
    pairs = (
        (cell_hbm, cell_ref), (frac_hbm, frac_ref), (fish_hbm, fish_ref),
        (force_hbm, force_ref), (velocity_hbm, velocity_ref),
    )
    copies = [pltpu.make_async_copy(a, b, sems.at[i]) for i, (a, b) in enumerate(pairs)]
    for copy in copies:
        copy.start()
    cells_x, cells_y, extent_x, extent_y = shape
    levels, comps = velocity_ref.shape[:2]
    slots = cell_ref.shape[3]
    row, col, even, even_y = position()
    parity_ref[0:1] = jnp.full((1, LANES), jnp.where(even, 1, 0), jnp.int32)
    parity_ref[1:2] = jnp.full((1, LANES), jnp.where(even_y, 1, 0), jnp.int32)
    base = jnp.where(even, -MARGIN // 4, cells_x // 8)
    for copy in copies[:-1]:
        copy.wait()
    mine = jnp.where(fish_ref[...] == row * lax.axis_size("gy") + col, 1.0, 0.0)
    count = FISH_MARK * jnp.sum(mine)
    level_ref[...] = cell_ref[2, 0]
    for first in range(0, slots, chunk):
        lanes = slice(first, first + chunk)
        offset_x = local_cell(cell_ref[0, 0, :, lanes], row * cells_x, extent_x)
        offset_y = local_cell(cell_ref[1, 0, :, lanes], col * cells_y, extent_y)
        slot = lax.broadcasted_iota(jnp.int32, (1, chunk), 1) + first
        alive = jnp.where(slot.astype(jnp.float32) < count, 1.0, 0.0)
        quarter, value = tile_weights(offset_x, four_weights(frac_ref[0, 0, :, lanes]))
        value = value * alive
        quarter_ref[:, lanes] = quarter
        value_ref[:, lanes] = value
        level = cell_ref[2, 0, :, lanes]
        pushes = [force_ref[c, 0, :, lanes] * value for c in range(comps)]
        for l in range(levels):
            for c in range(comps):
                force_out[l * comps + c, :, lanes] = twice(jnp.where(level == l, pushes[c], 0.0))
        quarter, value = doubled(
            *tile_weights(offset_y, four_weights(frac_ref[1, 0, :, lanes]))
        )
        dense_y_ref[:, lanes] = jnp.concatenate(
            [picked_tile(quarter, value, n) for n in range(0, cells_y + MARGIN, 2 * ROWS)]
            + [jnp.zeros((LANES - SPAN, chunk), jnp.bfloat16)]
            + [picked_tile(quarter, value, n) for n in range(-MARGIN, 0, 2 * ROWS)],
            axis=0,
        )
        half_spread(quarter_ref, force_out, dense_y_ref, half_ref, base, lanes)
    copies[-1].wait()
    finish_half(half_ref, velocity_ref, far_ref, even, cells_y)


def near_kernel(
    shape, chunk, velocity_ref, far_half_ref, force_ref, dense_y_ref, quarter_ref,
    grid_ref, near_ref, half_ref,
):
    cells_x, cells_y, _, _ = shape
    slots = quarter_ref.shape[1]
    rows = half_ref.shape[1]
    _, _, even, _ = position()
    base = jnp.where(even, cells_x // 8, -MARGIN // 4)
    for first in range(0, slots, chunk):
        lanes = slice(first, first + chunk)
        half_spread(quarter_ref, force_ref, dense_y_ref, half_ref, base, lanes)
    finish_half(half_ref, velocity_ref, near_ref, jnp.logical_not(even), cells_y)
    for ref, row in ((far_half_ref, jnp.where(even, 0, rows)), (half_ref, jnp.where(even, rows, 0))):
        place = pl.ds(pl.multiple_of(row, ROWS), rows)
        for k in range(ref.shape[0]):
            grid_ref[k, place] = ref[k]


def rolled(value, shift):
    shift = shift % LANES
    return pltpu.roll(value, shift, 1) if shift else value


def lane_index(rows):
    return lax.broadcasted_iota(jnp.int32, (rows, LANES), 1)


def ordered(parity, near_ref, far_ref, before_ref, after_ref):
    rows = near_ref.shape[0]
    even = jnp.broadcast_to(parity, (2 * ROWS, LANES)) != 0
    for row in range(0, rows, 2 * ROWS):
        near = near_ref[row : row + 2 * ROWS].astype(jnp.float32)
        far = far_ref[row : row + 2 * ROWS].astype(jnp.float32)
        before_ref[row : row + 2 * ROWS] = jnp.where(even, far, near)
        after_ref[row : row + 2 * ROWS] = jnp.where(even, near, far)


def strip_tile(ref, k, items, row):
    lane = lane_index(ROWS)
    inner = ref[k * STRIP + row : k * STRIP + row + ROWS]
    start = (items + k // EDGE_PER) * STRIP + row
    edge = rolled(ref[start : start + ROWS], -SPAN * (k % EDGE_PER))
    return inner, jnp.where((lane < MARGIN) | (lane >= LANES - MARGIN), edge, 0.0)


def extended_tile(grid_ref, before_ref, after_ref, k, row, cells_y):
    items, wide = grid_ref.shape[:2]
    near = PAD - MARGIN
    parts = []
    if near <= row < near + wide:
        place = slice(row - near, row - near + ROWS)
        parts.append((grid_ref[k, place, :cells_y], grid_ref[k, place, cells_y:]))
    if row < STRIP:
        parts.append(strip_tile(before_ref, k, items, row))
    if row >= wide + 2 * near - STRIP:
        parts.append(strip_tile(after_ref, k, items, row - (wide + 2 * near - STRIP)))
    return tuple(functools.reduce(jnp.add, part) for part in zip(*parts))


def pack_kernel(
    shape, parity_ref, grid_ref, far_x, near_x, far_ref, near_ref, before_ref, after_ref,
):
    cells_x, cells_y, _, _ = shape
    items = grid_ref.shape[0]
    groups = -(-items // EDGE_PER)
    rows = cells_x + 2 * PAD
    lane = lane_index(ROWS)
    ordered(parity_ref[0:1], near_x, far_x, before_ref, after_ref)
    even = jnp.broadcast_to(parity_ref[1:2], (2 * ROWS, LANES)) != 0
    up_halo = (lane >= LANES - REACH) & (lane < LANES - MARGIN)
    down_halo = (lane >= MARGIN) & (lane < REACH)

    def store(row, up, down):
        near_ref[row : row + 2 * ROWS] = jnp.where(even, up, down).astype(jnp.bfloat16)
        far_ref[row : row + 2 * ROWS] = jnp.where(even, down, up).astype(jnp.bfloat16)

    folded = {}
    for pair in range(0, rows, 2 * ROWS):
        packed = [[], []]
        for row in (pair, pair + ROWS):
            sums = [[None] * groups, [None] * groups]
            halo = None
            for k in range(items):
                inner, edge = extended_tile(grid_ref, before_ref, after_ref, k, row, cells_y)
                shift = SPAN * (k % EDGE_PER)
                sides = (
                    rolled(jnp.where(lane >= LANES - MARGIN, inner, edge), shift),
                    rolled(jnp.where(lane < MARGIN, inner, edge), shift),
                )
                for side, group in ((0, k // EDGE_PER), (1, k // EDGE_PER)):
                    old = sums[side][group]
                    sums[side][group] = sides[side] if old is None else old + sides[side]
                extra = rolled(jnp.where(up_halo | down_halo, inner, 0.0), REACH + HALO * k)
                halo = extra if halo is None else halo + extra
            fold, place = row // SPAN, row % SPAN
            used = lane < HALO * items
            turned = rolled(halo, -MARGIN - REACH)
            for side, value in enumerate((halo, turned)):
                value = rolled(jnp.where(used, value, 0.0), SPAN * fold)
                key = (side, place)
                folded[key] = folded[key] + value if key in folded else value
                packed[side].append(sums[side])
        for group in range(groups):
            up, down = (
                jnp.concatenate([part[group] for part in packed[side]], axis=0)
                for side in range(2)
            )
            store(group * rows + pair, up, down)
    for place in range(0, SPAN, 2 * ROWS):
        up, down = (
            jnp.concatenate([folded[side, place], folded[side, place + ROWS]], axis=0)
            for side in range(2)
        )
        store(groups * rows + place, up, down)


def around(ref, k, start, size):
    center = ref[k, start : start + size]
    back = ref[k, start - 1 : start - 1 + size]
    fore = ref[k, start + 1 : start + 1 + size]
    return center, back, fore, rolled(center, 1), rolled(center, -1)


def advect(moved_ref, carried_ref, levels, comps, rows):
    for start in range(ROWS, ROWS + rows, ROWS):
        for l in range(levels):
            pieces = [around(moved_ref, l * comps + c, start, ROWS) for c in range(comps)]
            speed_x, speed_y = COURANT * pieces[0][0], COURANT * pieces[1][0]
            ahead_x, astern_x = jnp.maximum(speed_x, 0.0), jnp.minimum(speed_x, 0.0)
            ahead_y, astern_y = jnp.maximum(speed_y, 0.0), jnp.minimum(speed_y, 0.0)
            for c in range(comps):
                center, back, fore, below, above = pieces[c]
                change = ahead_x * (center - back) + astern_x * (fore - center)
                change = change + ahead_y * (center - below) + astern_y * (above - center)
                carried_ref[l * comps + c, start : start + ROWS] = center - change


def sweep(ref, carried_ref, levels, comps, start, size):
    scale = 1.0 / (1.0 + 6.0 * VISCOUS)
    centers, results = [], []
    for k in range(levels * comps):
        center, back, fore, below, above = around(ref, k, start, size)
        centers.append(center)
        results.append(back + fore + below + above)
    for k in range(levels * comps):
        higher = min(k // comps + 1, levels - 1) * comps + k % comps
        lower = max(k // comps - 1, 0) * comps + k % comps
        summed = results[k] + centers[higher] + centers[lower]
        source = carried_ref[k, start : start + size]
        results[k] = scale * source + (VISCOUS * scale) * summed
    return results


def first_steps(moved_ref, carried_ref, sweep_ref, levels, comps, rows):
    advect(moved_ref, carried_ref, levels, comps, rows)
    for start in range(ROWS, ROWS + rows, ROWS):
        results = sweep(carried_ref, carried_ref, levels, comps, start, ROWS)
        for k in range(levels * comps):
            sweep_ref[k, start : start + ROWS] = results[k]


RIM = REACH + HALO
HALF = LANES // 2


def inner_kernel(
    shape, levels, parity_ref, grid_ref, far_x, near_x, inner_ref, rim_ref,
    moved_ref, carried_ref, sweep_ref, before_ref, after_ref,
):
    cells_x, cells_y, _, _ = shape
    items = grid_ref.shape[0]
    comps = items // levels
    wide_x = cells_x + SPAN
    rows = cells_x + 2 * PAD
    lane = lane_index(ROWS)
    ordered(parity_ref[0:1], near_x, far_x, before_ref, after_ref)
    for row in range(0, rows, ROWS):
        for k in range(items):
            inner, edge = extended_tile(grid_ref, before_ref, after_ref, k, row, cells_y)
            moved_ref[k, ROWS + row : 2 * ROWS + row] = inner
            low = jnp.where(lane < RIM, inner, jnp.where(lane >= LANES - MARGIN, edge, 0.0))
            high = jnp.where(lane >= LANES - RIM, inner, jnp.where(lane < MARGIN, edge, 0.0))
            rim_ref[k, row : row + ROWS] = low + rolled(high, HALF)
    first_steps(moved_ref, carried_ref, sweep_ref, levels, comps, rows)
    for row in range(0, wide_x, ROWS):
        start = ROWS + PAD - MARGIN + row
        results = sweep(sweep_ref, carried_ref, levels, comps, start, ROWS)
        for k in range(items):
            inner_ref[k, row : row + ROWS] = results[k]


def finish_kernel(
    shape, chunk, parity_ref, quarter_ref, value_ref, dense_y_ref, level_ref, inner_ref, rim_ref,
    far_y, near_y, next_ref, sampled_ref,
    moved_ref, carried_ref, sweep_ref, before_ref, after_ref, round_ref,
):
    cells_x, cells_y, _, _ = shape
    items = rim_ref.shape[0]
    groups = -(-items // EDGE_PER)
    levels, comps = next_ref.shape[:2]
    slots = level_ref.shape[1]
    wide_x = cells_x + SPAN
    rows = cells_x + 2 * PAD
    lane = lane_index(ROWS)
    ordered(parity_ref[1:2], near_y, far_y, before_ref, after_ref)
    turned = HALF + MARGIN + REACH
    high_halo = (lane >= turned) & (lane < turned + HALO * items)
    both = (lane + MARGIN) % HALF < SPAN
    outer = ((lane >= LANES - REACH) & (lane < LANES - MARGIN)) | (
        (lane >= HALF + MARGIN) & (lane < HALF + REACH)
    )
    windows = [(lane + (LANES + MARGIN - SPAN * slot)) % LANES < SPAN for slot in range(EDGE_PER)]
    for row in range(0, rows, ROWS):
        start = groups * rows + row % SPAN
        fold = SPAN * (row // SPAN)
        low = rolled(before_ref[start : start + ROWS], -fold)
        high = rolled(after_ref[start : start + ROWS], turned - fold)
        halo = jnp.where(high_halo, high, low)
        for group in range(groups):
            start = group * rows + row
            before = before_ref[start : start + ROWS]
            after = rolled(after_ref[start : start + ROWS], HALF)
            for k in range(group * EDGE_PER, min((group + 1) * EDGE_PER, items)):
                slot = k % EDGE_PER
                main = rolled(jnp.where(windows[slot], before, after), -SPAN * slot)
                value = rim_ref[k, row : row + ROWS] + jnp.where(both, main, 0.0)
                value = jnp.where(outer, rolled(halo, -REACH - HALO * k), value)
                moved_ref[k, ROWS + row : 2 * ROWS + row] = value

    first_steps(moved_ref, carried_ref, sweep_ref, levels, comps, rows)
    size = 2 * ROWS
    lane = lane_index(size)
    for row in range(0, wide_x, size):
        start = ROWS + PAD - MARGIN + row
        results = sweep(sweep_ref, carried_ref, levels, comps, start, size)
        for k in range(items):
            low, high = results[k], rolled(results[k], HALF)
            inner = inner_ref[k, row : row + size]
            inner = jnp.where(lane < REACH, low, jnp.where(lane >= LANES - REACH, high, inner))
            edge = jnp.where(lane < MARGIN, high, low)
            place = slice(k * wide_x + row, k * wide_x + row + size)
            round_ref[place, :cells_y] = inner.astype(jnp.bfloat16)
            round_ref[place, cells_y:] = edge.astype(jnp.bfloat16)
            if MARGIN <= row < MARGIN + cells_x:
                next_ref[k // comps, k % comps, row - MARGIN : row - MARGIN + size] = inner

    for first in range(0, slots, chunk):
        lanes = slice(first, first + chunk)
        level = level_ref[:, lanes]
        partial = jnp.dot(
            round_ref[...], dense_y_ref[:, lanes], preferred_element_type=jnp.float32
        )
        partial = partial.reshape(levels, comps, wide_x, chunk)
        quarter, value = quarter_ref[:, lanes], value_ref[:, lanes]
        heres = [quarter == (MARGIN - row) // 4 for row in range(0, wide_x, ROWS)]
        aboves = [level == l for l in range(levels - 1)]
        for c in range(comps):
            total = jnp.zeros((ROWS, chunk), jnp.float32)
            for row in range(0, wide_x, ROWS):
                picked = partial[levels - 1, c, row : row + ROWS]
                for l in range(levels - 2, -1, -1):
                    picked = jnp.where(aboves[l], partial[l, c, row : row + ROWS], picked)
                total = jnp.where(heres[row // ROWS], picked, total)
            sampled_ref[c, 0, :, lanes] = jnp.sum(total * value, axis=0, keepdims=True)


def whole(count):
    return [pl.BlockSpec(memory_space=pltpu.VMEM)] * count


def swap_pairs(axis):
    size = lax.axis_size(axis)
    if size % 2:
        raise ValueError("odd axis")
    far_pairs = [(i, (i - 1 if i % 2 == 0 else i + 1) % size) for i in range(size)]
    return far_pairs, [(i, i ^ 1) for i in range(size)]


def body(velocity, marker_cell, marker_frac, marker_force, fish_owner):
    levels, comps, cells_x, cells_y = velocity.shape
    slots = marker_cell.shape[3]
    items = levels * comps
    shape = (cells_x, cells_y, cells_x * lax.axis_size("gx"), cells_y * lax.axis_size("gy"))
    wide_x = cells_x + SPAN
    rows = cells_x + 2 * PAD
    chunk = min(512, slots)
    width = cells_y + LANES
    groups = -(-items // EDGE_PER)
    params = pltpu.CompilerParams(vmem_limit_bytes=40 * 1024 * 1024)
    edge_x = jax.ShapeDtypeStruct(((items + groups) * STRIP, LANES), jnp.bfloat16)
    half = (items, wide_x // 2, width)
    arrays = (fish_owner, velocity, marker_cell, marker_frac, marker_force)
    far_half, far, force, dense_y, quarter, value, level, parity = pl.pallas_call(
        functools.partial(far_kernel, shape, chunk),
        out_shape=(
            jax.ShapeDtypeStruct(half, jnp.float32),
            edge_x,
            jax.ShapeDtypeStruct((items, 2 * ROWS, slots), jnp.bfloat16),
            jax.ShapeDtypeStruct((width, slots), jnp.bfloat16),
            jax.ShapeDtypeStruct((ROWS, slots), jnp.int32),
            jax.ShapeDtypeStruct((ROWS, slots), jnp.float32),
            jax.ShapeDtypeStruct((1, slots), jnp.int32),
            jax.ShapeDtypeStruct((2, LANES), jnp.int32),
        ),
        in_specs=[pl.BlockSpec(memory_space=pltpu.HBM)] * 5,
        out_specs=tuple(whole(8)),
        scratch_shapes=[pltpu.VMEM(a.shape, a.dtype) for a in arrays]
        + [pltpu.SemaphoreType.DMA((5,))],
        compiler_params=params,
        name="spread_far",
    )(*(pltpu.with_memory_space_constraint(a, pltpu.HBM) for a in arrays))
    far_pairs, near_pairs = swap_pairs("gx")
    far_x = lax.ppermute(far, "gx", far_pairs)
    grid, near = pl.pallas_call(
        functools.partial(near_kernel, shape, chunk),
        out_shape=(jax.ShapeDtypeStruct((items, wide_x, width), jnp.float32), edge_x),
        in_specs=whole(5),
        out_specs=tuple(whole(2)),
        scratch_shapes=[pltpu.VMEM(half, jnp.float32)],
        compiler_params=params,
        cost_estimate=pl.CostEstimate(
            flops=items * wide_x * width * slots, bytes_accessed=4 * items * wide_x * width,
            transcendentals=0,
        ),
        name="spread_near",
    )(velocity, far_half, force, dense_y, quarter)
    near_x = lax.ppermute(near, "gx", near_pairs)
    edge_y = jax.ShapeDtypeStruct((groups * rows + SPAN, LANES), jnp.bfloat16)
    far, near = pl.pallas_call(
        functools.partial(pack_kernel, shape),
        out_shape=(edge_y, edge_y),
        in_specs=whole(4),
        out_specs=tuple(whole(2)),
        scratch_shapes=[pltpu.VMEM(edge_x.shape, jnp.float32)] * 2,
        compiler_params=params,
        name="pack",
    )(parity, grid, far_x, near_x)
    far_pairs, near_pairs = swap_pairs("gy")
    far_y = lax.ppermute(far, "gy", far_pairs)
    near_y = lax.ppermute(near, "gy", near_pairs)
    field = pltpu.VMEM((items, rows + 2 * ROWS, LANES), jnp.float32)
    inner, rim = pl.pallas_call(
        functools.partial(inner_kernel, shape, levels),
        out_shape=(
            jax.ShapeDtypeStruct((items, wide_x, LANES), jnp.float32),
            jax.ShapeDtypeStruct((items, rows, LANES), jnp.float32),
        ),
        in_specs=whole(4),
        out_specs=tuple(whole(2)),
        scratch_shapes=[field, field, field] + [pltpu.VMEM(edge_x.shape, jnp.float32)] * 2,
        compiler_params=params,
        cost_estimate=pl.CostEstimate(
            flops=40 * items * rows * LANES, bytes_accessed=16 * items * rows * LANES,
            transcendentals=0,
        ),
        name="inner",
    )(parity, grid, far_x, near_x)
    return pl.pallas_call(
        functools.partial(finish_kernel, shape, chunk),
        out_shape=(
            jax.ShapeDtypeStruct(velocity.shape, jnp.float32),
            jax.ShapeDtypeStruct((comps, 1, 1, slots), jnp.float32),
        ),
        in_specs=whole(9),
        out_specs=tuple(whole(2)),
        scratch_shapes=[field, field, field]
        + [pltpu.VMEM(edge_y.shape, jnp.float32)] * 2
        + [pltpu.VMEM((items * wide_x, width), jnp.bfloat16)],
        compiler_params=params,
        name="finish",
    )(parity, quarter, value, dense_y, level, inner, rim, far_y, near_y)


def solution(mesh):
    placed = (
        P(None, None, "gx", "gy"),
        P(None, "gx", "gy", None),
        P(None, "gx", "gy", None),
        P(None, "gx", "gy", None),
        P(),
    )
    return jax.shard_map(
        body,
        mesh=mesh,
        in_specs=placed,
        out_specs=(P(None, None, "gx", "gy"), P(None, "gx", "gy", None)),
        check_vma=False,
    )
```

```python
import functools

import jax
import jax.numpy as jnp
import numpy as np
from jax import lax
from jax.experimental import pallas as pl
from jax.experimental.pallas import tpu as pltpu
from jax.sharding import PartitionSpec as P

MARGIN = 16
FISH_MARK = 1024
HALO = 3
LANES = 128
COURANT = 0.25
VISCOUS = 1.5
ROWS = 8

REACH = MARGIN + HALO
PAD = -(-REACH // ROWS) * ROWS
STRIP = PAD + MARGIN
SPAN = 2 * MARGIN
EDGE_PER = LANES // SPAN


def half_turn(terms):
    nodes = 0.5 - 0.5 * np.cos(np.pi * (np.arange(64) + 0.5) / 64)
    square = nodes * nodes
    cosine = np.polynomial.polynomial.polyfit(square, np.cos(0.5 * np.pi * nodes), terms)
    sine = np.polynomial.polynomial.polyfit(square, np.sin(0.5 * np.pi * nodes) / nodes, terms)
    return [float(v) for v in cosine], [float(v) for v in sine]


COS_FIT, SIN_FIT = half_turn(6)


def horner(coefficients, value):
    total = jnp.full_like(value, coefficients[-1])
    for coefficient in coefficients[-2::-1]:
        total = total * value + coefficient
    return total


def four_weights(frac):
    square = frac * frac
    cosine = horner(COS_FIT, square)
    sine = frac * horner(SIN_FIT, square)
    return (0.25 - 0.25 * sine, 0.25 + 0.25 * cosine, 0.25 + 0.25 * sine, 0.25 - 0.25 * cosine)


def local_cell(cell, low, extent):
    offset = cell - low
    offset = jnp.where(offset < -MARGIN, offset + extent, offset)
    return jnp.where(offset >= extent - MARGIN, offset - extent, offset)


def position():
    row, col = lax.axis_index("gx"), lax.axis_index("gy")
    return row, col, row % 2 == 0, col % 2 == 0


def tile_weights(offset, weights):
    shift = lax.broadcasted_iota(jnp.int32, (ROWS, offset.shape[1]), 0) + 1 - offset
    quarter, phase = shift >> 2, shift & 3
    value = jnp.where(phase == 3, weights[3], weights[2])
    value = jnp.where(phase == 1, weights[1], value)
    return quarter, jnp.where(phase == 0, weights[0], value)


def doubled(quarter, value):
    quarter = jnp.concatenate([quarter, quarter + 2], axis=0).astype(jnp.float32)
    return quarter.astype(jnp.bfloat16), twice(value)


def twice(value):
    return jnp.concatenate([value, value], axis=0).astype(jnp.bfloat16)


def picked_tile(quarter, value, first):
    zero = jnp.zeros_like(value)
    return jnp.where(quarter == jnp.array(-first // 4, quarter.dtype), value, zero)


def half_spread(quarter_ref, force_ref, dense_y_ref, half_ref, base, lanes):
    items, rows = half_ref.shape[:2]
    quarter = quarter_ref[:, lanes] + base
    quarter = jnp.concatenate([quarter, quarter + 2], axis=0).astype(jnp.float32)
    quarter = quarter.astype(jnp.bfloat16)
    left = jnp.concatenate(
        [
            picked_tile(quarter, force_ref[k, :, lanes], row)
            for k in range(items)
            for row in range(0, rows, 2 * ROWS)
        ],
        axis=0,
    )
    total = lax.dot_general(
        left, dense_y_ref[:, lanes], (((1,), (1,)), ((), ())),
        preferred_element_type=jnp.float32,
    )
    total = total.reshape(half_ref.shape)
    if lanes.start:
        half_ref[...] += total
    else:
        half_ref[...] = total


def finish_half(half_ref, velocity_ref, out_ref, low, cells_y):
    items, rows = half_ref.shape[:2]
    comps = items // velocity_ref.shape[0]
    count = rows - MARGIN
    source = pl.ds(pl.multiple_of(jnp.where(low, 0, count), ROWS), count)
    target = pl.ds(pl.multiple_of(jnp.where(low, MARGIN, 0), ROWS), count)
    for k in range(items):
        half_ref[k, target, :cells_y] += velocity_ref[k // comps, k % comps, source]
    place = pl.ds(pl.multiple_of(jnp.where(low, 0, rows - STRIP), ROWS), STRIP)
    parts = [half_ref[k, place, :cells_y] for k in range(items)]
    for group in range(0, items, EDGE_PER):
        edges = []
        for k in range(group, min(group + EDGE_PER, items)):
            edges.append(rolled(half_ref[k, place, cells_y:], SPAN * (k - group)))
        parts.append(functools.reduce(jnp.add, edges))
    out_ref[...] = jnp.concatenate(parts, axis=0).astype(jnp.bfloat16)


def far_kernel(
    shape, chunk, fish_hbm, velocity_hbm, cell_hbm, frac_hbm, force_hbm,
    half_ref, far_ref, force_out, dense_y_ref, quarter_ref, value_ref,
    quarter_y_ref, value_y_ref, level_ref, parity_ref, velocity_ref,
    fish_ref, cell_ref, frac_ref, force_ref, sems,
):
    pairs = (
        (cell_hbm, cell_ref), (frac_hbm, frac_ref), (fish_hbm, fish_ref),
        (force_hbm, force_ref), (velocity_hbm, velocity_ref),
    )
    copies = [pltpu.make_async_copy(a, b, sems.at[i]) for i, (a, b) in enumerate(pairs)]
    for copy in copies:
        copy.start()
    cells_x, cells_y, extent_x, extent_y = shape
    levels, comps = velocity_ref.shape[:2]
    slots = cell_ref.shape[3]
    row, col, even, even_y = position()
    parity_ref[0:1] = jnp.full((1, LANES), jnp.where(even, 1, 0), jnp.int32)
    parity_ref[1:2] = jnp.full((1, LANES), jnp.where(even_y, 1, 0), jnp.int32)
    base = jnp.where(even, -MARGIN // 4, cells_x // 8)
    for copy in copies[:-1]:
        copy.wait()
    mine = jnp.where(fish_ref[...] == row * lax.axis_size("gy") + col, 1.0, 0.0)
    count = FISH_MARK * jnp.sum(mine)
    level_ref[...] = cell_ref[2, 0]
    for first in range(0, slots, chunk):
        lanes = slice(first, first + chunk)
        offset_x = local_cell(cell_ref[0, 0, :, lanes], row * cells_x, extent_x)
        offset_y = local_cell(cell_ref[1, 0, :, lanes], col * cells_y, extent_y)
        slot = lax.broadcasted_iota(jnp.int32, (1, chunk), 1) + first
        alive = jnp.where(slot.astype(jnp.float32) < count, 1.0, 0.0)
        quarter, value = tile_weights(offset_x, four_weights(frac_ref[0, 0, :, lanes]))
        value = value * alive
        quarter_ref[:, lanes] = quarter
        value_ref[:, lanes] = value
        level = cell_ref[2, 0, :, lanes]
        pushes = [force_ref[c, 0, :, lanes] * value for c in range(comps)]
        for l in range(levels):
            for c in range(comps):
                force_out[l * comps + c, :, lanes] = twice(jnp.where(level == l, pushes[c], 0.0))
        quarter, value = tile_weights(offset_y, four_weights(frac_ref[1, 0, :, lanes]))
        quarter_y_ref[:, lanes] = quarter
        value_y_ref[:, lanes] = value
        quarter, value = doubled(quarter, value)
        dense_y_ref[:, lanes] = jnp.concatenate(
            [picked_tile(quarter, value, n) for n in range(0, cells_y + MARGIN, 2 * ROWS)]
            + [jnp.zeros((LANES - SPAN, chunk), jnp.bfloat16)]
            + [picked_tile(quarter, value, n) for n in range(-MARGIN, 0, 2 * ROWS)],
            axis=0,
        )
        half_spread(quarter_ref, force_out, dense_y_ref, half_ref, base, lanes)
    copies[-1].wait()
    finish_half(half_ref, velocity_ref, far_ref, even, cells_y)


def near_kernel(
    shape, chunk, velocity_ref, far_half_ref, force_ref, dense_y_ref, quarter_ref,
    grid_ref, near_ref, half_ref,
):
    cells_x, cells_y, _, _ = shape
    slots = quarter_ref.shape[1]
    rows = half_ref.shape[1]
    _, _, even, _ = position()
    base = jnp.where(even, cells_x // 8, -MARGIN // 4)
    for first in range(0, slots, chunk):
        lanes = slice(first, first + chunk)
        half_spread(quarter_ref, force_ref, dense_y_ref, half_ref, base, lanes)
    finish_half(half_ref, velocity_ref, near_ref, jnp.logical_not(even), cells_y)
    for ref, row in ((far_half_ref, jnp.where(even, 0, rows)), (half_ref, jnp.where(even, rows, 0))):
        place = pl.ds(pl.multiple_of(row, ROWS), rows)
        for k in range(ref.shape[0]):
            grid_ref[k, place] = ref[k]


def rolled(value, shift):
    shift = shift % LANES
    return pltpu.roll(value, shift, 1) if shift else value


def lane_index(rows):
    return lax.broadcasted_iota(jnp.int32, (rows, LANES), 1)


def ordered(parity, near_ref, far_ref):
    even = jnp.broadcast_to(parity, near_ref.shape) != 0
    near, far = near_ref[...].astype(jnp.float32), far_ref[...].astype(jnp.float32)
    return jnp.where(even, far, near), jnp.where(even, near, far)


def joined(center, before, after):
    wide = center.shape[0]
    near = PAD - MARGIN
    overlap = STRIP - near
    return jnp.concatenate(
        [
            before[:near],
            center[:overlap] + before[near:],
            center[overlap : wide - overlap],
            center[wide - overlap :] + after[:overlap],
            after[overlap:],
        ],
        axis=0,
    )


def extended_rows(parity, grid_ref, near_ref, far_ref, cells_y):
    items = grid_ref.shape[0]
    groups = -(-items // EDGE_PER)
    size = groups * STRIP
    before, after = ordered(parity, near_ref, far_ref)
    packed = jnp.concatenate([before[items * STRIP :], after[items * STRIP :]], axis=0)
    lane = lane_index(2 * size)
    kept = (lane < MARGIN) | (lane >= LANES - MARGIN)
    edges = [jnp.where(kept, rolled(packed, -SPAN * slot), 0.0) for slot in range(EDGE_PER)]
    for k in range(items):
        place = slice(k * STRIP, (k + 1) * STRIP)
        inner = joined(grid_ref[k, :, :cells_y], before[place], after[place])
        start = k // EDGE_PER * STRIP
        edge = edges[k % EDGE_PER]
        edge = joined(
            grid_ref[k, :, cells_y:],
            edge[start : start + STRIP],
            edge[size + start : size + start + STRIP],
        )
        yield k, inner, edge


def pack_kernel(shape, parity_ref, grid_ref, far_x, near_x, far_ref, near_ref):
    cells_x, cells_y, _, _ = shape
    items = grid_ref.shape[0]
    groups = -(-items // EDGE_PER)
    rows = cells_x + 2 * PAD
    lane = lane_index(rows)
    even = jnp.broadcast_to(parity_ref[1:2], (rows, LANES)) != 0
    up_halo = (lane >= LANES - REACH) & (lane < LANES - MARGIN)
    down_halo = (lane >= MARGIN) & (lane < REACH)
    halos, ups, downs = None, None, None
    for k, inner, edge in extended_rows(parity_ref[0:1], grid_ref, near_x, far_x, cells_y):
        slot = k % EDGE_PER
        up = rolled(jnp.where(lane >= LANES - MARGIN, inner, edge), SPAN * slot)
        down = rolled(jnp.where(lane < MARGIN, inner, edge), SPAN * slot)
        halo = rolled(jnp.where(up_halo | down_halo, inner, 0.0), REACH + HALO * k)
        ups = ups + up if slot else up
        downs = downs + down if slot else down
        halos = halos + halo if k else halo
        if slot == EDGE_PER - 1 or k == items - 1:
            place = slice(k // EDGE_PER * rows, (k // EDGE_PER + 1) * rows)
            near_ref[place] = jnp.where(even, ups, downs).astype(jnp.bfloat16)
            far_ref[place] = jnp.where(even, downs, ups).astype(jnp.bfloat16)
    used = lane < HALO * items
    ups = jnp.where(used, halos, 0.0)
    downs = jnp.where(used, rolled(halos, -MARGIN - REACH), 0.0)
    folded = None
    for row in range(0, rows, SPAN):
        size = min(SPAN, rows - row)
        parts = [value[row : row + size] for value in (ups, downs)]
        if size < SPAN:
            parts = [jnp.concatenate([p, jnp.zeros((SPAN - size, LANES), p.dtype)], 0) for p in parts]
        part = rolled(jnp.concatenate(parts, axis=0), row)
        folded = folded + part if row else part
    up, down, even = folded[:SPAN], folded[SPAN:], even[:SPAN]
    near_ref[groups * rows :] = jnp.where(even, up, down).astype(jnp.bfloat16)
    far_ref[groups * rows :] = jnp.where(even, down, up).astype(jnp.bfloat16)


def around(ref, k, start, size):
    center = ref[k, start : start + size]
    back = ref[k, start - 1 : start - 1 + size]
    fore = ref[k, start + 1 : start + 1 + size]
    return center, back, fore, rolled(center, 1), rolled(center, -1)


def advect(moved_ref, carried_ref, levels, comps, rows):
    for start in range(ROWS, ROWS + rows, ROWS):
        for l in range(levels):
            pieces = [around(moved_ref, l * comps + c, start, ROWS) for c in range(comps)]
            speed_x, speed_y = COURANT * pieces[0][0], COURANT * pieces[1][0]
            ahead_x, astern_x = jnp.maximum(speed_x, 0.0), jnp.minimum(speed_x, 0.0)
            ahead_y, astern_y = jnp.maximum(speed_y, 0.0), jnp.minimum(speed_y, 0.0)
            for c in range(comps):
                center, back, fore, below, above = pieces[c]
                change = ahead_x * (center - back) + astern_x * (fore - center)
                change = change + ahead_y * (center - below) + astern_y * (above - center)
                carried_ref[l * comps + c, start : start + ROWS] = center - change


def sweep(ref, carried_ref, levels, comps, start, size):
    scale = 1.0 / (1.0 + 6.0 * VISCOUS)
    centers, results = [], []
    for k in range(levels * comps):
        center, back, fore, below, above = around(ref, k, start, size)
        centers.append(center)
        results.append(back + fore + below + above)
    for k in range(levels * comps):
        higher = min(k // comps + 1, levels - 1) * comps + k % comps
        lower = max(k // comps - 1, 0) * comps + k % comps
        summed = results[k] + centers[higher] + centers[lower]
        source = carried_ref[k, start : start + size]
        results[k] = scale * source + (VISCOUS * scale) * summed
    return results


def first_steps(moved_ref, carried_ref, sweep_ref, levels, comps, rows):
    advect(moved_ref, carried_ref, levels, comps, rows)
    for start in range(ROWS, ROWS + rows, ROWS):
        results = sweep(carried_ref, carried_ref, levels, comps, start, ROWS)
        for k in range(levels * comps):
            sweep_ref[k, start : start + ROWS] = results[k]


RIM = REACH + HALO
HALF = LANES // 2


def weight_kernel(
    shape, chunk, parity_ref, quarter_ref, value_ref, level_ref, inner_ref, rim_ref, parity_out
):
    parity_out[...] = parity_ref[...]
    _, cells_y, _, _ = shape
    slots = quarter_ref.shape[1]
    size = 2 * ROWS
    levels = inner_ref.shape[0] // LANES
    row = lax.broadcasted_iota(jnp.int32, (size, chunk), 0)

    def cut(tile, keep):
        return jnp.where(keep, tile.astype(jnp.float32), 0.0).astype(jnp.bfloat16)

    for first in range(0, slots, chunk):
        lanes = slice(first, first + chunk)
        level = level_ref[:, lanes]
        for l in range(levels):
            value = jnp.where(level == l, value_ref[:, lanes], 0.0)
            quarter, value = doubled(quarter_ref[:, lanes], value)
            for start in range(0, LANES, size):
                inner = picked_tile(quarter, value, start)
                if start < REACH:
                    inner = cut(inner, row + start >= REACH)
                if start + size > cells_y - REACH:
                    inner = cut(inner, row + start < cells_y - REACH)
                if start >= LANES - MARGIN:
                    rim = picked_tile(quarter, value, start - LANES)
                elif start + size > HALF - REACH and start < HALF + MARGIN:
                    rim = picked_tile(quarter, value, start + cells_y - HALF)
                    rim = cut(rim, row + start >= HALF - REACH) if start < HALF - REACH else rim
                elif start < REACH:
                    rim = picked_tile(quarter, value, start)
                    rim = cut(rim, row + start < REACH) if start + size > REACH else rim
                else:
                    rim = jnp.zeros_like(value)
                place = slice(l * LANES + start, l * LANES + start + size)
                inner_ref[place, lanes] = inner
                rim_ref[place, lanes] = rim


def sampled_part(round_ref, weight_ref, quarter_ref, value_ref, lanes, comps):
    wide_x = round_ref.shape[0] // comps
    partial = jnp.dot(round_ref[...], weight_ref[:, lanes], preferred_element_type=jnp.float32)
    quarter, value = quarter_ref[:, lanes], value_ref[:, lanes]
    totals = [jnp.zeros_like(value)] * comps
    for row in range(0, wide_x, ROWS):
        here = quarter == (MARGIN - row) // 4
        for c in range(comps):
            start = c * wide_x + row
            totals[c] = jnp.where(here, partial[start : start + ROWS], totals[c])
    return [jnp.sum(total * value, axis=0, keepdims=True) for total in totals]


def inner_kernel(
    shape, chunk, levels, parity_ref, quarter_ref, value_ref, weight_ref, grid_ref, far_x, near_x,
    inner_ref, rim_ref, sampled_ref, moved_ref, carried_ref, sweep_ref, round_ref,
):
    cells_x, cells_y, _, _ = shape
    items = grid_ref.shape[0]
    comps = items // levels
    slots = quarter_ref.shape[1]
    wide_x = cells_x + SPAN
    rows = cells_x + 2 * PAD
    lane = lane_index(rows)
    for k, inner, edge in extended_rows(parity_ref[0:1], grid_ref, near_x, far_x, cells_y):
        moved_ref[k, ROWS : ROWS + rows] = inner
        low = jnp.where(lane < RIM, inner, jnp.where(lane >= LANES - MARGIN, edge, 0.0))
        high = jnp.where(lane >= LANES - RIM, inner, jnp.where(lane < MARGIN, edge, 0.0))
        rim_ref[k] = low + rolled(high, HALF)
    first_steps(moved_ref, carried_ref, sweep_ref, levels, comps, rows)
    size = 2 * ROWS
    for row in range(0, wide_x, size):
        start = ROWS + PAD - MARGIN + row
        results = sweep(sweep_ref, carried_ref, levels, comps, start, size)
        for k in range(items):
            level, c = k // comps, k % comps
            place = slice(c * wide_x + row, c * wide_x + row + size)
            round_ref[place, level * LANES : (level + 1) * LANES] = results[k].astype(jnp.bfloat16)
            if MARGIN <= row < MARGIN + cells_x:
                inner_ref[k, row - MARGIN : row - MARGIN + size] = results[k]
    for first in range(0, slots, chunk):
        lanes = slice(first, first + chunk)
        parts = sampled_part(round_ref, weight_ref, quarter_ref, value_ref, lanes, comps)
        for c in range(comps):
            sampled_ref[c : c + 1, lanes] = parts[c]


def finish_kernel(
    shape, chunk, parity_ref, quarter_ref, value_ref, weight_ref, inner_ref, rim_ref, part_ref,
    far_y, near_y, next_ref, sampled_ref,
    moved_ref, carried_ref, sweep_ref, before_ref, after_ref, round_ref,
):
    cells_x, cells_y, _, _ = shape
    items = rim_ref.shape[0]
    groups = -(-items // EDGE_PER)
    levels, comps = next_ref.shape[:2]
    slots = quarter_ref.shape[1]
    wide_x = cells_x + SPAN
    rows = cells_x + 2 * PAD
    lane = lane_index(ROWS)
    before_ref[...], after_ref[...] = ordered(parity_ref[1:2], near_y, far_y)
    turned = HALF + MARGIN + REACH
    high_halo = (lane >= turned) & (lane < turned + HALO * items)
    both = (lane + MARGIN) % HALF < SPAN
    outer = ((lane >= LANES - REACH) & (lane < LANES - MARGIN)) | (
        (lane >= HALF + MARGIN) & (lane < HALF + REACH)
    )
    windows = [(lane + (LANES + MARGIN - SPAN * slot)) % LANES < SPAN for slot in range(EDGE_PER)]
    for row in range(0, rows, ROWS):
        start = groups * rows + row % SPAN
        fold = SPAN * (row // SPAN)
        low = rolled(before_ref[start : start + ROWS], -fold)
        high = rolled(after_ref[start : start + ROWS], turned - fold)
        halo = jnp.where(high_halo, high, low)
        for group in range(groups):
            start = group * rows + row
            before = before_ref[start : start + ROWS]
            after = rolled(after_ref[start : start + ROWS], HALF)
            for k in range(group * EDGE_PER, min((group + 1) * EDGE_PER, items)):
                slot = k % EDGE_PER
                main = rolled(jnp.where(windows[slot], before, after), -SPAN * slot)
                value = rim_ref[k, row : row + ROWS] + jnp.where(both, main, 0.0)
                value = jnp.where(outer, rolled(halo, -REACH - HALO * k), value)
                moved_ref[k, ROWS + row : 2 * ROWS + row] = value

    first_steps(moved_ref, carried_ref, sweep_ref, levels, comps, rows)
    size = 2 * ROWS
    lane = lane_index(size)
    for row in range(0, wide_x, size):
        start = ROWS + PAD - MARGIN + row
        results = sweep(sweep_ref, carried_ref, levels, comps, start, size)
        for k in range(items):
            level, c = k // comps, k % comps
            place = slice(c * wide_x + row, c * wide_x + row + size)
            round_ref[place, level * LANES : (level + 1) * LANES] = results[k].astype(jnp.bfloat16)
        if not MARGIN <= row < MARGIN + cells_x:
            continue
        place = slice(row - MARGIN, row - MARGIN + size)
        for k in range(items):
            low, high = results[k], rolled(results[k], HALF)
            inner = inner_ref[k, place]
            inner = jnp.where(lane < REACH, low, jnp.where(lane >= LANES - REACH, high, inner))
            next_ref[k // comps, k % comps, place] = inner

    for first in range(0, slots, chunk):
        lanes = slice(first, first + chunk)
        parts = sampled_part(round_ref, weight_ref, quarter_ref, value_ref, lanes, comps)
        for c in range(comps):
            sampled_ref[c, 0, :, lanes] = part_ref[c : c + 1, lanes] + parts[c]


def whole(count):
    return [pl.BlockSpec(memory_space=pltpu.VMEM)] * count


def swap_pairs(axis):
    size = lax.axis_size(axis)
    if size % 2:
        raise ValueError("odd axis")
    far_pairs = [(i, (i - 1 if i % 2 == 0 else i + 1) % size) for i in range(size)]
    return far_pairs, [(i, i ^ 1) for i in range(size)]


def body(velocity, marker_cell, marker_frac, marker_force, fish_owner):
    levels, comps, cells_x, cells_y = velocity.shape
    slots = marker_cell.shape[3]
    items = levels * comps
    shape = (cells_x, cells_y, cells_x * lax.axis_size("gx"), cells_y * lax.axis_size("gy"))
    wide_x = cells_x + SPAN
    rows = cells_x + 2 * PAD
    chunk = min(512, slots)
    width = cells_y + LANES
    groups = -(-items // EDGE_PER)
    params = pltpu.CompilerParams(vmem_limit_bytes=32 * 1024 * 1024)
    edge_x = jax.ShapeDtypeStruct(((items + groups) * STRIP, LANES), jnp.bfloat16)
    half = (items, wide_x // 2, width)
    arrays = (fish_owner, velocity, marker_cell, marker_frac, marker_force)
    far_half, far, force, dense_y, quarter, value, quarter_y, value_y, level, parity, near_velocity = (
        pl.pallas_call(
        functools.partial(far_kernel, shape, chunk),
        out_shape=(
            jax.ShapeDtypeStruct(half, jnp.float32),
            edge_x,
            jax.ShapeDtypeStruct((items, 2 * ROWS, slots), jnp.bfloat16),
            jax.ShapeDtypeStruct((width, slots), jnp.bfloat16),
            jax.ShapeDtypeStruct((ROWS, slots), jnp.int32),
            jax.ShapeDtypeStruct((ROWS, slots), jnp.float32),
            jax.ShapeDtypeStruct((ROWS, slots), jnp.int32),
            jax.ShapeDtypeStruct((ROWS, slots), jnp.float32),
            jax.ShapeDtypeStruct((1, slots), jnp.int32),
            jax.ShapeDtypeStruct((2, LANES), jnp.int32),
            jax.ShapeDtypeStruct(velocity.shape, velocity.dtype),
        ),
        in_specs=[pl.BlockSpec(memory_space=pltpu.HBM)] * 5,
        out_specs=tuple(whole(11)),
        scratch_shapes=[pltpu.VMEM(a.shape, a.dtype) for a in arrays if a is not velocity]
        + [pltpu.SemaphoreType.DMA((5,))],
        compiler_params=params,
        name="spread_far",
    )(*(pltpu.with_memory_space_constraint(a, pltpu.HBM) for a in arrays))
    )
    far_pairs, near_pairs = swap_pairs("gx")
    far_x = lax.ppermute(far, "gx", far_pairs)
    grid, near = pl.pallas_call(
        functools.partial(near_kernel, shape, chunk),
        out_shape=(jax.ShapeDtypeStruct((items, wide_x, width), jnp.float32), edge_x),
        in_specs=whole(5),
        out_specs=tuple(whole(2)),
        scratch_shapes=[pltpu.VMEM(half, jnp.float32)],
        compiler_params=params,
        cost_estimate=pl.CostEstimate(
            flops=items * wide_x * width * slots, bytes_accessed=4 * items * wide_x * width,
            transcendentals=0,
        ),
        name="spread_near",
    )(near_velocity, far_half, force, dense_y, quarter)
    near_x = lax.ppermute(near, "gx", near_pairs)
    weights = jax.ShapeDtypeStruct((levels * LANES, slots), jnp.bfloat16)
    inner_weight, rim_weight, parity = pl.pallas_call(
        functools.partial(weight_kernel, shape, chunk),
        out_shape=(weights, weights, jax.ShapeDtypeStruct(parity.shape, parity.dtype)),
        in_specs=whole(4),
        out_specs=tuple(whole(3)),
        compiler_params=params,
        cost_estimate=pl.CostEstimate(
            flops=2 * levels * LANES * slots, bytes_accessed=4 * levels * LANES * slots,
            transcendentals=0,
        ),
        name="weights",
    )(parity, quarter_y, value_y, level)
    edge_y = jax.ShapeDtypeStruct((groups * rows + SPAN, LANES), jnp.bfloat16)
    far, near = pl.pallas_call(
        functools.partial(pack_kernel, shape),
        out_shape=(edge_y, edge_y),
        in_specs=whole(4),
        out_specs=tuple(whole(2)),
        compiler_params=params,
        name="pack",
    )(parity, grid, far_x, near_x)
    far_pairs, near_pairs = swap_pairs("gy")
    far_y = lax.ppermute(far, "gy", far_pairs)
    near_y = lax.ppermute(near, "gy", near_pairs)
    field = pltpu.VMEM((items, rows + 2 * ROWS, LANES), jnp.float32)
    rounded = pltpu.VMEM((comps * wide_x, levels * LANES), jnp.bfloat16)
    inner, rim, part = pl.pallas_call(
        functools.partial(inner_kernel, shape, chunk, levels),
        out_shape=(
            jax.ShapeDtypeStruct((items, cells_x, LANES), jnp.float32),
            jax.ShapeDtypeStruct((items, rows, LANES), jnp.float32),
            jax.ShapeDtypeStruct((comps, slots), jnp.float32),
        ),
        in_specs=whole(7),
        out_specs=tuple(whole(3)),
        scratch_shapes=[field, field, field, rounded],
        compiler_params=params,
        cost_estimate=pl.CostEstimate(
            flops=2 * items * wide_x * LANES * slots, bytes_accessed=16 * items * rows * LANES,
            transcendentals=0,
        ),
        name="inner",
    )(parity, quarter, value, inner_weight, grid, far_x, near_x)
    strip_y = pltpu.VMEM(edge_y.shape, jnp.float32)
    return pl.pallas_call(
        functools.partial(finish_kernel, shape, chunk),
        out_shape=(
            jax.ShapeDtypeStruct(velocity.shape, jnp.float32),
            jax.ShapeDtypeStruct((comps, 1, 1, slots), jnp.float32),
        ),
        in_specs=whole(9),
        out_specs=tuple(whole(2)),
        scratch_shapes=[field, field, field, strip_y, strip_y, rounded],
        compiler_params=params,
        name="finish",
    )(parity, quarter, value, rim_weight, inner, rim, part, far_y, near_y)


def solution(mesh):
    placed = (
        P(None, None, "gx", "gy"),
        P(None, "gx", "gy", None),
        P(None, "gx", "gy", None),
        P(None, "gx", "gy", None),
        P(),
    )
    return jax.shard_map(
        body,
        mesh=mesh,
        in_specs=placed,
        out_specs=(P(None, None, "gx", "gy"), P(None, "gx", "gy", None)),
        check_vma=False,
    )
```

```python
import functools

import jax
import jax.numpy as jnp
import numpy as np
from jax import lax
from jax.experimental import pallas as pl
from jax.experimental.pallas import tpu as pltpu
from jax.sharding import PartitionSpec as P

MARGIN = 16
FISH_MARK = 1024
HALO = 3
LANES = 128
COURANT = 0.25
VISCOUS = 1.5
ROWS = 8

REACH = MARGIN + HALO
PAD = -(-REACH // ROWS) * ROWS
STRIP = PAD + MARGIN
SPAN = 2 * MARGIN
EDGE_PER = LANES // SPAN


def half_turn(terms):
    nodes = 0.5 - 0.5 * np.cos(np.pi * (np.arange(64) + 0.5) / 64)
    square = nodes * nodes
    cosine = np.polynomial.polynomial.polyfit(square, np.cos(0.5 * np.pi * nodes), terms)
    sine = np.polynomial.polynomial.polyfit(square, np.sin(0.5 * np.pi * nodes) / nodes, terms)
    return [float(v) for v in cosine], [float(v) for v in sine]


COS_FIT, SIN_FIT = half_turn(6)


def horner(coefficients, value):
    total = jnp.full_like(value, coefficients[-1])
    for coefficient in coefficients[-2::-1]:
        total = total * value + coefficient
    return total


def four_weights(frac):
    square = frac * frac
    cosine = horner(COS_FIT, square)
    sine = frac * horner(SIN_FIT, square)
    return (0.25 - 0.25 * sine, 0.25 + 0.25 * cosine, 0.25 + 0.25 * sine, 0.25 - 0.25 * cosine)


def local_cell(cell, low, extent):
    offset = cell - low
    offset = jnp.where(offset < -MARGIN, offset + extent, offset)
    return jnp.where(offset >= extent - MARGIN, offset - extent, offset)


def position():
    row, col = lax.axis_index("gx"), lax.axis_index("gy")
    return row, col, row % 2 == 0, col % 2 == 0


def tile_weights(offset, weights):
    shift = lax.broadcasted_iota(jnp.int32, (ROWS, offset.shape[1]), 0) + 1 - offset
    quarter, phase = shift >> 2, shift & 3
    value = jnp.where(phase == 3, weights[3], weights[2])
    value = jnp.where(phase == 1, weights[1], value)
    return quarter, jnp.where(phase == 0, weights[0], value)


def doubled(quarter, value):
    quarter = jnp.concatenate([quarter, quarter + 2], axis=0).astype(jnp.float32)
    return quarter.astype(jnp.bfloat16), twice(value)


def twice(value):
    return jnp.concatenate([value, value], axis=0).astype(jnp.bfloat16)


def picked_tile(quarter, value, first):
    zero = jnp.zeros_like(value)
    return jnp.where(quarter == jnp.array(-first // 4, quarter.dtype), value, zero)


def half_spread(quarter_ref, force_ref, dense_y_ref, half_ref, base, lanes):
    items, rows = half_ref.shape[:2]
    quarter = quarter_ref[:, lanes] + base
    quarter = jnp.concatenate([quarter, quarter + 2], axis=0).astype(jnp.float32)
    quarter = quarter.astype(jnp.bfloat16)
    left = jnp.concatenate(
        [
            picked_tile(quarter, force_ref[k, :, lanes], row)
            for k in range(items)
            for row in range(0, rows, 2 * ROWS)
        ],
        axis=0,
    )
    total = lax.dot_general(
        left, dense_y_ref[:, lanes], (((1,), (1,)), ((), ())),
        preferred_element_type=jnp.float32,
    )
    total = total.reshape(half_ref.shape)
    if lanes.start:
        half_ref[...] += total
    else:
        half_ref[...] = total


def finish_half(half_ref, velocity_ref, out_ref, low, cells_y):
    items, rows = half_ref.shape[:2]
    comps = items // velocity_ref.shape[0]
    count = rows - MARGIN
    source = pl.ds(pl.multiple_of(jnp.where(low, 0, count), ROWS), count)
    target = pl.ds(pl.multiple_of(jnp.where(low, MARGIN, 0), ROWS), count)
    for k in range(items):
        half_ref[k, target, :cells_y] += velocity_ref[k // comps, k % comps, source]
    place = pl.ds(pl.multiple_of(jnp.where(low, 0, rows - STRIP), ROWS), STRIP)
    parts = [half_ref[k, place, :cells_y] for k in range(items)]
    for group in range(0, items, EDGE_PER):
        edges = []
        for k in range(group, min(group + EDGE_PER, items)):
            edges.append(rolled(half_ref[k, place, cells_y:], SPAN * (k - group)))
        parts.append(functools.reduce(jnp.add, edges))
    out_ref[...] = jnp.concatenate(parts, axis=0).astype(jnp.bfloat16)


def far_kernel(
    shape, chunk, fish_hbm, velocity_hbm, cell_hbm, frac_hbm, force_hbm,
    half_ref, far_ref, force_out, dense_y_ref, quarter_ref, value_ref,
    quarter_y_ref, value_y_ref, level_ref, parity_ref, velocity_ref,
    fish_ref, cell_ref, frac_ref, force_ref, sems,
):
    pairs = (
        (cell_hbm, cell_ref), (frac_hbm, frac_ref), (fish_hbm, fish_ref),
        (force_hbm, force_ref), (velocity_hbm, velocity_ref),
    )
    copies = [pltpu.make_async_copy(a, b, sems.at[i]) for i, (a, b) in enumerate(pairs)]
    for copy in copies:
        copy.start()
    cells_x, cells_y, extent_x, extent_y = shape
    levels, comps = velocity_ref.shape[:2]
    slots = cell_ref.shape[3]
    row, col, even, even_y = position()
    parity_ref[0:1] = jnp.full((1, LANES), jnp.where(even, 1, 0), jnp.int32)
    parity_ref[1:2] = jnp.full((1, LANES), jnp.where(even_y, 1, 0), jnp.int32)
    base = jnp.where(even, -MARGIN // 4, cells_x // 8)
    for copy in copies[:-1]:
        copy.wait()
    mine = jnp.where(fish_ref[...] == row * lax.axis_size("gy") + col, 1.0, 0.0)
    count = FISH_MARK * jnp.sum(mine)
    level_ref[...] = cell_ref[2, 0]
    for first in range(0, slots, chunk):
        lanes = slice(first, first + chunk)
        offset_x = local_cell(cell_ref[0, 0, :, lanes], row * cells_x, extent_x)
        offset_y = local_cell(cell_ref[1, 0, :, lanes], col * cells_y, extent_y)
        slot = lax.broadcasted_iota(jnp.int32, (1, chunk), 1) + first
        alive = jnp.where(slot.astype(jnp.float32) < count, 1.0, 0.0)
        quarter, value = tile_weights(offset_x, four_weights(frac_ref[0, 0, :, lanes]))
        value = value * alive
        quarter_ref[:, lanes] = quarter
        value_ref[:, lanes] = value
        level = cell_ref[2, 0, :, lanes]
        pushes = [force_ref[c, 0, :, lanes] * value for c in range(comps)]
        for l in range(levels):
            for c in range(comps):
                force_out[l * comps + c, :, lanes] = twice(jnp.where(level == l, pushes[c], 0.0))
        quarter, value = tile_weights(offset_y, four_weights(frac_ref[1, 0, :, lanes]))
        quarter_y_ref[:, lanes] = quarter
        value_y_ref[:, lanes] = value
        quarter, value = doubled(quarter, value)
        dense_y_ref[:, lanes] = jnp.concatenate(
            [picked_tile(quarter, value, n) for n in range(0, cells_y + MARGIN, 2 * ROWS)]
            + [jnp.zeros((LANES - SPAN, chunk), jnp.bfloat16)]
            + [picked_tile(quarter, value, n) for n in range(-MARGIN, 0, 2 * ROWS)],
            axis=0,
        )
        half_spread(quarter_ref, force_out, dense_y_ref, half_ref, base, lanes)
    copies[-1].wait()
    finish_half(half_ref, velocity_ref, far_ref, even, cells_y)


def near_kernel(
    shape, chunk, velocity_ref, far_half_ref, force_ref, dense_y_ref, quarter_ref,
    grid_ref, near_ref, half_ref,
):
    cells_x, cells_y, _, _ = shape
    slots = quarter_ref.shape[1]
    rows = half_ref.shape[1]
    _, _, even, _ = position()
    base = jnp.where(even, cells_x // 8, -MARGIN // 4)
    for first in range(0, slots, chunk):
        lanes = slice(first, first + chunk)
        half_spread(quarter_ref, force_ref, dense_y_ref, half_ref, base, lanes)
    finish_half(half_ref, velocity_ref, near_ref, jnp.logical_not(even), cells_y)
    for ref, row in ((far_half_ref, jnp.where(even, 0, rows)), (half_ref, jnp.where(even, rows, 0))):
        place = pl.ds(pl.multiple_of(row, ROWS), rows)
        for k in range(ref.shape[0]):
            grid_ref[k, place] = ref[k]


def rolled(value, shift):
    shift = shift % LANES
    return pltpu.roll(value, shift, 1) if shift else value


def lane_index(rows):
    return lax.broadcasted_iota(jnp.int32, (rows, LANES), 1)


def ordered(parity, near_ref, far_ref):
    even = jnp.broadcast_to(parity, near_ref.shape) != 0
    near, far = near_ref[...].astype(jnp.float32), far_ref[...].astype(jnp.float32)
    return jnp.where(even, far, near), jnp.where(even, near, far)


def joined(center, before, after):
    wide = center.shape[0]
    near = PAD - MARGIN
    overlap = STRIP - near
    return jnp.concatenate(
        [
            before[:near],
            center[:overlap] + before[near:],
            center[overlap : wide - overlap],
            center[wide - overlap :] + after[:overlap],
            after[overlap:],
        ],
        axis=0,
    )


def extended_rows(parity, grid_ref, near_ref, far_ref, cells_y):
    items = grid_ref.shape[0]
    groups = -(-items // EDGE_PER)
    size = groups * STRIP
    before, after = ordered(parity, near_ref, far_ref)
    packed = jnp.concatenate([before[items * STRIP :], after[items * STRIP :]], axis=0)
    lane = lane_index(2 * size)
    kept = (lane < MARGIN) | (lane >= LANES - MARGIN)
    edges = [jnp.where(kept, rolled(packed, -SPAN * slot), 0.0) for slot in range(EDGE_PER)]
    for k in range(items):
        place = slice(k * STRIP, (k + 1) * STRIP)
        inner = joined(grid_ref[k, :, :cells_y], before[place], after[place])
        start = k // EDGE_PER * STRIP
        edge = edges[k % EDGE_PER]
        edge = joined(
            grid_ref[k, :, cells_y:],
            edge[start : start + STRIP],
            edge[size + start : size + start + STRIP],
        )
        yield k, inner, edge


def pack_kernel(shape, parity_ref, grid_ref, far_x, near_x, far_ref, near_ref):
    cells_x, cells_y, _, _ = shape
    items = grid_ref.shape[0]
    groups = -(-items // EDGE_PER)
    rows = cells_x + 2 * PAD
    lane = lane_index(rows)
    even = jnp.broadcast_to(parity_ref[1:2], (rows, LANES)) != 0
    up_halo = (lane >= LANES - REACH) & (lane < LANES - MARGIN)
    down_halo = (lane >= MARGIN) & (lane < REACH)
    halos, ups, downs = None, None, None
    for k, inner, edge in extended_rows(parity_ref[0:1], grid_ref, near_x, far_x, cells_y):
        slot = k % EDGE_PER
        up = rolled(jnp.where(lane >= LANES - MARGIN, inner, edge), SPAN * slot)
        down = rolled(jnp.where(lane < MARGIN, inner, edge), SPAN * slot)
        halo = rolled(jnp.where(up_halo | down_halo, inner, 0.0), REACH + HALO * k)
        ups = ups + up if slot else up
        downs = downs + down if slot else down
        halos = halos + halo if k else halo
        if slot == EDGE_PER - 1 or k == items - 1:
            place = slice(k // EDGE_PER * rows, (k // EDGE_PER + 1) * rows)
            near_ref[place] = jnp.where(even, ups, downs).astype(jnp.bfloat16)
            far_ref[place] = jnp.where(even, downs, ups).astype(jnp.bfloat16)
    used = lane < HALO * items
    ups = jnp.where(used, halos, 0.0)
    downs = jnp.where(used, rolled(halos, -MARGIN - REACH), 0.0)
    folded = None
    for row in range(0, rows, SPAN):
        size = min(SPAN, rows - row)
        parts = [value[row : row + size] for value in (ups, downs)]
        if size < SPAN:
            parts = [jnp.concatenate([p, jnp.zeros((SPAN - size, LANES), p.dtype)], 0) for p in parts]
        part = rolled(jnp.concatenate(parts, axis=0), row)
        folded = folded + part if row else part
    up, down, even = folded[:SPAN], folded[SPAN:], even[:SPAN]
    near_ref[groups * rows :] = jnp.where(even, up, down).astype(jnp.bfloat16)
    far_ref[groups * rows :] = jnp.where(even, down, up).astype(jnp.bfloat16)


def around(ref, k, start, size):
    center = ref[k, start : start + size]
    back = ref[k, start - 1 : start - 1 + size]
    fore = ref[k, start + 1 : start + 1 + size]
    return center, back, fore, rolled(center, 1), rolled(center, -1)


def advect(moved_ref, carried_ref, levels, comps, rows):
    for start in range(ROWS, ROWS + rows, ROWS):
        for l in range(levels):
            pieces = [around(moved_ref, l * comps + c, start, ROWS) for c in range(comps)]
            speed_x, speed_y = COURANT * pieces[0][0], COURANT * pieces[1][0]
            ahead_x, astern_x = jnp.maximum(speed_x, 0.0), jnp.minimum(speed_x, 0.0)
            ahead_y, astern_y = jnp.maximum(speed_y, 0.0), jnp.minimum(speed_y, 0.0)
            for c in range(comps):
                center, back, fore, below, above = pieces[c]
                change = ahead_x * (center - back) + astern_x * (fore - center)
                change = change + ahead_y * (center - below) + astern_y * (above - center)
                carried_ref[l * comps + c, start : start + ROWS] = center - change


def sweep(ref, carried_ref, levels, comps, start, size):
    scale = 1.0 / (1.0 + 6.0 * VISCOUS)
    centers, results = [], []
    for k in range(levels * comps):
        center, back, fore, below, above = around(ref, k, start, size)
        centers.append(center)
        results.append(back + fore + below + above)
    for k in range(levels * comps):
        higher = min(k // comps + 1, levels - 1) * comps + k % comps
        lower = max(k // comps - 1, 0) * comps + k % comps
        summed = results[k] + centers[higher] + centers[lower]
        source = carried_ref[k, start : start + size]
        results[k] = scale * source + (VISCOUS * scale) * summed
    return results


def first_steps(moved_ref, carried_ref, sweep_ref, levels, comps, rows):
    advect(moved_ref, carried_ref, levels, comps, rows)
    for start in range(ROWS, ROWS + rows, ROWS):
        results = sweep(carried_ref, carried_ref, levels, comps, start, ROWS)
        for k in range(levels * comps):
            sweep_ref[k, start : start + ROWS] = results[k]


RIM = REACH + HALO
HALF = LANES // 2


def weight_kernel(
    shape, chunk, parity_ref, quarter_ref, value_ref, level_ref, inner_ref, rim_ref, parity_out
):
    parity_out[...] = parity_ref[...]
    _, cells_y, _, _ = shape
    slots = quarter_ref.shape[1]
    size = 2 * ROWS
    levels = inner_ref.shape[0] // LANES
    row = lax.broadcasted_iota(jnp.int32, (size, chunk), 0)

    def cut(tile, keep):
        return jnp.where(keep, tile.astype(jnp.float32), 0.0).astype(jnp.bfloat16)

    for first in range(0, slots, chunk):
        lanes = slice(first, first + chunk)
        level = level_ref[:, lanes]
        for l in range(levels):
            value = jnp.where(level == l, value_ref[:, lanes], 0.0)
            quarter, value = doubled(quarter_ref[:, lanes], value)
            for start in range(0, LANES, size):
                inner = picked_tile(quarter, value, start)
                if start < REACH:
                    inner = cut(inner, row + start >= REACH)
                if start + size > cells_y - REACH:
                    inner = cut(inner, row + start < cells_y - REACH)
                if start >= LANES - MARGIN:
                    rim = picked_tile(quarter, value, start - LANES)
                elif start + size > HALF - REACH and start < HALF + MARGIN:
                    rim = picked_tile(quarter, value, start + cells_y - HALF)
                    rim = cut(rim, row + start >= HALF - REACH) if start < HALF - REACH else rim
                elif start < REACH:
                    rim = picked_tile(quarter, value, start)
                    rim = cut(rim, row + start < REACH) if start + size > REACH else rim
                else:
                    rim = jnp.zeros_like(value)
                place = slice(l * LANES + start, l * LANES + start + size)
                inner_ref[place, lanes] = inner
                rim_ref[place, lanes] = rim


def sampled_part(round_ref, weight_ref, quarter_ref, value_ref, lanes, comps):
    wide_x = round_ref.shape[0] // comps
    partial = jnp.dot(round_ref[...], weight_ref[:, lanes], preferred_element_type=jnp.float32)
    quarter, value = quarter_ref[:, lanes], value_ref[:, lanes]
    totals = [jnp.zeros_like(value)] * comps
    for row in range(0, wide_x, ROWS):
        here = quarter == (MARGIN - row) // 4
        for c in range(comps):
            start = c * wide_x + row
            totals[c] = jnp.where(here, partial[start : start + ROWS], totals[c])
    return [jnp.sum(total * value, axis=0, keepdims=True) for total in totals]


def inner_kernel(
    shape, chunk, levels, parity_ref, quarter_ref, value_ref, weight_ref, grid_ref, far_x, near_x,
    inner_ref, rim_ref, sampled_ref, moved_ref, carried_ref, sweep_ref, round_ref,
):
    cells_x, cells_y, _, _ = shape
    items = grid_ref.shape[0]
    comps = items // levels
    slots = quarter_ref.shape[1]
    wide_x = cells_x + SPAN
    rows = cells_x + 2 * PAD
    lane = lane_index(rows)
    for k, inner, edge in extended_rows(parity_ref[0:1], grid_ref, near_x, far_x, cells_y):
        moved_ref[k, ROWS : ROWS + rows] = inner
        low = jnp.where(lane < RIM, inner, jnp.where(lane >= LANES - MARGIN, edge, 0.0))
        high = jnp.where(lane >= LANES - RIM, inner, jnp.where(lane < MARGIN, edge, 0.0))
        rim_ref[k] = low + rolled(high, HALF)
    first_steps(moved_ref, carried_ref, sweep_ref, levels, comps, rows)
    size = 2 * ROWS
    for row in range(0, wide_x, size):
        start = ROWS + PAD - MARGIN + row
        results = sweep(sweep_ref, carried_ref, levels, comps, start, size)
        for k in range(items):
            level, c = k // comps, k % comps
            place = slice(c * wide_x + row, c * wide_x + row + size)
            round_ref[place, level * LANES : (level + 1) * LANES] = results[k].astype(jnp.bfloat16)
            if MARGIN <= row < MARGIN + cells_x:
                inner_ref[k, row - MARGIN : row - MARGIN + size] = results[k]
    for first in range(0, slots, chunk):
        lanes = slice(first, first + chunk)
        parts = sampled_part(round_ref, weight_ref, quarter_ref, value_ref, lanes, comps)
        for c in range(comps):
            sampled_ref[c : c + 1, lanes] = parts[c]


def unfolded(value, rows, groups):
    folded = value[groups * rows :]
    return jnp.concatenate(
        [rolled(folded, -row)[: min(SPAN, rows - row)] for row in range(0, rows, SPAN)], axis=0
    )


def finish_kernel(
    shape, chunk, parity_ref, quarter_ref, value_ref, weight_ref, inner_ref, rim_ref, part_ref,
    far_y, near_y, next_ref, sampled_ref, moved_ref, carried_ref, sweep_ref, round_ref,
):
    cells_x, cells_y, _, _ = shape
    items = rim_ref.shape[0]
    groups = -(-items // EDGE_PER)
    levels, comps = next_ref.shape[:2]
    slots = quarter_ref.shape[1]
    wide_x = cells_x + SPAN
    rows = cells_x + 2 * PAD
    lane = lane_index(rows)
    befores, afters = ordered(parity_ref[1:2], near_y, far_y)
    turned = HALF + MARGIN + REACH
    high_halo = (lane >= turned) & (lane < turned + HALO * items)
    both = (lane + MARGIN) % HALF < SPAN
    outer = ((lane >= LANES - REACH) & (lane < LANES - MARGIN)) | (
        (lane >= HALF + MARGIN) & (lane < HALF + REACH)
    )
    halo = jnp.where(
        high_halo, rolled(unfolded(afters, rows, groups), turned), unfolded(befores, rows, groups)
    )
    for group in range(groups):
        before = befores[group * rows : (group + 1) * rows]
        after = rolled(afters[group * rows : (group + 1) * rows], HALF)
        for k in range(group * EDGE_PER, min((group + 1) * EDGE_PER, items)):
            slot = k % EDGE_PER
            window = (lane + (LANES + MARGIN - SPAN * slot)) % LANES < SPAN
            main = rolled(jnp.where(window, before, after), -SPAN * slot)
            value = rim_ref[k] + jnp.where(both, main, 0.0)
            value = jnp.where(outer, rolled(halo, -REACH - HALO * k), value)
            moved_ref[k, ROWS : ROWS + rows] = value

    first_steps(moved_ref, carried_ref, sweep_ref, levels, comps, rows)
    size = 2 * ROWS
    lane = lane_index(size)
    for row in range(0, wide_x, size):
        start = ROWS + PAD - MARGIN + row
        results = sweep(sweep_ref, carried_ref, levels, comps, start, size)
        for k in range(items):
            level, c = k // comps, k % comps
            place = slice(c * wide_x + row, c * wide_x + row + size)
            round_ref[place, level * LANES : (level + 1) * LANES] = results[k].astype(jnp.bfloat16)
        if not MARGIN <= row < MARGIN + cells_x:
            continue
        place = slice(row - MARGIN, row - MARGIN + size)
        for k in range(items):
            low, high = results[k], rolled(results[k], HALF)
            inner = inner_ref[k, place]
            inner = jnp.where(lane < REACH, low, jnp.where(lane >= LANES - REACH, high, inner))
            next_ref[k // comps, k % comps, place] = inner

    for first in range(0, slots, chunk):
        lanes = slice(first, first + chunk)
        parts = sampled_part(round_ref, weight_ref, quarter_ref, value_ref, lanes, comps)
        for c in range(comps):
            sampled_ref[c, 0, :, lanes] = part_ref[c : c + 1, lanes] + parts[c]


def whole(count):
    return [pl.BlockSpec(memory_space=pltpu.VMEM)] * count


def swap_pairs(axis):
    size = lax.axis_size(axis)
    if size % 2:
        raise ValueError("odd axis")
    far_pairs = [(i, (i - 1 if i % 2 == 0 else i + 1) % size) for i in range(size)]
    return far_pairs, [(i, i ^ 1) for i in range(size)]


def body(velocity, marker_cell, marker_frac, marker_force, fish_owner):
    levels, comps, cells_x, cells_y = velocity.shape
    slots = marker_cell.shape[3]
    items = levels * comps
    shape = (cells_x, cells_y, cells_x * lax.axis_size("gx"), cells_y * lax.axis_size("gy"))
    wide_x = cells_x + SPAN
    rows = cells_x + 2 * PAD
    chunk = min(512, slots)
    width = cells_y + LANES
    groups = -(-items // EDGE_PER)
    params = pltpu.CompilerParams(vmem_limit_bytes=32 * 1024 * 1024)
    edge_x = jax.ShapeDtypeStruct(((items + groups) * STRIP, LANES), jnp.bfloat16)
    half = (items, wide_x // 2, width)
    arrays = (fish_owner, velocity, marker_cell, marker_frac, marker_force)
    far_half, far, force, dense_y, quarter, value, quarter_y, value_y, level, parity, near_velocity = (
        pl.pallas_call(
        functools.partial(far_kernel, shape, chunk),
        out_shape=(
            jax.ShapeDtypeStruct(half, jnp.float32),
            edge_x,
            jax.ShapeDtypeStruct((items, 2 * ROWS, slots), jnp.bfloat16),
            jax.ShapeDtypeStruct((width, slots), jnp.bfloat16),
            jax.ShapeDtypeStruct((ROWS, slots), jnp.int32),
            jax.ShapeDtypeStruct((ROWS, slots), jnp.float32),
            jax.ShapeDtypeStruct((ROWS, slots), jnp.int32),
            jax.ShapeDtypeStruct((ROWS, slots), jnp.float32),
            jax.ShapeDtypeStruct((1, slots), jnp.int32),
            jax.ShapeDtypeStruct((2, LANES), jnp.int32),
            jax.ShapeDtypeStruct(velocity.shape, velocity.dtype),
        ),
        in_specs=[pl.BlockSpec(memory_space=pltpu.HBM)] * 5,
        out_specs=tuple(whole(11)),
        scratch_shapes=[pltpu.VMEM(a.shape, a.dtype) for a in arrays if a is not velocity]
        + [pltpu.SemaphoreType.DMA((5,))],
        compiler_params=params,
        name="spread_far",
    )(*(pltpu.with_memory_space_constraint(a, pltpu.HBM) for a in arrays))
    )
    far_pairs, near_pairs = swap_pairs("gx")
    far_x = lax.ppermute(far, "gx", far_pairs)
    grid, near = pl.pallas_call(
        functools.partial(near_kernel, shape, chunk),
        out_shape=(jax.ShapeDtypeStruct((items, wide_x, width), jnp.float32), edge_x),
        in_specs=whole(5),
        out_specs=tuple(whole(2)),
        scratch_shapes=[pltpu.VMEM(half, jnp.float32)],
        compiler_params=params,
        cost_estimate=pl.CostEstimate(
            flops=items * wide_x * width * slots, bytes_accessed=4 * items * wide_x * width,
            transcendentals=0,
        ),
        name="spread_near",
    )(near_velocity, far_half, force, dense_y, quarter)
    near_x = lax.ppermute(near, "gx", near_pairs)
    weights = jax.ShapeDtypeStruct((levels * LANES, slots), jnp.bfloat16)
    inner_weight, rim_weight, parity = pl.pallas_call(
        functools.partial(weight_kernel, shape, chunk),
        out_shape=(weights, weights, jax.ShapeDtypeStruct(parity.shape, parity.dtype)),
        in_specs=whole(4),
        out_specs=tuple(whole(3)),
        compiler_params=params,
        cost_estimate=pl.CostEstimate(
            flops=2 * levels * LANES * slots, bytes_accessed=4 * levels * LANES * slots,
            transcendentals=0,
        ),
        name="weights",
    )(parity, quarter_y, value_y, level)
    edge_y = jax.ShapeDtypeStruct((groups * rows + SPAN, LANES), jnp.bfloat16)
    far, near = pl.pallas_call(
        functools.partial(pack_kernel, shape),
        out_shape=(edge_y, edge_y),
        in_specs=whole(4),
        out_specs=tuple(whole(2)),
        compiler_params=params,
        name="pack",
    )(parity, grid, far_x, near_x)
    far_pairs, near_pairs = swap_pairs("gy")
    far_y = lax.ppermute(far, "gy", far_pairs)
    near_y = lax.ppermute(near, "gy", near_pairs)
    field = pltpu.VMEM((items, rows + 2 * ROWS, LANES), jnp.float32)
    rounded = pltpu.VMEM((comps * wide_x, levels * LANES), jnp.bfloat16)
    inner, rim, part = pl.pallas_call(
        functools.partial(inner_kernel, shape, chunk, levels),
        out_shape=(
            jax.ShapeDtypeStruct((items, cells_x, LANES), jnp.float32),
            jax.ShapeDtypeStruct((items, rows, LANES), jnp.float32),
            jax.ShapeDtypeStruct((comps, slots), jnp.float32),
        ),
        in_specs=whole(7),
        out_specs=tuple(whole(3)),
        scratch_shapes=[field, field, field, rounded],
        compiler_params=params,
        cost_estimate=pl.CostEstimate(
            flops=2 * items * wide_x * LANES * slots, bytes_accessed=16 * items * rows * LANES,
            transcendentals=0,
        ),
        name="inner",
    )(parity, quarter, value, inner_weight, grid, far_x, near_x)
    return pl.pallas_call(
        functools.partial(finish_kernel, shape, chunk),
        out_shape=(
            jax.ShapeDtypeStruct(velocity.shape, jnp.float32),
            jax.ShapeDtypeStruct((comps, 1, 1, slots), jnp.float32),
        ),
        in_specs=whole(9),
        out_specs=tuple(whole(2)),
        scratch_shapes=[field, field, field, rounded],
        compiler_params=params,
        name="finish",
    )(parity, quarter, value, rim_weight, inner, rim, part, far_y, near_y)


def solution(mesh):
    placed = (
        P(None, None, "gx", "gy"),
        P(None, "gx", "gy", None),
        P(None, "gx", "gy", None),
        P(None, "gx", "gy", None),
        P(),
    )
    return jax.shard_map(
        body,
        mesh=mesh,
        in_specs=placed,
        out_specs=(P(None, None, "gx", "gy"), P(None, "gx", "gy", None)),
        check_vma=False,
    )
```

```python
import functools

import jax
import jax.numpy as jnp
import numpy as np
from jax import lax
from jax.experimental import pallas as pl
from jax.experimental.pallas import tpu as pltpu
from jax.sharding import PartitionSpec as P

MARGIN = 16
FISH_MARK = 1024
HALO = 3
LANES = 128
COURANT = 0.25
VISCOUS = 1.5
ROWS = 8

REACH = MARGIN + HALO
PAD = -(-REACH // ROWS) * ROWS
STRIP = PAD + MARGIN
SPAN = 2 * MARGIN
EDGE_PER = LANES // SPAN


def half_turn(terms):
    nodes = 0.5 - 0.5 * np.cos(np.pi * (np.arange(64) + 0.5) / 64)
    square = nodes * nodes
    cosine = np.polynomial.polynomial.polyfit(square, np.cos(0.5 * np.pi * nodes), terms)
    sine = np.polynomial.polynomial.polyfit(square, np.sin(0.5 * np.pi * nodes) / nodes, terms)
    return [float(v) for v in cosine], [float(v) for v in sine]


COS_FIT, SIN_FIT = half_turn(6)


def horner(coefficients, value):
    total = jnp.full_like(value, coefficients[-1])
    for coefficient in coefficients[-2::-1]:
        total = total * value + coefficient
    return total


def four_weights(frac):
    square = frac * frac
    cosine = horner(COS_FIT, square)
    sine = frac * horner(SIN_FIT, square)
    return (0.25 - 0.25 * sine, 0.25 + 0.25 * cosine, 0.25 + 0.25 * sine, 0.25 - 0.25 * cosine)


def local_cell(cell, low, extent):
    offset = cell - low
    offset = jnp.where(offset < -MARGIN, offset + extent, offset)
    return jnp.where(offset >= extent - MARGIN, offset - extent, offset)


def position():
    row, col = lax.axis_index("gx"), lax.axis_index("gy")
    return row, col, (row & 1) == 0, (col & 1) == 0


def tile_weights(offset, weights):
    shift = lax.broadcasted_iota(jnp.int32, (ROWS, offset.shape[1]), 0) + 1 - offset
    quarter, phase = shift >> 2, shift & 3
    value = jnp.where(phase == 3, weights[3], weights[2])
    value = jnp.where(phase == 1, weights[1], value)
    return quarter, jnp.where(phase == 0, weights[0], value)


def doubled(quarter, value):
    quarter = jnp.concatenate([quarter, quarter + 2], axis=0).astype(jnp.float32)
    return quarter.astype(jnp.bfloat16), twice(value)


def twice(value):
    return jnp.concatenate([value, value], axis=0).astype(jnp.bfloat16)


def picked_tile(quarter, value, first):
    zero = jnp.zeros_like(value)
    return jnp.where(quarter == jnp.array(-first // 4, quarter.dtype), value, zero)


def half_spread(quarter_ref, force_ref, dense_y_ref, half_ref, base, lanes):
    items, rows = half_ref.shape[:2]
    quarter = quarter_ref[:, lanes] + base
    quarter = jnp.concatenate([quarter, quarter + 2], axis=0).astype(jnp.float32)
    quarter = quarter.astype(jnp.bfloat16)
    left = jnp.concatenate(
        [
            picked_tile(quarter, force_ref[k, :, lanes], row)
            for k in range(items)
            for row in range(0, rows, 2 * ROWS)
        ],
        axis=0,
    )
    total = lax.dot_general(
        left, dense_y_ref[:, lanes], (((1,), (1,)), ((), ())),
        preferred_element_type=jnp.float32,
    )
    total = total.reshape(half_ref.shape)
    if lanes.start:
        half_ref[...] += total
    else:
        half_ref[...] = total


def finish_half(half_ref, velocity_ref, out_ref, low, cells_y):
    items, rows = half_ref.shape[:2]
    comps = items // velocity_ref.shape[0]
    count = rows - MARGIN
    source = pl.ds(pl.multiple_of(jnp.where(low, 0, count), ROWS), count)
    target = pl.ds(pl.multiple_of(jnp.where(low, MARGIN, 0), ROWS), count)
    for k in range(items):
        half_ref[k, target, :cells_y] += velocity_ref[k // comps, k % comps, source]
    place = pl.ds(pl.multiple_of(jnp.where(low, 0, rows - STRIP), ROWS), STRIP)
    parts = [half_ref[k, place, :cells_y] for k in range(items)]
    for group in range(0, items, EDGE_PER):
        edges = []
        for k in range(group, min(group + EDGE_PER, items)):
            edges.append(rolled(half_ref[k, place, cells_y:], SPAN * (k - group)))
        parts.append(functools.reduce(jnp.add, edges))
    out_ref[...] = jnp.concatenate(parts, axis=0).astype(jnp.bfloat16)


def far_kernel(
    shape, chunk, fish_hbm, velocity_hbm, cell_hbm, frac_hbm, force_hbm,
    half_ref, far_ref, force_out, dense_y_ref, quarter_ref, value_ref,
    quarter_y_ref, value_y_ref, level_ref, parity_ref, velocity_ref,
    fish_ref, cell_ref, frac_ref, force_ref, sems,
):
    pairs = (
        (cell_hbm, cell_ref), (frac_hbm, frac_ref), (fish_hbm, fish_ref),
        (force_hbm, force_ref), (velocity_hbm, velocity_ref),
    )
    copies = [pltpu.make_async_copy(a, b, sems.at[i]) for i, (a, b) in enumerate(pairs)]
    for copy in copies:
        copy.start()
    cells_x, cells_y, extent_x, extent_y = shape
    levels, comps = velocity_ref.shape[:2]
    slots = cell_ref.shape[3]
    row, col, even, even_y = position()
    parity_ref[0:1] = jnp.full((1, LANES), jnp.where(even, 1, 0), jnp.int32)
    parity_ref[1:2] = jnp.full((1, LANES), jnp.where(even_y, 1, 0), jnp.int32)
    base = jnp.where(even, -MARGIN // 4, cells_x // 8)
    for copy in copies[:-1]:
        copy.wait()
    mine = jnp.where(fish_ref[...] == row * lax.axis_size("gy") + col, 1.0, 0.0)
    count = FISH_MARK * jnp.sum(mine)
    level_ref[...] = cell_ref[2, 0]
    for first in range(0, slots, chunk):
        lanes = slice(first, first + chunk)
        offset_x = local_cell(cell_ref[0, 0, :, lanes], row * cells_x, extent_x)
        offset_y = local_cell(cell_ref[1, 0, :, lanes], col * cells_y, extent_y)
        slot = lax.broadcasted_iota(jnp.int32, (1, chunk), 1) + first
        alive = jnp.where(slot.astype(jnp.float32) < count, 1.0, 0.0)
        quarter, value = tile_weights(offset_x, four_weights(frac_ref[0, 0, :, lanes]))
        value = value * alive
        quarter_ref[:, lanes] = quarter
        value_ref[:, lanes] = value
        level = cell_ref[2, 0, :, lanes]
        pushes = [force_ref[c, 0, :, lanes] * value for c in range(comps)]
        for l in range(levels):
            for c in range(comps):
                force_out[l * comps + c, :, lanes] = twice(jnp.where(level == l, pushes[c], 0.0))
        quarter, value = tile_weights(offset_y, four_weights(frac_ref[1, 0, :, lanes]))
        quarter_y_ref[:, lanes] = quarter
        value_y_ref[:, lanes] = value
        quarter, value = doubled(quarter, value)
        dense_y_ref[:, lanes] = jnp.concatenate(
            [picked_tile(quarter, value, n) for n in range(0, cells_y + MARGIN, 2 * ROWS)]
            + [jnp.zeros((LANES - SPAN, chunk), jnp.bfloat16)]
            + [picked_tile(quarter, value, n) for n in range(-MARGIN, 0, 2 * ROWS)],
            axis=0,
        )
        half_spread(quarter_ref, force_out, dense_y_ref, half_ref, base, lanes)
    copies[-1].wait()
    finish_half(half_ref, velocity_ref, far_ref, even, cells_y)


def near_kernel(
    shape, chunk, velocity_ref, far_half_ref, force_ref, dense_y_ref, quarter_ref,
    grid_ref, near_ref, half_ref,
):
    cells_x, cells_y, _, _ = shape
    slots = quarter_ref.shape[1]
    rows = half_ref.shape[1]
    _, _, even, _ = position()
    base = jnp.where(even, cells_x // 8, -MARGIN // 4)
    for first in range(0, slots, chunk):
        lanes = slice(first, first + chunk)
        half_spread(quarter_ref, force_ref, dense_y_ref, half_ref, base, lanes)
    finish_half(half_ref, velocity_ref, near_ref, jnp.logical_not(even), cells_y)
    for ref, row in ((far_half_ref, jnp.where(even, 0, rows)), (half_ref, jnp.where(even, rows, 0))):
        place = pl.ds(pl.multiple_of(row, ROWS), rows)
        for k in range(ref.shape[0]):
            grid_ref[k, place] = ref[k]


def rolled(value, shift):
    shift = shift % LANES
    return pltpu.roll(value, shift, 1) if shift else value


def lane_index(rows):
    return lax.broadcasted_iota(jnp.int32, (rows, LANES), 1)


def ordered(parity, near_ref, far_ref):
    even = jnp.broadcast_to(parity, near_ref.shape) != 0
    near, far = near_ref[...].astype(jnp.float32), far_ref[...].astype(jnp.float32)
    return jnp.where(even, far, near), jnp.where(even, near, far)


def joined(center, before, after):
    wide = center.shape[0]
    near = PAD - MARGIN
    overlap = STRIP - near
    return jnp.concatenate(
        [
            before[:near],
            center[:overlap] + before[near:],
            center[overlap : wide - overlap],
            center[wide - overlap :] + after[:overlap],
            after[overlap:],
        ],
        axis=0,
    )


def extended_rows(parity, grid_ref, near_ref, far_ref, cells_y):
    items = grid_ref.shape[0]
    groups = -(-items // EDGE_PER)
    size = groups * STRIP
    before, after = ordered(parity, near_ref, far_ref)
    packed = jnp.concatenate([before[items * STRIP :], after[items * STRIP :]], axis=0)
    lane = lane_index(2 * size)
    kept = (lane < MARGIN) | (lane >= LANES - MARGIN)
    edges = [jnp.where(kept, rolled(packed, -SPAN * slot), 0.0) for slot in range(EDGE_PER)]
    for k in range(items):
        place = slice(k * STRIP, (k + 1) * STRIP)
        inner = joined(grid_ref[k, :, :cells_y], before[place], after[place])
        start = k // EDGE_PER * STRIP
        edge = edges[k % EDGE_PER]
        edge = joined(
            grid_ref[k, :, cells_y:],
            edge[start : start + STRIP],
            edge[size + start : size + start + STRIP],
        )
        yield k, inner, edge


def pack_kernel(shape, parity_ref, grid_ref, far_x, near_x, far_ref, near_ref):
    cells_x, cells_y, _, _ = shape
    items = grid_ref.shape[0]
    groups = -(-items // EDGE_PER)
    rows = cells_x + 2 * PAD
    lane = lane_index(rows)
    even = jnp.broadcast_to(parity_ref[1:2], (rows, LANES)) != 0
    up_halo = (lane >= LANES - REACH) & (lane < LANES - MARGIN)
    down_halo = (lane >= MARGIN) & (lane < REACH)
    halos, ups, downs = None, None, None
    for k, inner, edge in extended_rows(parity_ref[0:1], grid_ref, near_x, far_x, cells_y):
        slot = k % EDGE_PER
        up = rolled(jnp.where(lane >= LANES - MARGIN, inner, edge), SPAN * slot)
        down = rolled(jnp.where(lane < MARGIN, inner, edge), SPAN * slot)
        halo = rolled(jnp.where(up_halo | down_halo, inner, 0.0), REACH + HALO * k)
        ups = ups + up if slot else up
        downs = downs + down if slot else down
        halos = halos + halo if k else halo
        if slot == EDGE_PER - 1 or k == items - 1:
            place = slice(k // EDGE_PER * rows, (k // EDGE_PER + 1) * rows)
            near_ref[place] = jnp.where(even, ups, downs).astype(jnp.bfloat16)
            far_ref[place] = jnp.where(even, downs, ups).astype(jnp.bfloat16)
    used = lane < HALO * items
    ups = jnp.where(used, halos, 0.0)
    downs = jnp.where(used, rolled(halos, -MARGIN - REACH), 0.0)
    folded = None
    for row in range(0, rows, SPAN):
        size = min(SPAN, rows - row)
        parts = [value[row : row + size] for value in (ups, downs)]
        if size < SPAN:
            parts = [jnp.concatenate([p, jnp.zeros((SPAN - size, LANES), p.dtype)], 0) for p in parts]
        part = rolled(jnp.concatenate(parts, axis=0), row)
        folded = folded + part if row else part
    up, down, even = folded[:SPAN], folded[SPAN:], even[:SPAN]
    near_ref[groups * rows :] = jnp.where(even, up, down).astype(jnp.bfloat16)
    far_ref[groups * rows :] = jnp.where(even, down, up).astype(jnp.bfloat16)


def around(ref, k, start, size):
    center = ref[k, start : start + size]
    back = ref[k, start - 1 : start - 1 + size]
    fore = ref[k, start + 1 : start + 1 + size]
    return center, back, fore, rolled(center, 1), rolled(center, -1)


def advect(moved_ref, carried_ref, levels, comps, rows):
    for start in range(ROWS, ROWS + rows, ROWS):
        for l in range(levels):
            pieces = [around(moved_ref, l * comps + c, start, ROWS) for c in range(comps)]
            speed_x, speed_y = COURANT * pieces[0][0], COURANT * pieces[1][0]
            ahead_x, astern_x = jnp.maximum(speed_x, 0.0), jnp.minimum(speed_x, 0.0)
            ahead_y, astern_y = jnp.maximum(speed_y, 0.0), jnp.minimum(speed_y, 0.0)
            for c in range(comps):
                center, back, fore, below, above = pieces[c]
                change = ahead_x * (center - back) + astern_x * (fore - center)
                change = change + ahead_y * (center - below) + astern_y * (above - center)
                carried_ref[l * comps + c, start : start + ROWS] = center - change


def sweep(ref, carried_ref, levels, comps, start, size):
    scale = 1.0 / (1.0 + 6.0 * VISCOUS)
    centers, results = [], []
    for k in range(levels * comps):
        center, back, fore, below, above = around(ref, k, start, size)
        centers.append(center)
        results.append(back + fore + below + above)
    for k in range(levels * comps):
        higher = min(k // comps + 1, levels - 1) * comps + k % comps
        lower = max(k // comps - 1, 0) * comps + k % comps
        summed = results[k] + centers[higher] + centers[lower]
        source = carried_ref[k, start : start + size]
        results[k] = scale * source + (VISCOUS * scale) * summed
    return results


def first_steps(moved_ref, carried_ref, sweep_ref, levels, comps, rows):
    advect(moved_ref, carried_ref, levels, comps, rows)
    for start in range(ROWS, ROWS + rows, ROWS):
        results = sweep(carried_ref, carried_ref, levels, comps, start, ROWS)
        for k in range(levels * comps):
            sweep_ref[k, start : start + ROWS] = results[k]


RIM = REACH + HALO
HALF = LANES // 2


def weight_kernel(
    shape, chunk, parity_ref, quarter_ref, value_ref, level_ref, inner_ref, rim_ref, parity_out
):
    parity_out[...] = parity_ref[...]
    _, cells_y, _, _ = shape
    slots = quarter_ref.shape[1]
    size = 2 * ROWS
    levels = inner_ref.shape[0] // LANES
    row = lax.broadcasted_iota(jnp.int32, (size, chunk), 0)

    def cut(tile, keep):
        return jnp.where(keep, tile.astype(jnp.float32), 0.0).astype(jnp.bfloat16)

    for first in range(0, slots, chunk):
        lanes = slice(first, first + chunk)
        level = level_ref[:, lanes]
        for l in range(levels):
            value = jnp.where(level == l, value_ref[:, lanes], 0.0)
            quarter, value = doubled(quarter_ref[:, lanes], value)
            for start in range(0, LANES, size):
                inner = picked_tile(quarter, value, start)
                if start < REACH:
                    inner = cut(inner, row + start >= REACH)
                if start + size > cells_y - REACH:
                    inner = cut(inner, row + start < cells_y - REACH)
                if start >= LANES - MARGIN:
                    rim = picked_tile(quarter, value, start - LANES)
                elif start + size > HALF - REACH and start < HALF + MARGIN:
                    rim = picked_tile(quarter, value, start + cells_y - HALF)
                    rim = cut(rim, row + start >= HALF - REACH) if start < HALF - REACH else rim
                elif start < REACH:
                    rim = picked_tile(quarter, value, start)
                    rim = cut(rim, row + start < REACH) if start + size > REACH else rim
                else:
                    rim = jnp.zeros_like(value)
                place = slice(l * LANES + start, l * LANES + start + size)
                inner_ref[place, lanes] = inner
                rim_ref[place, lanes] = rim


def sampled_part(round_ref, weight_ref, quarter_ref, value_ref, lanes, comps):
    wide_x = round_ref.shape[0] // comps
    partial = jnp.dot(round_ref[...], weight_ref[:, lanes], preferred_element_type=jnp.float32)
    quarter, value = quarter_ref[:, lanes], value_ref[:, lanes]
    totals = [jnp.zeros_like(value)] * comps
    for row in range(0, wide_x, ROWS):
        here = quarter == (MARGIN - row) // 4
        for c in range(comps):
            start = c * wide_x + row
            totals[c] = jnp.where(here, partial[start : start + ROWS], totals[c])
    return [jnp.sum(total * value, axis=0, keepdims=True) for total in totals]


def inner_kernel(
    shape, chunk, levels, parity_ref, quarter_ref, value_ref, weight_ref, grid_ref, far_x, near_x,
    inner_ref, rim_ref, sampled_ref, moved_ref, carried_ref, sweep_ref, round_ref,
):
    cells_x, cells_y, _, _ = shape
    items = grid_ref.shape[0]
    comps = items // levels
    slots = quarter_ref.shape[1]
    wide_x = cells_x + SPAN
    rows = cells_x + 2 * PAD
    lane = lane_index(rows)
    for k, inner, edge in extended_rows(parity_ref[0:1], grid_ref, near_x, far_x, cells_y):
        moved_ref[k, ROWS : ROWS + rows] = inner
        low = jnp.where(lane < RIM, inner, jnp.where(lane >= LANES - MARGIN, edge, 0.0))
        high = jnp.where(lane >= LANES - RIM, inner, jnp.where(lane < MARGIN, edge, 0.0))
        rim_ref[k] = low + rolled(high, HALF)
    first_steps(moved_ref, carried_ref, sweep_ref, levels, comps, rows)
    size = 2 * ROWS
    for row in range(0, wide_x, size):
        start = ROWS + PAD - MARGIN + row
        results = sweep(sweep_ref, carried_ref, levels, comps, start, size)
        for k in range(items):
            level, c = k // comps, k % comps
            place = slice(c * wide_x + row, c * wide_x + row + size)
            round_ref[place, level * LANES : (level + 1) * LANES] = results[k].astype(jnp.bfloat16)
            if MARGIN <= row < MARGIN + cells_x:
                inner_ref[k, row - MARGIN : row - MARGIN + size] = results[k]
    for first in range(0, slots, chunk):
        lanes = slice(first, first + chunk)
        parts = sampled_part(round_ref, weight_ref, quarter_ref, value_ref, lanes, comps)
        for c in range(comps):
            sampled_ref[c : c + 1, lanes] = parts[c]


def unfolded(value, rows, groups):
    folded = value[groups * rows :]
    return jnp.concatenate(
        [rolled(folded, -row)[: min(SPAN, rows - row)] for row in range(0, rows, SPAN)], axis=0
    )


def finish_kernel(
    shape, chunk, parity_ref, quarter_ref, value_ref, weight_ref, inner_ref, rim_ref, part_ref,
    far_y, near_y, next_ref, sampled_ref, moved_ref, carried_ref, sweep_ref, round_ref,
):
    cells_x, cells_y, _, _ = shape
    items = rim_ref.shape[0]
    groups = -(-items // EDGE_PER)
    levels, comps = next_ref.shape[:2]
    slots = quarter_ref.shape[1]
    wide_x = cells_x + SPAN
    rows = cells_x + 2 * PAD
    lane = lane_index(rows)
    befores, afters = ordered(parity_ref[1:2], near_y, far_y)
    turned = HALF + MARGIN + REACH
    high_halo = (lane >= turned) & (lane < turned + HALO * items)
    both = ((lane + MARGIN) & (HALF - 1)) < SPAN
    outer = ((lane >= LANES - REACH) & (lane < LANES - MARGIN)) | (
        (lane >= HALF + MARGIN) & (lane < HALF + REACH)
    )
    halo = jnp.where(
        high_halo, rolled(unfolded(afters, rows, groups), turned), unfolded(befores, rows, groups)
    )
    for group in range(groups):
        before = befores[group * rows : (group + 1) * rows]
        after = rolled(afters[group * rows : (group + 1) * rows], HALF)
        for k in range(group * EDGE_PER, min((group + 1) * EDGE_PER, items)):
            slot = k % EDGE_PER
            window = ((lane + (LANES + MARGIN - SPAN * slot)) & (LANES - 1)) < SPAN
            main = rolled(jnp.where(window, before, after), -SPAN * slot)
            value = rim_ref[k] + jnp.where(both, main, 0.0)
            value = jnp.where(outer, rolled(halo, -REACH - HALO * k), value)
            moved_ref[k, ROWS : ROWS + rows] = value

    first_steps(moved_ref, carried_ref, sweep_ref, levels, comps, rows)
    size = 2 * ROWS
    lane = lane_index(size)
    for row in range(0, wide_x, size):
        start = ROWS + PAD - MARGIN + row
        results = sweep(sweep_ref, carried_ref, levels, comps, start, size)
        for k in range(items):
            level, c = k // comps, k % comps
            place = slice(c * wide_x + row, c * wide_x + row + size)
            round_ref[place, level * LANES : (level + 1) * LANES] = results[k].astype(jnp.bfloat16)
        if not MARGIN <= row < MARGIN + cells_x:
            continue
        place = slice(row - MARGIN, row - MARGIN + size)
        for k in range(items):
            low, high = results[k], rolled(results[k], HALF)
            inner = inner_ref[k, place]
            inner = jnp.where(lane < REACH, low, jnp.where(lane >= LANES - REACH, high, inner))
            next_ref[k // comps, k % comps, place] = inner

    for first in range(0, slots, chunk):
        lanes = slice(first, first + chunk)
        parts = sampled_part(round_ref, weight_ref, quarter_ref, value_ref, lanes, comps)
        for c in range(comps):
            sampled_ref[c, 0, :, lanes] = part_ref[c : c + 1, lanes] + parts[c]


def whole(count):
    return [pl.BlockSpec(memory_space=pltpu.VMEM)] * count


def swap_pairs(axis):
    size = lax.axis_size(axis)
    if size % 2:
        raise ValueError("odd axis")
    far_pairs = [(i, (i - 1 if i % 2 == 0 else i + 1) % size) for i in range(size)]
    return far_pairs, [(i, i ^ 1) for i in range(size)]


def body(velocity, marker_cell, marker_frac, marker_force, fish_owner):
    levels, comps, cells_x, cells_y = velocity.shape
    slots = marker_cell.shape[3]
    items = levels * comps
    shape = (cells_x, cells_y, cells_x * lax.axis_size("gx"), cells_y * lax.axis_size("gy"))
    wide_x = cells_x + SPAN
    rows = cells_x + 2 * PAD
    chunk = min(512, slots)
    width = cells_y + LANES
    groups = -(-items // EDGE_PER)
    params = pltpu.CompilerParams(vmem_limit_bytes=32 * 1024 * 1024)
    edge_x = jax.ShapeDtypeStruct(((items + groups) * STRIP, LANES), jnp.bfloat16)
    half = (items, wide_x // 2, width)
    arrays = (fish_owner, velocity, marker_cell, marker_frac, marker_force)
    far_half, far, force, dense_y, quarter, value, quarter_y, value_y, level, parity, near_velocity = (
        pl.pallas_call(
        functools.partial(far_kernel, shape, slots),
        out_shape=(
            jax.ShapeDtypeStruct(half, jnp.float32),
            edge_x,
            jax.ShapeDtypeStruct((items, 2 * ROWS, slots), jnp.bfloat16),
            jax.ShapeDtypeStruct((width, slots), jnp.bfloat16),
            jax.ShapeDtypeStruct((ROWS, slots), jnp.int32),
            jax.ShapeDtypeStruct((ROWS, slots), jnp.float32),
            jax.ShapeDtypeStruct((ROWS, slots), jnp.int32),
            jax.ShapeDtypeStruct((ROWS, slots), jnp.float32),
            jax.ShapeDtypeStruct((1, slots), jnp.int32),
            jax.ShapeDtypeStruct((2, LANES), jnp.int32),
            jax.ShapeDtypeStruct(velocity.shape, velocity.dtype),
        ),
        in_specs=[pl.BlockSpec(memory_space=pltpu.HBM)] * 5,
        out_specs=tuple(whole(11)),
        scratch_shapes=[pltpu.VMEM(a.shape, a.dtype) for a in arrays if a is not velocity]
        + [pltpu.SemaphoreType.DMA((5,))],
        compiler_params=params,
        name="spread_far",
    )(*(pltpu.with_memory_space_constraint(a, pltpu.HBM) for a in arrays))
    )
    far_pairs, near_pairs = swap_pairs("gx")
    far_x = lax.ppermute(far, "gx", far_pairs)
    grid, near = pl.pallas_call(
        functools.partial(near_kernel, shape, slots),
        out_shape=(jax.ShapeDtypeStruct((items, wide_x, width), jnp.float32), edge_x),
        in_specs=whole(5),
        out_specs=tuple(whole(2)),
        scratch_shapes=[pltpu.VMEM(half, jnp.float32)],
        compiler_params=params,
        cost_estimate=pl.CostEstimate(
            flops=items * wide_x * width * slots, bytes_accessed=4 * items * wide_x * width,
            transcendentals=0,
        ),
        name="spread_near",
    )(near_velocity, far_half, force, dense_y, quarter)
    near_x = lax.ppermute(near, "gx", near_pairs)
    weights = jax.ShapeDtypeStruct((levels * LANES, slots), jnp.bfloat16)
    inner_weight, rim_weight, parity = pl.pallas_call(
        functools.partial(weight_kernel, shape, chunk),
        out_shape=(weights, weights, jax.ShapeDtypeStruct(parity.shape, parity.dtype)),
        in_specs=whole(4),
        out_specs=tuple(whole(3)),
        compiler_params=params,
        cost_estimate=pl.CostEstimate(
            flops=2 * levels * LANES * slots, bytes_accessed=4 * levels * LANES * slots,
            transcendentals=0,
        ),
        name="weights",
    )(parity, quarter_y, value_y, level)
    edge_y = jax.ShapeDtypeStruct((groups * rows + SPAN, LANES), jnp.bfloat16)
    far, near = pl.pallas_call(
        functools.partial(pack_kernel, shape),
        out_shape=(edge_y, edge_y),
        in_specs=whole(4),
        out_specs=tuple(whole(2)),
        compiler_params=params,
        name="pack",
    )(parity, grid, far_x, near_x)
    far_pairs, near_pairs = swap_pairs("gy")
    far_y = lax.ppermute(far, "gy", far_pairs)
    near_y = lax.ppermute(near, "gy", near_pairs)
    field = pltpu.VMEM((items, rows + 2 * ROWS, LANES), jnp.float32)
    rounded = pltpu.VMEM((comps * wide_x, levels * LANES), jnp.bfloat16)
    inner, rim, part = pl.pallas_call(
        functools.partial(inner_kernel, shape, chunk, levels),
        out_shape=(
            jax.ShapeDtypeStruct((items, cells_x, LANES), jnp.float32),
            jax.ShapeDtypeStruct((items, rows, LANES), jnp.float32),
            jax.ShapeDtypeStruct((comps, slots), jnp.float32),
        ),
        in_specs=whole(7),
        out_specs=tuple(whole(3)),
        scratch_shapes=[field, field, field, rounded],
        compiler_params=params,
        cost_estimate=pl.CostEstimate(
            flops=2 * items * wide_x * LANES * slots, bytes_accessed=16 * items * rows * LANES,
            transcendentals=0,
        ),
        name="inner",
    )(parity, quarter, value, inner_weight, grid, far_x, near_x)
    return pl.pallas_call(
        functools.partial(finish_kernel, shape, chunk),
        out_shape=(
            jax.ShapeDtypeStruct(velocity.shape, jnp.float32),
            jax.ShapeDtypeStruct((comps, 1, 1, slots), jnp.float32),
        ),
        in_specs=whole(9),
        out_specs=tuple(whole(2)),
        scratch_shapes=[field, field, field, rounded],
        compiler_params=params,
        name="finish",
    )(parity, quarter, value, rim_weight, inner, rim, part, far_y, near_y)


def solution(mesh):
    placed = (
        P(None, None, "gx", "gy"),
        P(None, "gx", "gy", None),
        P(None, "gx", "gy", None),
        P(None, "gx", "gy", None),
        P(),
    )
    return jax.shard_map(
        body,
        mesh=mesh,
        in_specs=placed,
        out_specs=(P(None, None, "gx", "gy"), P(None, "gx", "gy", None)),
        check_vma=False,
    )
```

```python
import functools

import jax
import jax.numpy as jnp
import numpy as np
from jax import lax
from jax.experimental import pallas as pl
from jax.experimental.pallas import tpu as pltpu
from jax.sharding import PartitionSpec as P

MARGIN = 16
FISH_MARK = 1024
HALO = 3
LANES = 128
COURANT = 0.25
VISCOUS = 1.5
ROWS = 8

REACH = MARGIN + HALO
PAD = -(-REACH // ROWS) * ROWS
STRIP = PAD + MARGIN
SPAN = 2 * MARGIN
EDGE_PER = LANES // SPAN


def half_turn(terms):
    nodes = 0.5 - 0.5 * np.cos(np.pi * (np.arange(64) + 0.5) / 64)
    square = nodes * nodes
    cosine = np.polynomial.polynomial.polyfit(square, np.cos(0.5 * np.pi * nodes), terms)
    sine = np.polynomial.polynomial.polyfit(square, np.sin(0.5 * np.pi * nodes) / nodes, terms)
    return [float(v) for v in cosine], [float(v) for v in sine]


COS_FIT, SIN_FIT = half_turn(6)


def horner(coefficients, value):
    total = jnp.full_like(value, coefficients[-1])
    for coefficient in coefficients[-2::-1]:
        total = total * value + coefficient
    return total


def four_weights(frac):
    square = frac * frac
    cosine = horner(COS_FIT, square)
    sine = frac * horner(SIN_FIT, square)
    return (0.25 - 0.25 * sine, 0.25 + 0.25 * cosine, 0.25 + 0.25 * sine, 0.25 - 0.25 * cosine)


def local_cell(cell, low, extent):
    offset = cell - low
    offset = jnp.where(offset < -MARGIN, offset + extent, offset)
    return jnp.where(offset >= extent - MARGIN, offset - extent, offset)


def position():
    row, col = lax.axis_index("gx"), lax.axis_index("gy")
    return row, col, (row & 1) == 0, (col & 1) == 0


def tile_weights(offset, weights):
    shift = lax.broadcasted_iota(jnp.int32, (ROWS, offset.shape[1]), 0) + 1 - offset
    quarter, phase = shift >> 2, shift & 3
    value = jnp.where(phase == 3, weights[3], weights[2])
    value = jnp.where(phase == 1, weights[1], value)
    return quarter, jnp.where(phase == 0, weights[0], value)


def doubled(quarter, value):
    quarter = jnp.concatenate([quarter, quarter + 2], axis=0).astype(jnp.float32)
    return quarter.astype(jnp.bfloat16), twice(value)


def twice(value):
    return jnp.concatenate([value, value], axis=0).astype(jnp.bfloat16)


def picked_tile(quarter, value, first):
    zero = jnp.zeros_like(value)
    return jnp.where(quarter == jnp.array(-first // 4, quarter.dtype), value, zero)


def half_spread(quarter_ref, force_ref, dense_y_ref, half_ref, base, lanes):
    items, rows = half_ref.shape[:2]
    quarter = quarter_ref[:, lanes] + base
    quarter = jnp.concatenate([quarter, quarter + 2], axis=0).astype(jnp.float32)
    quarter = quarter.astype(jnp.bfloat16)
    left = jnp.concatenate(
        [
            picked_tile(quarter, force_ref[k, :, lanes], row)
            for k in range(items)
            for row in range(0, rows, 2 * ROWS)
        ],
        axis=0,
    )
    total = lax.dot_general(
        left, dense_y_ref[:, lanes], (((1,), (1,)), ((), ())),
        preferred_element_type=jnp.float32,
    )
    total = total.reshape(half_ref.shape)
    if lanes.start:
        half_ref[...] += total
    else:
        half_ref[...] = total


def finish_half(half_ref, velocity_ref, out_ref, low, cells_y):
    items, rows = half_ref.shape[:2]
    comps = items // velocity_ref.shape[0]
    count = rows - MARGIN
    source = pl.ds(pl.multiple_of(jnp.where(low, 0, count), ROWS), count)
    target = pl.ds(pl.multiple_of(jnp.where(low, MARGIN, 0), ROWS), count)
    for k in range(items):
        half_ref[k, target, :cells_y] += velocity_ref[k // comps, k % comps, source]
    place = pl.ds(pl.multiple_of(jnp.where(low, 0, rows - STRIP), ROWS), STRIP)
    parts = [half_ref[k, place, :cells_y] for k in range(items)]
    for group in range(0, items, EDGE_PER):
        edges = []
        for k in range(group, min(group + EDGE_PER, items)):
            edges.append(rolled(half_ref[k, place, cells_y:], SPAN * (k - group)))
        parts.append(functools.reduce(jnp.add, edges))
    out_ref[...] = jnp.concatenate(parts, axis=0).astype(jnp.bfloat16)


def far_kernel(
    shape, chunk, fish_hbm, velocity_hbm, cell_hbm, frac_hbm, force_hbm,
    half_ref, far_ref, force_out, dense_y_ref, quarter_ref, value_ref,
    quarter_y_ref, value_y_ref, level_ref, parity_ref, velocity_ref,
    fish_ref, cell_ref, frac_ref, force_ref, sems,
):
    pairs = (
        (cell_hbm, cell_ref), (frac_hbm, frac_ref), (fish_hbm, fish_ref),
        (force_hbm, force_ref), (velocity_hbm, velocity_ref),
    )
    copies = [pltpu.make_async_copy(a, b, sems.at[i]) for i, (a, b) in enumerate(pairs)]
    for copy in copies:
        copy.start()
    cells_x, cells_y, extent_x, extent_y = shape
    levels, comps = velocity_ref.shape[:2]
    slots = cell_ref.shape[3]
    row, col, even, even_y = position()
    parity_ref[0:1] = jnp.full((1, LANES), jnp.where(even, 1, 0), jnp.int32)
    parity_ref[1:2] = jnp.full((1, LANES), jnp.where(even_y, 1, 0), jnp.int32)
    base = jnp.where(even, -MARGIN // 4, cells_x // 8)
    for copy in copies[:-1]:
        copy.wait()
    mine = jnp.where(fish_ref[...] == row * lax.axis_size("gy") + col, 1.0, 0.0)
    count = FISH_MARK * jnp.sum(mine)
    level_ref[...] = cell_ref[2, 0]
    for first in range(0, slots, chunk):
        lanes = slice(first, first + chunk)
        offset_x = local_cell(cell_ref[0, 0, :, lanes], row * cells_x, extent_x)
        offset_y = local_cell(cell_ref[1, 0, :, lanes], col * cells_y, extent_y)
        slot = lax.broadcasted_iota(jnp.int32, (1, chunk), 1) + first
        alive = jnp.where(slot.astype(jnp.float32) < count, 1.0, 0.0)
        quarter, value = tile_weights(offset_x, four_weights(frac_ref[0, 0, :, lanes]))
        value = value * alive
        quarter_ref[:, lanes] = quarter
        value_ref[:, lanes] = value
        level = cell_ref[2, 0, :, lanes]
        pushes = [force_ref[c, 0, :, lanes] * value for c in range(comps)]
        for l in range(levels):
            for c in range(comps):
                force_out[l * comps + c, :, lanes] = twice(jnp.where(level == l, pushes[c], 0.0))
        quarter, value = tile_weights(offset_y, four_weights(frac_ref[1, 0, :, lanes]))
        quarter_y_ref[:, lanes] = quarter
        value_y_ref[:, lanes] = value
        quarter, value = doubled(quarter, value)
        dense_y_ref[:, lanes] = jnp.concatenate(
            [picked_tile(quarter, value, n) for n in range(0, cells_y + MARGIN, 2 * ROWS)]
            + [jnp.zeros((LANES - SPAN, chunk), jnp.bfloat16)]
            + [picked_tile(quarter, value, n) for n in range(-MARGIN, 0, 2 * ROWS)],
            axis=0,
        )
        half_spread(quarter_ref, force_out, dense_y_ref, half_ref, base, lanes)
    copies[-1].wait()
    finish_half(half_ref, velocity_ref, far_ref, even, cells_y)


def near_kernel(
    shape, chunk, velocity_ref, far_half_ref, force_ref, dense_y_ref, quarter_ref,
    grid_ref, near_ref, half_ref,
):
    cells_x, cells_y, _, _ = shape
    slots = quarter_ref.shape[1]
    rows = half_ref.shape[1]
    _, _, even, _ = position()
    base = jnp.where(even, cells_x // 8, -MARGIN // 4)
    for first in range(0, slots, chunk):
        lanes = slice(first, first + chunk)
        half_spread(quarter_ref, force_ref, dense_y_ref, half_ref, base, lanes)
    finish_half(half_ref, velocity_ref, near_ref, jnp.logical_not(even), cells_y)
    for ref, row in ((far_half_ref, jnp.where(even, 0, rows)), (half_ref, jnp.where(even, rows, 0))):
        place = pl.ds(pl.multiple_of(row, ROWS), rows)
        for k in range(ref.shape[0]):
            grid_ref[k, place] = ref[k]


def rolled(value, shift):
    shift = shift % LANES
    return pltpu.roll(value, shift, 1) if shift else value


def lane_index(rows):
    return lax.broadcasted_iota(jnp.int32, (rows, LANES), 1)


def ordered(parity, near_ref, far_ref):
    even = jnp.broadcast_to(parity, near_ref.shape) != 0
    near, far = near_ref[...].astype(jnp.float32), far_ref[...].astype(jnp.float32)
    return jnp.where(even, far, near), jnp.where(even, near, far)


def joined(center, before, after):
    wide = center.shape[0]
    near = PAD - MARGIN
    overlap = STRIP - near
    return jnp.concatenate(
        [
            before[:near],
            center[:overlap] + before[near:],
            center[overlap : wide - overlap],
            center[wide - overlap :] + after[:overlap],
            after[overlap:],
        ],
        axis=0,
    )


def extended_rows(parity, grid_ref, near_ref, far_ref, cells_y):
    items = grid_ref.shape[0]
    groups = -(-items // EDGE_PER)
    size = groups * STRIP
    before, after = ordered(parity, near_ref, far_ref)
    packed = jnp.concatenate([before[items * STRIP :], after[items * STRIP :]], axis=0)
    lane = lane_index(2 * size)
    kept = (lane < MARGIN) | (lane >= LANES - MARGIN)
    edges = [jnp.where(kept, rolled(packed, -SPAN * slot), 0.0) for slot in range(EDGE_PER)]
    for k in range(items):
        place = slice(k * STRIP, (k + 1) * STRIP)
        inner = joined(grid_ref[k, :, :cells_y], before[place], after[place])
        start = k // EDGE_PER * STRIP
        edge = edges[k % EDGE_PER]
        edge = joined(
            grid_ref[k, :, cells_y:],
            edge[start : start + STRIP],
            edge[size + start : size + start + STRIP],
        )
        yield k, inner, edge


def pack_kernel(shape, parity_ref, grid_ref, far_x, near_x, far_ref, near_ref):
    cells_x, cells_y, _, _ = shape
    items = grid_ref.shape[0]
    groups = -(-items // EDGE_PER)
    rows = cells_x + 2 * PAD
    lane = lane_index(rows)
    up_halo = (lane >= LANES - REACH) & (lane < LANES - MARGIN)
    down_halo = (lane >= MARGIN) & (lane < REACH)
    halos, ups, downs = None, None, None
    packed = [[], []]
    for k, inner, edge in extended_rows(parity_ref[0:1], grid_ref, near_x, far_x, cells_y):
        slot = k % EDGE_PER
        up = rolled(jnp.where(lane >= LANES - MARGIN, inner, edge), SPAN * slot)
        down = rolled(jnp.where(lane < MARGIN, inner, edge), SPAN * slot)
        halo = rolled(jnp.where(up_halo | down_halo, inner, 0.0), REACH + HALO * k)
        ups = ups + up if slot else up
        downs = downs + down if slot else down
        halos = halos + halo if k else halo
        if slot == EDGE_PER - 1 or k == items - 1:
            packed[0].append(squeezed(ups))
            packed[1].append(squeezed(downs))
    halos = squeezed(halos)
    rows = halos.shape[0]
    used = lane_index(rows) < HALO * items
    ups = jnp.where(used, halos, 0.0)
    downs = jnp.where(used, rolled(halos, -MARGIN - REACH), 0.0)
    folded = None
    for row in range(0, rows, SPAN):
        size = min(SPAN, rows - row)
        parts = [value[row : row + size] for value in (ups, downs)]
        if size < SPAN:
            parts = [jnp.concatenate([p, jnp.zeros((SPAN - size, LANES), p.dtype)], 0) for p in parts]
        part = rolled(jnp.concatenate(parts, axis=0), row)
        folded = folded + part if row else part
    up = jnp.concatenate(packed[0] + [folded[:SPAN]], axis=0)
    down = jnp.concatenate(packed[1] + [folded[SPAN:]], axis=0)
    even = jnp.broadcast_to(parity_ref[1:2], up.shape) != 0
    near_ref[...] = jnp.where(even, up, down).astype(jnp.bfloat16)
    far_ref[...] = jnp.where(even, down, up).astype(jnp.bfloat16)


def squeezed(value):
    row = lax.broadcasted_iota(jnp.int32, (ROWS, LANES), 0)
    shared = jnp.where(row >= PAD - REACH, value[:ROWS], value[-ROWS:])
    return jnp.concatenate([shared, value[ROWS:-ROWS]], axis=0)


def expanded(value):
    return jnp.concatenate([value, value[:ROWS]], axis=0)


def around(ref, k, start, size):
    center = ref[k, start : start + size]
    back = ref[k, start - 1 : start - 1 + size]
    fore = ref[k, start + 1 : start + 1 + size]
    return center, back, fore, rolled(center, 1), rolled(center, -1)


def advect(moved_ref, carried_ref, levels, comps, rows):
    for start in range(ROWS, ROWS + rows, ROWS):
        for l in range(levels):
            pieces = [around(moved_ref, l * comps + c, start, ROWS) for c in range(comps)]
            speed_x, speed_y = COURANT * pieces[0][0], COURANT * pieces[1][0]
            ahead_x, astern_x = jnp.maximum(speed_x, 0.0), jnp.minimum(speed_x, 0.0)
            ahead_y, astern_y = jnp.maximum(speed_y, 0.0), jnp.minimum(speed_y, 0.0)
            for c in range(comps):
                center, back, fore, below, above = pieces[c]
                change = ahead_x * (center - back) + astern_x * (fore - center)
                change = change + ahead_y * (center - below) + astern_y * (above - center)
                carried_ref[l * comps + c, start : start + ROWS] = center - change


def sweep(ref, carried_ref, levels, comps, start, size):
    scale = 1.0 / (1.0 + 6.0 * VISCOUS)
    centers, results = [], []
    for k in range(levels * comps):
        center, back, fore, below, above = around(ref, k, start, size)
        centers.append(center)
        results.append(back + fore + below + above)
    for k in range(levels * comps):
        higher = min(k // comps + 1, levels - 1) * comps + k % comps
        lower = max(k // comps - 1, 0) * comps + k % comps
        summed = results[k] + centers[higher] + centers[lower]
        source = carried_ref[k, start : start + size]
        results[k] = scale * source + (VISCOUS * scale) * summed
    return results


def first_steps(moved_ref, carried_ref, sweep_ref, levels, comps, rows):
    advect(moved_ref, carried_ref, levels, comps, rows)
    for start in range(ROWS, ROWS + rows, ROWS):
        results = sweep(carried_ref, carried_ref, levels, comps, start, ROWS)
        for k in range(levels * comps):
            sweep_ref[k, start : start + ROWS] = results[k]


RIM = REACH + HALO
HALF = LANES // 2


def weight_kernel(
    shape, chunk, parity_ref, quarter_ref, value_ref, level_ref, inner_ref, rim_ref, parity_out
):
    parity_out[...] = parity_ref[...]
    _, cells_y, _, _ = shape
    slots = quarter_ref.shape[1]
    size = 2 * ROWS
    levels = inner_ref.shape[0] // LANES
    row = lax.broadcasted_iota(jnp.int32, (size, chunk), 0)

    def cut(tile, keep):
        return jnp.where(keep, tile.astype(jnp.float32), 0.0).astype(jnp.bfloat16)

    for first in range(0, slots, chunk):
        lanes = slice(first, first + chunk)
        level = level_ref[:, lanes]
        for l in range(levels):
            value = jnp.where(level == l, value_ref[:, lanes], 0.0)
            quarter, value = doubled(quarter_ref[:, lanes], value)
            for start in range(0, LANES, size):
                inner = picked_tile(quarter, value, start)
                if start < REACH:
                    inner = cut(inner, row + start >= REACH)
                if start + size > cells_y - REACH:
                    inner = cut(inner, row + start < cells_y - REACH)
                if start >= LANES - MARGIN:
                    rim = picked_tile(quarter, value, start - LANES)
                elif start + size > HALF - REACH and start < HALF + MARGIN:
                    rim = picked_tile(quarter, value, start + cells_y - HALF)
                    rim = cut(rim, row + start >= HALF - REACH) if start < HALF - REACH else rim
                elif start < REACH:
                    rim = picked_tile(quarter, value, start)
                    rim = cut(rim, row + start < REACH) if start + size > REACH else rim
                else:
                    rim = jnp.zeros_like(value)
                place = slice(l * LANES + start, l * LANES + start + size)
                inner_ref[place, lanes] = inner
                rim_ref[place, lanes] = rim


def sampled_part(round_ref, weight_ref, quarter_ref, value_ref, lanes, comps):
    wide_x = round_ref.shape[0] // comps
    partial = jnp.dot(round_ref[...], weight_ref[:, lanes], preferred_element_type=jnp.float32)
    quarter, value = quarter_ref[:, lanes], value_ref[:, lanes]
    totals = [jnp.zeros_like(value)] * comps
    for row in range(0, wide_x, ROWS):
        here = quarter == (MARGIN - row) // 4
        for c in range(comps):
            start = c * wide_x + row
            totals[c] = jnp.where(here, partial[start : start + ROWS], totals[c])
    return [jnp.sum(total * value, axis=0, keepdims=True) for total in totals]


def inner_kernel(
    shape, chunk, levels, parity_ref, quarter_ref, value_ref, weight_ref, grid_ref, far_x, near_x,
    inner_ref, rim_ref, sampled_ref, moved_ref, carried_ref, sweep_ref, round_ref,
):
    cells_x, cells_y, _, _ = shape
    items = grid_ref.shape[0]
    comps = items // levels
    slots = quarter_ref.shape[1]
    wide_x = cells_x + SPAN
    rows = cells_x + 2 * PAD
    lane = lane_index(rows)
    for k, inner, edge in extended_rows(parity_ref[0:1], grid_ref, near_x, far_x, cells_y):
        moved_ref[k, ROWS : ROWS + rows] = inner
        low = jnp.where(lane < RIM, inner, jnp.where(lane >= LANES - MARGIN, edge, 0.0))
        high = jnp.where(lane >= LANES - RIM, inner, jnp.where(lane < MARGIN, edge, 0.0))
        rim_ref[k] = low + rolled(high, HALF)
    first_steps(moved_ref, carried_ref, sweep_ref, levels, comps, rows)
    size = 2 * ROWS
    for row in range(0, wide_x, size):
        start = ROWS + PAD - MARGIN + row
        results = sweep(sweep_ref, carried_ref, levels, comps, start, size)
        for k in range(items):
            level, c = k // comps, k % comps
            place = slice(c * wide_x + row, c * wide_x + row + size)
            round_ref[place, level * LANES : (level + 1) * LANES] = results[k].astype(jnp.bfloat16)
            if MARGIN <= row < MARGIN + cells_x:
                inner_ref[k, row - MARGIN : row - MARGIN + size] = results[k]
    for first in range(0, slots, chunk):
        lanes = slice(first, first + chunk)
        parts = sampled_part(round_ref, weight_ref, quarter_ref, value_ref, lanes, comps)
        for c in range(comps):
            sampled_ref[c : c + 1, lanes] = parts[c]


def unfolded(folded, rows):
    return expanded(
        jnp.concatenate(
            [rolled(folded, -row)[: min(SPAN, rows - row)] for row in range(0, rows, SPAN)], axis=0
        )
    )


def finish_kernel(
    shape, chunk, parity_ref, quarter_ref, value_ref, weight_ref, inner_ref, rim_ref, part_ref,
    far_y, near_y, next_hbm, sampled_ref,
    moved_ref, carried_ref, sweep_ref, round_ref, next_ref, sem,
):
    cells_x, cells_y, _, _ = shape
    items = rim_ref.shape[0]
    groups = -(-items // EDGE_PER)
    levels, comps = next_ref.shape[:2]
    slots = quarter_ref.shape[1]
    wide_x = cells_x + SPAN
    rows = cells_x + 2 * PAD
    lane = lane_index(rows)
    befores, afters = ordered(parity_ref[1:2], near_y, far_y)
    turned = HALF + MARGIN + REACH
    high_halo = (lane >= turned) & (lane < turned + HALO * items)
    both = ((lane + MARGIN) & (HALF - 1)) < SPAN
    outer = ((lane >= LANES - REACH) & (lane < LANES - MARGIN)) | (
        (lane >= HALF + MARGIN) & (lane < HALF + REACH)
    )
    size = rows - ROWS
    halo = jnp.where(
        high_halo,
        rolled(unfolded(afters[groups * size :], size), turned),
        unfolded(befores[groups * size :], size),
    )
    for group in range(groups):
        before = expanded(befores[group * size : (group + 1) * size])
        after = expanded(rolled(afters[group * size : (group + 1) * size], HALF))
        for k in range(group * EDGE_PER, min((group + 1) * EDGE_PER, items)):
            slot = k % EDGE_PER
            window = ((lane + (LANES + MARGIN - SPAN * slot)) & (LANES - 1)) < SPAN
            main = rolled(jnp.where(window, before, after), -SPAN * slot)
            value = rim_ref[k] + jnp.where(both, main, 0.0)
            value = jnp.where(outer, rolled(halo, -REACH - HALO * k), value)
            moved_ref[k, ROWS : ROWS + rows] = value

    first_steps(moved_ref, carried_ref, sweep_ref, levels, comps, rows)
    size = 2 * ROWS
    lane = lane_index(size)
    for row in range(0, wide_x, size):
        start = ROWS + PAD - MARGIN + row
        results = sweep(sweep_ref, carried_ref, levels, comps, start, size)
        for k in range(items):
            level, c = k // comps, k % comps
            place = slice(c * wide_x + row, c * wide_x + row + size)
            round_ref[place, level * LANES : (level + 1) * LANES] = results[k].astype(jnp.bfloat16)
        if not MARGIN <= row < MARGIN + cells_x:
            continue
        place = slice(row - MARGIN, row - MARGIN + size)
        for k in range(items):
            low, high = results[k], rolled(results[k], HALF)
            inner = inner_ref[k, place]
            inner = jnp.where(lane < REACH, low, jnp.where(lane >= LANES - REACH, high, inner))
            next_ref[k // comps, k % comps, place] = inner
    copy = pltpu.make_async_copy(next_ref, next_hbm, sem)
    copy.start()

    for first in range(0, slots, chunk):
        lanes = slice(first, first + chunk)
        parts = sampled_part(round_ref, weight_ref, quarter_ref, value_ref, lanes, comps)
        for c in range(comps):
            sampled_ref[c, 0, :, lanes] = part_ref[c : c + 1, lanes] + parts[c]
    copy.wait()


def whole(count):
    return [pl.BlockSpec(memory_space=pltpu.VMEM)] * count


def swap_pairs(axis):
    size = lax.axis_size(axis)
    if size % 2:
        raise ValueError("odd axis")
    far_pairs = [(i, (i - 1 if i % 2 == 0 else i + 1) % size) for i in range(size)]
    return far_pairs, [(i, i ^ 1) for i in range(size)]


def body(velocity, marker_cell, marker_frac, marker_force, fish_owner):
    levels, comps, cells_x, cells_y = velocity.shape
    slots = marker_cell.shape[3]
    items = levels * comps
    shape = (cells_x, cells_y, cells_x * lax.axis_size("gx"), cells_y * lax.axis_size("gy"))
    wide_x = cells_x + SPAN
    rows = cells_x + 2 * PAD
    chunk = min(512, slots)
    width = cells_y + LANES
    groups = -(-items // EDGE_PER)
    params = pltpu.CompilerParams(vmem_limit_bytes=32 * 1024 * 1024)
    edge_x = jax.ShapeDtypeStruct(((items + groups) * STRIP, LANES), jnp.bfloat16)
    half = (items, wide_x // 2, width)
    arrays = (fish_owner, velocity, marker_cell, marker_frac, marker_force)
    far_half, far, force, dense_y, quarter, value, quarter_y, value_y, level, parity, near_velocity = (
        pl.pallas_call(
        functools.partial(far_kernel, shape, slots),
        out_shape=(
            jax.ShapeDtypeStruct(half, jnp.float32),
            edge_x,
            jax.ShapeDtypeStruct((items, 2 * ROWS, slots), jnp.bfloat16),
            jax.ShapeDtypeStruct((width, slots), jnp.bfloat16),
            jax.ShapeDtypeStruct((ROWS, slots), jnp.int32),
            jax.ShapeDtypeStruct((ROWS, slots), jnp.float32),
            jax.ShapeDtypeStruct((ROWS, slots), jnp.int32),
            jax.ShapeDtypeStruct((ROWS, slots), jnp.float32),
            jax.ShapeDtypeStruct((1, slots), jnp.int32),
            jax.ShapeDtypeStruct((2, LANES), jnp.int32),
            jax.ShapeDtypeStruct(velocity.shape, velocity.dtype),
        ),
        in_specs=[pl.BlockSpec(memory_space=pltpu.HBM)] * 5,
        out_specs=tuple(whole(11)),
        scratch_shapes=[pltpu.VMEM(a.shape, a.dtype) for a in arrays if a is not velocity]
        + [pltpu.SemaphoreType.DMA((5,))],
        compiler_params=params,
        name="spread_far",
    )(*(pltpu.with_memory_space_constraint(a, pltpu.HBM) for a in arrays))
    )
    far_pairs, near_pairs = swap_pairs("gx")
    far_x = lax.ppermute(far, "gx", far_pairs)
    grid, near = pl.pallas_call(
        functools.partial(near_kernel, shape, slots),
        out_shape=(jax.ShapeDtypeStruct((items, wide_x, width), jnp.float32), edge_x),
        in_specs=whole(5),
        out_specs=tuple(whole(2)),
        scratch_shapes=[pltpu.VMEM(half, jnp.float32)],
        compiler_params=params,
        cost_estimate=pl.CostEstimate(
            flops=items * wide_x * width * slots, bytes_accessed=4 * items * wide_x * width,
            transcendentals=0,
        ),
        name="spread_near",
    )(near_velocity, far_half, force, dense_y, quarter)
    near_x = lax.ppermute(near, "gx", near_pairs)
    weights = jax.ShapeDtypeStruct((levels * LANES, slots), jnp.bfloat16)
    inner_weight, rim_weight, parity = pl.pallas_call(
        functools.partial(weight_kernel, shape, chunk),
        out_shape=(weights, weights, jax.ShapeDtypeStruct(parity.shape, parity.dtype)),
        in_specs=whole(4),
        out_specs=tuple(whole(3)),
        compiler_params=params,
        cost_estimate=pl.CostEstimate(
            flops=2 * levels * LANES * slots, bytes_accessed=4 * levels * LANES * slots,
            transcendentals=0,
        ),
        name="weights",
    )(parity, quarter_y, value_y, level)
    edge_y = jax.ShapeDtypeStruct((groups * (rows - ROWS) + SPAN, LANES), jnp.bfloat16)
    far, near = pl.pallas_call(
        functools.partial(pack_kernel, shape),
        out_shape=(edge_y, edge_y),
        in_specs=whole(4),
        out_specs=tuple(whole(2)),
        compiler_params=params,
        name="pack",
    )(parity, grid, far_x, near_x)
    far_pairs, near_pairs = swap_pairs("gy")
    far_y = lax.ppermute(far, "gy", far_pairs)
    near_y = lax.ppermute(near, "gy", near_pairs)
    field = pltpu.VMEM((items, rows + 2 * ROWS, LANES), jnp.float32)
    rounded = pltpu.VMEM((comps * wide_x, levels * LANES), jnp.bfloat16)
    inner, rim, part = pl.pallas_call(
        functools.partial(inner_kernel, shape, chunk, levels),
        out_shape=(
            jax.ShapeDtypeStruct((items, cells_x, LANES), jnp.float32),
            jax.ShapeDtypeStruct((items, rows, LANES), jnp.float32),
            jax.ShapeDtypeStruct((comps, slots), jnp.float32),
        ),
        in_specs=whole(7),
        out_specs=tuple(whole(3)),
        scratch_shapes=[field, field, field, rounded],
        compiler_params=params,
        cost_estimate=pl.CostEstimate(
            flops=2 * items * wide_x * LANES * slots, bytes_accessed=16 * items * rows * LANES,
            transcendentals=0,
        ),
        name="inner",
    )(parity, quarter, value, inner_weight, grid, far_x, near_x)
    return pl.pallas_call(
        functools.partial(finish_kernel, shape, chunk),
        out_shape=(
            jax.ShapeDtypeStruct(velocity.shape, jnp.float32),
            jax.ShapeDtypeStruct((comps, 1, 1, slots), jnp.float32),
        ),
        in_specs=whole(9),
        out_specs=(pl.BlockSpec(memory_space=pltpu.HBM), whole(1)[0]),
        scratch_shapes=[field, field, field, rounded, pltpu.VMEM(velocity.shape, velocity.dtype)]
        + [pltpu.SemaphoreType.DMA],
        compiler_params=params,
        name="finish",
    )(parity, quarter, value, rim_weight, inner, rim, part, far_y, near_y)


def solution(mesh):
    placed = (
        P(None, None, "gx", "gy"),
        P(None, "gx", "gy", None),
        P(None, "gx", "gy", None),
        P(None, "gx", "gy", None),
        P(),
    )
    return jax.shard_map(
        body,
        mesh=mesh,
        in_specs=placed,
        out_specs=(P(None, None, "gx", "gy"), P(None, "gx", "gy", None)),
        check_vma=False,
    )
```

```python
import functools

import jax
import jax.numpy as jnp
import numpy as np
from jax import lax
from jax.experimental import pallas as pl
from jax.experimental.pallas import tpu as pltpu
from jax.sharding import PartitionSpec as P

MARGIN = 16
FISH_MARK = 1024
HALO = 3
LANES = 128
COURANT = 0.25
VISCOUS = 1.5
ROWS = 8

REACH = MARGIN + HALO
PAD = -(-REACH // ROWS) * ROWS
STRIP = PAD + MARGIN
SPAN = 2 * MARGIN
EDGE_PER = LANES // SPAN


def half_turn(terms):
    nodes = 0.5 - 0.5 * np.cos(np.pi * (np.arange(64) + 0.5) / 64)
    square = nodes * nodes
    cosine = np.polynomial.polynomial.polyfit(square, np.cos(0.5 * np.pi * nodes), terms)
    sine = np.polynomial.polynomial.polyfit(square, np.sin(0.5 * np.pi * nodes) / nodes, terms)
    return [float(v) for v in cosine], [float(v) for v in sine]


COS_FIT, SIN_FIT = half_turn(6)


def horner(coefficients, value):
    total = jnp.full_like(value, coefficients[-1])
    for coefficient in coefficients[-2::-1]:
        total = total * value + coefficient
    return total


def four_weights(frac):
    square = frac * frac
    cosine = horner(COS_FIT, square)
    sine = frac * horner(SIN_FIT, square)
    return (0.25 - 0.25 * sine, 0.25 + 0.25 * cosine, 0.25 + 0.25 * sine, 0.25 - 0.25 * cosine)


def local_cell(cell, low, extent):
    offset = cell - low
    offset = jnp.where(offset < -MARGIN, offset + extent, offset)
    return jnp.where(offset >= extent - MARGIN, offset - extent, offset)


def position():
    row, col = lax.axis_index("gx"), lax.axis_index("gy")
    return row, col, (row & 1) == 0, (col & 1) == 0


def tile_weights(offset, weights):
    shift = lax.broadcasted_iota(jnp.int32, (ROWS, offset.shape[1]), 0) + 1 - offset
    quarter, phase = shift >> 2, shift & 3
    value = jnp.where(phase == 3, weights[3], weights[2])
    value = jnp.where(phase == 1, weights[1], value)
    return quarter, jnp.where(phase == 0, weights[0], value)


def doubled(quarter, value):
    quarter = jnp.concatenate([quarter, quarter + 2], axis=0).astype(jnp.float32)
    return quarter.astype(jnp.bfloat16), twice(value)


def twice(value):
    return jnp.concatenate([value, value], axis=0).astype(jnp.bfloat16)


def picked_tile(quarter, value, first):
    zero = jnp.zeros_like(value)
    return jnp.where(quarter == jnp.array(-first // 4, quarter.dtype), value, zero)


def half_spread(quarter_ref, force_ref, dense_y_ref, half_ref, base, lanes):
    items, rows = half_ref.shape[:2]
    quarter = quarter_ref[:, lanes] + base
    quarter = jnp.concatenate([quarter, quarter + 2], axis=0).astype(jnp.float32)
    quarter = quarter.astype(jnp.bfloat16)
    left = jnp.concatenate(
        [
            picked_tile(quarter, force_ref[k, :, lanes], row)
            for k in range(items)
            for row in range(0, rows, 2 * ROWS)
        ],
        axis=0,
    )
    total = lax.dot_general(
        left, dense_y_ref[:, lanes], (((1,), (1,)), ((), ())),
        preferred_element_type=jnp.float32,
    )
    total = total.reshape(half_ref.shape)
    if lanes.start:
        half_ref[...] += total
    else:
        half_ref[...] = total


def finish_half(half_ref, velocity_ref, out_ref, low, cells_y):
    items, rows = half_ref.shape[:2]
    comps = items // velocity_ref.shape[0]
    count = rows - MARGIN
    source = pl.ds(pl.multiple_of(jnp.where(low, 0, count), ROWS), count)
    target = pl.ds(pl.multiple_of(jnp.where(low, MARGIN, 0), ROWS), count)
    for k in range(items):
        half_ref[k, target, :cells_y] += velocity_ref[k // comps, k % comps, source]
    place = pl.ds(pl.multiple_of(jnp.where(low, 0, rows - STRIP), ROWS), STRIP)
    parts = [half_ref[k, place, :cells_y] for k in range(items)]
    for group in range(0, items, EDGE_PER):
        edges = []
        for k in range(group, min(group + EDGE_PER, items)):
            edges.append(rolled(half_ref[k, place, cells_y:], SPAN * (k - group)))
        parts.append(functools.reduce(jnp.add, edges))
    out_ref[...] = jnp.concatenate(parts, axis=0).astype(jnp.bfloat16)


def far_kernel(
    shape, chunk, fish_hbm, velocity_hbm, cell_hbm, frac_hbm, force_hbm,
    half_ref, far_ref, force_out, dense_y_ref, quarter_ref, value_ref,
    quarter_y_ref, value_y_ref, level_ref, parity_ref, velocity_ref,
    fish_ref, cell_ref, frac_ref, force_ref, sems,
):
    pairs = (
        (cell_hbm, cell_ref), (frac_hbm, frac_ref), (fish_hbm, fish_ref),
        (force_hbm, force_ref), (velocity_hbm, velocity_ref),
    )
    copies = [pltpu.make_async_copy(a, b, sems.at[i]) for i, (a, b) in enumerate(pairs)]
    for copy in copies:
        copy.start()
    cells_x, cells_y, extent_x, extent_y = shape
    levels, comps = velocity_ref.shape[:2]
    slots = cell_ref.shape[3]
    row, col, even, even_y = position()
    parity_ref[0:1] = jnp.full((1, LANES), jnp.where(even, 1, 0), jnp.int32)
    parity_ref[1:2] = jnp.full((1, LANES), jnp.where(even_y, 1, 0), jnp.int32)
    base = jnp.where(even, -MARGIN // 4, cells_x // 8)
    for copy in copies[:-1]:
        copy.wait()
    mine = jnp.where(fish_ref[...] == row * lax.axis_size("gy") + col, 1.0, 0.0)
    count = FISH_MARK * jnp.sum(mine)
    level_ref[...] = cell_ref[2, 0]
    for first in range(0, slots, chunk):
        lanes = slice(first, first + chunk)
        offset_x = local_cell(cell_ref[0, 0, :, lanes], row * cells_x, extent_x)
        offset_y = local_cell(cell_ref[1, 0, :, lanes], col * cells_y, extent_y)
        slot = lax.broadcasted_iota(jnp.int32, (1, chunk), 1) + first
        alive = jnp.where(slot.astype(jnp.float32) < count, 1.0, 0.0)
        quarter, value = tile_weights(offset_x, four_weights(frac_ref[0, 0, :, lanes]))
        value = value * alive
        quarter_ref[:, lanes] = quarter
        value_ref[:, lanes] = value
        level = cell_ref[2, 0, :, lanes]
        pushes = [force_ref[c, 0, :, lanes] * value for c in range(comps)]
        for l in range(levels):
            for c in range(comps):
                force_out[l * comps + c, :, lanes] = twice(jnp.where(level == l, pushes[c], 0.0))
        quarter, value = tile_weights(offset_y, four_weights(frac_ref[1, 0, :, lanes]))
        quarter_y_ref[:, lanes] = quarter
        value_y_ref[:, lanes] = value
        quarter, value = doubled(quarter, value)
        dense_y_ref[:, lanes] = jnp.concatenate(
            [picked_tile(quarter, value, n) for n in range(0, cells_y + MARGIN, 2 * ROWS)]
            + [jnp.zeros((LANES - SPAN, chunk), jnp.bfloat16)]
            + [picked_tile(quarter, value, n) for n in range(-MARGIN, 0, 2 * ROWS)],
            axis=0,
        )
        half_spread(quarter_ref, force_out, dense_y_ref, half_ref, base, lanes)
    copies[-1].wait()
    finish_half(half_ref, velocity_ref, far_ref, even, cells_y)


def near_kernel(
    shape, chunk, velocity_ref, far_half_ref, force_ref, dense_y_ref, quarter_ref,
    grid_ref, near_ref, half_ref,
):
    cells_x, cells_y, _, _ = shape
    slots = quarter_ref.shape[1]
    rows = half_ref.shape[1]
    _, _, even, _ = position()
    base = jnp.where(even, cells_x // 8, -MARGIN // 4)
    for first in range(0, slots, chunk):
        lanes = slice(first, first + chunk)
        half_spread(quarter_ref, force_ref, dense_y_ref, half_ref, base, lanes)
    finish_half(half_ref, velocity_ref, near_ref, jnp.logical_not(even), cells_y)
    for ref, row in ((far_half_ref, jnp.where(even, 0, rows)), (half_ref, jnp.where(even, rows, 0))):
        place = pl.ds(pl.multiple_of(row, ROWS), rows)
        for k in range(ref.shape[0]):
            grid_ref[k, place] = ref[k]


def rolled(value, shift):
    shift = shift % LANES
    return pltpu.roll(value, shift, 1) if shift else value


def lane_index(rows):
    return lax.broadcasted_iota(jnp.int32, (rows, LANES), 1)


def ordered(parity, near_ref, far_ref):
    even = jnp.broadcast_to(parity, near_ref.shape) != 0
    near, far = near_ref[...].astype(jnp.float32), far_ref[...].astype(jnp.float32)
    return jnp.where(even, far, near), jnp.where(even, near, far)


def joined(center, before, after):
    wide = center.shape[0]
    near = PAD - MARGIN
    overlap = STRIP - near
    return jnp.concatenate(
        [
            before[:near],
            center[:overlap] + before[near:],
            center[overlap : wide - overlap],
            center[wide - overlap :] + after[:overlap],
            after[overlap:],
        ],
        axis=0,
    )


def extended_rows(parity, grid_ref, near_ref, far_ref, cells_y):
    items = grid_ref.shape[0]
    groups = -(-items // EDGE_PER)
    size = groups * STRIP
    before, after = ordered(parity, near_ref, far_ref)
    packed = jnp.concatenate([before[items * STRIP :], after[items * STRIP :]], axis=0)
    lane = lane_index(2 * size)
    kept = (lane < MARGIN) | (lane >= LANES - MARGIN)
    edges = [jnp.where(kept, rolled(packed, -SPAN * slot), 0.0) for slot in range(EDGE_PER)]
    for k in range(items):
        place = slice(k * STRIP, (k + 1) * STRIP)
        inner = joined(grid_ref[k, :, :cells_y], before[place], after[place])
        start = k // EDGE_PER * STRIP
        edge = edges[k % EDGE_PER]
        edge = joined(
            grid_ref[k, :, cells_y:],
            edge[start : start + STRIP],
            edge[size + start : size + start + STRIP],
        )
        yield k, inner, edge


def pack_kernel(shape, parity_ref, grid_ref, far_x, near_x, far_ref, near_ref):
    cells_x, cells_y, _, _ = shape
    items = grid_ref.shape[0]
    groups = -(-items // EDGE_PER)
    rows = cells_x + 2 * PAD
    lane = lane_index(rows)
    up_halo = (lane >= LANES - REACH) & (lane < LANES - MARGIN)
    down_halo = (lane >= MARGIN) & (lane < REACH)
    halos, ups, downs = None, None, None
    packed = [[], []]
    for k, inner, edge in extended_rows(parity_ref[0:1], grid_ref, near_x, far_x, cells_y):
        slot = k % EDGE_PER
        up = rolled(jnp.where(lane >= LANES - MARGIN, inner, edge), SPAN * slot)
        down = rolled(jnp.where(lane < MARGIN, inner, edge), SPAN * slot)
        halo = rolled(jnp.where(up_halo | down_halo, inner, 0.0), REACH + HALO * k)
        ups = ups + up if slot else up
        downs = downs + down if slot else down
        halos = halos + halo if k else halo
        if slot == EDGE_PER - 1 or k == items - 1:
            packed[0].append(squeezed(ups))
            packed[1].append(squeezed(downs))
    halos = squeezed(halos)
    rows = halos.shape[0]
    used = lane_index(rows) < HALO * items
    ups = jnp.where(used, halos, 0.0)
    downs = jnp.where(used, rolled(halos, -MARGIN - REACH), 0.0)
    folded = None
    for row in range(0, rows, SPAN):
        size = min(SPAN, rows - row)
        parts = [value[row : row + size] for value in (ups, downs)]
        if size < SPAN:
            parts = [jnp.concatenate([p, jnp.zeros((SPAN - size, LANES), p.dtype)], 0) for p in parts]
        part = rolled(jnp.concatenate(parts, axis=0), row)
        folded = folded + part if row else part
    up = jnp.concatenate(packed[0] + [folded[:SPAN]], axis=0)
    down = jnp.concatenate(packed[1] + [folded[SPAN:]], axis=0)
    even = jnp.broadcast_to(parity_ref[1:2], up.shape) != 0
    near_ref[...] = jnp.where(even, up, down).astype(jnp.bfloat16)
    far_ref[...] = jnp.where(even, down, up).astype(jnp.bfloat16)


def squeezed(value):
    row = lax.broadcasted_iota(jnp.int32, (ROWS, LANES), 0)
    shared = jnp.where(row >= PAD - REACH, value[:ROWS], value[-ROWS:])
    return jnp.concatenate([shared, value[ROWS:-ROWS]], axis=0)


def expanded(value):
    return jnp.concatenate([value, value[:ROWS]], axis=0)


def around(ref, k, start, size):
    center = ref[k, pl.ds(start, size)]
    back = ref[k, pl.ds(start - 1, size)]
    fore = ref[k, pl.ds(start + 1, size)]
    return center, back, fore, rolled(center, 1), rolled(center, -1)


def tiles(count, body):
    def step(index, carry):
        body(index)
        return carry

    lax.fori_loop(0, count, step, 0)


def tile_start(index, size=ROWS):
    return pl.multiple_of(index * size, size)


def sweep(ref, carried_ref, levels, comps, start, size):
    scale = 1.0 / (1.0 + 6.0 * VISCOUS)
    centers, results = [], []
    for k in range(levels * comps):
        center, back, fore, below, above = around(ref, k, start, size)
        centers.append(center)
        results.append(back + fore + below + above)
    for k in range(levels * comps):
        higher = min(k // comps + 1, levels - 1) * comps + k % comps
        lower = max(k // comps - 1, 0) * comps + k % comps
        summed = results[k] + centers[higher] + centers[lower]
        source = carried_ref[k, pl.ds(start, size)]
        results[k] = scale * source + (VISCOUS * scale) * summed
    return results


def first_steps(moved_ref, carried_ref, sweep_ref, levels, comps, rows):
    def advect(index):
        start = ROWS + tile_start(index)
        for l in range(levels):
            pieces = [around(moved_ref, l * comps + c, start, ROWS) for c in range(comps)]
            speed_x, speed_y = COURANT * pieces[0][0], COURANT * pieces[1][0]
            ahead_x, astern_x = jnp.maximum(speed_x, 0.0), jnp.minimum(speed_x, 0.0)
            ahead_y, astern_y = jnp.maximum(speed_y, 0.0), jnp.minimum(speed_y, 0.0)
            for c in range(comps):
                center, back, fore, below, above = pieces[c]
                change = ahead_x * (center - back) + astern_x * (fore - center)
                change = change + ahead_y * (center - below) + astern_y * (above - center)
                carried_ref[l * comps + c, pl.ds(start, ROWS)] = center - change

    def first_sweep(index):
        start = ROWS + tile_start(index)
        results = sweep(carried_ref, carried_ref, levels, comps, start, ROWS)
        for k in range(levels * comps):
            sweep_ref[k, pl.ds(start, ROWS)] = results[k]

    tiles(rows // ROWS, advect)
    tiles(rows // ROWS, first_sweep)


RIM = REACH + HALO
HALF = LANES // 2


def weight_kernel(
    shape, chunk, parity_ref, quarter_ref, value_ref, level_ref, inner_ref, rim_ref, parity_out
):
    parity_out[...] = parity_ref[...]
    _, cells_y, _, _ = shape
    slots = quarter_ref.shape[1]
    size = 2 * ROWS
    levels = inner_ref.shape[0] // LANES
    row = lax.broadcasted_iota(jnp.int32, (size, chunk), 0)

    def cut(tile, keep):
        return jnp.where(keep, tile.astype(jnp.float32), 0.0).astype(jnp.bfloat16)

    for first in range(0, slots, chunk):
        lanes = slice(first, first + chunk)
        level = level_ref[:, lanes]
        for l in range(levels):
            value = jnp.where(level == l, value_ref[:, lanes], 0.0)
            quarter, value = doubled(quarter_ref[:, lanes], value)
            for start in range(0, LANES, size):
                inner = picked_tile(quarter, value, start)
                if start < REACH:
                    inner = cut(inner, row + start >= REACH)
                if start + size > cells_y - REACH:
                    inner = cut(inner, row + start < cells_y - REACH)
                if start >= LANES - MARGIN:
                    rim = picked_tile(quarter, value, start - LANES)
                elif start + size > HALF - REACH and start < HALF + MARGIN:
                    rim = picked_tile(quarter, value, start + cells_y - HALF)
                    rim = cut(rim, row + start >= HALF - REACH) if start < HALF - REACH else rim
                elif start < REACH:
                    rim = picked_tile(quarter, value, start)
                    rim = cut(rim, row + start < REACH) if start + size > REACH else rim
                else:
                    rim = jnp.zeros_like(value)
                place = slice(l * LANES + start, l * LANES + start + size)
                inner_ref[place, lanes] = inner
                rim_ref[place, lanes] = rim


def sampled_part(round_ref, weight_ref, quarter_ref, value_ref, lanes, comps):
    wide_x = round_ref.shape[0] // comps
    partial = jnp.dot(round_ref[...], weight_ref[:, lanes], preferred_element_type=jnp.float32)
    quarter, value = quarter_ref[:, lanes], value_ref[:, lanes]
    totals = [jnp.zeros_like(value)] * comps
    for row in range(0, wide_x, ROWS):
        here = quarter == (MARGIN - row) // 4
        for c in range(comps):
            start = c * wide_x + row
            totals[c] = jnp.where(here, partial[start : start + ROWS], totals[c])
    return [jnp.sum(total * value, axis=0, keepdims=True) for total in totals]


def inner_kernel(
    shape, chunk, levels, parity_ref, quarter_ref, value_ref, weight_ref, grid_ref, far_x, near_x,
    inner_ref, rim_ref, sampled_ref, moved_ref, carried_ref, sweep_ref, round_ref,
):
    cells_x, cells_y, _, _ = shape
    items = grid_ref.shape[0]
    comps = items // levels
    slots = quarter_ref.shape[1]
    wide_x = cells_x + SPAN
    rows = cells_x + 2 * PAD
    lane = lane_index(rows)
    for k, inner, edge in extended_rows(parity_ref[0:1], grid_ref, near_x, far_x, cells_y):
        moved_ref[k, ROWS : ROWS + rows] = inner
        low = jnp.where(lane < RIM, inner, jnp.where(lane >= LANES - MARGIN, edge, 0.0))
        high = jnp.where(lane >= LANES - RIM, inner, jnp.where(lane < MARGIN, edge, 0.0))
        rim_ref[k] = low + rolled(high, HALF)
    first_steps(moved_ref, carried_ref, sweep_ref, levels, comps, rows)
    size = 2 * ROWS
    for row in range(0, wide_x, size):
        start = ROWS + PAD - MARGIN + row
        results = sweep(sweep_ref, carried_ref, levels, comps, start, size)
        for k in range(items):
            level, c = k // comps, k % comps
            place = slice(c * wide_x + row, c * wide_x + row + size)
            round_ref[place, level * LANES : (level + 1) * LANES] = results[k].astype(jnp.bfloat16)
            if MARGIN <= row < MARGIN + cells_x:
                inner_ref[k, row - MARGIN : row - MARGIN + size] = results[k]
    for first in range(0, slots, chunk):
        lanes = slice(first, first + chunk)
        parts = sampled_part(round_ref, weight_ref, quarter_ref, value_ref, lanes, comps)
        for c in range(comps):
            sampled_ref[c : c + 1, lanes] = parts[c]


def unfolded(folded, rows):
    return expanded(
        jnp.concatenate(
            [rolled(folded, -row)[: min(SPAN, rows - row)] for row in range(0, rows, SPAN)], axis=0
        )
    )


def finish_kernel(
    shape, chunk, parity_ref, quarter_ref, value_ref, weight_ref, inner_ref, rim_ref, part_ref,
    far_y, near_y, next_ref, sampled_ref, moved_ref, carried_ref, sweep_ref, round_ref,
):
    cells_x, cells_y, _, _ = shape
    items = rim_ref.shape[0]
    groups = -(-items // EDGE_PER)
    levels, comps = next_ref.shape[:2]
    slots = quarter_ref.shape[1]
    wide_x = cells_x + SPAN
    rows = cells_x + 2 * PAD
    lane = lane_index(rows)
    befores, afters = ordered(parity_ref[1:2], near_y, far_y)
    turned = HALF + MARGIN + REACH
    high_halo = (lane >= turned) & (lane < turned + HALO * items)
    both = ((lane + MARGIN) & (HALF - 1)) < SPAN
    outer = ((lane >= LANES - REACH) & (lane < LANES - MARGIN)) | (
        (lane >= HALF + MARGIN) & (lane < HALF + REACH)
    )
    size = rows - ROWS
    halo = jnp.where(
        high_halo,
        rolled(unfolded(afters[groups * size :], size), turned),
        unfolded(befores[groups * size :], size),
    )
    for group in range(groups):
        before = expanded(befores[group * size : (group + 1) * size])
        after = expanded(rolled(afters[group * size : (group + 1) * size], HALF))
        for k in range(group * EDGE_PER, min((group + 1) * EDGE_PER, items)):
            slot = k % EDGE_PER
            window = ((lane + (LANES + MARGIN - SPAN * slot)) & (LANES - 1)) < SPAN
            main = rolled(jnp.where(window, before, after), -SPAN * slot)
            value = rim_ref[k] + jnp.where(both, main, 0.0)
            value = jnp.where(outer, rolled(halo, -REACH - HALO * k), value)
            moved_ref[k, ROWS : ROWS + rows] = value

    first_steps(moved_ref, carried_ref, sweep_ref, levels, comps, rows)
    size = 2 * ROWS
    lane = lane_index(size)
    for row in range(0, wide_x, size):
        start = ROWS + PAD - MARGIN + row
        results = sweep(sweep_ref, carried_ref, levels, comps, start, size)
        for k in range(items):
            level, c = k // comps, k % comps
            place = slice(c * wide_x + row, c * wide_x + row + size)
            round_ref[place, level * LANES : (level + 1) * LANES] = results[k].astype(jnp.bfloat16)
        if not MARGIN <= row < MARGIN + cells_x:
            continue
        place = slice(row - MARGIN, row - MARGIN + size)
        for k in range(items):
            low, high = results[k], rolled(results[k], HALF)
            inner = inner_ref[k, place]
            inner = jnp.where(lane < REACH, low, jnp.where(lane >= LANES - REACH, high, inner))
            next_ref[k // comps, k % comps, place] = inner

    for first in range(0, slots, chunk):
        lanes = slice(first, first + chunk)
        parts = sampled_part(round_ref, weight_ref, quarter_ref, value_ref, lanes, comps)
        for c in range(comps):
            sampled_ref[c, 0, :, lanes] = part_ref[c : c + 1, lanes] + parts[c]


def whole(count):
    return [pl.BlockSpec(memory_space=pltpu.VMEM)] * count


def swap_pairs(axis):
    size = lax.axis_size(axis)
    if size % 2:
        raise ValueError("odd axis")
    far_pairs = [(i, (i - 1 if i % 2 == 0 else i + 1) % size) for i in range(size)]
    return far_pairs, [(i, i ^ 1) for i in range(size)]


def body(velocity, marker_cell, marker_frac, marker_force, fish_owner):
    levels, comps, cells_x, cells_y = velocity.shape
    slots = marker_cell.shape[3]
    items = levels * comps
    shape = (cells_x, cells_y, cells_x * lax.axis_size("gx"), cells_y * lax.axis_size("gy"))
    wide_x = cells_x + SPAN
    rows = cells_x + 2 * PAD
    chunk = min(512, slots)
    width = cells_y + LANES
    groups = -(-items // EDGE_PER)
    params = pltpu.CompilerParams(vmem_limit_bytes=32 * 1024 * 1024)
    edge_x = jax.ShapeDtypeStruct(((items + groups) * STRIP, LANES), jnp.bfloat16)
    half = (items, wide_x // 2, width)
    arrays = (fish_owner, velocity, marker_cell, marker_frac, marker_force)
    far_half, far, force, dense_y, quarter, value, quarter_y, value_y, level, parity, near_velocity = (
        pl.pallas_call(
        functools.partial(far_kernel, shape, slots),
        out_shape=(
            jax.ShapeDtypeStruct(half, jnp.float32),
            edge_x,
            jax.ShapeDtypeStruct((items, 2 * ROWS, slots), jnp.bfloat16),
            jax.ShapeDtypeStruct((width, slots), jnp.bfloat16),
            jax.ShapeDtypeStruct((ROWS, slots), jnp.int32),
            jax.ShapeDtypeStruct((ROWS, slots), jnp.float32),
            jax.ShapeDtypeStruct((ROWS, slots), jnp.int32),
            jax.ShapeDtypeStruct((ROWS, slots), jnp.float32),
            jax.ShapeDtypeStruct((1, slots), jnp.int32),
            jax.ShapeDtypeStruct((2, LANES), jnp.int32),
            jax.ShapeDtypeStruct(velocity.shape, velocity.dtype),
        ),
        in_specs=[pl.BlockSpec(memory_space=pltpu.HBM)] * 5,
        out_specs=tuple(whole(11)),
        scratch_shapes=[pltpu.VMEM(a.shape, a.dtype) for a in arrays if a is not velocity]
        + [pltpu.SemaphoreType.DMA((5,))],
        compiler_params=params,
        name="spread_far",
    )(*(pltpu.with_memory_space_constraint(a, pltpu.HBM) for a in arrays))
    )
    far_pairs, near_pairs = swap_pairs("gx")
    far_x = lax.ppermute(far, "gx", far_pairs)
    grid, near = pl.pallas_call(
        functools.partial(near_kernel, shape, slots),
        out_shape=(jax.ShapeDtypeStruct((items, wide_x, width), jnp.float32), edge_x),
        in_specs=whole(5),
        out_specs=tuple(whole(2)),
        scratch_shapes=[pltpu.VMEM(half, jnp.float32)],
        compiler_params=params,
        cost_estimate=pl.CostEstimate(
            flops=items * wide_x * width * slots, bytes_accessed=4 * items * wide_x * width,
            transcendentals=0,
        ),
        name="spread_near",
    )(near_velocity, far_half, force, dense_y, quarter)
    near_x = lax.ppermute(near, "gx", near_pairs)
    weights = jax.ShapeDtypeStruct((levels * LANES, slots), jnp.bfloat16)
    inner_weight, rim_weight, parity = pl.pallas_call(
        functools.partial(weight_kernel, shape, chunk),
        out_shape=(weights, weights, jax.ShapeDtypeStruct(parity.shape, parity.dtype)),
        in_specs=whole(4),
        out_specs=tuple(whole(3)),
        compiler_params=params,
        cost_estimate=pl.CostEstimate(
            flops=2 * levels * LANES * slots, bytes_accessed=4 * levels * LANES * slots,
            transcendentals=0,
        ),
        name="weights",
    )(parity, quarter_y, value_y, level)
    edge_y = jax.ShapeDtypeStruct((groups * (rows - ROWS) + SPAN, LANES), jnp.bfloat16)
    far, near = pl.pallas_call(
        functools.partial(pack_kernel, shape),
        out_shape=(edge_y, edge_y),
        in_specs=whole(4),
        out_specs=tuple(whole(2)),
        compiler_params=params,
        name="pack",
    )(parity, grid, far_x, near_x)
    far_pairs, near_pairs = swap_pairs("gy")
    far_y = lax.ppermute(far, "gy", far_pairs)
    near_y = lax.ppermute(near, "gy", near_pairs)
    field = pltpu.VMEM((items, rows + 2 * ROWS, LANES), jnp.float32)
    rounded = pltpu.VMEM((comps * wide_x, levels * LANES), jnp.bfloat16)
    inner, rim, part = pl.pallas_call(
        functools.partial(inner_kernel, shape, chunk, levels),
        out_shape=(
            jax.ShapeDtypeStruct((items, cells_x, LANES), jnp.float32),
            jax.ShapeDtypeStruct((items, rows, LANES), jnp.float32),
            jax.ShapeDtypeStruct((comps, slots), jnp.float32),
        ),
        in_specs=whole(7),
        out_specs=tuple(whole(3)),
        scratch_shapes=[field, field, field, rounded],
        compiler_params=params,
        cost_estimate=pl.CostEstimate(
            flops=2 * items * wide_x * LANES * slots, bytes_accessed=16 * items * rows * LANES,
            transcendentals=0,
        ),
        name="inner",
    )(parity, quarter, value, inner_weight, grid, far_x, near_x)
    return pl.pallas_call(
        functools.partial(finish_kernel, shape, chunk),
        out_shape=(
            jax.ShapeDtypeStruct(velocity.shape, jnp.float32),
            jax.ShapeDtypeStruct((comps, 1, 1, slots), jnp.float32),
        ),
        in_specs=whole(9),
        out_specs=tuple(whole(2)),
        scratch_shapes=[field, field, field, rounded],
        compiler_params=params,
        name="finish",
    )(parity, quarter, value, rim_weight, inner, rim, part, far_y, near_y)


def solution(mesh):
    placed = (
        P(None, None, "gx", "gy"),
        P(None, "gx", "gy", None),
        P(None, "gx", "gy", None),
        P(None, "gx", "gy", None),
        P(),
    )
    return jax.shard_map(
        body,
        mesh=mesh,
        in_specs=placed,
        out_specs=(P(None, None, "gx", "gy"), P(None, "gx", "gy", None)),
        check_vma=False,
    )
```

```python
import functools

import jax
import jax.numpy as jnp
import numpy as np
from jax import lax
from jax.experimental import pallas as pl
from jax.experimental.pallas import tpu as pltpu
from jax.sharding import PartitionSpec as P

MARGIN = 16
FISH_MARK = 1024
HALO = 3
LANES = 128
COURANT = 0.25
VISCOUS = 1.5
ROWS = 8
STEP = 2 * ROWS

REACH = MARGIN + HALO
PAD = -(-REACH // ROWS) * ROWS
STRIP = PAD + MARGIN
SPAN = 2 * MARGIN
EDGE_PER = LANES // SPAN


def half_turn(terms):
    nodes = 0.5 - 0.5 * np.cos(np.pi * (np.arange(64) + 0.5) / 64)
    square = nodes * nodes
    cosine = np.polynomial.polynomial.polyfit(square, np.cos(0.5 * np.pi * nodes), terms)
    sine = np.polynomial.polynomial.polyfit(square, np.sin(0.5 * np.pi * nodes) / nodes, terms)
    return [float(v) for v in cosine], [float(v) for v in sine]


COS_FIT, SIN_FIT = half_turn(6)


def horner(coefficients, value):
    total = jnp.full_like(value, coefficients[-1])
    for coefficient in coefficients[-2::-1]:
        total = total * value + coefficient
    return total


def four_weights(frac):
    square = frac * frac
    cosine = horner(COS_FIT, square)
    sine = frac * horner(SIN_FIT, square)
    return (0.25 - 0.25 * sine, 0.25 + 0.25 * cosine, 0.25 + 0.25 * sine, 0.25 - 0.25 * cosine)


def local_cell(cell, low, extent):
    offset = cell - low
    offset = jnp.where(offset < -MARGIN, offset + extent, offset)
    return jnp.where(offset >= extent - MARGIN, offset - extent, offset)


def position():
    row, col = lax.axis_index("gx"), lax.axis_index("gy")
    return row, col, (row & 1) == 0, (col & 1) == 0


def tile_weights(offset, weights):
    shift = lax.broadcasted_iota(jnp.int32, (ROWS, offset.shape[1]), 0) + 1 - offset
    quarter, phase = shift >> 2, shift & 3
    value = jnp.where(phase == 3, weights[3], weights[2])
    value = jnp.where(phase == 1, weights[1], value)
    return quarter, jnp.where(phase == 0, weights[0], value)


def doubled(quarter, value):
    quarter = jnp.concatenate([quarter, quarter + 2], axis=0).astype(jnp.float32)
    return quarter.astype(jnp.bfloat16), twice(value)


def twice(value):
    return jnp.concatenate([value, value], axis=0).astype(jnp.bfloat16)


def picked_tile(quarter, value, first):
    zero = jnp.zeros_like(value)
    return jnp.where(quarter == jnp.array(-first // 4, quarter.dtype), value, zero)


def half_spread(quarter_ref, force_ref, dense_y_ref, half_ref, base, lanes):
    items, rows = half_ref.shape[:2]
    quarter = quarter_ref[:, lanes] + base
    quarter = jnp.concatenate([quarter, quarter + 2], axis=0).astype(jnp.float32)
    quarter = quarter.astype(jnp.bfloat16)
    left = jnp.concatenate(
        [
            picked_tile(quarter, force_ref[k, :, lanes], row)
            for k in range(items)
            for row in range(0, rows, 2 * ROWS)
        ],
        axis=0,
    )
    total = lax.dot_general(
        left, dense_y_ref[:, lanes], (((1,), (1,)), ((), ())),
        preferred_element_type=jnp.float32,
    )
    total = total.reshape(half_ref.shape)
    if lanes.start:
        half_ref[...] += total
    else:
        half_ref[...] = total


def finish_half(half_ref, velocity_ref, out_ref, low, cells_y):
    items, rows = half_ref.shape[:2]
    comps = items // velocity_ref.shape[0]
    count = rows - MARGIN
    source = pl.ds(pl.multiple_of(jnp.where(low, 0, count), ROWS), count)
    target = pl.ds(pl.multiple_of(jnp.where(low, MARGIN, 0), ROWS), count)
    for k in range(items):
        half_ref[k, target, :cells_y] += velocity_ref[k // comps, k % comps, source]
    place = pl.ds(pl.multiple_of(jnp.where(low, 0, rows - STRIP), ROWS), STRIP)
    parts = [half_ref[k, place, :cells_y] for k in range(items)]
    for group in range(0, items, EDGE_PER):
        edges = []
        for k in range(group, min(group + EDGE_PER, items)):
            edges.append(rolled(half_ref[k, place, cells_y:], SPAN * (k - group)))
        parts.append(functools.reduce(jnp.add, edges))
    out_ref[...] = jnp.concatenate(parts, axis=0).astype(jnp.bfloat16)


def far_kernel(
    shape, chunk, fish_hbm, velocity_hbm, cell_hbm, frac_hbm, force_hbm,
    half_ref, far_ref, force_out, dense_y_ref, quarter_ref, value_ref,
    quarter_y_ref, value_y_ref, level_ref, parity_ref, velocity_ref,
    fish_ref, cell_ref, frac_ref, force_ref, sems,
):
    pairs = (
        (cell_hbm, cell_ref), (frac_hbm, frac_ref), (fish_hbm, fish_ref),
        (force_hbm, force_ref), (velocity_hbm, velocity_ref),
    )
    copies = [pltpu.make_async_copy(a, b, sems.at[i]) for i, (a, b) in enumerate(pairs)]
    for copy in copies:
        copy.start()
    cells_x, cells_y, extent_x, extent_y = shape
    levels, comps = velocity_ref.shape[:2]
    slots = cell_ref.shape[3]
    row, col, even, even_y = position()
    parity_ref[0:1] = jnp.full((1, LANES), jnp.where(even, 1, 0), jnp.int32)
    parity_ref[1:2] = jnp.full((1, LANES), jnp.where(even_y, 1, 0), jnp.int32)
    base = jnp.where(even, -MARGIN // 4, cells_x // 8)
    for copy in copies[:-1]:
        copy.wait()
    mine = jnp.where(fish_ref[...] == row * lax.axis_size("gy") + col, 1.0, 0.0)
    count = FISH_MARK * jnp.sum(mine)
    level_ref[...] = cell_ref[2, 0]
    for first in range(0, slots, chunk):
        lanes = slice(first, first + chunk)
        offset_x = local_cell(cell_ref[0, 0, :, lanes], row * cells_x, extent_x)
        offset_y = local_cell(cell_ref[1, 0, :, lanes], col * cells_y, extent_y)
        slot = lax.broadcasted_iota(jnp.int32, (1, chunk), 1) + first
        alive = jnp.where(slot.astype(jnp.float32) < count, 1.0, 0.0)
        quarter, value = tile_weights(offset_x, four_weights(frac_ref[0, 0, :, lanes]))
        value = value * alive
        quarter_ref[:, lanes] = quarter
        value_ref[:, lanes] = value
        level = cell_ref[2, 0, :, lanes]
        pushes = [force_ref[c, 0, :, lanes] * value for c in range(comps)]
        for l in range(levels):
            for c in range(comps):
                force_out[l * comps + c, :, lanes] = twice(jnp.where(level == l, pushes[c], 0.0))
        quarter, value = tile_weights(offset_y, four_weights(frac_ref[1, 0, :, lanes]))
        quarter_y_ref[:, lanes] = quarter
        value_y_ref[:, lanes] = value
        quarter, value = doubled(quarter, value)
        dense_y_ref[:, lanes] = jnp.concatenate(
            [picked_tile(quarter, value, n) for n in range(0, cells_y + MARGIN, 2 * ROWS)]
            + [jnp.zeros((LANES - SPAN, chunk), jnp.bfloat16)]
            + [picked_tile(quarter, value, n) for n in range(-MARGIN, 0, 2 * ROWS)],
            axis=0,
        )
        half_spread(quarter_ref, force_out, dense_y_ref, half_ref, base, lanes)
    copies[-1].wait()
    finish_half(half_ref, velocity_ref, far_ref, even, cells_y)


def near_kernel(
    shape, chunk, velocity_ref, far_half_ref, force_ref, dense_y_ref, quarter_ref,
    grid_ref, near_ref, half_ref,
):
    cells_x, cells_y, _, _ = shape
    slots = quarter_ref.shape[1]
    rows = half_ref.shape[1]
    _, _, even, _ = position()
    base = jnp.where(even, cells_x // 8, -MARGIN // 4)
    for first in range(0, slots, chunk):
        lanes = slice(first, first + chunk)
        half_spread(quarter_ref, force_ref, dense_y_ref, half_ref, base, lanes)
    finish_half(half_ref, velocity_ref, near_ref, jnp.logical_not(even), cells_y)
    for ref, row in ((far_half_ref, jnp.where(even, 0, rows)), (half_ref, jnp.where(even, rows, 0))):
        place = pl.ds(pl.multiple_of(row, ROWS), rows)
        for k in range(ref.shape[0]):
            grid_ref[k, place] = ref[k]


def rolled(value, shift):
    shift = shift % LANES
    return pltpu.roll(value, shift, 1) if shift else value


def lane_index(rows):
    return lax.broadcasted_iota(jnp.int32, (rows, LANES), 1)


def ordered(parity, near_ref, far_ref):
    even = jnp.broadcast_to(parity, near_ref.shape) != 0
    near, far = near_ref[...].astype(jnp.float32), far_ref[...].astype(jnp.float32)
    return jnp.where(even, far, near), jnp.where(even, near, far)


def joined(center, before, after):
    wide = center.shape[0]
    near = PAD - MARGIN
    overlap = STRIP - near
    return jnp.concatenate(
        [
            before[:near],
            center[:overlap] + before[near:],
            center[overlap : wide - overlap],
            center[wide - overlap :] + after[:overlap],
            after[overlap:],
        ],
        axis=0,
    )


def extended_rows(parity, grid_ref, near_ref, far_ref, cells_y):
    items = grid_ref.shape[0]
    groups = -(-items // EDGE_PER)
    size = groups * STRIP
    before, after = ordered(parity, near_ref, far_ref)
    packed = jnp.concatenate([before[items * STRIP :], after[items * STRIP :]], axis=0)
    lane = lane_index(2 * size)
    kept = (lane < MARGIN) | (lane >= LANES - MARGIN)
    edges = [jnp.where(kept, rolled(packed, -SPAN * slot), 0.0) for slot in range(EDGE_PER)]
    for k in range(items):
        place = slice(k * STRIP, (k + 1) * STRIP)
        inner = joined(grid_ref[k, :, :cells_y], before[place], after[place])
        start = k // EDGE_PER * STRIP
        edge = edges[k % EDGE_PER]
        edge = joined(
            grid_ref[k, :, cells_y:],
            edge[start : start + STRIP],
            edge[size + start : size + start + STRIP],
        )
        yield k, inner, edge


def pack_kernel(shape, parity_ref, grid_ref, far_x, near_x, far_ref, near_ref):
    cells_x, cells_y, _, _ = shape
    items = grid_ref.shape[0]
    groups = -(-items // EDGE_PER)
    rows = cells_x + 2 * PAD
    lane = lane_index(rows)
    up_halo = (lane >= LANES - REACH) & (lane < LANES - MARGIN)
    down_halo = (lane >= MARGIN) & (lane < REACH)
    halos, ups, downs = None, None, None
    packed = [[], []]
    for k, inner, edge in extended_rows(parity_ref[0:1], grid_ref, near_x, far_x, cells_y):
        slot = k % EDGE_PER
        up = rolled(jnp.where(lane >= LANES - MARGIN, inner, edge), SPAN * slot)
        down = rolled(jnp.where(lane < MARGIN, inner, edge), SPAN * slot)
        halo = rolled(jnp.where(up_halo | down_halo, inner, 0.0), REACH + HALO * k)
        ups = ups + up if slot else up
        downs = downs + down if slot else down
        halos = halos + halo if k else halo
        if slot == EDGE_PER - 1 or k == items - 1:
            packed[0].append(squeezed(ups))
            packed[1].append(squeezed(downs))
    halos = squeezed(halos)
    rows = halos.shape[0]
    used = lane_index(rows) < HALO * items
    ups = jnp.where(used, halos, 0.0)
    downs = jnp.where(used, rolled(halos, -MARGIN - REACH), 0.0)
    folded = None
    for row in range(0, rows, SPAN):
        size = min(SPAN, rows - row)
        parts = [value[row : row + size] for value in (ups, downs)]
        if size < SPAN:
            parts = [jnp.concatenate([p, jnp.zeros((SPAN - size, LANES), p.dtype)], 0) for p in parts]
        part = rolled(jnp.concatenate(parts, axis=0), row)
        folded = folded + part if row else part
    up = jnp.concatenate(packed[0] + [folded[:SPAN]], axis=0)
    down = jnp.concatenate(packed[1] + [folded[SPAN:]], axis=0)
    even = jnp.broadcast_to(parity_ref[1:2], up.shape) != 0
    near_ref[...] = jnp.where(even, up, down).astype(jnp.bfloat16)
    far_ref[...] = jnp.where(even, down, up).astype(jnp.bfloat16)


def squeezed(value):
    row = lax.broadcasted_iota(jnp.int32, (ROWS, LANES), 0)
    shared = jnp.where(row >= PAD - REACH, value[:ROWS], value[-ROWS:])
    return jnp.concatenate([shared, value[ROWS:-ROWS]], axis=0)


def expanded(value):
    return jnp.concatenate([value, value[:ROWS]], axis=0)


def around(ref, k, start, size):
    center = ref[k, start : start + size]
    back = ref[k, start - 1 : start - 1 + size]
    fore = ref[k, start + 1 : start + 1 + size]
    return center, back, fore, rolled(center, 1), rolled(center, -1)


def advect(moved_ref, carried_ref, levels, comps, rows):
    for start in range(ROWS, ROWS + rows, STEP):
        for l in range(levels):
            pieces = [around(moved_ref, l * comps + c, start, STEP) for c in range(comps)]
            speed_x, speed_y = COURANT * pieces[0][0], COURANT * pieces[1][0]
            ahead_x, astern_x = jnp.maximum(speed_x, 0.0), jnp.minimum(speed_x, 0.0)
            ahead_y, astern_y = jnp.maximum(speed_y, 0.0), jnp.minimum(speed_y, 0.0)
            for c in range(comps):
                center, back, fore, below, above = pieces[c]
                change = ahead_x * (center - back) + astern_x * (fore - center)
                change = change + ahead_y * (center - below) + astern_y * (above - center)
                carried_ref[l * comps + c, start : start + STEP] = center - change


def sweep(ref, carried_ref, levels, comps, start, size):
    scale = 1.0 / (1.0 + 6.0 * VISCOUS)
    centers, results = [], []
    for k in range(levels * comps):
        center, back, fore, below, above = around(ref, k, start, size)
        centers.append(center)
        results.append(back + fore + below + above)
    for k in range(levels * comps):
        higher = min(k // comps + 1, levels - 1) * comps + k % comps
        lower = max(k // comps - 1, 0) * comps + k % comps
        summed = results[k] + centers[higher] + centers[lower]
        source = carried_ref[k, start : start + size]
        results[k] = scale * source + (VISCOUS * scale) * summed
    return results


def first_steps(moved_ref, carried_ref, sweep_ref, levels, comps, rows):
    advect(moved_ref, carried_ref, levels, comps, rows)
    for start in range(ROWS, ROWS + rows, STEP):
        results = sweep(carried_ref, carried_ref, levels, comps, start, STEP)
        for k in range(levels * comps):
            sweep_ref[k, start : start + STEP] = results[k]


RIM = REACH + HALO
HALF = LANES // 2


def weight_kernel(
    shape, chunk, parity_ref, quarter_ref, value_ref, level_ref, inner_ref, rim_ref, parity_out
):
    parity_out[...] = parity_ref[...]
    _, cells_y, _, _ = shape
    slots = quarter_ref.shape[1]
    size = 2 * ROWS
    levels = inner_ref.shape[0] // LANES
    row = lax.broadcasted_iota(jnp.int32, (size, chunk), 0)

    def cut(tile, keep):
        return jnp.where(keep, tile.astype(jnp.float32), 0.0).astype(jnp.bfloat16)

    for first in range(0, slots, chunk):
        lanes = slice(first, first + chunk)
        level = level_ref[:, lanes]
        for l in range(levels):
            value = jnp.where(level == l, value_ref[:, lanes], 0.0)
            quarter, value = doubled(quarter_ref[:, lanes], value)
            for start in range(0, LANES, size):
                inner = picked_tile(quarter, value, start)
                if start < REACH:
                    inner = cut(inner, row + start >= REACH)
                if start + size > cells_y - REACH:
                    inner = cut(inner, row + start < cells_y - REACH)
                if start >= LANES - MARGIN:
                    rim = picked_tile(quarter, value, start - LANES)
                elif start + size > HALF - REACH and start < HALF + MARGIN:
                    rim = picked_tile(quarter, value, start + cells_y - HALF)
                    rim = cut(rim, row + start >= HALF - REACH) if start < HALF - REACH else rim
                elif start < REACH:
                    rim = picked_tile(quarter, value, start)
                    rim = cut(rim, row + start < REACH) if start + size > REACH else rim
                else:
                    rim = jnp.zeros_like(value)
                place = slice(l * LANES + start, l * LANES + start + size)
                inner_ref[place, lanes] = inner
                rim_ref[place, lanes] = rim


def sampled_part(round_ref, weight_ref, quarter_ref, value_ref, lanes, comps):
    wide_x = round_ref.shape[0] // comps
    partial = jnp.dot(round_ref[...], weight_ref[:, lanes], preferred_element_type=jnp.float32)
    quarter, value = quarter_ref[:, lanes], value_ref[:, lanes]
    totals = [jnp.zeros_like(value)] * comps
    for row in range(0, wide_x, ROWS):
        here = quarter == (MARGIN - row) // 4
        for c in range(comps):
            start = c * wide_x + row
            totals[c] = jnp.where(here, partial[start : start + ROWS], totals[c])
    return [jnp.sum(total * value, axis=0, keepdims=True) for total in totals]


def inner_kernel(
    shape, chunk, levels, parity_ref, quarter_ref, value_ref, weight_ref, grid_ref, far_x, near_x,
    inner_ref, rim_ref, sampled_ref, moved_ref, carried_ref, sweep_ref, round_ref,
):
    cells_x, cells_y, _, _ = shape
    items = grid_ref.shape[0]
    comps = items // levels
    slots = quarter_ref.shape[1]
    wide_x = cells_x + SPAN
    rows = cells_x + 2 * PAD
    lane = lane_index(rows)
    for k, inner, edge in extended_rows(parity_ref[0:1], grid_ref, near_x, far_x, cells_y):
        moved_ref[k, ROWS : ROWS + rows] = inner
        low = jnp.where(lane < RIM, inner, jnp.where(lane >= LANES - MARGIN, edge, 0.0))
        high = jnp.where(lane >= LANES - RIM, inner, jnp.where(lane < MARGIN, edge, 0.0))
        rim_ref[k] = low + rolled(high, HALF)
    first_steps(moved_ref, carried_ref, sweep_ref, levels, comps, rows)
    size = 2 * ROWS
    for row in range(0, wide_x, size):
        start = ROWS + PAD - MARGIN + row
        results = sweep(sweep_ref, carried_ref, levels, comps, start, size)
        for k in range(items):
            level, c = k // comps, k % comps
            place = slice(c * wide_x + row, c * wide_x + row + size)
            round_ref[place, level * LANES : (level + 1) * LANES] = results[k].astype(jnp.bfloat16)
            if MARGIN <= row < MARGIN + cells_x:
                inner_ref[k, row - MARGIN : row - MARGIN + size] = results[k]
    for first in range(0, slots, chunk):
        lanes = slice(first, first + chunk)
        parts = sampled_part(round_ref, weight_ref, quarter_ref, value_ref, lanes, comps)
        for c in range(comps):
            sampled_ref[c : c + 1, lanes] = parts[c]


def unfolded(folded, rows):
    return expanded(
        jnp.concatenate(
            [rolled(folded, -row)[: min(SPAN, rows - row)] for row in range(0, rows, SPAN)], axis=0
        )
    )


def finish_kernel(
    shape, chunk, parity_ref, quarter_ref, value_ref, weight_ref, inner_ref, rim_ref, part_ref,
    far_y, near_y, next_ref, sampled_ref, moved_ref, carried_ref, sweep_ref, round_ref,
):
    cells_x, cells_y, _, _ = shape
    items = rim_ref.shape[0]
    groups = -(-items // EDGE_PER)
    levels, comps = next_ref.shape[:2]
    slots = quarter_ref.shape[1]
    wide_x = cells_x + SPAN
    rows = cells_x + 2 * PAD
    lane = lane_index(rows)
    befores, afters = ordered(parity_ref[1:2], near_y, far_y)
    turned = HALF + MARGIN + REACH
    high_halo = (lane >= turned) & (lane < turned + HALO * items)
    both = ((lane + MARGIN) & (HALF - 1)) < SPAN
    outer = ((lane >= LANES - REACH) & (lane < LANES - MARGIN)) | (
        (lane >= HALF + MARGIN) & (lane < HALF + REACH)
    )
    size = rows - ROWS
    halo = jnp.where(
        high_halo,
        rolled(unfolded(afters[groups * size :], size), turned),
        unfolded(befores[groups * size :], size),
    )
    for group in range(groups):
        before = expanded(befores[group * size : (group + 1) * size])
        after = expanded(rolled(afters[group * size : (group + 1) * size], HALF))
        for k in range(group * EDGE_PER, min((group + 1) * EDGE_PER, items)):
            slot = k % EDGE_PER
            window = ((lane + (LANES + MARGIN - SPAN * slot)) & (LANES - 1)) < SPAN
            main = rolled(jnp.where(window, before, after), -SPAN * slot)
            value = rim_ref[k] + jnp.where(both, main, 0.0)
            value = jnp.where(outer, rolled(halo, -REACH - HALO * k), value)
            moved_ref[k, ROWS : ROWS + rows] = value

    first_steps(moved_ref, carried_ref, sweep_ref, levels, comps, rows)
    size = 2 * ROWS
    lane = lane_index(size)
    for row in range(0, wide_x, size):
        start = ROWS + PAD - MARGIN + row
        results = sweep(sweep_ref, carried_ref, levels, comps, start, size)
        for k in range(items):
            level, c = k // comps, k % comps
            place = slice(c * wide_x + row, c * wide_x + row + size)
            round_ref[place, level * LANES : (level + 1) * LANES] = results[k].astype(jnp.bfloat16)
        if not MARGIN <= row < MARGIN + cells_x:
            continue
        place = slice(row - MARGIN, row - MARGIN + size)
        for k in range(items):
            low, high = results[k], rolled(results[k], HALF)
            inner = inner_ref[k, place]
            inner = jnp.where(lane < REACH, low, jnp.where(lane >= LANES - REACH, high, inner))
            next_ref[k // comps, k % comps, place] = inner

    for first in range(0, slots, chunk):
        lanes = slice(first, first + chunk)
        parts = sampled_part(round_ref, weight_ref, quarter_ref, value_ref, lanes, comps)
        for c in range(comps):
            sampled_ref[c, 0, :, lanes] = part_ref[c : c + 1, lanes] + parts[c]


def whole(count):
    return [pl.BlockSpec(memory_space=pltpu.VMEM)] * count


def swap_pairs(axis):
    size = lax.axis_size(axis)
    if size % 2:
        raise ValueError("odd axis")
    far_pairs = [(i, (i - 1 if i % 2 == 0 else i + 1) % size) for i in range(size)]
    return far_pairs, [(i, i ^ 1) for i in range(size)]


def body(velocity, marker_cell, marker_frac, marker_force, fish_owner):
    levels, comps, cells_x, cells_y = velocity.shape
    slots = marker_cell.shape[3]
    items = levels * comps
    shape = (cells_x, cells_y, cells_x * lax.axis_size("gx"), cells_y * lax.axis_size("gy"))
    wide_x = cells_x + SPAN
    rows = cells_x + 2 * PAD
    chunk = min(512, slots)
    width = cells_y + LANES
    groups = -(-items // EDGE_PER)
    params = pltpu.CompilerParams(vmem_limit_bytes=32 * 1024 * 1024)
    edge_x = jax.ShapeDtypeStruct(((items + groups) * STRIP, LANES), jnp.bfloat16)
    half = (items, wide_x // 2, width)
    arrays = (fish_owner, velocity, marker_cell, marker_frac, marker_force)
    far_half, far, force, dense_y, quarter, value, quarter_y, value_y, level, parity, near_velocity = (
        pl.pallas_call(
        functools.partial(far_kernel, shape, slots),
        out_shape=(
            jax.ShapeDtypeStruct(half, jnp.float32),
            edge_x,
            jax.ShapeDtypeStruct((items, 2 * ROWS, slots), jnp.bfloat16),
            jax.ShapeDtypeStruct((width, slots), jnp.bfloat16),
            jax.ShapeDtypeStruct((ROWS, slots), jnp.int32),
            jax.ShapeDtypeStruct((ROWS, slots), jnp.float32),
            jax.ShapeDtypeStruct((ROWS, slots), jnp.int32),
            jax.ShapeDtypeStruct((ROWS, slots), jnp.float32),
            jax.ShapeDtypeStruct((1, slots), jnp.int32),
            jax.ShapeDtypeStruct((2, LANES), jnp.int32),
            jax.ShapeDtypeStruct(velocity.shape, velocity.dtype),
        ),
        in_specs=[pl.BlockSpec(memory_space=pltpu.HBM)] * 5,
        out_specs=tuple(whole(11)),
        scratch_shapes=[pltpu.VMEM(a.shape, a.dtype) for a in arrays if a is not velocity]
        + [pltpu.SemaphoreType.DMA((5,))],
        compiler_params=params,
        name="spread_far",
    )(*(pltpu.with_memory_space_constraint(a, pltpu.HBM) for a in arrays))
    )
    far_pairs, near_pairs = swap_pairs("gx")
    far_x = lax.ppermute(far, "gx", far_pairs)
    grid, near = pl.pallas_call(
        functools.partial(near_kernel, shape, slots),
        out_shape=(jax.ShapeDtypeStruct((items, wide_x, width), jnp.float32), edge_x),
        in_specs=whole(5),
        out_specs=tuple(whole(2)),
        scratch_shapes=[pltpu.VMEM(half, jnp.float32)],
        compiler_params=params,
        cost_estimate=pl.CostEstimate(
            flops=items * wide_x * width * slots, bytes_accessed=4 * items * wide_x * width,
            transcendentals=0,
        ),
        name="spread_near",
    )(near_velocity, far_half, force, dense_y, quarter)
    near_x = lax.ppermute(near, "gx", near_pairs)
    weights = jax.ShapeDtypeStruct((levels * LANES, slots), jnp.bfloat16)
    inner_weight, rim_weight, parity = pl.pallas_call(
        functools.partial(weight_kernel, shape, chunk),
        out_shape=(weights, weights, jax.ShapeDtypeStruct(parity.shape, parity.dtype)),
        in_specs=whole(4),
        out_specs=tuple(whole(3)),
        compiler_params=params,
        cost_estimate=pl.CostEstimate(
            flops=2 * levels * LANES * slots, bytes_accessed=4 * levels * LANES * slots,
            transcendentals=0,
        ),
        name="weights",
    )(parity, quarter_y, value_y, level)
    edge_y = jax.ShapeDtypeStruct((groups * (rows - ROWS) + SPAN, LANES), jnp.bfloat16)
    far, near = pl.pallas_call(
        functools.partial(pack_kernel, shape),
        out_shape=(edge_y, edge_y),
        in_specs=whole(4),
        out_specs=tuple(whole(2)),
        compiler_params=params,
        name="pack",
    )(parity, grid, far_x, near_x)
    far_pairs, near_pairs = swap_pairs("gy")
    far_y = lax.ppermute(far, "gy", far_pairs)
    near_y = lax.ppermute(near, "gy", near_pairs)
    field = pltpu.VMEM((items, rows + 2 * ROWS, LANES), jnp.float32)
    rounded = pltpu.VMEM((comps * wide_x, levels * LANES), jnp.bfloat16)
    inner, rim, part = pl.pallas_call(
        functools.partial(inner_kernel, shape, chunk, levels),
        out_shape=(
            jax.ShapeDtypeStruct((items, cells_x, LANES), jnp.float32),
            jax.ShapeDtypeStruct((items, rows, LANES), jnp.float32),
            jax.ShapeDtypeStruct((comps, slots), jnp.float32),
        ),
        in_specs=whole(7),
        out_specs=tuple(whole(3)),
        scratch_shapes=[field, field, field, rounded],
        compiler_params=params,
        cost_estimate=pl.CostEstimate(
            flops=2 * items * wide_x * LANES * slots, bytes_accessed=16 * items * rows * LANES,
            transcendentals=0,
        ),
        name="inner",
    )(parity, quarter, value, inner_weight, grid, far_x, near_x)
    return pl.pallas_call(
        functools.partial(finish_kernel, shape, chunk),
        out_shape=(
            jax.ShapeDtypeStruct(velocity.shape, jnp.float32),
            jax.ShapeDtypeStruct((comps, 1, 1, slots), jnp.float32),
        ),
        in_specs=whole(9),
        out_specs=tuple(whole(2)),
        scratch_shapes=[field, field, field, rounded],
        compiler_params=params,
        name="finish",
    )(parity, quarter, value, rim_weight, inner, rim, part, far_y, near_y)


def solution(mesh):
    placed = (
        P(None, None, "gx", "gy"),
        P(None, "gx", "gy", None),
        P(None, "gx", "gy", None),
        P(None, "gx", "gy", None),
        P(),
    )
    return jax.shard_map(
        body,
        mesh=mesh,
        in_specs=placed,
        out_specs=(P(None, None, "gx", "gy"), P(None, "gx", "gy", None)),
        check_vma=False,
    )
```

```python
import functools

import jax
import jax.numpy as jnp
import numpy as np
from jax import lax
from jax.experimental import pallas as pl
from jax.experimental.pallas import tpu as pltpu
from jax.sharding import PartitionSpec as P

MARGIN = 16
FISH_MARK = 1024
HALO = 3
LANES = 128
COURANT = 0.25
VISCOUS = 1.5
ROWS = 8
STEP = 2 * ROWS

REACH = MARGIN + HALO
PAD = -(-REACH // ROWS) * ROWS
STRIP = PAD + MARGIN
SPAN = 2 * MARGIN
EDGE_PER = LANES // SPAN


def half_turn(terms):
    nodes = 0.5 - 0.5 * np.cos(np.pi * (np.arange(64) + 0.5) / 64)
    square = nodes * nodes
    cosine = np.polynomial.polynomial.polyfit(square, np.cos(0.5 * np.pi * nodes), terms)
    sine = np.polynomial.polynomial.polyfit(square, np.sin(0.5 * np.pi * nodes) / nodes, terms)
    return [float(v) for v in cosine], [float(v) for v in sine]


COS_FIT, SIN_FIT = half_turn(6)


def horner(coefficients, value):
    total = jnp.full_like(value, coefficients[-1])
    for coefficient in coefficients[-2::-1]:
        total = total * value + coefficient
    return total


def four_weights(frac):
    square = frac * frac
    cosine = horner(COS_FIT, square)
    sine = frac * horner(SIN_FIT, square)
    return (0.25 - 0.25 * sine, 0.25 + 0.25 * cosine, 0.25 + 0.25 * sine, 0.25 - 0.25 * cosine)


def local_cell(cell, low, extent):
    offset = cell - low
    offset = jnp.where(offset < -MARGIN, offset + extent, offset)
    return jnp.where(offset >= extent - MARGIN, offset - extent, offset)


def position():
    row, col = lax.axis_index("gx"), lax.axis_index("gy")
    return row, col, (row & 1) == 0, (col & 1) == 0


def tile_weights(offset, weights):
    shift = lax.broadcasted_iota(jnp.int32, (ROWS, offset.shape[1]), 0) + 1 - offset
    quarter, phase = shift >> 2, shift & 3
    value = jnp.where(phase == 3, weights[3], weights[2])
    value = jnp.where(phase == 1, weights[1], value)
    return quarter, jnp.where(phase == 0, weights[0], value)


def doubled(quarter, value):
    quarter = jnp.concatenate([quarter, quarter + 2], axis=0).astype(jnp.float32)
    return quarter.astype(jnp.bfloat16), twice(value)


def twice(value):
    return jnp.concatenate([value, value], axis=0).astype(jnp.bfloat16)


def picked_tile(quarter, value, first):
    zero = jnp.zeros_like(value)
    return jnp.where(quarter == jnp.array(-first // 4, quarter.dtype), value, zero)


def half_spread(quarter_ref, force_ref, dense_y_ref, half_ref, base, lanes):
    items, rows = half_ref.shape[:2]
    quarter = quarter_ref[:, lanes] + base
    quarter = jnp.concatenate([quarter, quarter + 2], axis=0).astype(jnp.float32)
    quarter = quarter.astype(jnp.bfloat16)
    left = jnp.concatenate(
        [
            picked_tile(quarter, force_ref[k, :, lanes], row)
            for k in range(items)
            for row in range(0, rows, 2 * ROWS)
        ],
        axis=0,
    )
    total = lax.dot_general(
        left, dense_y_ref[:, lanes], (((1,), (1,)), ((), ())),
        preferred_element_type=jnp.float32,
    )
    total = total.reshape(half_ref.shape)
    if lanes.start:
        half_ref[...] += total
    else:
        half_ref[...] = total


def finish_half(half_ref, velocity_ref, out_ref, low, cells_y):
    items, rows = half_ref.shape[:2]
    comps = items // velocity_ref.shape[0]
    count = rows - MARGIN
    source = pl.ds(pl.multiple_of(jnp.where(low, 0, count), ROWS), count)
    target = pl.ds(pl.multiple_of(jnp.where(low, MARGIN, 0), ROWS), count)
    for k in range(items):
        half_ref[k, target, :cells_y] += velocity_ref[k // comps, k % comps, source]
    place = pl.ds(pl.multiple_of(jnp.where(low, 0, rows - STRIP), ROWS), STRIP)
    parts = [half_ref[k, place, :cells_y] for k in range(items)]
    for group in range(0, items, EDGE_PER):
        edges = []
        for k in range(group, min(group + EDGE_PER, items)):
            edges.append(rolled(half_ref[k, place, cells_y:], SPAN * (k - group)))
        parts.append(functools.reduce(jnp.add, edges))
    out_ref[...] = jnp.concatenate(parts, axis=0).astype(jnp.bfloat16)


def far_kernel(
    shape, chunk, fish_hbm, velocity_hbm, cell_hbm, frac_hbm, force_hbm,
    half_ref, far_ref, force_out, dense_y_ref, quarter_ref, value_ref,
    quarter_y_ref, value_y_ref, level_ref, parity_ref, velocity_ref,
    fish_ref, cell_ref, frac_ref, force_ref, sems,
):
    pairs = (
        (cell_hbm, cell_ref), (frac_hbm, frac_ref), (fish_hbm, fish_ref),
        (force_hbm, force_ref), (velocity_hbm, velocity_ref),
    )
    copies = [pltpu.make_async_copy(a, b, sems.at[i]) for i, (a, b) in enumerate(pairs)]
    for copy in copies:
        copy.start()
    cells_x, cells_y, extent_x, extent_y = shape
    levels, comps = velocity_ref.shape[:2]
    slots = cell_ref.shape[3]
    row, col, even, even_y = position()
    parity_ref[0:1] = jnp.full((1, LANES), jnp.where(even, 1, 0), jnp.int32)
    parity_ref[1:2] = jnp.full((1, LANES), jnp.where(even_y, 1, 0), jnp.int32)
    base = jnp.where(even, -MARGIN // 4, cells_x // 8)
    for copy in copies[:-1]:
        copy.wait()
    mine = jnp.where(fish_ref[...] == row * lax.axis_size("gy") + col, 1.0, 0.0)
    count = FISH_MARK * jnp.sum(mine)
    level_ref[...] = cell_ref[2, 0]
    for first in range(0, slots, chunk):
        lanes = slice(first, first + chunk)
        offset_x = local_cell(cell_ref[0, 0, :, lanes], row * cells_x, extent_x)
        offset_y = local_cell(cell_ref[1, 0, :, lanes], col * cells_y, extent_y)
        slot = lax.broadcasted_iota(jnp.int32, (1, chunk), 1) + first
        alive = jnp.where(slot.astype(jnp.float32) < count, 1.0, 0.0)
        quarter, value = tile_weights(offset_x, four_weights(frac_ref[0, 0, :, lanes]))
        value = value * alive
        quarter_ref[:, lanes] = quarter
        value_ref[:, lanes] = value
        level = cell_ref[2, 0, :, lanes]
        pushes = [force_ref[c, 0, :, lanes] * value for c in range(comps)]
        for l in range(levels):
            for c in range(comps):
                force_out[l * comps + c, :, lanes] = twice(jnp.where(level == l, pushes[c], 0.0))
        quarter, value = tile_weights(offset_y, four_weights(frac_ref[1, 0, :, lanes]))
        quarter_y_ref[:, lanes] = quarter
        value_y_ref[:, lanes] = value
        quarter, value = doubled(quarter, value)
        dense_y_ref[:, lanes] = jnp.concatenate(
            [picked_tile(quarter, value, n) for n in range(0, cells_y + MARGIN, 2 * ROWS)]
            + [jnp.zeros((LANES - SPAN, chunk), jnp.bfloat16)]
            + [picked_tile(quarter, value, n) for n in range(-MARGIN, 0, 2 * ROWS)],
            axis=0,
        )
        half_spread(quarter_ref, force_out, dense_y_ref, half_ref, base, lanes)
    copies[-1].wait()
    finish_half(half_ref, velocity_ref, far_ref, even, cells_y)


def near_kernel(
    shape, chunk, velocity_ref, far_half_ref, force_ref, dense_y_ref, quarter_ref,
    grid_ref, near_ref, half_ref,
):
    cells_x, cells_y, _, _ = shape
    slots = quarter_ref.shape[1]
    rows = half_ref.shape[1]
    _, _, even, _ = position()
    base = jnp.where(even, cells_x // 8, -MARGIN // 4)
    for first in range(0, slots, chunk):
        lanes = slice(first, first + chunk)
        half_spread(quarter_ref, force_ref, dense_y_ref, half_ref, base, lanes)
    finish_half(half_ref, velocity_ref, near_ref, jnp.logical_not(even), cells_y)
    for ref, row in ((far_half_ref, jnp.where(even, 0, rows)), (half_ref, jnp.where(even, rows, 0))):
        place = pl.ds(pl.multiple_of(row, ROWS), rows)
        for k in range(ref.shape[0]):
            grid_ref[k, place] = ref[k]


def rolled(value, shift):
    shift = shift % LANES
    return pltpu.roll(value, shift, 1) if shift else value


def lane_index(rows):
    return lax.broadcasted_iota(jnp.int32, (rows, LANES), 1)


def ordered(parity, near_ref, far_ref):
    even = jnp.broadcast_to(parity, near_ref.shape) != 0
    near, far = near_ref[...].astype(jnp.float32), far_ref[...].astype(jnp.float32)
    return jnp.where(even, far, near), jnp.where(even, near, far)


def joined(center, before, after):
    wide = center.shape[0]
    near = PAD - MARGIN
    overlap = STRIP - near
    return jnp.concatenate(
        [
            before[:near],
            center[:overlap] + before[near:],
            center[overlap : wide - overlap],
            center[wide - overlap :] + after[:overlap],
            after[overlap:],
        ],
        axis=0,
    )


def extended_rows(parity, grid_ref, near_ref, far_ref, cells_y):
    items = grid_ref.shape[0]
    groups = -(-items // EDGE_PER)
    size = groups * STRIP
    before, after = ordered(parity, near_ref, far_ref)
    packed = jnp.concatenate([before[items * STRIP :], after[items * STRIP :]], axis=0)
    lane = lane_index(2 * size)
    kept = (lane < MARGIN) | (lane >= LANES - MARGIN)
    edges = [jnp.where(kept, rolled(packed, -SPAN * slot), 0.0) for slot in range(EDGE_PER)]
    for k in range(items):
        place = slice(k * STRIP, (k + 1) * STRIP)
        inner = joined(grid_ref[k, :, :cells_y], before[place], after[place])
        start = k // EDGE_PER * STRIP
        edge = edges[k % EDGE_PER]
        edge = joined(
            grid_ref[k, :, cells_y:],
            edge[start : start + STRIP],
            edge[size + start : size + start + STRIP],
        )
        yield k, inner, edge


def pack_kernel(shape, parity_ref, grid_ref, far_x, near_x, near_ref, far_ref):
    cells_x, cells_y, _, _ = shape
    items = grid_ref.shape[0]
    groups = -(-items // EDGE_PER)
    rows = cells_x + 2 * PAD
    lane = lane_index(rows)
    up_halo = (lane >= LANES - REACH) & (lane < LANES - MARGIN)
    down_halo = (lane >= MARGIN) & (lane < REACH)
    halos, ups, downs = None, None, None
    packed = [[], []]
    for k, inner, edge in extended_rows(parity_ref[0:1], grid_ref, near_x, far_x, cells_y):
        slot = k % EDGE_PER
        up = rolled(jnp.where(lane >= LANES - MARGIN, inner, edge), SPAN * slot)
        down = rolled(jnp.where(lane < MARGIN, inner, edge), SPAN * slot)
        halo = rolled(jnp.where(up_halo | down_halo, inner, 0.0), REACH + HALO * k)
        ups = ups + up if slot else up
        downs = downs + down if slot else down
        halos = halos + halo if k else halo
        if slot == EDGE_PER - 1 or k == items - 1:
            packed[0].append(squeezed(ups))
            packed[1].append(squeezed(downs))
    halos = squeezed(halos)
    rows = halos.shape[0]
    used = lane_index(rows) < HALO * items
    ups = jnp.where(used, halos, 0.0)
    downs = jnp.where(used, rolled(halos, -MARGIN - REACH), 0.0)
    folded = None
    for row in range(0, rows, SPAN):
        size = min(SPAN, rows - row)
        parts = [value[row : row + size] for value in (ups, downs)]
        if size < SPAN:
            parts = [jnp.concatenate([p, jnp.zeros((SPAN - size, LANES), p.dtype)], 0) for p in parts]
        part = rolled(jnp.concatenate(parts, axis=0), row)
        folded = folded + part if row else part
    up = jnp.concatenate(packed[0] + [folded[:SPAN]], axis=0)
    down = jnp.concatenate(packed[1] + [folded[SPAN:]], axis=0)
    even = jnp.broadcast_to(parity_ref[1:2], up.shape) != 0
    near_ref[...] = jnp.where(even, up, down).astype(jnp.bfloat16)
    far_ref[...] = jnp.where(even, down, up).astype(jnp.bfloat16)


def squeezed(value):
    row = lax.broadcasted_iota(jnp.int32, (ROWS, LANES), 0)
    shared = jnp.where(row >= PAD - REACH, value[:ROWS], value[-ROWS:])
    return jnp.concatenate([shared, value[ROWS:-ROWS]], axis=0)


def expanded(value):
    return jnp.concatenate([value, value[:ROWS]], axis=0)


def around(ref, k, start, size):
    center = ref[k, start : start + size]
    back = ref[k, start - 1 : start - 1 + size]
    fore = ref[k, start + 1 : start + 1 + size]
    return center, back, fore, rolled(center, 1), rolled(center, -1)


def advect(moved_ref, carried_ref, levels, comps, rows):
    for start in range(ROWS, ROWS + rows, STEP):
        for l in range(levels):
            pieces = [around(moved_ref, l * comps + c, start, STEP) for c in range(comps)]
            speed_x, speed_y = COURANT * pieces[0][0], COURANT * pieces[1][0]
            ahead_x, astern_x = jnp.maximum(speed_x, 0.0), jnp.minimum(speed_x, 0.0)
            ahead_y, astern_y = jnp.maximum(speed_y, 0.0), jnp.minimum(speed_y, 0.0)
            for c in range(comps):
                center, back, fore, below, above = pieces[c]
                change = ahead_x * (center - back) + astern_x * (fore - center)
                change = change + ahead_y * (center - below) + astern_y * (above - center)
                carried_ref[l * comps + c, start : start + STEP] = center - change


def sweep(ref, carried_ref, levels, comps, start, size):
    scale = 1.0 / (1.0 + 6.0 * VISCOUS)
    centers, results = [], []
    for k in range(levels * comps):
        center, back, fore, below, above = around(ref, k, start, size)
        centers.append(center)
        results.append(back + fore + below + above)
    for k in range(levels * comps):
        higher = min(k // comps + 1, levels - 1) * comps + k % comps
        lower = max(k // comps - 1, 0) * comps + k % comps
        summed = results[k] + centers[higher] + centers[lower]
        source = carried_ref[k, start : start + size]
        results[k] = scale * source + (VISCOUS * scale) * summed
    return results


def first_steps(moved_ref, carried_ref, sweep_ref, levels, comps, rows):
    advect(moved_ref, carried_ref, levels, comps, rows)
    for start in range(ROWS, ROWS + rows, STEP):
        results = sweep(carried_ref, carried_ref, levels, comps, start, STEP)
        for k in range(levels * comps):
            sweep_ref[k, start : start + STEP] = results[k]


RIM = REACH + HALO
HALF = LANES // 2


def weight_kernel(
    shape, chunk, parity_ref, quarter_ref, value_ref, level_ref, inner_ref, rim_ref, parity_out
):
    parity_out[...] = parity_ref[...]
    _, cells_y, _, _ = shape
    slots = quarter_ref.shape[1]
    size = 2 * ROWS
    levels = inner_ref.shape[0] // LANES
    row = lax.broadcasted_iota(jnp.int32, (size, chunk), 0)

    def cut(tile, keep):
        return jnp.where(keep, tile.astype(jnp.float32), 0.0).astype(jnp.bfloat16)

    for first in range(0, slots, chunk):
        lanes = slice(first, first + chunk)
        level = level_ref[:, lanes]
        for l in range(levels):
            value = jnp.where(level == l, value_ref[:, lanes], 0.0)
            quarter, value = doubled(quarter_ref[:, lanes], value)
            for start in range(0, LANES, size):
                inner = picked_tile(quarter, value, start)
                if start < REACH:
                    inner = cut(inner, row + start >= REACH)
                if start + size > cells_y - REACH:
                    inner = cut(inner, row + start < cells_y - REACH)
                if start >= LANES - MARGIN:
                    rim = picked_tile(quarter, value, start - LANES)
                elif start + size > HALF - REACH and start < HALF + MARGIN:
                    rim = picked_tile(quarter, value, start + cells_y - HALF)
                    rim = cut(rim, row + start >= HALF - REACH) if start < HALF - REACH else rim
                elif start < REACH:
                    rim = picked_tile(quarter, value, start)
                    rim = cut(rim, row + start < REACH) if start + size > REACH else rim
                else:
                    rim = jnp.zeros_like(value)
                place = slice(l * LANES + start, l * LANES + start + size)
                inner_ref[place, lanes] = inner
                rim_ref[place, lanes] = rim


def sampled_part(round_ref, weight_ref, quarter_ref, value_ref, lanes, comps):
    wide_x = round_ref.shape[0] // comps
    partial = jnp.dot(round_ref[...], weight_ref[:, lanes], preferred_element_type=jnp.float32)
    quarter, value = quarter_ref[:, lanes], value_ref[:, lanes]
    totals = [jnp.zeros_like(value)] * comps
    for row in range(0, wide_x, ROWS):
        here = quarter == (MARGIN - row) // 4
        for c in range(comps):
            start = c * wide_x + row
            totals[c] = jnp.where(here, partial[start : start + ROWS], totals[c])
    return [jnp.sum(total * value, axis=0, keepdims=True) for total in totals]


def inner_kernel(
    shape, chunk, levels, parity_ref, quarter_ref, value_ref, weight_ref, grid_ref, far_x, near_x,
    inner_ref, rim_ref, sampled_ref, moved_ref, carried_ref, sweep_ref, round_ref,
):
    cells_x, cells_y, _, _ = shape
    items = grid_ref.shape[0]
    comps = items // levels
    slots = quarter_ref.shape[1]
    wide_x = cells_x + SPAN
    rows = cells_x + 2 * PAD
    lane = lane_index(rows)
    for k, inner, edge in extended_rows(parity_ref[0:1], grid_ref, near_x, far_x, cells_y):
        moved_ref[k, ROWS : ROWS + rows] = inner
        low = jnp.where(lane < RIM, inner, jnp.where(lane >= LANES - MARGIN, edge, 0.0))
        high = jnp.where(lane >= LANES - RIM, inner, jnp.where(lane < MARGIN, edge, 0.0))
        rim_ref[k] = low + rolled(high, HALF)
    first_steps(moved_ref, carried_ref, sweep_ref, levels, comps, rows)
    size = 2 * ROWS
    for row in range(0, wide_x, size):
        start = ROWS + PAD - MARGIN + row
        results = sweep(sweep_ref, carried_ref, levels, comps, start, size)
        for k in range(items):
            level, c = k // comps, k % comps
            place = slice(c * wide_x + row, c * wide_x + row + size)
            round_ref[place, level * LANES : (level + 1) * LANES] = results[k].astype(jnp.bfloat16)
            if MARGIN <= row < MARGIN + cells_x:
                inner_ref[k, row - MARGIN : row - MARGIN + size] = results[k]
    for first in range(0, slots, chunk):
        lanes = slice(first, first + chunk)
        parts = sampled_part(round_ref, weight_ref, quarter_ref, value_ref, lanes, comps)
        for c in range(comps):
            sampled_ref[c : c + 1, lanes] = parts[c]


def unfolded(folded, rows):
    return expanded(
        jnp.concatenate(
            [rolled(folded, -row)[: min(SPAN, rows - row)] for row in range(0, rows, SPAN)], axis=0
        )
    )


def finish_kernel(
    shape, chunk, parity_ref, quarter_ref, value_ref, weight_ref, inner_ref, rim_ref, part_ref,
    near_y, far_y, next_ref, sampled_ref, moved_ref, carried_ref, sweep_ref, round_ref,
):
    cells_x, cells_y, _, _ = shape
    items = rim_ref.shape[0]
    groups = -(-items // EDGE_PER)
    levels, comps = next_ref.shape[:2]
    slots = quarter_ref.shape[1]
    wide_x = cells_x + SPAN
    rows = cells_x + 2 * PAD
    lane = lane_index(rows)
    befores, afters = ordered(parity_ref[1:2], near_y, far_y)
    turned = HALF + MARGIN + REACH
    high_halo = (lane >= turned) & (lane < turned + HALO * items)
    both = ((lane + MARGIN) & (HALF - 1)) < SPAN
    outer = ((lane >= LANES - REACH) & (lane < LANES - MARGIN)) | (
        (lane >= HALF + MARGIN) & (lane < HALF + REACH)
    )
    size = rows - ROWS
    halo = jnp.where(
        high_halo,
        rolled(unfolded(afters[groups * size :], size), turned),
        unfolded(befores[groups * size :], size),
    )
    for group in range(groups):
        before = expanded(befores[group * size : (group + 1) * size])
        after = expanded(rolled(afters[group * size : (group + 1) * size], HALF))
        for k in range(group * EDGE_PER, min((group + 1) * EDGE_PER, items)):
            slot = k % EDGE_PER
            window = ((lane + (LANES + MARGIN - SPAN * slot)) & (LANES - 1)) < SPAN
            main = rolled(jnp.where(window, before, after), -SPAN * slot)
            value = rim_ref[k] + jnp.where(both, main, 0.0)
            value = jnp.where(outer, rolled(halo, -REACH - HALO * k), value)
            moved_ref[k, ROWS : ROWS + rows] = value

    first_steps(moved_ref, carried_ref, sweep_ref, levels, comps, rows)
    size = 2 * ROWS
    lane = lane_index(size)
    for row in range(0, wide_x, size):
        start = ROWS + PAD - MARGIN + row
        results = sweep(sweep_ref, carried_ref, levels, comps, start, size)
        for k in range(items):
            level, c = k // comps, k % comps
            place = slice(c * wide_x + row, c * wide_x + row + size)
            round_ref[place, level * LANES : (level + 1) * LANES] = results[k].astype(jnp.bfloat16)
        if not MARGIN <= row < MARGIN + cells_x:
            continue
        place = slice(row - MARGIN, row - MARGIN + size)
        for k in range(items):
            low, high = results[k], rolled(results[k], HALF)
            inner = inner_ref[k, place]
            inner = jnp.where(lane < REACH, low, jnp.where(lane >= LANES - REACH, high, inner))
            next_ref[k // comps, k % comps, place] = inner

    for first in range(0, slots, chunk):
        lanes = slice(first, first + chunk)
        parts = sampled_part(round_ref, weight_ref, quarter_ref, value_ref, lanes, comps)
        for c in range(comps):
            sampled_ref[c, 0, :, lanes] = part_ref[c : c + 1, lanes] + parts[c]


def whole(count):
    return [pl.BlockSpec(memory_space=pltpu.VMEM)] * count


def swap_pairs(axis):
    size = lax.axis_size(axis)
    if size % 2:
        raise ValueError("odd axis")
    far_pairs = [(i, (i - 1 if i % 2 == 0 else i + 1) % size) for i in range(size)]
    return far_pairs, [(i, i ^ 1) for i in range(size)]


def body(velocity, marker_cell, marker_frac, marker_force, fish_owner):
    levels, comps, cells_x, cells_y = velocity.shape
    slots = marker_cell.shape[3]
    items = levels * comps
    shape = (cells_x, cells_y, cells_x * lax.axis_size("gx"), cells_y * lax.axis_size("gy"))
    wide_x = cells_x + SPAN
    rows = cells_x + 2 * PAD
    chunk = min(512, slots)
    width = cells_y + LANES
    groups = -(-items // EDGE_PER)
    params = pltpu.CompilerParams(vmem_limit_bytes=32 * 1024 * 1024)
    edge_x = jax.ShapeDtypeStruct(((items + groups) * STRIP, LANES), jnp.bfloat16)
    half = (items, wide_x // 2, width)
    arrays = (fish_owner, velocity, marker_cell, marker_frac, marker_force)
    far_half, far, force, dense_y, quarter, value, quarter_y, value_y, level, parity, near_velocity = (
        pl.pallas_call(
        functools.partial(far_kernel, shape, slots),
        out_shape=(
            jax.ShapeDtypeStruct(half, jnp.float32),
            edge_x,
            jax.ShapeDtypeStruct((items, 2 * ROWS, slots), jnp.bfloat16),
            jax.ShapeDtypeStruct((width, slots), jnp.bfloat16),
            jax.ShapeDtypeStruct((ROWS, slots), jnp.int32),
            jax.ShapeDtypeStruct((ROWS, slots), jnp.float32),
            jax.ShapeDtypeStruct((ROWS, slots), jnp.int32),
            jax.ShapeDtypeStruct((ROWS, slots), jnp.float32),
            jax.ShapeDtypeStruct((1, slots), jnp.int32),
            jax.ShapeDtypeStruct((2, LANES), jnp.int32),
            jax.ShapeDtypeStruct(velocity.shape, velocity.dtype),
        ),
        in_specs=[pl.BlockSpec(memory_space=pltpu.HBM)] * 5,
        out_specs=tuple(whole(11)),
        scratch_shapes=[pltpu.VMEM(a.shape, a.dtype) for a in arrays if a is not velocity]
        + [pltpu.SemaphoreType.DMA((5,))],
        compiler_params=params,
        name="spread_far",
    )(*(pltpu.with_memory_space_constraint(a, pltpu.HBM) for a in arrays))
    )
    far_pairs, near_pairs = swap_pairs("gx")
    far_x = lax.ppermute(far, "gx", far_pairs)
    grid, near = pl.pallas_call(
        functools.partial(near_kernel, shape, slots),
        out_shape=(jax.ShapeDtypeStruct((items, wide_x, width), jnp.float32), edge_x),
        in_specs=whole(5),
        out_specs=tuple(whole(2)),
        scratch_shapes=[pltpu.VMEM(half, jnp.float32)],
        compiler_params=params,
        cost_estimate=pl.CostEstimate(
            flops=items * wide_x * width * slots, bytes_accessed=4 * items * wide_x * width,
            transcendentals=0,
        ),
        name="spread_near",
    )(near_velocity, far_half, force, dense_y, quarter)
    near_x = lax.ppermute(near, "gx", near_pairs)
    weights = jax.ShapeDtypeStruct((levels * LANES, slots), jnp.bfloat16)
    inner_weight, rim_weight, parity = pl.pallas_call(
        functools.partial(weight_kernel, shape, chunk),
        out_shape=(weights, weights, jax.ShapeDtypeStruct(parity.shape, parity.dtype)),
        in_specs=whole(4),
        out_specs=tuple(whole(3)),
        compiler_params=params,
        cost_estimate=pl.CostEstimate(
            flops=2 * levels * LANES * slots, bytes_accessed=4 * levels * LANES * slots,
            transcendentals=0,
        ),
        name="weights",
    )(parity, quarter_y, value_y, level)
    edge_y = jax.ShapeDtypeStruct((groups * (rows - ROWS) + SPAN, LANES), jnp.bfloat16)
    near, far = pl.pallas_call(
        functools.partial(pack_kernel, shape),
        out_shape=(edge_y, edge_y),
        in_specs=whole(4),
        out_specs=tuple(whole(2)),
        compiler_params=params,
        name="pack",
    )(parity, grid, far_x, near_x)
    far_pairs, near_pairs = swap_pairs("gy")
    near_y = lax.ppermute(near, "gy", near_pairs)
    far_y = lax.ppermute(far, "gy", far_pairs)
    field = pltpu.VMEM((items, rows + 2 * ROWS, LANES), jnp.float32)
    rounded = pltpu.VMEM((comps * wide_x, levels * LANES), jnp.bfloat16)
    inner, rim, part = pl.pallas_call(
        functools.partial(inner_kernel, shape, chunk, levels),
        out_shape=(
            jax.ShapeDtypeStruct((items, cells_x, LANES), jnp.float32),
            jax.ShapeDtypeStruct((items, rows, LANES), jnp.float32),
            jax.ShapeDtypeStruct((comps, slots), jnp.float32),
        ),
        in_specs=whole(7),
        out_specs=tuple(whole(3)),
        scratch_shapes=[field, field, field, rounded],
        compiler_params=params,
        cost_estimate=pl.CostEstimate(
            flops=2 * items * wide_x * LANES * slots, bytes_accessed=16 * items * rows * LANES,
            transcendentals=0,
        ),
        name="inner",
    )(parity, quarter, value, inner_weight, grid, far_x, near_x)
    return pl.pallas_call(
        functools.partial(finish_kernel, shape, chunk),
        out_shape=(
            jax.ShapeDtypeStruct(velocity.shape, jnp.float32),
            jax.ShapeDtypeStruct((comps, 1, 1, slots), jnp.float32),
        ),
        in_specs=whole(9),
        out_specs=tuple(whole(2)),
        scratch_shapes=[field, field, field, rounded],
        compiler_params=params,
        name="finish",
    )(parity, quarter, value, rim_weight, inner, rim, part, near_y, far_y)


def solution(mesh):
    placed = (
        P(None, None, "gx", "gy"),
        P(None, "gx", "gy", None),
        P(None, "gx", "gy", None),
        P(None, "gx", "gy", None),
        P(),
    )
    return jax.shard_map(
        body,
        mesh=mesh,
        in_specs=placed,
        out_specs=(P(None, None, "gx", "gy"), P(None, "gx", "gy", None)),
        check_vma=False,
    )
```

```python
import functools

import jax
import jax.numpy as jnp
import numpy as np
from jax import lax
from jax.experimental import pallas as pl
from jax.experimental.pallas import tpu as pltpu
from jax.sharding import PartitionSpec as P

MARGIN = 16
FISH_MARK = 1024
HALO = 3
LANES = 128
COURANT = 0.25
VISCOUS = 1.5
ROWS = 8
STEP = 2 * ROWS

REACH = MARGIN + HALO
PAD = -(-REACH // ROWS) * ROWS
STRIP = PAD + MARGIN
SPAN = 2 * MARGIN
EDGE_PER = LANES // SPAN


def half_turn(terms):
    nodes = 0.5 - 0.5 * np.cos(np.pi * (np.arange(64) + 0.5) / 64)
    square = nodes * nodes
    cosine = np.polynomial.polynomial.polyfit(square, np.cos(0.5 * np.pi * nodes), terms)
    sine = np.polynomial.polynomial.polyfit(square, np.sin(0.5 * np.pi * nodes) / nodes, terms)
    return [float(v) for v in cosine], [float(v) for v in sine]


COS_FIT, SIN_FIT = half_turn(6)


def horner(coefficients, value):
    total = jnp.full_like(value, coefficients[-1])
    for coefficient in coefficients[-2::-1]:
        total = total * value + coefficient
    return total


def four_weights(frac):
    square = frac * frac
    cosine = horner(COS_FIT, square)
    sine = frac * horner(SIN_FIT, square)
    return (0.25 - 0.25 * sine, 0.25 + 0.25 * cosine, 0.25 + 0.25 * sine, 0.25 - 0.25 * cosine)


def local_cell(cell, low, extent):
    offset = cell - low
    offset = jnp.where(offset < -MARGIN, offset + extent, offset)
    return jnp.where(offset >= extent - MARGIN, offset - extent, offset)


def position():
    row, col = lax.axis_index("gx"), lax.axis_index("gy")
    return row, col, (row & 1) == 0, (col & 1) == 0


def tile_weights(offset, weights):
    shift = lax.broadcasted_iota(jnp.int32, (ROWS, offset.shape[1]), 0) + 1 - offset
    quarter, phase = shift >> 2, shift & 3
    value = jnp.where(phase == 3, weights[3], weights[2])
    value = jnp.where(phase == 1, weights[1], value)
    return quarter, jnp.where(phase == 0, weights[0], value)


def doubled(quarter, value):
    quarter = jnp.concatenate([quarter, quarter + 2], axis=0).astype(jnp.float32)
    return quarter.astype(jnp.bfloat16), twice(value)


def twice(value):
    return jnp.concatenate([value, value], axis=0).astype(jnp.bfloat16)


def picked_tile(quarter, value, first):
    zero = jnp.zeros_like(value)
    return jnp.where(quarter == jnp.array(-first // 4, quarter.dtype), value, zero)


def half_spread(quarter_ref, force_ref, dense_y_ref, half_ref, base, lanes):
    items, rows = half_ref.shape[:2]
    quarter = quarter_ref[:, lanes] + base
    quarter = jnp.concatenate([quarter, quarter + 2], axis=0).astype(jnp.float32)
    quarter = quarter.astype(jnp.bfloat16)
    left = jnp.concatenate(
        [
            picked_tile(quarter, force_ref[k, :, lanes], row)
            for k in range(items)
            for row in range(0, rows, 2 * ROWS)
        ],
        axis=0,
    )
    total = lax.dot_general(
        left, dense_y_ref[:, lanes], (((1,), (1,)), ((), ())),
        preferred_element_type=jnp.float32,
    )
    total = total.reshape(half_ref.shape)
    if lanes.start:
        half_ref[...] += total
    else:
        half_ref[...] = total


def finish_half(half_ref, velocity_ref, out_ref, low, cells_y):
    items, rows = half_ref.shape[:2]
    comps = items // velocity_ref.shape[0]
    count = rows - MARGIN
    source = pl.ds(pl.multiple_of(jnp.where(low, 0, count), ROWS), count)
    target = pl.ds(pl.multiple_of(jnp.where(low, MARGIN, 0), ROWS), count)
    for k in range(items):
        half_ref[k, target, :cells_y] += velocity_ref[k // comps, k % comps, source]
    place = pl.ds(pl.multiple_of(jnp.where(low, 0, rows - STRIP), ROWS), STRIP)
    parts = [half_ref[k, place, :cells_y] for k in range(items)]
    for group in range(0, items, EDGE_PER):
        edges = []
        for k in range(group, min(group + EDGE_PER, items)):
            edges.append(rolled(half_ref[k, place, cells_y:], SPAN * (k - group)))
        parts.append(functools.reduce(jnp.add, edges))
    out_ref[...] = jnp.concatenate(parts, axis=0).astype(jnp.bfloat16)


def far_kernel(
    shape, chunk, fish_hbm, velocity_hbm, cell_hbm, frac_hbm, force_hbm,
    half_ref, far_ref, force_out, dense_y_ref, quarter_ref, value_ref,
    quarter_y_ref, value_y_ref, level_ref, parity_ref, velocity_ref,
    fish_ref, cell_ref, frac_ref, force_ref, sems,
):
    pairs = (
        (cell_hbm, cell_ref), (frac_hbm, frac_ref), (fish_hbm, fish_ref),
        (force_hbm, force_ref), (velocity_hbm, velocity_ref),
    )
    copies = [pltpu.make_async_copy(a, b, sems.at[i]) for i, (a, b) in enumerate(pairs)]
    for copy in copies:
        copy.start()
    cells_x, cells_y, extent_x, extent_y = shape
    levels, comps = velocity_ref.shape[:2]
    slots = cell_ref.shape[3]
    row, col, even, even_y = position()
    parity_ref[0:1] = jnp.full((1, LANES), jnp.where(even, 1, 0), jnp.int32)
    parity_ref[1:2] = jnp.full((1, LANES), jnp.where(even_y, 1, 0), jnp.int32)
    base = jnp.where(even, -MARGIN // 4, cells_x // 8)
    for copy in copies[:-1]:
        copy.wait()
    mine = jnp.where(fish_ref[...] == row * lax.axis_size("gy") + col, 1.0, 0.0)
    count = FISH_MARK * jnp.sum(mine)
    level_ref[...] = cell_ref[2, 0]
    for first in range(0, slots, chunk):
        lanes = slice(first, first + chunk)
        offset_x = local_cell(cell_ref[0, 0, :, lanes], row * cells_x, extent_x)
        offset_y = local_cell(cell_ref[1, 0, :, lanes], col * cells_y, extent_y)
        slot = lax.broadcasted_iota(jnp.int32, (1, chunk), 1) + first
        alive = jnp.where(slot.astype(jnp.float32) < count, 1.0, 0.0)
        quarter, value = tile_weights(offset_x, four_weights(frac_ref[0, 0, :, lanes]))
        value = value * alive
        quarter_ref[:, lanes] = quarter
        value_ref[:, lanes] = value
        level = cell_ref[2, 0, :, lanes]
        pushes = [force_ref[c, 0, :, lanes] * value for c in range(comps)]
        for l in range(levels):
            for c in range(comps):
                force_out[l * comps + c, :, lanes] = twice(jnp.where(level == l, pushes[c], 0.0))
        quarter, value = tile_weights(offset_y, four_weights(frac_ref[1, 0, :, lanes]))
        quarter_y_ref[:, lanes] = quarter
        value_y_ref[:, lanes] = value
        quarter, value = doubled(quarter, value)
        dense_y_ref[:, lanes] = jnp.concatenate(
            [picked_tile(quarter, value, n) for n in range(0, cells_y + MARGIN, 2 * ROWS)]
            + [jnp.zeros((LANES - SPAN, chunk), jnp.bfloat16)]
            + [picked_tile(quarter, value, n) for n in range(-MARGIN, 0, 2 * ROWS)],
            axis=0,
        )
        half_spread(quarter_ref, force_out, dense_y_ref, half_ref, base, lanes)
    copies[-1].wait()
    finish_half(half_ref, velocity_ref, far_ref, even, cells_y)


def near_kernel(
    shape, chunk, velocity_ref, far_half_ref, force_ref, dense_y_ref, quarter_ref,
    grid_ref, near_ref, half_ref,
):
    cells_x, cells_y, _, _ = shape
    slots = quarter_ref.shape[1]
    rows = half_ref.shape[1]
    _, _, even, _ = position()
    base = jnp.where(even, cells_x // 8, -MARGIN // 4)
    for first in range(0, slots, chunk):
        lanes = slice(first, first + chunk)
        half_spread(quarter_ref, force_ref, dense_y_ref, half_ref, base, lanes)
    finish_half(half_ref, velocity_ref, near_ref, jnp.logical_not(even), cells_y)
    for ref, row in ((far_half_ref, jnp.where(even, 0, rows)), (half_ref, jnp.where(even, rows, 0))):
        place = pl.ds(pl.multiple_of(row, ROWS), rows)
        for k in range(ref.shape[0]):
            grid_ref[k, place] = ref[k]


def rolled(value, shift):
    shift = shift % LANES
    return pltpu.roll(value, shift, 1) if shift else value


def lane_index(rows):
    return lax.broadcasted_iota(jnp.int32, (rows, LANES), 1)


def ordered(parity, near_ref, far_ref):
    even = jnp.broadcast_to(parity.astype(jnp.float32), (2 * ROWS, LANES)).astype(jnp.bfloat16)
    even = jnp.concatenate([even] * (near_ref.shape[0] // (2 * ROWS)), axis=0) != 0
    near, far = near_ref[...], far_ref[...]
    before, after = jnp.where(even, far, near), jnp.where(even, near, far)
    return before.astype(jnp.float32), after.astype(jnp.float32)


def joined(center, before, after):
    wide = center.shape[0]
    near = PAD - MARGIN
    overlap = STRIP - near
    return jnp.concatenate(
        [
            before[:near],
            center[:overlap] + before[near:],
            center[overlap : wide - overlap],
            center[wide - overlap :] + after[:overlap],
            after[overlap:],
        ],
        axis=0,
    )


def extended_rows(parity, grid_ref, near_ref, far_ref, cells_y):
    items = grid_ref.shape[0]
    groups = -(-items // EDGE_PER)
    size = groups * STRIP
    before, after = ordered(parity, near_ref, far_ref)
    packed = jnp.concatenate([before[items * STRIP :], after[items * STRIP :]], axis=0)
    lane = lane_index(2 * size)
    kept = (lane < MARGIN) | (lane >= LANES - MARGIN)
    edges = [jnp.where(kept, rolled(packed, -SPAN * slot), 0.0) for slot in range(EDGE_PER)]
    for k in range(items):
        place = slice(k * STRIP, (k + 1) * STRIP)
        inner = joined(grid_ref[k, :, :cells_y], before[place], after[place])
        start = k // EDGE_PER * STRIP
        edge = edges[k % EDGE_PER]
        edge = joined(
            grid_ref[k, :, cells_y:],
            edge[start : start + STRIP],
            edge[size + start : size + start + STRIP],
        )
        yield k, inner, edge


def pack_kernel(shape, parity_ref, grid_ref, far_x, near_x, near_ref, far_ref):
    cells_x, cells_y, _, _ = shape
    items = grid_ref.shape[0]
    groups = -(-items // EDGE_PER)
    rows = cells_x + 2 * PAD
    lane = lane_index(rows)
    up_halo = (lane >= LANES - REACH) & (lane < LANES - MARGIN)
    down_halo = (lane >= MARGIN) & (lane < REACH)
    halos, ups, downs = None, None, None
    packed = [[], []]
    for k, inner, edge in extended_rows(parity_ref[0:1], grid_ref, near_x, far_x, cells_y):
        slot = k % EDGE_PER
        up = rolled(jnp.where(lane >= LANES - MARGIN, inner, edge), SPAN * slot)
        down = rolled(jnp.where(lane < MARGIN, inner, edge), SPAN * slot)
        halo = rolled(jnp.where(up_halo | down_halo, inner, 0.0), REACH + HALO * k)
        ups = ups + up if slot else up
        downs = downs + down if slot else down
        halos = halos + halo if k else halo
        if slot == EDGE_PER - 1 or k == items - 1:
            packed[0].append(squeezed(ups))
            packed[1].append(squeezed(downs))
    halos = squeezed(halos)
    rows = halos.shape[0]
    used = lane_index(rows) < HALO * items
    ups = jnp.where(used, halos, 0.0)
    downs = jnp.where(used, rolled(halos, -MARGIN - REACH), 0.0)
    folded = None
    for row in range(0, rows, SPAN):
        size = min(SPAN, rows - row)
        parts = [value[row : row + size] for value in (ups, downs)]
        if size < SPAN:
            parts = [jnp.concatenate([p, jnp.zeros((SPAN - size, LANES), p.dtype)], 0) for p in parts]
        part = rolled(jnp.concatenate(parts, axis=0), row)
        folded = folded + part if row else part
    up = jnp.concatenate(packed[0] + [folded[:SPAN]], axis=0)
    down = jnp.concatenate(packed[1] + [folded[SPAN:]], axis=0)
    even = jnp.broadcast_to(parity_ref[1:2], up.shape) != 0
    near_ref[...] = jnp.where(even, up, down).astype(jnp.bfloat16)
    far_ref[...] = jnp.where(even, down, up).astype(jnp.bfloat16)


def squeezed(value):
    row = lax.broadcasted_iota(jnp.int32, (ROWS, LANES), 0)
    shared = jnp.where(row >= PAD - REACH, value[:ROWS], value[-ROWS:])
    return jnp.concatenate([shared, value[ROWS:-ROWS]], axis=0)


def expanded(value):
    return jnp.concatenate([value, value[:ROWS]], axis=0)


def around(ref, k, start, size):
    center = ref[k, start : start + size]
    back = ref[k, start - 1 : start - 1 + size]
    fore = ref[k, start + 1 : start + 1 + size]
    return center, back, fore, rolled(center, 1), rolled(center, -1)


def advect(moved_ref, carried_ref, levels, comps, rows):
    for start in range(ROWS, ROWS + rows, STEP):
        for l in range(levels):
            pieces = [around(moved_ref, l * comps + c, start, STEP) for c in range(comps)]
            speed_x, speed_y = COURANT * pieces[0][0], COURANT * pieces[1][0]
            ahead_x, astern_x = jnp.maximum(speed_x, 0.0), jnp.minimum(speed_x, 0.0)
            ahead_y, astern_y = jnp.maximum(speed_y, 0.0), jnp.minimum(speed_y, 0.0)
            for c in range(comps):
                center, back, fore, below, above = pieces[c]
                change = ahead_x * (center - back) + astern_x * (fore - center)
                change = change + ahead_y * (center - below) + astern_y * (above - center)
                carried_ref[l * comps + c, start : start + STEP] = center - change


def sweep(ref, carried_ref, levels, comps, start, size):
    scale = 1.0 / (1.0 + 6.0 * VISCOUS)
    centers, results = [], []
    for k in range(levels * comps):
        center, back, fore, below, above = around(ref, k, start, size)
        centers.append(center)
        results.append(back + fore + below + above)
    for k in range(levels * comps):
        higher = min(k // comps + 1, levels - 1) * comps + k % comps
        lower = max(k // comps - 1, 0) * comps + k % comps
        summed = results[k] + centers[higher] + centers[lower]
        source = carried_ref[k, start : start + size]
        results[k] = scale * source + (VISCOUS * scale) * summed
    return results


def first_steps(moved_ref, carried_ref, sweep_ref, levels, comps, rows):
    advect(moved_ref, carried_ref, levels, comps, rows)
    for start in range(ROWS, ROWS + rows, STEP):
        results = sweep(carried_ref, carried_ref, levels, comps, start, STEP)
        for k in range(levels * comps):
            sweep_ref[k, start : start + STEP] = results[k]


RIM = REACH + HALO
HALF = LANES // 2


def weight_kernel(
    shape, chunk, parity_ref, quarter_ref, value_ref, level_ref, inner_ref, rim_ref, parity_out
):
    parity_out[...] = parity_ref[...]
    _, cells_y, _, _ = shape
    slots = quarter_ref.shape[1]
    size = 2 * ROWS
    levels = inner_ref.shape[0] // LANES
    row = lax.broadcasted_iota(jnp.int32, (size, chunk), 0)

    def cut(tile, keep):
        return jnp.where(keep, tile.astype(jnp.float32), 0.0).astype(jnp.bfloat16)

    for first in range(0, slots, chunk):
        lanes = slice(first, first + chunk)
        level = level_ref[:, lanes]
        for l in range(levels):
            value = jnp.where(level == l, value_ref[:, lanes], 0.0)
            quarter, value = doubled(quarter_ref[:, lanes], value)
            for start in range(0, LANES, size):
                inner = picked_tile(quarter, value, start)
                if start < REACH:
                    inner = cut(inner, row + start >= REACH)
                if start + size > cells_y - REACH:
                    inner = cut(inner, row + start < cells_y - REACH)
                if start >= LANES - MARGIN:
                    rim = picked_tile(quarter, value, start - LANES)
                elif start + size > HALF - REACH and start < HALF + MARGIN:
                    rim = picked_tile(quarter, value, start + cells_y - HALF)
                    rim = cut(rim, row + start >= HALF - REACH) if start < HALF - REACH else rim
                elif start < REACH:
                    rim = picked_tile(quarter, value, start)
                    rim = cut(rim, row + start < REACH) if start + size > REACH else rim
                else:
                    rim = jnp.zeros_like(value)
                place = slice(l * LANES + start, l * LANES + start + size)
                inner_ref[place, lanes] = inner
                rim_ref[place, lanes] = rim


def sampled_part(round_ref, weight_ref, quarter_ref, value_ref, lanes, comps):
    wide_x = round_ref.shape[0] // comps
    partial = jnp.dot(round_ref[...], weight_ref[:, lanes], preferred_element_type=jnp.float32)
    quarter, value = quarter_ref[:, lanes], value_ref[:, lanes]
    totals = [jnp.zeros_like(value)] * comps
    for row in range(0, wide_x, ROWS):
        here = quarter == (MARGIN - row) // 4
        for c in range(comps):
            start = c * wide_x + row
            totals[c] = jnp.where(here, partial[start : start + ROWS], totals[c])
    return [jnp.sum(total * value, axis=0, keepdims=True) for total in totals]


def inner_kernel(
    shape, chunk, levels, parity_ref, quarter_ref, value_ref, weight_ref, grid_ref, far_x, near_x,
    inner_ref, rim_ref, sampled_ref, moved_ref, carried_ref, sweep_ref, round_ref,
):
    cells_x, cells_y, _, _ = shape
    items = grid_ref.shape[0]
    comps = items // levels
    slots = quarter_ref.shape[1]
    wide_x = cells_x + SPAN
    rows = cells_x + 2 * PAD
    lane = lane_index(rows)
    for k, inner, edge in extended_rows(parity_ref[0:1], grid_ref, near_x, far_x, cells_y):
        moved_ref[k, ROWS : ROWS + rows] = inner
        low = jnp.where(lane < RIM, inner, jnp.where(lane >= LANES - MARGIN, edge, 0.0))
        high = jnp.where(lane >= LANES - RIM, inner, jnp.where(lane < MARGIN, edge, 0.0))
        rim_ref[k] = low + rolled(high, HALF)
    first_steps(moved_ref, carried_ref, sweep_ref, levels, comps, rows)
    size = 2 * ROWS
    for row in range(0, wide_x, size):
        start = ROWS + PAD - MARGIN + row
        results = sweep(sweep_ref, carried_ref, levels, comps, start, size)
        for k in range(items):
            level, c = k // comps, k % comps
            place = slice(c * wide_x + row, c * wide_x + row + size)
            round_ref[place, level * LANES : (level + 1) * LANES] = results[k].astype(jnp.bfloat16)
            if MARGIN <= row < MARGIN + cells_x:
                inner_ref[k, row - MARGIN : row - MARGIN + size] = results[k]
    for first in range(0, slots, chunk):
        lanes = slice(first, first + chunk)
        parts = sampled_part(round_ref, weight_ref, quarter_ref, value_ref, lanes, comps)
        for c in range(comps):
            sampled_ref[c : c + 1, lanes] = parts[c]


def unfolded(folded, rows):
    return expanded(
        jnp.concatenate(
            [rolled(folded, -row)[: min(SPAN, rows - row)] for row in range(0, rows, SPAN)], axis=0
        )
    )


def finish_kernel(
    shape, chunk, parity_ref, quarter_ref, value_ref, weight_ref, inner_ref, rim_ref, part_ref,
    near_y, far_y, next_ref, sampled_ref, moved_ref, carried_ref, sweep_ref, round_ref,
):
    cells_x, cells_y, _, _ = shape
    items = rim_ref.shape[0]
    groups = -(-items // EDGE_PER)
    levels, comps = next_ref.shape[:2]
    slots = quarter_ref.shape[1]
    wide_x = cells_x + SPAN
    rows = cells_x + 2 * PAD
    lane = lane_index(rows)
    befores, afters = ordered(parity_ref[1:2], near_y, far_y)
    turned = HALF + MARGIN + REACH
    high_halo = (lane >= turned) & (lane < turned + HALO * items)
    both = ((lane + MARGIN) & (HALF - 1)) < SPAN
    outer = ((lane >= LANES - REACH) & (lane < LANES - MARGIN)) | (
        (lane >= HALF + MARGIN) & (lane < HALF + REACH)
    )
    size = rows - ROWS
    halo = jnp.where(
        high_halo,
        rolled(unfolded(afters[groups * size :], size), turned),
        unfolded(befores[groups * size :], size),
    )
    for group in range(groups):
        before = expanded(befores[group * size : (group + 1) * size])
        after = expanded(rolled(afters[group * size : (group + 1) * size], HALF))
        for k in range(group * EDGE_PER, min((group + 1) * EDGE_PER, items)):
            slot = k % EDGE_PER
            window = ((lane + (LANES + MARGIN - SPAN * slot)) & (LANES - 1)) < SPAN
            main = rolled(jnp.where(window, before, after), -SPAN * slot)
            value = rim_ref[k] + jnp.where(both, main, 0.0)
            value = jnp.where(outer, rolled(halo, -REACH - HALO * k), value)
            moved_ref[k, ROWS : ROWS + rows] = value

    first_steps(moved_ref, carried_ref, sweep_ref, levels, comps, rows)
    size = 2 * ROWS
    lane = lane_index(size)
    for row in range(0, wide_x, size):
        start = ROWS + PAD - MARGIN + row
        results = sweep(sweep_ref, carried_ref, levels, comps, start, size)
        for k in range(items):
            level, c = k // comps, k % comps
            place = slice(c * wide_x + row, c * wide_x + row + size)
            round_ref[place, level * LANES : (level + 1) * LANES] = results[k].astype(jnp.bfloat16)
        if not MARGIN <= row < MARGIN + cells_x:
            continue
        place = slice(row - MARGIN, row - MARGIN + size)
        for k in range(items):
            low, high = results[k], rolled(results[k], HALF)
            inner = inner_ref[k, place]
            inner = jnp.where(lane < REACH, low, jnp.where(lane >= LANES - REACH, high, inner))
            next_ref[k // comps, k % comps, place] = inner

    for first in range(0, slots, chunk):
        lanes = slice(first, first + chunk)
        parts = sampled_part(round_ref, weight_ref, quarter_ref, value_ref, lanes, comps)
        for c in range(comps):
            sampled_ref[c, 0, :, lanes] = part_ref[c : c + 1, lanes] + parts[c]


def whole(count):
    return [pl.BlockSpec(memory_space=pltpu.VMEM)] * count


def swap_pairs(axis):
    size = lax.axis_size(axis)
    if size % 2:
        raise ValueError("odd axis")
    far_pairs = [(i, (i - 1 if i % 2 == 0 else i + 1) % size) for i in range(size)]
    return far_pairs, [(i, i ^ 1) for i in range(size)]


def body(velocity, marker_cell, marker_frac, marker_force, fish_owner):
    levels, comps, cells_x, cells_y = velocity.shape
    slots = marker_cell.shape[3]
    items = levels * comps
    shape = (cells_x, cells_y, cells_x * lax.axis_size("gx"), cells_y * lax.axis_size("gy"))
    wide_x = cells_x + SPAN
    rows = cells_x + 2 * PAD
    chunk = min(512, slots)
    width = cells_y + LANES
    groups = -(-items // EDGE_PER)
    params = pltpu.CompilerParams(vmem_limit_bytes=32 * 1024 * 1024)
    edge_x = jax.ShapeDtypeStruct(((items + groups) * STRIP, LANES), jnp.bfloat16)
    half = (items, wide_x // 2, width)
    arrays = (fish_owner, velocity, marker_cell, marker_frac, marker_force)
    far_half, far, force, dense_y, quarter, value, quarter_y, value_y, level, parity, near_velocity = (
        pl.pallas_call(
        functools.partial(far_kernel, shape, slots),
        out_shape=(
            jax.ShapeDtypeStruct(half, jnp.float32),
            edge_x,
            jax.ShapeDtypeStruct((items, 2 * ROWS, slots), jnp.bfloat16),
            jax.ShapeDtypeStruct((width, slots), jnp.bfloat16),
            jax.ShapeDtypeStruct((ROWS, slots), jnp.int32),
            jax.ShapeDtypeStruct((ROWS, slots), jnp.float32),
            jax.ShapeDtypeStruct((ROWS, slots), jnp.int32),
            jax.ShapeDtypeStruct((ROWS, slots), jnp.float32),
            jax.ShapeDtypeStruct((1, slots), jnp.int32),
            jax.ShapeDtypeStruct((2, LANES), jnp.int32),
            jax.ShapeDtypeStruct(velocity.shape, velocity.dtype),
        ),
        in_specs=[pl.BlockSpec(memory_space=pltpu.HBM)] * 5,
        out_specs=tuple(whole(11)),
        scratch_shapes=[pltpu.VMEM(a.shape, a.dtype) for a in arrays if a is not velocity]
        + [pltpu.SemaphoreType.DMA((5,))],
        compiler_params=params,
        name="spread_far",
    )(*(pltpu.with_memory_space_constraint(a, pltpu.HBM) for a in arrays))
    )
    far_pairs, near_pairs = swap_pairs("gx")
    far_x = lax.ppermute(far, "gx", far_pairs)
    grid, near = pl.pallas_call(
        functools.partial(near_kernel, shape, slots),
        out_shape=(jax.ShapeDtypeStruct((items, wide_x, width), jnp.float32), edge_x),
        in_specs=whole(5),
        out_specs=tuple(whole(2)),
        scratch_shapes=[pltpu.VMEM(half, jnp.float32)],
        compiler_params=params,
        cost_estimate=pl.CostEstimate(
            flops=items * wide_x * width * slots, bytes_accessed=4 * items * wide_x * width,
            transcendentals=0,
        ),
        name="spread_near",
    )(near_velocity, far_half, force, dense_y, quarter)
    near_x = lax.ppermute(near, "gx", near_pairs)
    weights = jax.ShapeDtypeStruct((levels * LANES, slots), jnp.bfloat16)
    inner_weight, rim_weight, parity = pl.pallas_call(
        functools.partial(weight_kernel, shape, chunk),
        out_shape=(weights, weights, jax.ShapeDtypeStruct(parity.shape, parity.dtype)),
        in_specs=whole(4),
        out_specs=tuple(whole(3)),
        compiler_params=params,
        cost_estimate=pl.CostEstimate(
            flops=2 * levels * LANES * slots, bytes_accessed=4 * levels * LANES * slots,
            transcendentals=0,
        ),
        name="weights",
    )(parity, quarter_y, value_y, level)
    edge_y = jax.ShapeDtypeStruct((groups * (rows - ROWS) + SPAN, LANES), jnp.bfloat16)
    near, far = pl.pallas_call(
        functools.partial(pack_kernel, shape),
        out_shape=(edge_y, edge_y),
        in_specs=whole(4),
        out_specs=tuple(whole(2)),
        compiler_params=params,
        name="pack",
    )(parity, grid, far_x, near_x)
    far_pairs, near_pairs = swap_pairs("gy")
    near_y = lax.ppermute(near, "gy", near_pairs)
    far_y = lax.ppermute(far, "gy", far_pairs)
    field = pltpu.VMEM((items, rows + 2 * ROWS, LANES), jnp.float32)
    rounded = pltpu.VMEM((comps * wide_x, levels * LANES), jnp.bfloat16)
    inner, rim, part = pl.pallas_call(
        functools.partial(inner_kernel, shape, slots, levels),
        out_shape=(
            jax.ShapeDtypeStruct((items, cells_x, LANES), jnp.float32),
            jax.ShapeDtypeStruct((items, rows, LANES), jnp.float32),
            jax.ShapeDtypeStruct((comps, slots), jnp.float32),
        ),
        in_specs=whole(7),
        out_specs=tuple(whole(3)),
        scratch_shapes=[field, field, field, rounded],
        compiler_params=params,
        cost_estimate=pl.CostEstimate(
            flops=2 * items * wide_x * LANES * slots, bytes_accessed=16 * items * rows * LANES,
            transcendentals=0,
        ),
        name="inner",
    )(parity, quarter, value, inner_weight, grid, far_x, near_x)
    return pl.pallas_call(
        functools.partial(finish_kernel, shape, slots),
        out_shape=(
            jax.ShapeDtypeStruct(velocity.shape, jnp.float32),
            jax.ShapeDtypeStruct((comps, 1, 1, slots), jnp.float32),
        ),
        in_specs=whole(9),
        out_specs=tuple(whole(2)),
        scratch_shapes=[field, field, field, rounded],
        compiler_params=params,
        name="finish",
    )(parity, quarter, value, rim_weight, inner, rim, part, near_y, far_y)


def solution(mesh):
    placed = (
        P(None, None, "gx", "gy"),
        P(None, "gx", "gy", None),
        P(None, "gx", "gy", None),
        P(None, "gx", "gy", None),
        P(),
    )
    return jax.shard_map(
        body,
        mesh=mesh,
        in_specs=placed,
        out_specs=(P(None, None, "gx", "gy"), P(None, "gx", "gy", None)),
        check_vma=False,
    )
```

```python
import functools

import jax
import jax.numpy as jnp
import numpy as np
from jax import lax
from jax.experimental import pallas as pl
from jax.experimental.pallas import tpu as pltpu
from jax.sharding import PartitionSpec as P

MARGIN = 16
FISH_MARK = 1024
HALO = 3
LANES = 128
COURANT = 0.25
VISCOUS = 1.5
ROWS = 8
STEP = 2 * ROWS

REACH = MARGIN + HALO
PAD = -(-REACH // ROWS) * ROWS
STRIP = PAD + MARGIN
SPAN = 2 * MARGIN
EDGE_PER = LANES // SPAN


def half_turn(terms):
    nodes = 0.5 - 0.5 * np.cos(np.pi * (np.arange(64) + 0.5) / 64)
    square = nodes * nodes
    cosine = np.polynomial.polynomial.polyfit(square, np.cos(0.5 * np.pi * nodes), terms)
    sine = np.polynomial.polynomial.polyfit(square, np.sin(0.5 * np.pi * nodes) / nodes, terms)
    return [float(v) for v in cosine], [float(v) for v in sine]


COS_FIT, SIN_FIT = half_turn(6)


def horner(coefficients, value):
    total = jnp.full_like(value, coefficients[-1])
    for coefficient in coefficients[-2::-1]:
        total = total * value + coefficient
    return total


def four_weights(frac):
    square = frac * frac
    cosine = horner(COS_FIT, square)
    sine = frac * horner(SIN_FIT, square)
    return (0.25 - 0.25 * sine, 0.25 + 0.25 * cosine, 0.25 + 0.25 * sine, 0.25 - 0.25 * cosine)


def local_cell(cell, low, extent):
    offset = cell - low
    offset = jnp.where(offset < -MARGIN, offset + extent, offset)
    return jnp.where(offset >= extent - MARGIN, offset - extent, offset)


def position():
    row, col = lax.axis_index("gx"), lax.axis_index("gy")
    return row, col, (row & 1) == 0, (col & 1) == 0


def tile_weights(offset, weights):
    shift = lax.broadcasted_iota(jnp.int32, (ROWS, offset.shape[1]), 0) + 1 - offset
    quarter, phase = shift >> 2, shift & 3
    value = jnp.where(phase == 3, weights[3], weights[2])
    value = jnp.where(phase == 1, weights[1], value)
    return quarter, jnp.where(phase == 0, weights[0], value)


def doubled(quarter, value):
    quarter = jnp.concatenate([quarter, quarter + 2], axis=0).astype(jnp.float32)
    return quarter.astype(jnp.bfloat16), twice(value)


def twice(value):
    return jnp.concatenate([value, value], axis=0).astype(jnp.bfloat16)


def picked_tile(quarter, value, first):
    zero = jnp.zeros_like(value)
    return jnp.where(quarter == jnp.array(-first // 4, quarter.dtype), value, zero)


def half_spread(quarter_ref, force_ref, dense_y_ref, half_ref, base, lanes):
    items, rows = half_ref.shape[:2]
    quarter = quarter_ref[:, lanes] + base
    quarter = jnp.concatenate([quarter, quarter + 2], axis=0).astype(jnp.float32)
    quarter = quarter.astype(jnp.bfloat16)
    left = jnp.concatenate(
        [
            picked_tile(quarter, force_ref[k, :, lanes], row)
            for k in range(items)
            for row in range(0, rows, 2 * ROWS)
        ],
        axis=0,
    )
    total = lax.dot_general(
        left, dense_y_ref[:, lanes], (((1,), (1,)), ((), ())),
        preferred_element_type=jnp.float32,
    )
    total = total.reshape(half_ref.shape)
    if lanes.start:
        half_ref[...] += total
    else:
        half_ref[...] = total


def finish_half(half_ref, velocity_ref, out_ref, low, cells_y):
    items, rows = half_ref.shape[:2]
    comps = items // velocity_ref.shape[0]
    count = rows - MARGIN
    source = pl.ds(pl.multiple_of(jnp.where(low, 0, count), ROWS), count)
    target = pl.ds(pl.multiple_of(jnp.where(low, MARGIN, 0), ROWS), count)
    for k in range(items):
        half_ref[k, target, :cells_y] += velocity_ref[k // comps, k % comps, source]
    place = pl.ds(pl.multiple_of(jnp.where(low, 0, rows - STRIP), ROWS), STRIP)
    parts = [half_ref[k, place, :cells_y] for k in range(items)]
    for group in range(0, items, EDGE_PER):
        edges = []
        for k in range(group, min(group + EDGE_PER, items)):
            edges.append(rolled(half_ref[k, place, cells_y:], SPAN * (k - group)))
        parts.append(functools.reduce(jnp.add, edges))
    out_ref[...] = jnp.concatenate(parts, axis=0).astype(jnp.bfloat16)


def far_kernel(
    shape, chunk, fish_hbm, velocity_hbm, cell_hbm, frac_hbm, force_hbm,
    half_ref, far_ref, force_out, dense_y_ref, quarter_ref, value_ref,
    quarter_y_ref, value_y_ref, level_ref, parity_ref, velocity_ref,
    fish_ref, cell_ref, frac_ref, force_ref, sems,
):
    pairs = (
        (cell_hbm, cell_ref), (frac_hbm, frac_ref), (fish_hbm, fish_ref),
        (force_hbm, force_ref), (velocity_hbm, velocity_ref),
    )
    copies = [pltpu.make_async_copy(a, b, sems.at[i]) for i, (a, b) in enumerate(pairs)]
    for copy in copies:
        copy.start()
    cells_x, cells_y, extent_x, extent_y = shape
    levels, comps = velocity_ref.shape[:2]
    slots = cell_ref.shape[3]
    row, col, even, even_y = position()
    parity_ref[0:1] = jnp.full((1, LANES), jnp.where(even, 1, 0), jnp.int32)
    parity_ref[1:2] = jnp.full((1, LANES), jnp.where(even_y, 1, 0), jnp.int32)
    base = jnp.where(even, -MARGIN // 4, cells_x // 8)
    for copy in copies[:-1]:
        copy.wait()
    mine = jnp.where(fish_ref[...] == row * lax.axis_size("gy") + col, 1.0, 0.0)
    count = FISH_MARK * jnp.sum(mine)
    level_ref[...] = cell_ref[2, 0]
    for first in range(0, slots, chunk):
        lanes = slice(first, first + chunk)
        offset_x = local_cell(cell_ref[0, 0, :, lanes], row * cells_x, extent_x)
        offset_y = local_cell(cell_ref[1, 0, :, lanes], col * cells_y, extent_y)
        slot = lax.broadcasted_iota(jnp.int32, (1, chunk), 1) + first
        alive = jnp.where(slot.astype(jnp.float32) < count, 1.0, 0.0)
        quarter, value = tile_weights(offset_x, four_weights(frac_ref[0, 0, :, lanes]))
        value = value * alive
        quarter_ref[:, lanes] = quarter
        value_ref[:, lanes] = value
        level = cell_ref[2, 0, :, lanes]
        pushes = [force_ref[c, 0, :, lanes] * value for c in range(comps)]
        for l in range(levels):
            for c in range(comps):
                force_out[l * comps + c, :, lanes] = twice(jnp.where(level == l, pushes[c], 0.0))
        quarter, value = tile_weights(offset_y, four_weights(frac_ref[1, 0, :, lanes]))
        quarter_y_ref[:, lanes] = quarter
        value_y_ref[:, lanes] = value
        quarter, value = doubled(quarter, value)
        dense_y_ref[:, lanes] = jnp.concatenate(
            [picked_tile(quarter, value, n) for n in range(0, cells_y + MARGIN, 2 * ROWS)]
            + [jnp.zeros((LANES - SPAN, chunk), jnp.bfloat16)]
            + [picked_tile(quarter, value, n) for n in range(-MARGIN, 0, 2 * ROWS)],
            axis=0,
        )
        half_spread(quarter_ref, force_out, dense_y_ref, half_ref, base, lanes)
    copies[-1].wait()
    finish_half(half_ref, velocity_ref, far_ref, even, cells_y)


def near_kernel(
    shape, chunk, velocity_ref, far_half_ref, force_ref, dense_y_ref, quarter_ref,
    grid_ref, near_ref, half_ref,
):
    cells_x, cells_y, _, _ = shape
    slots = quarter_ref.shape[1]
    rows = half_ref.shape[1]
    _, _, even, _ = position()
    base = jnp.where(even, cells_x // 8, -MARGIN // 4)
    for first in range(0, slots, chunk):
        lanes = slice(first, first + chunk)
        half_spread(quarter_ref, force_ref, dense_y_ref, half_ref, base, lanes)
    finish_half(half_ref, velocity_ref, near_ref, jnp.logical_not(even), cells_y)
    for ref, row in ((far_half_ref, jnp.where(even, 0, rows)), (half_ref, jnp.where(even, rows, 0))):
        place = pl.ds(pl.multiple_of(row, ROWS), rows)
        for k in range(ref.shape[0]):
            grid_ref[k, place] = ref[k]


def rolled(value, shift):
    shift = shift % LANES
    return pltpu.roll(value, shift, 1) if shift else value


def lane_index(rows):
    return lax.broadcasted_iota(jnp.int32, (rows, LANES), 1)


def ordered(parity, near_ref, far_ref):
    even = jnp.broadcast_to(parity, near_ref.shape) != 0
    near, far = near_ref[...].astype(jnp.float32), far_ref[...].astype(jnp.float32)
    return jnp.where(even, far, near), jnp.where(even, near, far)


def joined(center, before, after):
    wide = center.shape[0]
    near = PAD - MARGIN
    overlap = STRIP - near
    return jnp.concatenate(
        [
            before[:near],
            center[:overlap] + before[near:],
            center[overlap : wide - overlap],
            center[wide - overlap :] + after[:overlap],
            after[overlap:],
        ],
        axis=0,
    )


def extended_rows(parity, grid_ref, near_ref, far_ref, cells_y):
    items = grid_ref.shape[0]
    groups = -(-items // EDGE_PER)
    size = groups * STRIP
    before, after = ordered(parity, near_ref, far_ref)
    packed = jnp.concatenate([before[items * STRIP :], after[items * STRIP :]], axis=0)
    lane = lane_index(2 * size)
    kept = (lane < MARGIN) | (lane >= LANES - MARGIN)
    edges = [jnp.where(kept, rolled(packed, -SPAN * slot), 0.0) for slot in range(EDGE_PER)]
    for k in range(items):
        place = slice(k * STRIP, (k + 1) * STRIP)
        inner = joined(grid_ref[k, :, :cells_y], before[place], after[place])
        start = k // EDGE_PER * STRIP
        edge = edges[k % EDGE_PER]
        edge = joined(
            grid_ref[k, :, cells_y:],
            edge[start : start + STRIP],
            edge[size + start : size + start + STRIP],
        )
        yield k, inner, edge


def pack_kernel(shape, parity_ref, grid_ref, far_x, near_x, near_ref, far_ref):
    cells_x, cells_y, _, _ = shape
    items = grid_ref.shape[0]
    groups = -(-items // EDGE_PER)
    rows = cells_x + 2 * PAD
    lane = lane_index(rows)
    up_halo = (lane >= LANES - REACH) & (lane < LANES - MARGIN)
    down_halo = (lane >= MARGIN) & (lane < REACH)
    halos, ups, downs = None, None, None
    packed = [[], []]
    for k, inner, edge in extended_rows(parity_ref[0:1], grid_ref, near_x, far_x, cells_y):
        slot = k % EDGE_PER
        up = rolled(jnp.where(lane >= LANES - MARGIN, inner, edge), SPAN * slot)
        down = rolled(jnp.where(lane < MARGIN, inner, edge), SPAN * slot)
        halo = rolled(jnp.where(up_halo | down_halo, inner, 0.0), REACH + HALO * k)
        ups = ups + up if slot else up
        downs = downs + down if slot else down
        halos = halos + halo if k else halo
        if slot == EDGE_PER - 1 or k == items - 1:
            packed[0].append(squeezed(ups))
            packed[1].append(squeezed(downs))
    halos = squeezed(halos)
    rows = halos.shape[0]
    used = lane_index(rows) < HALO * items
    ups = jnp.where(used, halos, 0.0)
    downs = jnp.where(used, rolled(halos, -MARGIN - REACH), 0.0)
    folded = None
    for row in range(0, rows, SPAN):
        size = min(SPAN, rows - row)
        parts = [value[row : row + size] for value in (ups, downs)]
        if size < SPAN:
            parts = [jnp.concatenate([p, jnp.zeros((SPAN - size, LANES), p.dtype)], 0) for p in parts]
        part = rolled(jnp.concatenate(parts, axis=0), row)
        folded = folded + part if row else part
    up = jnp.concatenate(packed[0] + [folded[:SPAN]], axis=0)
    down = jnp.concatenate(packed[1] + [folded[SPAN:]], axis=0)
    even = jnp.broadcast_to(parity_ref[1:2], up.shape) != 0
    near_ref[...] = jnp.where(even, up, down).astype(jnp.bfloat16)
    far_ref[...] = jnp.where(even, down, up).astype(jnp.bfloat16)


def squeezed(value):
    row = lax.broadcasted_iota(jnp.int32, (ROWS, LANES), 0)
    shared = jnp.where(row >= PAD - REACH, value[:ROWS], value[-ROWS:])
    return jnp.concatenate([shared, value[ROWS:-ROWS]], axis=0)


def expanded(value):
    return jnp.concatenate([value, value[:ROWS]], axis=0)


def around(ref, k, start, size):
    center = ref[k, start : start + size]
    back = ref[k, start - 1 : start - 1 + size]
    fore = ref[k, start + 1 : start + 1 + size]
    return center, back, fore, rolled(center, 1), rolled(center, -1)


def advect(moved_ref, carried_ref, levels, comps, rows):
    for start in range(ROWS, ROWS + rows, STEP):
        for l in range(levels):
            pieces = [around(moved_ref, l * comps + c, start, STEP) for c in range(comps)]
            speed_x, speed_y = COURANT * pieces[0][0], COURANT * pieces[1][0]
            ahead_x, astern_x = jnp.maximum(speed_x, 0.0), jnp.minimum(speed_x, 0.0)
            ahead_y, astern_y = jnp.maximum(speed_y, 0.0), jnp.minimum(speed_y, 0.0)
            for c in range(comps):
                center, back, fore, below, above = pieces[c]
                change = ahead_x * (center - back) + astern_x * (fore - center)
                change = change + ahead_y * (center - below) + astern_y * (above - center)
                carried_ref[l * comps + c, start : start + STEP] = center - change


def sweep(ref, carried_ref, levels, comps, start, size):
    scale = 1.0 / (1.0 + 6.0 * VISCOUS)
    centers, results = [], []
    for k in range(levels * comps):
        center, back, fore, below, above = around(ref, k, start, size)
        centers.append(center)
        results.append(back + fore + below + above)
    for k in range(levels * comps):
        higher = min(k // comps + 1, levels - 1) * comps + k % comps
        lower = max(k // comps - 1, 0) * comps + k % comps
        summed = results[k] + centers[higher] + centers[lower]
        source = carried_ref[k, start : start + size]
        results[k] = scale * source + (VISCOUS * scale) * summed
    return results


def first_steps(moved_ref, carried_ref, sweep_ref, levels, comps, rows):
    advect(moved_ref, carried_ref, levels, comps, rows)
    for start in range(ROWS, ROWS + rows, STEP):
        results = sweep(carried_ref, carried_ref, levels, comps, start, STEP)
        for k in range(levels * comps):
            sweep_ref[k, start : start + STEP] = results[k]


RIM = REACH + HALO
HALF = LANES // 2


def weight_kernel(
    shape, chunk, parity_ref, quarter_ref, value_ref, level_ref, inner_ref, rim_ref, parity_out
):
    parity_out[...] = parity_ref[...]
    _, cells_y, _, _ = shape
    slots = quarter_ref.shape[1]
    size = 2 * ROWS
    levels = inner_ref.shape[0] // LANES
    row = lax.broadcasted_iota(jnp.int32, (size, chunk), 0)

    def cut(tile, keep):
        return jnp.where(keep, tile.astype(jnp.float32), 0.0).astype(jnp.bfloat16)

    for first in range(0, slots, chunk):
        lanes = slice(first, first + chunk)
        level = level_ref[:, lanes]
        for l in range(levels):
            value = jnp.where(level == l, value_ref[:, lanes], 0.0)
            quarter, value = doubled(quarter_ref[:, lanes], value)
            for start in range(0, LANES, size):
                inner = picked_tile(quarter, value, start)
                if start < REACH:
                    inner = cut(inner, row + start >= REACH)
                if start + size > cells_y - REACH:
                    inner = cut(inner, row + start < cells_y - REACH)
                if start >= LANES - MARGIN:
                    rim = picked_tile(quarter, value, start - LANES)
                elif start + size > HALF - REACH and start < HALF + MARGIN:
                    rim = picked_tile(quarter, value, start + cells_y - HALF)
                    rim = cut(rim, row + start >= HALF - REACH) if start < HALF - REACH else rim
                elif start < REACH:
                    rim = picked_tile(quarter, value, start)
                    rim = cut(rim, row + start < REACH) if start + size > REACH else rim
                else:
                    rim = jnp.zeros_like(value)
                place = slice(l * LANES + start, l * LANES + start + size)
                inner_ref[place, lanes] = inner
                rim_ref[place, lanes] = rim


def sampled_part(round_ref, weight_ref, quarter_ref, value_ref, lanes, comps):
    wide_x = round_ref.shape[0] // comps
    partial = jnp.dot(round_ref[...], weight_ref[:, lanes], preferred_element_type=jnp.float32)
    quarter, value = quarter_ref[:, lanes], value_ref[:, lanes]
    totals = [jnp.zeros_like(value)] * comps
    for row in range(0, wide_x, ROWS):
        here = quarter == (MARGIN - row) // 4
        for c in range(comps):
            start = c * wide_x + row
            totals[c] = jnp.where(here, partial[start : start + ROWS], totals[c])
    return [jnp.sum(total * value, axis=0, keepdims=True) for total in totals]


def inner_kernel(
    shape, chunk, levels, parity_ref, quarter_ref, value_ref, weight_ref, grid_ref, far_x, near_x,
    inner_ref, rim_ref, sampled_ref, moved_ref, carried_ref, sweep_ref, round_ref,
):
    cells_x, cells_y, _, _ = shape
    items = grid_ref.shape[0]
    comps = items // levels
    slots = quarter_ref.shape[1]
    wide_x = cells_x + SPAN
    rows = cells_x + 2 * PAD
    lane = lane_index(rows)
    for k, inner, edge in extended_rows(parity_ref[0:1], grid_ref, near_x, far_x, cells_y):
        moved_ref[k, ROWS : ROWS + rows] = inner
        low = jnp.where(lane < RIM, inner, jnp.where(lane >= LANES - MARGIN, edge, 0.0))
        high = jnp.where(lane >= LANES - RIM, inner, jnp.where(lane < MARGIN, edge, 0.0))
        rim_ref[k] = low + rolled(high, HALF)
    first_steps(moved_ref, carried_ref, sweep_ref, levels, comps, rows)
    size = 2 * ROWS
    for row in range(0, wide_x, size):
        start = ROWS + PAD - MARGIN + row
        results = sweep(sweep_ref, carried_ref, levels, comps, start, size)
        for k in range(items):
            level, c = k // comps, k % comps
            place = slice(c * wide_x + row, c * wide_x + row + size)
            round_ref[place, level * LANES : (level + 1) * LANES] = results[k].astype(jnp.bfloat16)
            if MARGIN <= row < MARGIN + cells_x:
                inner_ref[k, row - MARGIN : row - MARGIN + size] = results[k]
    for first in range(0, slots, chunk):
        lanes = slice(first, first + chunk)
        parts = sampled_part(round_ref, weight_ref, quarter_ref, value_ref, lanes, comps)
        for c in range(comps):
            sampled_ref[c : c + 1, lanes] = parts[c]


def unfolded(folded, rows):
    return expanded(
        jnp.concatenate(
            [rolled(folded, -row)[: min(SPAN, rows - row)] for row in range(0, rows, SPAN)], axis=0
        )
    )


def finish_kernel(
    shape, chunk, parity_ref, quarter_ref, value_ref, weight_ref, inner_ref, rim_ref, part_ref,
    near_y, far_y, next_hbm, sampled_hbm,
    moved_ref, carried_ref, sweep_ref, round_ref, next_ref, sampled_ref, sems,
):
    cells_x, cells_y, _, _ = shape
    items = rim_ref.shape[0]
    groups = -(-items // EDGE_PER)
    levels, comps = next_ref.shape[:2]
    slots = quarter_ref.shape[1]
    wide_x = cells_x + SPAN
    rows = cells_x + 2 * PAD
    lane = lane_index(rows)
    befores, afters = ordered(parity_ref[1:2], near_y, far_y)
    turned = HALF + MARGIN + REACH
    high_halo = (lane >= turned) & (lane < turned + HALO * items)
    both = ((lane + MARGIN) & (HALF - 1)) < SPAN
    outer = ((lane >= LANES - REACH) & (lane < LANES - MARGIN)) | (
        (lane >= HALF + MARGIN) & (lane < HALF + REACH)
    )
    size = rows - ROWS
    halo = jnp.where(
        high_halo,
        rolled(unfolded(afters[groups * size :], size), turned),
        unfolded(befores[groups * size :], size),
    )
    for group in range(groups):
        before = expanded(befores[group * size : (group + 1) * size])
        after = expanded(rolled(afters[group * size : (group + 1) * size], HALF))
        for k in range(group * EDGE_PER, min((group + 1) * EDGE_PER, items)):
            slot = k % EDGE_PER
            window = ((lane + (LANES + MARGIN - SPAN * slot)) & (LANES - 1)) < SPAN
            main = rolled(jnp.where(window, before, after), -SPAN * slot)
            value = rim_ref[k] + jnp.where(both, main, 0.0)
            value = jnp.where(outer, rolled(halo, -REACH - HALO * k), value)
            moved_ref[k, ROWS : ROWS + rows] = value

    first_steps(moved_ref, carried_ref, sweep_ref, levels, comps, rows)
    size = 2 * ROWS
    lane = lane_index(size)
    for row in range(0, wide_x, size):
        start = ROWS + PAD - MARGIN + row
        results = sweep(sweep_ref, carried_ref, levels, comps, start, size)
        for k in range(items):
            level, c = k // comps, k % comps
            place = slice(c * wide_x + row, c * wide_x + row + size)
            round_ref[place, level * LANES : (level + 1) * LANES] = results[k].astype(jnp.bfloat16)
        if not MARGIN <= row < MARGIN + cells_x:
            continue
        place = slice(row - MARGIN, row - MARGIN + size)
        for k in range(items):
            low, high = results[k], rolled(results[k], HALF)
            inner = inner_ref[k, place]
            inner = jnp.where(lane < REACH, low, jnp.where(lane >= LANES - REACH, high, inner))
            next_ref[k // comps, k % comps, place] = inner

    for first in range(0, slots, chunk):
        lanes = slice(first, first + chunk)
        parts = sampled_part(round_ref, weight_ref, quarter_ref, value_ref, lanes, comps)
        for c in range(comps):
            sampled_ref[c, 0, :, lanes] = part_ref[c : c + 1, lanes] + parts[c]
    pieces = [(next_ref.at[k // comps, k % comps], next_hbm.at[k // comps, k % comps]) for k in range(items)]
    pieces.append((sampled_ref, sampled_hbm))
    copies = [pltpu.make_async_copy(a, b, sems.at[i]) for i, (a, b) in enumerate(pieces)]
    for copy in copies:
        copy.start()
    for copy in copies:
        copy.wait()


def whole(count):
    return [pl.BlockSpec(memory_space=pltpu.VMEM)] * count


def swap_pairs(axis):
    size = lax.axis_size(axis)
    if size % 2:
        raise ValueError("odd axis")
    far_pairs = [(i, (i - 1 if i % 2 == 0 else i + 1) % size) for i in range(size)]
    return far_pairs, [(i, i ^ 1) for i in range(size)]


def body(velocity, marker_cell, marker_frac, marker_force, fish_owner):
    levels, comps, cells_x, cells_y = velocity.shape
    slots = marker_cell.shape[3]
    items = levels * comps
    shape = (cells_x, cells_y, cells_x * lax.axis_size("gx"), cells_y * lax.axis_size("gy"))
    wide_x = cells_x + SPAN
    rows = cells_x + 2 * PAD
    chunk = min(512, slots)
    width = cells_y + LANES
    groups = -(-items // EDGE_PER)
    params = pltpu.CompilerParams(vmem_limit_bytes=32 * 1024 * 1024)
    edge_x = jax.ShapeDtypeStruct(((items + groups) * STRIP, LANES), jnp.bfloat16)
    half = (items, wide_x // 2, width)
    arrays = (fish_owner, velocity, marker_cell, marker_frac, marker_force)
    far_half, far, force, dense_y, quarter, value, quarter_y, value_y, level, parity, near_velocity = (
        pl.pallas_call(
        functools.partial(far_kernel, shape, slots),
        out_shape=(
            jax.ShapeDtypeStruct(half, jnp.float32),
            edge_x,
            jax.ShapeDtypeStruct((items, 2 * ROWS, slots), jnp.bfloat16),
            jax.ShapeDtypeStruct((width, slots), jnp.bfloat16),
            jax.ShapeDtypeStruct((ROWS, slots), jnp.int32),
            jax.ShapeDtypeStruct((ROWS, slots), jnp.float32),
            jax.ShapeDtypeStruct((ROWS, slots), jnp.int32),
            jax.ShapeDtypeStruct((ROWS, slots), jnp.float32),
            jax.ShapeDtypeStruct((1, slots), jnp.int32),
            jax.ShapeDtypeStruct((2, LANES), jnp.int32),
            jax.ShapeDtypeStruct(velocity.shape, velocity.dtype),
        ),
        in_specs=[pl.BlockSpec(memory_space=pltpu.HBM)] * 5,
        out_specs=tuple(whole(11)),
        scratch_shapes=[pltpu.VMEM(a.shape, a.dtype) for a in arrays if a is not velocity]
        + [pltpu.SemaphoreType.DMA((5,))],
        compiler_params=params,
        name="spread_far",
    )(*(pltpu.with_memory_space_constraint(a, pltpu.HBM) for a in arrays))
    )
    far_pairs, near_pairs = swap_pairs("gx")
    far_x = lax.ppermute(far, "gx", far_pairs)
    grid, near = pl.pallas_call(
        functools.partial(near_kernel, shape, slots),
        out_shape=(jax.ShapeDtypeStruct((items, wide_x, width), jnp.float32), edge_x),
        in_specs=whole(5),
        out_specs=tuple(whole(2)),
        scratch_shapes=[pltpu.VMEM(half, jnp.float32)],
        compiler_params=params,
        cost_estimate=pl.CostEstimate(
            flops=items * wide_x * width * slots, bytes_accessed=4 * items * wide_x * width,
            transcendentals=0,
        ),
        name="spread_near",
    )(near_velocity, far_half, force, dense_y, quarter)
    near_x = lax.ppermute(near, "gx", near_pairs)
    weights = jax.ShapeDtypeStruct((levels * LANES, slots), jnp.bfloat16)
    inner_weight, rim_weight, parity = pl.pallas_call(
        functools.partial(weight_kernel, shape, chunk),
        out_shape=(weights, weights, jax.ShapeDtypeStruct(parity.shape, parity.dtype)),
        in_specs=whole(4),
        out_specs=tuple(whole(3)),
        compiler_params=params,
        cost_estimate=pl.CostEstimate(
            flops=2 * levels * LANES * slots, bytes_accessed=4 * levels * LANES * slots,
            transcendentals=0,
        ),
        name="weights",
    )(parity, quarter_y, value_y, level)
    edge_y = jax.ShapeDtypeStruct((groups * (rows - ROWS) + SPAN, LANES), jnp.bfloat16)
    near, far = pl.pallas_call(
        functools.partial(pack_kernel, shape),
        out_shape=(edge_y, edge_y),
        in_specs=whole(4),
        out_specs=tuple(whole(2)),
        compiler_params=params,
        name="pack",
    )(parity, grid, far_x, near_x)
    far_pairs, near_pairs = swap_pairs("gy")
    near_y = lax.ppermute(near, "gy", near_pairs)
    far_y = lax.ppermute(far, "gy", far_pairs)
    field = pltpu.VMEM((items, rows + 2 * ROWS, LANES), jnp.float32)
    rounded = pltpu.VMEM((comps * wide_x, levels * LANES), jnp.bfloat16)
    inner, rim, part = pl.pallas_call(
        functools.partial(inner_kernel, shape, chunk, levels),
        out_shape=(
            jax.ShapeDtypeStruct((items, cells_x, LANES), jnp.float32),
            jax.ShapeDtypeStruct((items, rows, LANES), jnp.float32),
            jax.ShapeDtypeStruct((comps, slots), jnp.float32),
        ),
        in_specs=whole(7),
        out_specs=tuple(whole(3)),
        scratch_shapes=[field, field, field, rounded],
        compiler_params=params,
        cost_estimate=pl.CostEstimate(
            flops=2 * items * wide_x * LANES * slots, bytes_accessed=16 * items * rows * LANES,
            transcendentals=0,
        ),
        name="inner",
    )(parity, quarter, value, inner_weight, grid, far_x, near_x)
    return pl.pallas_call(
        functools.partial(finish_kernel, shape, chunk),
        out_shape=(
            jax.ShapeDtypeStruct(velocity.shape, jnp.float32),
            jax.ShapeDtypeStruct((comps, 1, 1, slots), jnp.float32),
        ),
        in_specs=whole(9),
        out_specs=(pl.BlockSpec(memory_space=pltpu.HBM),) * 2,
        scratch_shapes=[field, field, field, rounded, pltpu.VMEM(velocity.shape, velocity.dtype)]
        + [pltpu.VMEM((comps, 1, 1, slots), jnp.float32), pltpu.SemaphoreType.DMA((items + 1,))],
        compiler_params=params,
        name="finish",
    )(parity, quarter, value, rim_weight, inner, rim, part, near_y, far_y)


def solution(mesh):
    placed = (
        P(None, None, "gx", "gy"),
        P(None, "gx", "gy", None),
        P(None, "gx", "gy", None),
        P(None, "gx", "gy", None),
        P(),
    )
    return jax.shard_map(
        body,
        mesh=mesh,
        in_specs=placed,
        out_specs=(P(None, None, "gx", "gy"), P(None, "gx", "gy", None)),
        check_vma=False,
    )
```

```python
import functools

import jax
import jax.numpy as jnp
import numpy as np
from jax import lax
from jax.experimental import pallas as pl
from jax.experimental.pallas import tpu as pltpu
from jax.sharding import PartitionSpec as P

MARGIN = 16
FISH_MARK = 1024
HALO = 3
LANES = 128
COURANT = 0.25
VISCOUS = 1.5
ROWS = 8
STEP = 2 * ROWS

REACH = MARGIN + HALO
PAD = -(-REACH // ROWS) * ROWS
STRIP = PAD + MARGIN
SPAN = 2 * MARGIN
EDGE_PER = LANES // SPAN


def half_turn(terms):
    nodes = 0.5 - 0.5 * np.cos(np.pi * (np.arange(64) + 0.5) / 64)
    square = nodes * nodes
    cosine = np.polynomial.polynomial.polyfit(square, np.cos(0.5 * np.pi * nodes), terms)
    sine = np.polynomial.polynomial.polyfit(square, np.sin(0.5 * np.pi * nodes) / nodes, terms)
    return [float(v) for v in cosine], [float(v) for v in sine]


COS_FIT, SIN_FIT = half_turn(6)


def horner(coefficients, value):
    total = jnp.full_like(value, coefficients[-1])
    for coefficient in coefficients[-2::-1]:
        total = total * value + coefficient
    return total


def four_weights(frac):
    square = frac * frac
    cosine = horner(COS_FIT, square)
    sine = frac * horner(SIN_FIT, square)
    return (0.25 - 0.25 * sine, 0.25 + 0.25 * cosine, 0.25 + 0.25 * sine, 0.25 - 0.25 * cosine)


def local_cell(cell, low, extent):
    offset = cell - low
    offset = jnp.where(offset < -MARGIN, offset + extent, offset)
    return jnp.where(offset >= extent - MARGIN, offset - extent, offset)


def position():
    row, col = lax.axis_index("gx"), lax.axis_index("gy")
    return row, col, (row & 1) == 0, (col & 1) == 0


def tile_weights(offset, weights):
    shift = lax.broadcasted_iota(jnp.int32, (ROWS, offset.shape[1]), 0) + 1 - offset
    quarter, phase = shift >> 2, shift & 3
    value = jnp.where(phase == 3, weights[3], weights[2])
    value = jnp.where(phase == 1, weights[1], value)
    return quarter, jnp.where(phase == 0, weights[0], value)


def doubled(quarter, value):
    quarter = jnp.concatenate([quarter, quarter + 2], axis=0).astype(jnp.float32)
    return quarter.astype(jnp.bfloat16), twice(value)


def twice(value):
    return jnp.concatenate([value, value], axis=0).astype(jnp.bfloat16)


def picked_tile(quarter, value, first):
    zero = jnp.zeros_like(value)
    return jnp.where(quarter == jnp.array(-first // 4, quarter.dtype), value, zero)


def half_spread(quarter_ref, force_ref, dense_y_ref, half_ref, base, lanes):
    items, rows = half_ref.shape[:2]
    quarter = quarter_ref[:, lanes] + base
    quarter = jnp.concatenate([quarter, quarter + 2], axis=0).astype(jnp.float32)
    quarter = quarter.astype(jnp.bfloat16)
    left = jnp.concatenate(
        [
            picked_tile(quarter, force_ref[k, :, lanes], row)
            for k in range(items)
            for row in range(0, rows, 2 * ROWS)
        ],
        axis=0,
    )
    total = lax.dot_general(
        left, dense_y_ref[:, lanes], (((1,), (1,)), ((), ())),
        preferred_element_type=jnp.float32,
    )
    total = total.reshape(half_ref.shape)
    if lanes.start:
        half_ref[...] += total
    else:
        half_ref[...] = total


def finish_half(half_ref, velocity_ref, out_ref, low, cells_y):
    items, rows = half_ref.shape[:2]
    comps = items // velocity_ref.shape[0]
    count = rows - MARGIN
    source = pl.ds(pl.multiple_of(jnp.where(low, 0, count), ROWS), count)
    target = pl.ds(pl.multiple_of(jnp.where(low, MARGIN, 0), ROWS), count)
    for k in range(items):
        half_ref[k, target, :cells_y] += velocity_ref[k // comps, k % comps, source]
    place = pl.ds(pl.multiple_of(jnp.where(low, 0, rows - STRIP), ROWS), STRIP)
    parts = [half_ref[k, place, :cells_y] for k in range(items)]
    for group in range(0, items, EDGE_PER):
        edges = []
        for k in range(group, min(group + EDGE_PER, items)):
            edges.append(rolled(half_ref[k, place, cells_y:], SPAN * (k - group)))
        parts.append(functools.reduce(jnp.add, edges))
    out_ref[...] = jnp.concatenate(parts, axis=0).astype(jnp.bfloat16)


def far_kernel(
    shape, fish_hbm, velocity_hbm, cell_hbm, frac_hbm, force_hbm,
    half_ref, far_ref, force_out, dense_y_ref, quarter_ref, value_ref,
    quarter_y_ref, value_y_ref, level_ref, parity_ref, velocity_ref,
    fish_ref, cell_ref, frac_ref, force_ref, sems,
):
    pairs = (
        (cell_hbm, cell_ref), (frac_hbm, frac_ref), (fish_hbm, fish_ref),
        (force_hbm, force_ref), (velocity_hbm, velocity_ref),
    )
    copies = [pltpu.make_async_copy(a, b, sems.at[i]) for i, (a, b) in enumerate(pairs)]
    for copy in copies:
        copy.start()
    cells_x, cells_y, extent_x, extent_y = shape
    levels, comps = velocity_ref.shape[:2]
    slots = cell_ref.shape[3]
    row, col, even, even_y = position()
    parity_ref[0:1] = jnp.full((1, LANES), jnp.where(even, 1, 0), jnp.int32)
    parity_ref[1:2] = jnp.full((1, LANES), jnp.where(even_y, 1, 0), jnp.int32)
    base = jnp.where(even, -MARGIN // 4, cells_x // 8)
    for copy in copies[:2]:
        copy.wait()
    level_ref[...] = cell_ref[2, 0]
    offset_x = local_cell(cell_ref[0, 0], row * cells_x, extent_x)
    offset_y = local_cell(cell_ref[1, 0], col * cells_y, extent_y)
    quarter_x, value_x = tile_weights(offset_x, four_weights(frac_ref[0, 0]))
    quarter_ref[...] = quarter_x
    quarter, value = tile_weights(offset_y, four_weights(frac_ref[1, 0]))
    quarter_y_ref[...] = quarter
    value_y_ref[...] = value
    quarter, value = doubled(quarter, value)
    dense_y_ref[...] = jnp.concatenate(
        [picked_tile(quarter, value, n) for n in range(0, cells_y + MARGIN, 2 * ROWS)]
        + [jnp.zeros((LANES - SPAN, slots), jnp.bfloat16)]
        + [picked_tile(quarter, value, n) for n in range(-MARGIN, 0, 2 * ROWS)],
        axis=0,
    )
    for copy in copies[2:-1]:
        copy.wait()
    mine = jnp.where(fish_ref[...] == row * lax.axis_size("gy") + col, 1.0, 0.0)
    count = FISH_MARK * jnp.sum(mine)
    slot = lax.broadcasted_iota(jnp.int32, (1, slots), 1)
    value = value_x * jnp.where(slot.astype(jnp.float32) < count, 1.0, 0.0)
    value_ref[...] = value
    level = cell_ref[2, 0]
    pushes = [force_ref[c, 0] * value for c in range(comps)]
    for l in range(levels):
        for c in range(comps):
            force_out[l * comps + c] = twice(jnp.where(level == l, pushes[c], 0.0))
    half_spread(quarter_ref, force_out, dense_y_ref, half_ref, base, slice(0, slots))
    copies[-1].wait()
    finish_half(half_ref, velocity_ref, far_ref, even, cells_y)


def near_kernel(
    shape, chunk, velocity_ref, far_half_ref, force_ref, dense_y_ref, quarter_ref,
    grid_ref, near_ref, half_ref,
):
    cells_x, cells_y, _, _ = shape
    slots = quarter_ref.shape[1]
    rows = half_ref.shape[1]
    _, _, even, _ = position()
    base = jnp.where(even, cells_x // 8, -MARGIN // 4)
    for first in range(0, slots, chunk):
        lanes = slice(first, first + chunk)
        half_spread(quarter_ref, force_ref, dense_y_ref, half_ref, base, lanes)
    finish_half(half_ref, velocity_ref, near_ref, jnp.logical_not(even), cells_y)
    for ref, row in ((far_half_ref, jnp.where(even, 0, rows)), (half_ref, jnp.where(even, rows, 0))):
        place = pl.ds(pl.multiple_of(row, ROWS), rows)
        for k in range(ref.shape[0]):
            grid_ref[k, place] = ref[k]


def rolled(value, shift):
    shift = shift % LANES
    return pltpu.roll(value, shift, 1) if shift else value


def lane_index(rows):
    return lax.broadcasted_iota(jnp.int32, (rows, LANES), 1)


def ordered(parity, near_ref, far_ref):
    even = jnp.broadcast_to(parity, near_ref.shape) != 0
    near, far = near_ref[...].astype(jnp.float32), far_ref[...].astype(jnp.float32)
    return jnp.where(even, far, near), jnp.where(even, near, far)


def joined(center, before, after):
    wide = center.shape[0]
    near = PAD - MARGIN
    overlap = STRIP - near
    return jnp.concatenate(
        [
            before[:near],
            center[:overlap] + before[near:],
            center[overlap : wide - overlap],
            center[wide - overlap :] + after[:overlap],
            after[overlap:],
        ],
        axis=0,
    )


def extended_rows(parity, grid_ref, near_ref, far_ref, cells_y):
    items = grid_ref.shape[0]
    groups = -(-items // EDGE_PER)
    size = groups * STRIP
    before, after = ordered(parity, near_ref, far_ref)
    packed = jnp.concatenate([before[items * STRIP :], after[items * STRIP :]], axis=0)
    lane = lane_index(2 * size)
    kept = (lane < MARGIN) | (lane >= LANES - MARGIN)
    edges = [jnp.where(kept, rolled(packed, -SPAN * slot), 0.0) for slot in range(EDGE_PER)]
    for k in range(items):
        place = slice(k * STRIP, (k + 1) * STRIP)
        inner = joined(grid_ref[k, :, :cells_y], before[place], after[place])
        start = k // EDGE_PER * STRIP
        edge = edges[k % EDGE_PER]
        edge = joined(
            grid_ref[k, :, cells_y:],
            edge[start : start + STRIP],
            edge[size + start : size + start + STRIP],
        )
        yield k, inner, edge


def pack_kernel(shape, parity_ref, grid_ref, far_x, near_x, near_ref, far_ref):
    cells_x, cells_y, _, _ = shape
    items = grid_ref.shape[0]
    groups = -(-items // EDGE_PER)
    rows = cells_x + 2 * PAD
    lane = lane_index(rows)
    up_halo = (lane >= LANES - REACH) & (lane < LANES - MARGIN)
    down_halo = (lane >= MARGIN) & (lane < REACH)
    halos, ups, downs = None, None, None
    packed = [[], []]
    for k, inner, edge in extended_rows(parity_ref[0:1], grid_ref, near_x, far_x, cells_y):
        slot = k % EDGE_PER
        up = rolled(jnp.where(lane >= LANES - MARGIN, inner, edge), SPAN * slot)
        down = rolled(jnp.where(lane < MARGIN, inner, edge), SPAN * slot)
        halo = rolled(jnp.where(up_halo | down_halo, inner, 0.0), REACH + HALO * k)
        ups = ups + up if slot else up
        downs = downs + down if slot else down
        halos = halos + halo if k else halo
        if slot == EDGE_PER - 1 or k == items - 1:
            packed[0].append(squeezed(ups))
            packed[1].append(squeezed(downs))
    halos = squeezed(halos)
    rows = halos.shape[0]
    used = lane_index(rows) < HALO * items
    ups = jnp.where(used, halos, 0.0)
    downs = jnp.where(used, rolled(halos, -MARGIN - REACH), 0.0)
    folded = None
    for row in range(0, rows, SPAN):
        size = min(SPAN, rows - row)
        parts = [value[row : row + size] for value in (ups, downs)]
        if size < SPAN:
            parts = [jnp.concatenate([p, jnp.zeros((SPAN - size, LANES), p.dtype)], 0) for p in parts]
        part = rolled(jnp.concatenate(parts, axis=0), row)
        folded = folded + part if row else part
    up = jnp.concatenate(packed[0] + [folded[:SPAN]], axis=0)
    down = jnp.concatenate(packed[1] + [folded[SPAN:]], axis=0)
    even = jnp.broadcast_to(parity_ref[1:2], up.shape) != 0
    near_ref[...] = jnp.where(even, up, down).astype(jnp.bfloat16)
    far_ref[...] = jnp.where(even, down, up).astype(jnp.bfloat16)


def squeezed(value):
    row = lax.broadcasted_iota(jnp.int32, (ROWS, LANES), 0)
    shared = jnp.where(row >= PAD - REACH, value[:ROWS], value[-ROWS:])
    return jnp.concatenate([shared, value[ROWS:-ROWS]], axis=0)


def expanded(value):
    return jnp.concatenate([value, value[:ROWS]], axis=0)


def around(ref, k, start, size):
    center = ref[k, start : start + size]
    back = ref[k, start - 1 : start - 1 + size]
    fore = ref[k, start + 1 : start + 1 + size]
    return center, back, fore, rolled(center, 1), rolled(center, -1)


def advect(moved_ref, carried_ref, levels, comps, rows):
    for start in range(ROWS, ROWS + rows, STEP):
        for l in range(levels):
            pieces = [around(moved_ref, l * comps + c, start, STEP) for c in range(comps)]
            speed_x, speed_y = COURANT * pieces[0][0], COURANT * pieces[1][0]
            ahead_x, astern_x = jnp.maximum(speed_x, 0.0), jnp.minimum(speed_x, 0.0)
            ahead_y, astern_y = jnp.maximum(speed_y, 0.0), jnp.minimum(speed_y, 0.0)
            for c in range(comps):
                center, back, fore, below, above = pieces[c]
                change = ahead_x * (center - back) + astern_x * (fore - center)
                change = change + ahead_y * (center - below) + astern_y * (above - center)
                carried_ref[l * comps + c, start : start + STEP] = center - change


def sweep(ref, carried_ref, levels, comps, start, size):
    scale = 1.0 / (1.0 + 6.0 * VISCOUS)
    centers, results = [], []
    for k in range(levels * comps):
        center, back, fore, below, above = around(ref, k, start, size)
        centers.append(center)
        results.append(back + fore + below + above)
    for k in range(levels * comps):
        higher = min(k // comps + 1, levels - 1) * comps + k % comps
        lower = max(k // comps - 1, 0) * comps + k % comps
        summed = results[k] + centers[higher] + centers[lower]
        source = carried_ref[k, start : start + size]
        results[k] = scale * source + (VISCOUS * scale) * summed
    return results


def first_steps(moved_ref, carried_ref, sweep_ref, levels, comps, rows):
    advect(moved_ref, carried_ref, levels, comps, rows)
    for start in range(ROWS, ROWS + rows, STEP):
        results = sweep(carried_ref, carried_ref, levels, comps, start, STEP)
        for k in range(levels * comps):
            sweep_ref[k, start : start + STEP] = results[k]


RIM = REACH + HALO
HALF = LANES // 2


def weight_kernel(
    shape, chunk, parity_ref, quarter_ref, value_ref, level_ref, inner_ref, rim_ref, parity_out
):
    parity_out[...] = parity_ref[...]
    _, cells_y, _, _ = shape
    slots = quarter_ref.shape[1]
    size = 2 * ROWS
    levels = inner_ref.shape[0] // LANES
    row = lax.broadcasted_iota(jnp.int32, (size, chunk), 0)

    def cut(tile, keep):
        return jnp.where(keep, tile.astype(jnp.float32), 0.0).astype(jnp.bfloat16)

    for first in range(0, slots, chunk):
        lanes = slice(first, first + chunk)
        level = level_ref[:, lanes]
        for l in range(levels):
            value = jnp.where(level == l, value_ref[:, lanes], 0.0)
            quarter, value = doubled(quarter_ref[:, lanes], value)
            for start in range(0, LANES, size):
                inner = picked_tile(quarter, value, start)
                if start < REACH:
                    inner = cut(inner, row + start >= REACH)
                if start + size > cells_y - REACH:
                    inner = cut(inner, row + start < cells_y - REACH)
                if start >= LANES - MARGIN:
                    rim = picked_tile(quarter, value, start - LANES)
                elif start + size > HALF - REACH and start < HALF + MARGIN:
                    rim = picked_tile(quarter, value, start + cells_y - HALF)
                    rim = cut(rim, row + start >= HALF - REACH) if start < HALF - REACH else rim
                elif start < REACH:
                    rim = picked_tile(quarter, value, start)
                    rim = cut(rim, row + start < REACH) if start + size > REACH else rim
                else:
                    rim = jnp.zeros_like(value)
                place = slice(l * LANES + start, l * LANES + start + size)
                inner_ref[place, lanes] = inner
                rim_ref[place, lanes] = rim


def sampled_part(round_ref, weight_ref, quarter_ref, value_ref, lanes, comps):
    wide_x = round_ref.shape[0] // comps
    partial = jnp.dot(round_ref[...], weight_ref[:, lanes], preferred_element_type=jnp.float32)
    quarter, value = quarter_ref[:, lanes], value_ref[:, lanes]
    totals = [jnp.zeros_like(value)] * comps
    for row in range(0, wide_x, ROWS):
        here = quarter == (MARGIN - row) // 4
        for c in range(comps):
            start = c * wide_x + row
            totals[c] = jnp.where(here, partial[start : start + ROWS], totals[c])
    return [jnp.sum(total * value, axis=0, keepdims=True) for total in totals]


def inner_kernel(
    shape, chunk, levels, parity_ref, quarter_ref, value_ref, weight_ref, grid_ref, far_x, near_x,
    inner_ref, rim_ref, sampled_ref, moved_ref, carried_ref, sweep_ref, round_ref,
):
    cells_x, cells_y, _, _ = shape
    items = grid_ref.shape[0]
    comps = items // levels
    slots = quarter_ref.shape[1]
    wide_x = cells_x + SPAN
    rows = cells_x + 2 * PAD
    lane = lane_index(rows)
    for k, inner, edge in extended_rows(parity_ref[0:1], grid_ref, near_x, far_x, cells_y):
        moved_ref[k, ROWS : ROWS + rows] = inner
        low = jnp.where(lane < RIM, inner, jnp.where(lane >= LANES - MARGIN, edge, 0.0))
        high = jnp.where(lane >= LANES - RIM, inner, jnp.where(lane < MARGIN, edge, 0.0))
        rim_ref[k] = low + rolled(high, HALF)
    first_steps(moved_ref, carried_ref, sweep_ref, levels, comps, rows)
    size = 2 * ROWS
    for row in range(0, wide_x, size):
        start = ROWS + PAD - MARGIN + row
        results = sweep(sweep_ref, carried_ref, levels, comps, start, size)
        for k in range(items):
            level, c = k // comps, k % comps
            place = slice(c * wide_x + row, c * wide_x + row + size)
            round_ref[place, level * LANES : (level + 1) * LANES] = results[k].astype(jnp.bfloat16)
            if MARGIN <= row < MARGIN + cells_x:
                inner_ref[k, row - MARGIN : row - MARGIN + size] = results[k]
    for first in range(0, slots, chunk):
        lanes = slice(first, first + chunk)
        parts = sampled_part(round_ref, weight_ref, quarter_ref, value_ref, lanes, comps)
        for c in range(comps):
            sampled_ref[c : c + 1, lanes] = parts[c]


def unfolded(folded, rows):
    return expanded(
        jnp.concatenate(
            [rolled(folded, -row)[: min(SPAN, rows - row)] for row in range(0, rows, SPAN)], axis=0
        )
    )


def finish_kernel(
    shape, chunk, parity_ref, quarter_ref, value_ref, weight_ref, inner_ref, rim_ref, part_ref,
    near_y, far_y, next_ref, sampled_ref, moved_ref, carried_ref, sweep_ref, round_ref,
):
    cells_x, cells_y, _, _ = shape
    items = rim_ref.shape[0]
    groups = -(-items // EDGE_PER)
    levels, comps = next_ref.shape[:2]
    slots = quarter_ref.shape[1]
    wide_x = cells_x + SPAN
    rows = cells_x + 2 * PAD
    lane = lane_index(rows)
    befores, afters = ordered(parity_ref[1:2], near_y, far_y)
    turned = HALF + MARGIN + REACH
    high_halo = (lane >= turned) & (lane < turned + HALO * items)
    both = ((lane + MARGIN) & (HALF - 1)) < SPAN
    outer = ((lane >= LANES - REACH) & (lane < LANES - MARGIN)) | (
        (lane >= HALF + MARGIN) & (lane < HALF + REACH)
    )
    size = rows - ROWS
    halo = jnp.where(
        high_halo,
        rolled(unfolded(afters[groups * size :], size), turned),
        unfolded(befores[groups * size :], size),
    )
    for group in range(groups):
        before = expanded(befores[group * size : (group + 1) * size])
        after = expanded(rolled(afters[group * size : (group + 1) * size], HALF))
        for k in range(group * EDGE_PER, min((group + 1) * EDGE_PER, items)):
            slot = k % EDGE_PER
            window = ((lane + (LANES + MARGIN - SPAN * slot)) & (LANES - 1)) < SPAN
            main = rolled(jnp.where(window, before, after), -SPAN * slot)
            value = rim_ref[k] + jnp.where(both, main, 0.0)
            value = jnp.where(outer, rolled(halo, -REACH - HALO * k), value)
            moved_ref[k, ROWS : ROWS + rows] = value

    first_steps(moved_ref, carried_ref, sweep_ref, levels, comps, rows)
    size = 2 * ROWS
    lane = lane_index(size)
    for row in range(0, wide_x, size):
        start = ROWS + PAD - MARGIN + row
        results = sweep(sweep_ref, carried_ref, levels, comps, start, size)
        for k in range(items):
            level, c = k // comps, k % comps
            place = slice(c * wide_x + row, c * wide_x + row + size)
            round_ref[place, level * LANES : (level + 1) * LANES] = results[k].astype(jnp.bfloat16)
        if not MARGIN <= row < MARGIN + cells_x:
            continue
        place = slice(row - MARGIN, row - MARGIN + size)
        for k in range(items):
            low, high = results[k], rolled(results[k], HALF)
            inner = inner_ref[k, place]
            inner = jnp.where(lane < REACH, low, jnp.where(lane >= LANES - REACH, high, inner))
            next_ref[k // comps, k % comps, place] = inner

    for first in range(0, slots, chunk):
        lanes = slice(first, first + chunk)
        parts = sampled_part(round_ref, weight_ref, quarter_ref, value_ref, lanes, comps)
        for c in range(comps):
            sampled_ref[c, 0, :, lanes] = part_ref[c : c + 1, lanes] + parts[c]


def whole(count):
    return [pl.BlockSpec(memory_space=pltpu.VMEM)] * count


def swap_pairs(axis):
    size = lax.axis_size(axis)
    if size % 2:
        raise ValueError("odd axis")
    far_pairs = [(i, (i - 1 if i % 2 == 0 else i + 1) % size) for i in range(size)]
    return far_pairs, [(i, i ^ 1) for i in range(size)]


def body(velocity, marker_cell, marker_frac, marker_force, fish_owner):
    levels, comps, cells_x, cells_y = velocity.shape
    slots = marker_cell.shape[3]
    items = levels * comps
    shape = (cells_x, cells_y, cells_x * lax.axis_size("gx"), cells_y * lax.axis_size("gy"))
    wide_x = cells_x + SPAN
    rows = cells_x + 2 * PAD
    chunk = min(512, slots)
    width = cells_y + LANES
    groups = -(-items // EDGE_PER)
    params = pltpu.CompilerParams(vmem_limit_bytes=32 * 1024 * 1024)
    edge_x = jax.ShapeDtypeStruct(((items + groups) * STRIP, LANES), jnp.bfloat16)
    half = (items, wide_x // 2, width)
    arrays = (fish_owner, velocity, marker_cell, marker_frac, marker_force)
    far_half, far, force, dense_y, quarter, value, quarter_y, value_y, level, parity, near_velocity = (
        pl.pallas_call(
        functools.partial(far_kernel, shape),
        out_shape=(
            jax.ShapeDtypeStruct(half, jnp.float32),
            edge_x,
            jax.ShapeDtypeStruct((items, 2 * ROWS, slots), jnp.bfloat16),
            jax.ShapeDtypeStruct((width, slots), jnp.bfloat16),
            jax.ShapeDtypeStruct((ROWS, slots), jnp.int32),
            jax.ShapeDtypeStruct((ROWS, slots), jnp.float32),
            jax.ShapeDtypeStruct((ROWS, slots), jnp.int32),
            jax.ShapeDtypeStruct((ROWS, slots), jnp.float32),
            jax.ShapeDtypeStruct((1, slots), jnp.int32),
            jax.ShapeDtypeStruct((2, LANES), jnp.int32),
            jax.ShapeDtypeStruct(velocity.shape, velocity.dtype),
        ),
        in_specs=[pl.BlockSpec(memory_space=pltpu.HBM)] * 5,
        out_specs=tuple(whole(11)),
        scratch_shapes=[pltpu.VMEM(a.shape, a.dtype) for a in arrays if a is not velocity]
        + [pltpu.SemaphoreType.DMA((5,))],
        compiler_params=params,
        name="spread_far",
    )(*(pltpu.with_memory_space_constraint(a, pltpu.HBM) for a in arrays))
    )
    far_pairs, near_pairs = swap_pairs("gx")
    far_x = lax.ppermute(far, "gx", far_pairs)
    grid, near = pl.pallas_call(
        functools.partial(near_kernel, shape, slots),
        out_shape=(jax.ShapeDtypeStruct((items, wide_x, width), jnp.float32), edge_x),
        in_specs=whole(5),
        out_specs=tuple(whole(2)),
        scratch_shapes=[pltpu.VMEM(half, jnp.float32)],
        compiler_params=params,
        cost_estimate=pl.CostEstimate(
            flops=items * wide_x * width * slots, bytes_accessed=4 * items * wide_x * width,
            transcendentals=0,
        ),
        name="spread_near",
    )(near_velocity, far_half, force, dense_y, quarter)
    near_x = lax.ppermute(near, "gx", near_pairs)
    weights = jax.ShapeDtypeStruct((levels * LANES, slots), jnp.bfloat16)
    inner_weight, rim_weight, parity = pl.pallas_call(
        functools.partial(weight_kernel, shape, chunk),
        out_shape=(weights, weights, jax.ShapeDtypeStruct(parity.shape, parity.dtype)),
        in_specs=whole(4),
        out_specs=tuple(whole(3)),
        compiler_params=params,
        cost_estimate=pl.CostEstimate(
            flops=2 * levels * LANES * slots, bytes_accessed=4 * levels * LANES * slots,
            transcendentals=0,
        ),
        name="weights",
    )(parity, quarter_y, value_y, level)
    edge_y = jax.ShapeDtypeStruct((groups * (rows - ROWS) + SPAN, LANES), jnp.bfloat16)
    near, far = pl.pallas_call(
        functools.partial(pack_kernel, shape),
        out_shape=(edge_y, edge_y),
        in_specs=whole(4),
        out_specs=tuple(whole(2)),
        compiler_params=params,
        name="pack",
    )(parity, grid, far_x, near_x)
    far_pairs, near_pairs = swap_pairs("gy")
    near_y = lax.ppermute(near, "gy", near_pairs)
    far_y = lax.ppermute(far, "gy", far_pairs)
    field = pltpu.VMEM((items, rows + 2 * ROWS, LANES), jnp.float32)
    rounded = pltpu.VMEM((comps * wide_x, levels * LANES), jnp.bfloat16)
    inner, rim, part = pl.pallas_call(
        functools.partial(inner_kernel, shape, chunk, levels),
        out_shape=(
            jax.ShapeDtypeStruct((items, cells_x, LANES), jnp.float32),
            jax.ShapeDtypeStruct((items, rows, LANES), jnp.float32),
            jax.ShapeDtypeStruct((comps, slots), jnp.float32),
        ),
        in_specs=whole(7),
        out_specs=tuple(whole(3)),
        scratch_shapes=[field, field, field, rounded],
        compiler_params=params,
        cost_estimate=pl.CostEstimate(
            flops=2 * items * wide_x * LANES * slots, bytes_accessed=16 * items * rows * LANES,
            transcendentals=0,
        ),
        name="inner",
    )(parity, quarter, value, inner_weight, grid, far_x, near_x)
    return pl.pallas_call(
        functools.partial(finish_kernel, shape, chunk),
        out_shape=(
            jax.ShapeDtypeStruct(velocity.shape, jnp.float32),
            jax.ShapeDtypeStruct((comps, 1, 1, slots), jnp.float32),
        ),
        in_specs=whole(9),
        out_specs=tuple(whole(2)),
        scratch_shapes=[field, field, field, rounded],
        compiler_params=params,
        name="finish",
    )(parity, quarter, value, rim_weight, inner, rim, part, near_y, far_y)


def solution(mesh):
    placed = (
        P(None, None, "gx", "gy"),
        P(None, "gx", "gy", None),
        P(None, "gx", "gy", None),
        P(None, "gx", "gy", None),
        P(),
    )
    return jax.shard_map(
        body,
        mesh=mesh,
        in_specs=placed,
        out_specs=(P(None, None, "gx", "gy"), P(None, "gx", "gy", None)),
        check_vma=False,
    )
```

```python
import functools

import jax
import jax.numpy as jnp
import numpy as np
from jax import lax
from jax.experimental import pallas as pl
from jax.experimental.pallas import tpu as pltpu
from jax.sharding import PartitionSpec as P

MARGIN = 16
FISH_MARK = 1024
HALO = 3
LANES = 128
COURANT = 0.25
VISCOUS = 1.5
ROWS = 8
STEP = 2 * ROWS

REACH = MARGIN + HALO
PAD = -(-REACH // ROWS) * ROWS
STRIP = PAD + MARGIN
SPAN = 2 * MARGIN
EDGE_PER = LANES // SPAN


def half_turn(terms):
    nodes = 0.5 - 0.5 * np.cos(np.pi * (np.arange(64) + 0.5) / 64)
    square = nodes * nodes
    cosine = np.polynomial.polynomial.polyfit(square, np.cos(0.5 * np.pi * nodes), terms)
    sine = np.polynomial.polynomial.polyfit(square, np.sin(0.5 * np.pi * nodes) / nodes, terms)
    return [float(v) for v in cosine], [float(v) for v in sine]


COS_FIT, SIN_FIT = half_turn(6)


def horner(coefficients, value):
    total = jnp.full_like(value, coefficients[-1])
    for coefficient in coefficients[-2::-1]:
        total = total * value + coefficient
    return total


def four_weights(frac):
    square = frac * frac
    cosine = horner(COS_FIT, square)
    sine = frac * horner(SIN_FIT, square)
    return (0.25 - 0.25 * sine, 0.25 + 0.25 * cosine, 0.25 + 0.25 * sine, 0.25 - 0.25 * cosine)


def local_cell(cell, low, extent):
    offset = cell - low
    offset = jnp.where(offset < -MARGIN, offset + extent, offset)
    return jnp.where(offset >= extent - MARGIN, offset - extent, offset)


def position():
    row, col = lax.axis_index("gx"), lax.axis_index("gy")
    return row, col, (row & 1) == 0, (col & 1) == 0


def tile_weights(offset, weights):
    shift = lax.broadcasted_iota(jnp.int32, (ROWS, offset.shape[1]), 0) + 1 - offset
    quarter, phase = shift >> 2, shift & 3
    value = jnp.where(phase == 3, weights[3], weights[2])
    value = jnp.where(phase == 1, weights[1], value)
    return quarter, jnp.where(phase == 0, weights[0], value)


def doubled(quarter, value):
    quarter = jnp.concatenate([quarter, quarter + 2], axis=0).astype(jnp.float32)
    return quarter.astype(jnp.bfloat16), twice(value)


def twice(value):
    return jnp.concatenate([value, value], axis=0).astype(jnp.bfloat16)


def picked_tile(quarter, value, first):
    zero = jnp.zeros_like(value)
    return jnp.where(quarter == jnp.array(-first // 4, quarter.dtype), value, zero)


def half_spread(quarter_ref, force_ref, dense_y_ref, half_ref, base, lanes):
    items, rows = half_ref.shape[:2]
    quarter = quarter_ref[:, lanes] + base
    quarter = jnp.concatenate([quarter, quarter + 2], axis=0).astype(jnp.float32)
    quarter = quarter.astype(jnp.bfloat16)
    left = jnp.concatenate(
        [
            picked_tile(quarter, force_ref[k, :, lanes], row)
            for k in range(items)
            for row in range(0, rows, 2 * ROWS)
        ],
        axis=0,
    )
    total = lax.dot_general(
        left, dense_y_ref[:, lanes], (((1,), (1,)), ((), ())),
        preferred_element_type=jnp.float32,
    )
    total = total.reshape(half_ref.shape)
    if lanes.start:
        half_ref[...] += total
    else:
        half_ref[...] = total


def finish_half(half_ref, velocity_ref, out_ref, low, cells_y):
    items, rows = half_ref.shape[:2]
    comps = items // velocity_ref.shape[0]
    count = rows - MARGIN
    source = pl.ds(pl.multiple_of(jnp.where(low, 0, count), ROWS), count)
    target = pl.ds(pl.multiple_of(jnp.where(low, MARGIN, 0), ROWS), count)
    for k in range(items):
        half_ref[k, target, :cells_y] += velocity_ref[k // comps, k % comps, source]
    place = pl.ds(pl.multiple_of(jnp.where(low, 0, rows - STRIP), ROWS), STRIP)
    parts = [half_ref[k, place, :cells_y] for k in range(items)]
    for group in range(0, items, EDGE_PER):
        edges = []
        for k in range(group, min(group + EDGE_PER, items)):
            edges.append(rolled(half_ref[k, place, cells_y:], SPAN * (k - group)))
        parts.append(functools.reduce(jnp.add, edges))
    out_ref[...] = jnp.concatenate(parts, axis=0).astype(jnp.bfloat16)


def far_kernel(
    shape, chunk, fish_hbm, velocity_hbm, cell_hbm, frac_hbm, force_hbm,
    half_ref, far_ref, force_out, dense_y_ref, quarter_ref, value_ref,
    quarter_y_ref, value_y_ref, level_ref, parity_ref, velocity_ref,
    fish_ref, cell_ref, frac_ref, force_ref, sems,
):
    pairs = (
        (cell_hbm, cell_ref), (frac_hbm, frac_ref), (fish_hbm, fish_ref),
        (force_hbm, force_ref), (velocity_hbm, velocity_ref),
    )
    copies = [pltpu.make_async_copy(a, b, sems.at[i]) for i, (a, b) in enumerate(pairs)]
    for copy in copies:
        copy.start()
    cells_x, cells_y, extent_x, extent_y = shape
    levels, comps = velocity_ref.shape[:2]
    slots = cell_ref.shape[3]
    row, col, even, even_y = position()
    parity_ref[0:1] = jnp.full((1, LANES), jnp.where(even, 1, 0), jnp.int32)
    parity_ref[1:2] = jnp.full((1, LANES), jnp.where(even_y, 1, 0), jnp.int32)
    base = jnp.where(even, -MARGIN // 4, cells_x // 8)
    for copy in copies[:-1]:
        copy.wait()
    mine = jnp.where(fish_ref[...] == row * lax.axis_size("gy") + col, 1.0, 0.0)
    count = FISH_MARK * jnp.sum(mine)
    level_ref[...] = cell_ref[2, 0]
    for first in range(0, slots, chunk):
        lanes = slice(first, first + chunk)
        offset_x = local_cell(cell_ref[0, 0, :, lanes], row * cells_x, extent_x)
        offset_y = local_cell(cell_ref[1, 0, :, lanes], col * cells_y, extent_y)
        slot = lax.broadcasted_iota(jnp.int32, (1, chunk), 1) + first
        alive = jnp.where(slot.astype(jnp.float32) < count, 1.0, 0.0)
        quarter, value = tile_weights(offset_x, four_weights(frac_ref[0, 0, :, lanes]))
        value = value * alive
        quarter_ref[:, lanes] = quarter
        value_ref[:, lanes] = value
        level = cell_ref[2, 0, :, lanes]
        pushes = [twice(force_ref[c, 0, :, lanes] * value) for c in range(comps)]
        level = jnp.broadcast_to(level.astype(jnp.float32), pushes[0].shape).astype(jnp.bfloat16)
        for l in range(levels):
            here = level == jnp.array(l, jnp.bfloat16)
            for c in range(comps):
                push = jnp.where(here, pushes[c], jnp.zeros_like(pushes[c]))
                force_out[l * comps + c, :, lanes] = push
        quarter, value = tile_weights(offset_y, four_weights(frac_ref[1, 0, :, lanes]))
        quarter_y_ref[:, lanes] = quarter
        value_y_ref[:, lanes] = value
        quarter, value = doubled(quarter, value)
        dense_y_ref[:, lanes] = jnp.concatenate(
            [picked_tile(quarter, value, n) for n in range(0, cells_y + MARGIN, 2 * ROWS)]
            + [jnp.zeros((LANES - SPAN, chunk), jnp.bfloat16)]
            + [picked_tile(quarter, value, n) for n in range(-MARGIN, 0, 2 * ROWS)],
            axis=0,
        )
        half_spread(quarter_ref, force_out, dense_y_ref, half_ref, base, lanes)
    copies[-1].wait()
    finish_half(half_ref, velocity_ref, far_ref, even, cells_y)


def near_kernel(
    shape, chunk, velocity_ref, far_half_ref, force_ref, dense_y_ref, quarter_ref,
    grid_ref, near_ref, half_ref,
):
    cells_x, cells_y, _, _ = shape
    slots = quarter_ref.shape[1]
    rows = half_ref.shape[1]
    _, _, even, _ = position()
    base = jnp.where(even, cells_x // 8, -MARGIN // 4)
    for first in range(0, slots, chunk):
        lanes = slice(first, first + chunk)
        half_spread(quarter_ref, force_ref, dense_y_ref, half_ref, base, lanes)
    finish_half(half_ref, velocity_ref, near_ref, jnp.logical_not(even), cells_y)
    for ref, row in ((far_half_ref, jnp.where(even, 0, rows)), (half_ref, jnp.where(even, rows, 0))):
        place = pl.ds(pl.multiple_of(row, ROWS), rows)
        for k in range(ref.shape[0]):
            grid_ref[k, place] = ref[k]


def rolled(value, shift):
    shift = shift % LANES
    return pltpu.roll(value, shift, 1) if shift else value


def lane_index(rows):
    return lax.broadcasted_iota(jnp.int32, (rows, LANES), 1)


def ordered(parity, near_ref, far_ref):
    even = jnp.broadcast_to(parity, near_ref.shape) != 0
    near, far = near_ref[...].astype(jnp.float32), far_ref[...].astype(jnp.float32)
    return jnp.where(even, far, near), jnp.where(even, near, far)


def joined(center, before, after):
    wide = center.shape[0]
    near = PAD - MARGIN
    overlap = STRIP - near
    return jnp.concatenate(
        [
            before[:near],
            center[:overlap] + before[near:],
            center[overlap : wide - overlap],
            center[wide - overlap :] + after[:overlap],
            after[overlap:],
        ],
        axis=0,
    )


def extended_rows(parity, grid_ref, near_ref, far_ref, cells_y):
    items = grid_ref.shape[0]
    groups = -(-items // EDGE_PER)
    size = groups * STRIP
    before, after = ordered(parity, near_ref, far_ref)
    packed = jnp.concatenate([before[items * STRIP :], after[items * STRIP :]], axis=0)
    lane = lane_index(2 * size)
    kept = (lane < MARGIN) | (lane >= LANES - MARGIN)
    edges = [jnp.where(kept, rolled(packed, -SPAN * slot), 0.0) for slot in range(EDGE_PER)]
    for k in range(items):
        place = slice(k * STRIP, (k + 1) * STRIP)
        inner = joined(grid_ref[k, :, :cells_y], before[place], after[place])
        start = k // EDGE_PER * STRIP
        edge = edges[k % EDGE_PER]
        edge = joined(
            grid_ref[k, :, cells_y:],
            edge[start : start + STRIP],
            edge[size + start : size + start + STRIP],
        )
        yield k, inner, edge


def pack_kernel(shape, parity_ref, grid_ref, far_x, near_x, near_ref, far_ref):
    cells_x, cells_y, _, _ = shape
    items = grid_ref.shape[0]
    groups = -(-items // EDGE_PER)
    rows = cells_x + 2 * PAD
    lane = lane_index(rows)
    up_halo = (lane >= LANES - REACH) & (lane < LANES - MARGIN)
    down_halo = (lane >= MARGIN) & (lane < REACH)
    halos, ups, downs = None, None, None
    packed = [[], []]
    for k, inner, edge in extended_rows(parity_ref[0:1], grid_ref, near_x, far_x, cells_y):
        slot = k % EDGE_PER
        up = rolled(jnp.where(lane >= LANES - MARGIN, inner, edge), SPAN * slot)
        down = rolled(jnp.where(lane < MARGIN, inner, edge), SPAN * slot)
        halo = rolled(jnp.where(up_halo | down_halo, inner, 0.0), REACH + HALO * k)
        ups = ups + up if slot else up
        downs = downs + down if slot else down
        halos = halos + halo if k else halo
        if slot == EDGE_PER - 1 or k == items - 1:
            packed[0].append(squeezed(ups))
            packed[1].append(squeezed(downs))
    halos = squeezed(halos)
    rows = halos.shape[0]
    used = lane_index(rows) < HALO * items
    ups = jnp.where(used, halos, 0.0)
    downs = jnp.where(used, rolled(halos, -MARGIN - REACH), 0.0)
    folded = None
    for row in range(0, rows, SPAN):
        size = min(SPAN, rows - row)
        parts = [value[row : row + size] for value in (ups, downs)]
        if size < SPAN:
            parts = [jnp.concatenate([p, jnp.zeros((SPAN - size, LANES), p.dtype)], 0) for p in parts]
        part = rolled(jnp.concatenate(parts, axis=0), row)
        folded = folded + part if row else part
    up = jnp.concatenate(packed[0] + [folded[:SPAN]], axis=0)
    down = jnp.concatenate(packed[1] + [folded[SPAN:]], axis=0)
    even = jnp.broadcast_to(parity_ref[1:2], up.shape) != 0
    near_ref[...] = jnp.where(even, up, down).astype(jnp.bfloat16)
    far_ref[...] = jnp.where(even, down, up).astype(jnp.bfloat16)


def squeezed(value):
    row = lax.broadcasted_iota(jnp.int32, (ROWS, LANES), 0)
    shared = jnp.where(row >= PAD - REACH, value[:ROWS], value[-ROWS:])
    return jnp.concatenate([shared, value[ROWS:-ROWS]], axis=0)


def expanded(value):
    return jnp.concatenate([value, value[:ROWS]], axis=0)


def around(ref, k, start, size):
    center = ref[k, start : start + size]
    back = ref[k, start - 1 : start - 1 + size]
    fore = ref[k, start + 1 : start + 1 + size]
    return center, back, fore, rolled(center, 1), rolled(center, -1)


def advect(moved_ref, carried_ref, levels, comps, rows):
    for start in range(ROWS, ROWS + rows, STEP):
        for l in range(levels):
            pieces = [around(moved_ref, l * comps + c, start, STEP) for c in range(comps)]
            speed_x, speed_y = COURANT * pieces[0][0], COURANT * pieces[1][0]
            ahead_x, astern_x = jnp.maximum(speed_x, 0.0), jnp.minimum(speed_x, 0.0)
            ahead_y, astern_y = jnp.maximum(speed_y, 0.0), jnp.minimum(speed_y, 0.0)
            for c in range(comps):
                center, back, fore, below, above = pieces[c]
                change = ahead_x * (center - back) + astern_x * (fore - center)
                change = change + ahead_y * (center - below) + astern_y * (above - center)
                carried_ref[l * comps + c, start : start + STEP] = center - change


def sweep(ref, carried_ref, levels, comps, start, size):
    scale = 1.0 / (1.0 + 6.0 * VISCOUS)
    centers, results = [], []
    for k in range(levels * comps):
        center, back, fore, below, above = around(ref, k, start, size)
        centers.append(center)
        results.append(back + fore + below + above)
    for k in range(levels * comps):
        higher = min(k // comps + 1, levels - 1) * comps + k % comps
        lower = max(k // comps - 1, 0) * comps + k % comps
        summed = results[k] + centers[higher] + centers[lower]
        source = carried_ref[k, start : start + size]
        results[k] = scale * source + (VISCOUS * scale) * summed
    return results


def first_steps(moved_ref, carried_ref, sweep_ref, levels, comps, rows):
    advect(moved_ref, carried_ref, levels, comps, rows)
    for start in range(ROWS, ROWS + rows, STEP):
        results = sweep(carried_ref, carried_ref, levels, comps, start, STEP)
        for k in range(levels * comps):
            sweep_ref[k, start : start + STEP] = results[k]


RIM = REACH + HALO
HALF = LANES // 2


def weight_kernel(
    shape, chunk, parity_ref, quarter_ref, value_ref, level_ref, inner_ref, rim_ref, parity_out
):
    parity_out[...] = parity_ref[...]
    _, cells_y, _, _ = shape
    slots = quarter_ref.shape[1]
    size = 2 * ROWS
    levels = inner_ref.shape[0] // LANES
    row = lax.broadcasted_iota(jnp.int32, (size, chunk), 0)

    def cut(tile, keep):
        return jnp.where(keep, tile.astype(jnp.float32), 0.0).astype(jnp.bfloat16)

    for first in range(0, slots, chunk):
        lanes = slice(first, first + chunk)
        level = level_ref[:, lanes]
        for l in range(levels):
            value = jnp.where(level == l, value_ref[:, lanes], 0.0)
            quarter, value = doubled(quarter_ref[:, lanes], value)
            for start in range(0, LANES, size):
                inner = picked_tile(quarter, value, start)
                if start < REACH:
                    inner = cut(inner, row + start >= REACH)
                if start + size > cells_y - REACH:
                    inner = cut(inner, row + start < cells_y - REACH)
                if start >= LANES - MARGIN:
                    rim = picked_tile(quarter, value, start - LANES)
                elif start + size > HALF - REACH and start < HALF + MARGIN:
                    rim = picked_tile(quarter, value, start + cells_y - HALF)
                    rim = cut(rim, row + start >= HALF - REACH) if start < HALF - REACH else rim
                elif start < REACH:
                    rim = picked_tile(quarter, value, start)
                    rim = cut(rim, row + start < REACH) if start + size > REACH else rim
                else:
                    rim = jnp.zeros_like(value)
                place = slice(l * LANES + start, l * LANES + start + size)
                inner_ref[place, lanes] = inner
                rim_ref[place, lanes] = rim


def sampled_part(round_ref, weight_ref, quarter_ref, value_ref, lanes, comps):
    wide_x = round_ref.shape[0] // comps
    partial = jnp.dot(round_ref[...], weight_ref[:, lanes], preferred_element_type=jnp.float32)
    quarter, value = quarter_ref[:, lanes], value_ref[:, lanes]
    totals = [jnp.zeros_like(value)] * comps
    for row in range(0, wide_x, ROWS):
        here = quarter == (MARGIN - row) // 4
        for c in range(comps):
            start = c * wide_x + row
            totals[c] = jnp.where(here, partial[start : start + ROWS], totals[c])
    return [jnp.sum(total * value, axis=0, keepdims=True) for total in totals]


def inner_kernel(
    shape, chunk, levels, parity_ref, quarter_ref, value_ref, weight_ref, grid_ref, far_x, near_x,
    inner_ref, rim_ref, sampled_ref, moved_ref, carried_ref, sweep_ref, round_ref,
):
    cells_x, cells_y, _, _ = shape
    items = grid_ref.shape[0]
    comps = items // levels
    slots = quarter_ref.shape[1]
    wide_x = cells_x + SPAN
    rows = cells_x + 2 * PAD
    lane = lane_index(rows)
    for k, inner, edge in extended_rows(parity_ref[0:1], grid_ref, near_x, far_x, cells_y):
        moved_ref[k, ROWS : ROWS + rows] = inner
        low = jnp.where(lane < RIM, inner, jnp.where(lane >= LANES - MARGIN, edge, 0.0))
        high = jnp.where(lane >= LANES - RIM, inner, jnp.where(lane < MARGIN, edge, 0.0))
        rim_ref[k] = low + rolled(high, HALF)
    first_steps(moved_ref, carried_ref, sweep_ref, levels, comps, rows)
    size = 2 * ROWS
    for row in range(0, wide_x, size):
        start = ROWS + PAD - MARGIN + row
        results = sweep(sweep_ref, carried_ref, levels, comps, start, size)
        for k in range(items):
            level, c = k // comps, k % comps
            place = slice(c * wide_x + row, c * wide_x + row + size)
            round_ref[place, level * LANES : (level + 1) * LANES] = results[k].astype(jnp.bfloat16)
            if MARGIN <= row < MARGIN + cells_x:
                inner_ref[k, row - MARGIN : row - MARGIN + size] = results[k]
    for first in range(0, slots, chunk):
        lanes = slice(first, first + chunk)
        parts = sampled_part(round_ref, weight_ref, quarter_ref, value_ref, lanes, comps)
        for c in range(comps):
            sampled_ref[c : c + 1, lanes] = parts[c]


def unfolded(folded, rows):
    return expanded(
        jnp.concatenate(
            [rolled(folded, -row)[: min(SPAN, rows - row)] for row in range(0, rows, SPAN)], axis=0
        )
    )


def finish_kernel(
    shape, chunk, parity_ref, quarter_ref, value_ref, weight_ref, inner_ref, rim_ref, part_ref,
    near_y, far_y, next_ref, sampled_ref, moved_ref, carried_ref, sweep_ref, round_ref,
):
    cells_x, cells_y, _, _ = shape
    items = rim_ref.shape[0]
    groups = -(-items // EDGE_PER)
    levels, comps = next_ref.shape[:2]
    slots = quarter_ref.shape[1]
    wide_x = cells_x + SPAN
    rows = cells_x + 2 * PAD
    lane = lane_index(rows)
    befores, afters = ordered(parity_ref[1:2], near_y, far_y)
    turned = HALF + MARGIN + REACH
    high_halo = (lane >= turned) & (lane < turned + HALO * items)
    both = ((lane + MARGIN) & (HALF - 1)) < SPAN
    outer = ((lane >= LANES - REACH) & (lane < LANES - MARGIN)) | (
        (lane >= HALF + MARGIN) & (lane < HALF + REACH)
    )
    size = rows - ROWS
    halo = jnp.where(
        high_halo,
        rolled(unfolded(afters[groups * size :], size), turned),
        unfolded(befores[groups * size :], size),
    )
    for group in range(groups):
        before = expanded(befores[group * size : (group + 1) * size])
        after = expanded(rolled(afters[group * size : (group + 1) * size], HALF))
        for k in range(group * EDGE_PER, min((group + 1) * EDGE_PER, items)):
            slot = k % EDGE_PER
            window = ((lane + (LANES + MARGIN - SPAN * slot)) & (LANES - 1)) < SPAN
            main = rolled(jnp.where(window, before, after), -SPAN * slot)
            value = rim_ref[k] + jnp.where(both, main, 0.0)
            value = jnp.where(outer, rolled(halo, -REACH - HALO * k), value)
            moved_ref[k, ROWS : ROWS + rows] = value

    first_steps(moved_ref, carried_ref, sweep_ref, levels, comps, rows)
    size = 2 * ROWS
    lane = lane_index(size)
    for row in range(0, wide_x, size):
        start = ROWS + PAD - MARGIN + row
        results = sweep(sweep_ref, carried_ref, levels, comps, start, size)
        for k in range(items):
            level, c = k // comps, k % comps
            place = slice(c * wide_x + row, c * wide_x + row + size)
            round_ref[place, level * LANES : (level + 1) * LANES] = results[k].astype(jnp.bfloat16)
        if not MARGIN <= row < MARGIN + cells_x:
            continue
        place = slice(row - MARGIN, row - MARGIN + size)
        for k in range(items):
            low, high = results[k], rolled(results[k], HALF)
            inner = inner_ref[k, place]
            inner = jnp.where(lane < REACH, low, jnp.where(lane >= LANES - REACH, high, inner))
            next_ref[k // comps, k % comps, place] = inner

    for first in range(0, slots, chunk):
        lanes = slice(first, first + chunk)
        parts = sampled_part(round_ref, weight_ref, quarter_ref, value_ref, lanes, comps)
        for c in range(comps):
            sampled_ref[c, 0, :, lanes] = part_ref[c : c + 1, lanes] + parts[c]


def whole(count):
    return [pl.BlockSpec(memory_space=pltpu.VMEM)] * count


def swap_pairs(axis):
    size = lax.axis_size(axis)
    if size % 2:
        raise ValueError("odd axis")
    far_pairs = [(i, (i - 1 if i % 2 == 0 else i + 1) % size) for i in range(size)]
    return far_pairs, [(i, i ^ 1) for i in range(size)]


def body(velocity, marker_cell, marker_frac, marker_force, fish_owner):
    levels, comps, cells_x, cells_y = velocity.shape
    slots = marker_cell.shape[3]
    items = levels * comps
    shape = (cells_x, cells_y, cells_x * lax.axis_size("gx"), cells_y * lax.axis_size("gy"))
    wide_x = cells_x + SPAN
    rows = cells_x + 2 * PAD
    chunk = min(512, slots)
    width = cells_y + LANES
    groups = -(-items // EDGE_PER)
    params = pltpu.CompilerParams(vmem_limit_bytes=32 * 1024 * 1024)
    edge_x = jax.ShapeDtypeStruct(((items + groups) * STRIP, LANES), jnp.bfloat16)
    half = (items, wide_x // 2, width)
    arrays = (fish_owner, velocity, marker_cell, marker_frac, marker_force)
    far_half, far, force, dense_y, quarter, value, quarter_y, value_y, level, parity, near_velocity = (
        pl.pallas_call(
        functools.partial(far_kernel, shape, min(1024, slots)),
        out_shape=(
            jax.ShapeDtypeStruct(half, jnp.float32),
            edge_x,
            jax.ShapeDtypeStruct((items, 2 * ROWS, slots), jnp.bfloat16),
            jax.ShapeDtypeStruct((width, slots), jnp.bfloat16),
            jax.ShapeDtypeStruct((ROWS, slots), jnp.int32),
            jax.ShapeDtypeStruct((ROWS, slots), jnp.float32),
            jax.ShapeDtypeStruct((ROWS, slots), jnp.int32),
            jax.ShapeDtypeStruct((ROWS, slots), jnp.float32),
            jax.ShapeDtypeStruct((1, slots), jnp.int32),
            jax.ShapeDtypeStruct((2, LANES), jnp.int32),
            jax.ShapeDtypeStruct(velocity.shape, velocity.dtype),
        ),
        in_specs=[pl.BlockSpec(memory_space=pltpu.HBM)] * 5,
        out_specs=tuple(whole(11)),
        scratch_shapes=[pltpu.VMEM(a.shape, a.dtype) for a in arrays if a is not velocity]
        + [pltpu.SemaphoreType.DMA((5,))],
        compiler_params=params,
        name="spread_far",
    )(*(pltpu.with_memory_space_constraint(a, pltpu.HBM) for a in arrays))
    )
    far_pairs, near_pairs = swap_pairs("gx")
    far_x = lax.ppermute(far, "gx", far_pairs)
    grid, near = pl.pallas_call(
        functools.partial(near_kernel, shape, slots),
        out_shape=(jax.ShapeDtypeStruct((items, wide_x, width), jnp.float32), edge_x),
        in_specs=whole(5),
        out_specs=tuple(whole(2)),
        scratch_shapes=[pltpu.VMEM(half, jnp.float32)],
        compiler_params=params,
        cost_estimate=pl.CostEstimate(
            flops=items * wide_x * width * slots, bytes_accessed=4 * items * wide_x * width,
            transcendentals=0,
        ),
        name="spread_near",
    )(near_velocity, far_half, force, dense_y, quarter)
    near_x = lax.ppermute(near, "gx", near_pairs)
    weights = jax.ShapeDtypeStruct((levels * LANES, slots), jnp.bfloat16)
    inner_weight, rim_weight, parity = pl.pallas_call(
        functools.partial(weight_kernel, shape, chunk),
        out_shape=(weights, weights, jax.ShapeDtypeStruct(parity.shape, parity.dtype)),
        in_specs=whole(4),
        out_specs=tuple(whole(3)),
        compiler_params=params,
        cost_estimate=pl.CostEstimate(
            flops=2 * levels * LANES * slots, bytes_accessed=4 * levels * LANES * slots,
            transcendentals=0,
        ),
        name="weights",
    )(parity, quarter_y, value_y, level)
    edge_y = jax.ShapeDtypeStruct((groups * (rows - ROWS) + SPAN, LANES), jnp.bfloat16)
    near, far = pl.pallas_call(
        functools.partial(pack_kernel, shape),
        out_shape=(edge_y, edge_y),
        in_specs=whole(4),
        out_specs=tuple(whole(2)),
        compiler_params=params,
        name="pack",
    )(parity, grid, far_x, near_x)
    far_pairs, near_pairs = swap_pairs("gy")
    near_y = lax.ppermute(near, "gy", near_pairs)
    far_y = lax.ppermute(far, "gy", far_pairs)
    field = pltpu.VMEM((items, rows + 2 * ROWS, LANES), jnp.float32)
    rounded = pltpu.VMEM((comps * wide_x, levels * LANES), jnp.bfloat16)
    inner, rim, part = pl.pallas_call(
        functools.partial(inner_kernel, shape, chunk, levels),
        out_shape=(
            jax.ShapeDtypeStruct((items, cells_x, LANES), jnp.float32),
            jax.ShapeDtypeStruct((items, rows, LANES), jnp.float32),
            jax.ShapeDtypeStruct((comps, slots), jnp.float32),
        ),
        in_specs=whole(7),
        out_specs=tuple(whole(3)),
        scratch_shapes=[field, field, field, rounded],
        compiler_params=params,
        cost_estimate=pl.CostEstimate(
            flops=2 * items * wide_x * LANES * slots, bytes_accessed=16 * items * rows * LANES,
            transcendentals=0,
        ),
        name="inner",
    )(parity, quarter, value, inner_weight, grid, far_x, near_x)
    return pl.pallas_call(
        functools.partial(finish_kernel, shape, chunk),
        out_shape=(
            jax.ShapeDtypeStruct(velocity.shape, jnp.float32),
            jax.ShapeDtypeStruct((comps, 1, 1, slots), jnp.float32),
        ),
        in_specs=whole(9),
        out_specs=tuple(whole(2)),
        scratch_shapes=[field, field, field, rounded],
        compiler_params=params,
        name="finish",
    )(parity, quarter, value, rim_weight, inner, rim, part, near_y, far_y)


def solution(mesh):
    placed = (
        P(None, None, "gx", "gy"),
        P(None, "gx", "gy", None),
        P(None, "gx", "gy", None),
        P(None, "gx", "gy", None),
        P(),
    )
    return jax.shard_map(
        body,
        mesh=mesh,
        in_specs=placed,
        out_specs=(P(None, None, "gx", "gy"), P(None, "gx", "gy", None)),
        check_vma=False,
    )
```
